32 devices in a mesh: batch: 8 (over z, y), seq: 4 (over x, core).
Axes of the slice: x: 2, y: 2, z: 4, core: 2. Of those that a mesh axis runs over, the one named last changes fastest.
Arguments:
- layer_activations: bfloat16 [8, 4096, 512], P('batch', 'seq'), may hold values from -6 to 6
- sequence_extents: int32 [8], P('batch'), may hold values from 3073 to 4096, as said below
- position_cluster_label: int32 [8, 4096], P('batch', 'seq'), may hold values from 0 to 31, as said below
- cluster_sharpness: float32 [1], replicated, may hold values from 0.7 to 1.4
- heed_scale_factor: bfloat16 [512], replicated, may hold values from 0.5 to 1.5
- triple_entry_matrix: bfloat16 [512, 1536], replicated, may hold values from -0.25 to 0.25
- heed_exit_matrix: bfloat16 [512, 512], replicated, may hold values from -6 to 6
- blend_scale_factor: bfloat16 [512], replicated, may hold values from 0.5 to 1.5
- router_matrix: bfloat16 [512, 2], replicated, may hold values from -0.25 to 0.25
- specialist_entry_matrix: bfloat16 [2, 512, 2048], replicated, may hold values from -1 to 1
- specialist_exit_matrix: bfloat16 [2, 2048, 512], replicated, may hold values from -2 to 2
- upstream_derivative: bfloat16 [8, 4096, 512], P('batch', 'seq'), may hold values from -6 to 6
Outputs:
- block_out: bfloat16 [8, 4096, 512], P('batch', 'seq')
- tokens_grad: bfloat16 [8, 4096, 512], P('batch', 'seq')
- grad_gain_attn: float32 [512], replicated
- grad_qkv: float32 [512, 1536], replicated
- grad_out: float32 [512, 512], replicated
- grad_gain_mix: float32 [512], replicated
- grad_ctrl: float32 [512, 2], replicated
- grad_in: float32 [2, 512, 2048], replicated
- grad_down: float32 [2, 2048, 512], replicated
The draws below stay inside these ranges and needn't reach their ends.
Inputs may be any that keep to these rules, and one draw needn't show every extreme that they name: `sequence_extents`: one sequence has length 4096 in every draw. `position_cluster_label`: within the 1 x 1024 positions that share a batch index and a seq index, every value is held by exactly 32 positions, in no causal order.
All inputs are finite; a program needn't handle non-finite values.
Results may differ from the reference program's by a relative error of at most 0.024.
Values may be sent and summed in bfloat16 or wider, within the bound.
No kernel may reach another device: no remote copies, remote signals or barrier semaphores. Data moves between devices by JAX's collectives and lax.ppermute only.
A program may use at most 256 MiB of HBM per device.

```python
import jax
import jax.numpy as jnp
from jax import lax

D = 512
HEADS = 8
HEAD = 64
H = 2048
EXPERTS = 2
GROUP = 32
LEN = 4096
SEQ_DEV = 1
POS_DEV = 1024
SEQS = 8
GROUPS_DEV = 32
N_SEQ = 4


def draw_sequence_extents(key, part):
    key = jax.random.fold_in(key, 11)
    first_key, second_key = jax.random.split(key)
    base_len = jax.random.randint(first_key, (SEQS,), LEN - POS_DEV + 1, LEN + 1)
    chosen = jax.random.randint(second_key, (), 0, SEQS)
    return jnp.where(jnp.arange(SEQS) == chosen, LEN, base_len).astype(jnp.int32)


def draw_position_cluster_label(key, part):
    key = jax.random.fold_in(key, 23)
    batch_blocks = SEQS // SEQ_DEV
    seq_blocks = LEN // POS_DEV
    block_size = SEQ_DEV * POS_DEV
    block_keys = jax.random.split(key, batch_blocks * seq_blocks)

    def one_block(block_key):
        return jax.random.permutation(block_key, block_size) // GROUP
    slots = jax.vmap(one_block)(block_keys)
    slots = slots.reshape(batch_blocks, seq_blocks, SEQ_DEV, POS_DEV).transpose(0, 2, 1, 3)
    return slots.reshape(SEQS, LEN).astype(jnp.int32)


def levels(key, extent, cuts, low, high):
    level, own = 1.0, jax.random.fold_in(key, 6)
    for axis_at, blocks in cuts:
        heights = jnp.exp(jax.random.uniform(jax.random.fold_in(own, axis_at), (blocks,), jnp.float32, low / len(cuts), high / len(cuts)))
        level = level * jnp.repeat(heights, extent[axis_at] // blocks).reshape([-1 if axis == axis_at else 1 for axis in range(len(extent))])
    return level


def centred(own_key, dims, width, bound, shards=(), kind=jnp.bfloat16):
    values = width * jax.random.normal(own_key, dims, jnp.float32)
    if shards:
        values = values * levels(own_key, dims, shards, -0.22, 0.18)
    return jnp.clip(values, -bound, bound).astype(kind)


def setup_inputs(seed: int = 0) -> dict:
    arg_keys = jax.random.split(jax.random.key(seed), 13)
    return {
        "layer_activations": centred(arg_keys[0], (SEQS, LEN, D), 1.0, 6.0, ((0, 8), (1, 4))),
        "sequence_extents": draw_sequence_extents(jax.random.fold_in(arg_keys[12], 71), 0),
        "position_cluster_label": draw_position_cluster_label(jax.random.fold_in(arg_keys[12], 71), 0),
        "cluster_sharpness": jnp.clip(jax.random.uniform(arg_keys[3], (1,), jnp.float32, 0.7, 1.4), 0.7, 1.4),
        "heed_scale_factor": jnp.clip(1.0 + 0.1 * jax.random.normal(arg_keys[4], (D,), jnp.float32), 0.5, 1.5).astype(jnp.bfloat16),
        "triple_entry_matrix": centred(arg_keys[5], (D, 3 * D), D ** -0.5, 0.25),
        "heed_exit_matrix": centred(arg_keys[6], (D, D), (max(D * 4 // LEN, 1)) ** -0.5, 6.0),
        "blend_scale_factor": jnp.clip(1.0 + 0.1 * jax.random.normal(arg_keys[7], (D,), jnp.float32), 0.5, 1.5).astype(jnp.bfloat16),
        "router_matrix": centred(arg_keys[8], (D, EXPERTS), D ** -0.5, 0.25),
        "specialist_entry_matrix": centred(arg_keys[9], (EXPERTS, D, H), (D // 16) ** -0.5, 1.0),
        "specialist_exit_matrix": centred(arg_keys[10], (EXPERTS, H, D), (max(H // 256, 1)) ** -0.5, 2.0),
        "upstream_derivative": centred(arg_keys[11], (SEQS, LEN, D), 1.0, 6.0, ((0, 8), (1, 4))),
    }


EPSILON = 1e-06
MASKED = -1e+30
HIGHEST = lax.Precision.HIGHEST

@jax.custom_vjp
def low(v):
    return lax.optimization_barrier(v.astype(jnp.bfloat16)).astype(jnp.float32)

@jax.custom_vjp
def low_back(v):
    return v

def low_keep(v):
    return (low(v), None)

def low_pass(kept, grad):
    return (grad,)

def back_keep(v):
    return (v, None)

def back_low(kept, grad):
    return (low(grad),)
low.defvjp(low_keep, low_pass)
low_back.defvjp(back_keep, back_low)

def rms_norm(values, gain):
    inverse = lax.rsqrt(lax.optimization_barrier(jnp.mean(values * values, axis=-1, keepdims=True)) + EPSILON)
    return values * inverse * gain

def cluster_blend_shares(logit_vals, cluster_assignment):
    spread_mask = cluster_assignment[:, :, None]
    masked_vals = jnp.where(spread_mask, logit_vals[None, :, :], -jnp.inf)
    group_peak = lax.optimization_barrier(jnp.max(masked_vals, axis=1))
    token_peak = lax.optimization_barrier(jnp.sum(jnp.where(spread_mask, group_peak[:, None, :], 0.0), axis=0))
    raised = jnp.exp(logit_vals - token_peak)
    group_total = lax.optimization_barrier(jnp.sum(jnp.where(spread_mask, raised[None, :, :], 0.0), axis=1))
    token_total = lax.optimization_barrier(jnp.sum(jnp.where(spread_mask, group_total[:, None, :], 0.0), axis=0))
    return raised / token_total

def seq_attention(pieces):
    query_seq, key_seq, value_seq, limit_len = pieces
    block_rows = min(512, LEN)
    score_scale = HEAD ** (-0.5)
    query_blocks = query_seq.reshape(LEN // block_rows, block_rows, HEADS, HEAD)
    starts = jnp.arange(LEN // block_rows, dtype=jnp.int32) * block_rows
    key_pos = jnp.arange(LEN, dtype=jnp.int32)

    def row_block(parts):
        query_block, start_row = parts
        query_pos = start_row + jnp.arange(block_rows, dtype=jnp.int32)
        raw_scores = jnp.einsum('qhd,khd->hqk', query_block, key_seq, precision=HIGHEST) * score_scale
        scores = low_back(raw_scores)
        allowed = (key_pos[None, :] <= query_pos[:, None]) & (key_pos[None, :] < limit_len)
        scores = jnp.where(allowed[None, :, :], scores, MASKED)
        row_peak = lax.optimization_barrier(jnp.max(scores, axis=2, keepdims=True))
        raised = jnp.exp(scores - row_peak)
        attn_probs = low(raised / lax.optimization_barrier(jnp.sum(raised, axis=2, keepdims=True)))
        return jnp.einsum('hqk,khd->qhd', attn_probs, value_seq, precision=HIGHEST)
    result = lax.map(jax.checkpoint(row_block), (query_blocks, starts))
    return result.reshape(LEN, HEADS, HEAD)

def blend_portion(blend_lines, score_lines, assigned_lines, sharpness_divisor, expand_matrix, contract_matrix):
    cluster_assignment = assigned_lines[None, :] == jnp.arange(GROUPS_DEV, dtype=jnp.int32)[:, None]
    blend_coefficients = low(cluster_blend_shares(score_lines / sharpness_divisor, cluster_assignment))
    mixing = jnp.where(cluster_assignment[None, :, :], blend_coefficients.T[:, None, :], 0.0)
    mixed = low(low_back(jnp.einsum('egt,td->egd', mixing, blend_lines, precision=HIGHEST)))
    inner = low_back(jnp.einsum('egd,edh->egh', mixed, expand_matrix, precision=HIGHEST))
    active = low(jax.nn.gelu(inner, approximate=False))
    expert_out = low(low_back(jnp.einsum('egh,ehd->egd', active, contract_matrix, precision=HIGHEST)))
    return jnp.einsum('egt,egd->td', mixing, expert_out, precision=HIGHEST)

def layer_apply_step(layer_arguments, first_scale_factor, triple_matrix, exit_matrix, second_scale_factor, router_coefficients, expand_matrix, contract_matrix, extent_segment, assignment_segment, sharpness_divisor):
    flat_rows = layer_arguments.reshape(SEQ_DEV * LEN, D)
    normed = low(rms_norm(flat_rows, first_scale_factor))
    qkv_vals = low(low_back(jnp.dot(normed, triple_matrix, precision=HIGHEST)))
    qkv_vals = qkv_vals.reshape(SEQ_DEV, LEN, 3, HEADS, HEAD)
    attended = lax.map(seq_attention, (qkv_vals[:, :, 0], qkv_vals[:, :, 1], qkv_vals[:, :, 2], extent_segment))
    attended = low(low_back(attended.reshape(SEQ_DEV * LEN, D)))
    branch = low_back(jnp.dot(attended, exit_matrix, precision=HIGHEST))
    resid = flat_rows + branch
    blend_lines = low(rms_norm(resid, second_scale_factor))
    logit_vals = low_back(jnp.dot(blend_lines, router_coefficients, precision=HIGHEST))
    parts_in = blend_lines.reshape(SEQ_DEV, N_SEQ, POS_DEV, D).transpose(1, 0, 2, 3).reshape(N_SEQ, SEQ_DEV * POS_DEV, D)
    parts_logit = logit_vals.reshape(SEQ_DEV, N_SEQ, POS_DEV, EXPERTS).transpose(1, 0, 2, 3).reshape(N_SEQ, SEQ_DEV * POS_DEV, EXPERTS)
    parts_slot = assignment_segment.reshape(SEQ_DEV, N_SEQ, POS_DEV).transpose(1, 0, 2).reshape(N_SEQ, SEQ_DEV * POS_DEV)

    def one_part(lines_entering, lines_scored, lines_assigned):
        return blend_portion(lines_entering, lines_scored, lines_assigned, sharpness_divisor, expand_matrix, contract_matrix)
    spread = jax.vmap(one_part)(parts_in, parts_logit, parts_slot)
    spread = spread.reshape(N_SEQ, SEQ_DEV, POS_DEV, D).transpose(1, 0, 2, 3).reshape(SEQ_DEV * LEN, D)
    return (resid + spread).reshape(SEQ_DEV, LEN, D)

def reference(layer_activations, sequence_extents, position_cluster_label, cluster_sharpness, heed_scale_factor, triple_entry_matrix, heed_exit_matrix, blend_scale_factor, router_matrix, specialist_entry_matrix, specialist_exit_matrix, upstream_derivative):
    params = (heed_scale_factor.astype(jnp.float32), triple_entry_matrix.astype(jnp.float32), heed_exit_matrix.astype(jnp.float32), blend_scale_factor.astype(jnp.float32), router_matrix.astype(jnp.float32), specialist_entry_matrix.astype(jnp.float32), specialist_exit_matrix.astype(jnp.float32))
    blocks = SEQS // SEQ_DEV
    sharpness_divisor = cluster_sharpness[0].astype(jnp.float32)
    xs_in = layer_activations.reshape(blocks, SEQ_DEV, LEN, D)
    xs_cot = upstream_derivative.reshape(blocks, SEQ_DEV, LEN, D)
    xs_len = sequence_extents.reshape(blocks, SEQ_DEV)
    xs_slot = position_cluster_label.reshape(blocks, SEQ_DEV, LEN)

    def scan_step(running, scan_item):
        x_block, cot_block, extent_segment, assignment_segment = scan_item

        def forward_fn(layer_arguments, first_scale_factor, triple_matrix, exit_matrix, second_scale_factor, router_coefficients, expand_matrix, contract_matrix):
            return layer_apply_step(layer_arguments, first_scale_factor, triple_matrix, exit_matrix, second_scale_factor, router_coefficients, expand_matrix, contract_matrix, extent_segment, assignment_segment, sharpness_divisor)
        out_block, pullback = jax.vjp(forward_fn, x_block.astype(jnp.float32), params[0], params[1], params[2], params[3], params[4], params[5], params[6])
        gradients = pullback(cot_block.astype(jnp.float32))
        new_running = tuple((summed + increment for summed, increment in zip(running, gradients[1:])))
        return (new_running, (out_block.astype(jnp.bfloat16), gradients[0].astype(jnp.bfloat16)))
    start_sums = tuple((jnp.zeros(weight_arr.shape, jnp.float32) for weight_arr in params))
    final_sums, outputs = lax.scan(scan_step, start_sums, (xs_in, xs_cot, xs_len, xs_slot))
    block_out = outputs[0].reshape(SEQS, LEN, D)
    tokens_grad = outputs[1].reshape(SEQS, LEN, D)
    return (block_out, tokens_grad, final_sums[0], final_sums[1], final_sums[2], final_sums[3], final_sums[4], final_sums[5], final_sums[6])
```

```python
import jax
import jax.numpy as jnp
from jax import lax
from jax.experimental import pallas as pl
from jax.experimental.pallas import tpu as pltpu
from jax.sharding import PartitionSpec as P

HEADS = 8
HEAD = 64
GROUP = 32
EPSILON = 1e-06
LOG2E = 1.4426950408889634
SC = 0.125 * LOG2E
bf = jnp.bfloat16
f32 = jnp.float32
CORE = [(0, 1), (1, 0), (2, 3), (3, 2)]
CHIP = [(0, 2), (1, 3), (2, 0), (3, 1)]
UP = [(0, 2), (1, 3)]
DOWN = [(2, 0), (3, 1)]

BQ=512; NK=2048; NQ=2048
NT=(((1,),(1,)),((),()))
TN=(((0,),(0,)),((),()))
def row_iota(shape): return lax.broadcasted_iota(jnp.int32,shape,0)
def col_iota(shape): return lax.broadcasted_iota(jnp.int32,shape,1)

def scores(kv, q, s_ref, slot, kmax, q0, limit, causal, CH=512):
    mx=None
    for k0 in range(0,kmax,CH):
        s=lax.dot_general(kv[k0:k0+CH,:],q,NT,preferred_element_type=f32)
        if causal:
            if k0>=1024:
                kp=row_iota(s.shape)+k0
                s=jnp.where(kp<limit,s,-1e30)
            if k0+CH>q0:
                s=jnp.where(row_iota(s.shape)+(k0-q0)<=col_iota(s.shape),s,-1e30)
        s_ref[slot,k0:k0+CH,:]=s
        m=jnp.max(s,axis=0,keepdims=True)
        mx=m if mx is None else jnp.maximum(mx,m)
    return mx
def finish(vt, s_ref, slot, mx, kmax, p_ref, o_ref, st_ref, q0, i, CH=512):
    mc=mx*SC
    acc=None
    for k0 in range(0,kmax,CH):
        p=jnp.exp2(s_ref[slot,k0:k0+CH,:]*SC-mc).astype(bf)
        p_ref[0,i,k0:k0+CH,:]=p
        d=jnp.dot(vt[:,k0:k0+CH],p,preferred_element_type=f32)
        acc=d if acc is None else acc+d
    l=acc[0:1,:]
    o_ref[0,:,q0:q0+BQ]=(acc[64:128,:]*(1.0/l)).astype(bf)
    st_ref[0,0:1,q0:q0+BQ]=mc
    st_ref[0,1:2,q0:q0+BQ]=l
def local_fwd_kernel(lim_ref, q_ref, kv_ref, p_ref, o_ref, st_ref, s_ref, vt_ref):
    limit=lim_ref[0]
    kv=kv_ref[...]
    vt=kv.T
    vt_ref[...]=jnp.where(row_iota(vt.shape)<64,jnp.ones((),bf),vt)
    nb=NQ//BQ
    mxs=[None]*nb
    mxs[0]=scores(kv_ref,q_ref[0:BQ,:],s_ref,0,BQ,0,limit,True)
    for i in range(nb):
        if i+1<nb:
            mxs[i+1]=scores(kv_ref,q_ref[(i+1)*BQ:(i+2)*BQ,:],s_ref,(i+1)%2,(i+2)*BQ,(i+1)*BQ,limit,True)
        finish(vt_ref,s_ref,i%2,mxs[i],(i+1)*BQ,p_ref,o_ref,st_ref,i*BQ,i)
def local_fwd(lim, qkv, heads=4):
    return pl.pallas_call(local_fwd_kernel, grid=(heads,),
        in_specs=[pl.BlockSpec(memory_space=pltpu.SMEM),
                  pl.BlockSpec((NQ,128),lambda h:(0,2*h)),pl.BlockSpec((NK,128),lambda h:(0,2*h+1))],
        out_specs=[pl.BlockSpec((1,NQ//BQ,NK,BQ),lambda h:(h,0,0,0)),pl.BlockSpec((1,64,NQ),lambda h:(h,0,0)),pl.BlockSpec((1,8,NQ),lambda h:(h,0,0))],
        out_shape=[jax.ShapeDtypeStruct((heads,NQ//BQ,NK,BQ),bf),jax.ShapeDtypeStruct((heads,64,NQ),bf),jax.ShapeDtypeStruct((heads,8,NQ),f32)],
        scratch_shapes=[pltpu.VMEM((2,NK,BQ),f32),pltpu.VMEM((128,NK),bf)],
        compiler_params=pltpu.CompilerParams(vmem_limit_bytes=56*2**20))(lim,qkv,qkv)
def cross_fwd_kernel(q_ref, kv_ref, p_ref, o_ref, st_ref, s_ref, vt_ref):
    vt=kv_ref[...].T
    vt_ref[...]=jnp.where(row_iota(vt.shape)<64,jnp.ones((),bf),vt)
    nb=NQ//BQ
    mxs=[None]*nb
    mxs[0]=scores(kv_ref,q_ref[0:BQ,:],s_ref,0,NK,0,None,False)
    for i in range(nb):
        if i+1<nb:
            mxs[i+1]=scores(kv_ref,q_ref[(i+1)*BQ:(i+2)*BQ,:],s_ref,(i+1)%2,NK,(i+1)*BQ,None,False)
        finish(vt_ref,s_ref,i%2,mxs[i],NK,p_ref,o_ref,st_ref,i*BQ,i)
def cross_fwd(q, kv):
    return pl.pallas_call(cross_fwd_kernel, grid=(1,),
        in_specs=[pl.BlockSpec((NQ,128),lambda h:(0,0)),pl.BlockSpec((NK,128),lambda h:(0,0))],
        out_specs=[pl.BlockSpec((1,NQ//BQ,NK,BQ),lambda h:(h,0,0,0)),pl.BlockSpec((1,64,NQ),lambda h:(h,0,0)),pl.BlockSpec((1,8,NQ),lambda h:(h,0,0))],
        out_shape=[jax.ShapeDtypeStruct((1,NQ//BQ,NK,BQ),bf),jax.ShapeDtypeStruct((1,64,NQ),bf),jax.ShapeDtypeStruct((1,8,NQ),f32)],
        scratch_shapes=[pltpu.VMEM((2,NK,BQ),f32),pltpu.VMEM((128,NK),bf)],
        compiler_params=pltpu.CompilerParams(vmem_limit_bytes=56*2**20))(q,kv)

def bwd_block(kv_ref, kt_ref, q_ref, doT, delta, p_ref, i, kmax, q0, dkv_ref, dq_ref, CH=512, first=None):
    dob=doT.astype(bf)
    zer=jnp.zeros((64,BQ),bf)
    rhs=jnp.concatenate([zer,dob],axis=0)
    q=q_ref[q0:q0+BQ,:]
    dnat=rhs.T
    acc=None
    for k0 in range(0,kmax,CH):
        dp=jnp.dot(kv_ref[k0:k0+CH,:],rhs,preferred_element_type=f32)
        p=p_ref[0,i,k0:k0+CH,:]
        ds=(p.astype(f32)*(dp-delta)).astype(bf)
        d=jnp.dot(kt_ref[:,k0:k0+CH],ds,preferred_element_type=f32)
        acc=d if acc is None else acc+d
        g=jnp.dot(ds,q,preferred_element_type=f32)+jnp.dot(p,dnat,preferred_element_type=f32)
        isfirst = (i==0) if first is None else (k0>=first)
        if isfirst: dkv_ref[0,k0:k0+CH,:]=g
        else: dkv_ref[0,k0:k0+CH,:]+=g
    dq_ref[0,:,q0:q0+BQ]=(acc*0.125).astype(dq_ref.dtype)
def local_bwd_kernel(q_ref, kv_ref, p_ref, do_ref, st_ref, dkv_ref, dq_ref, kt_ref):
    kt_ref[...]=kv_ref[...].T[0:64,:]
    for i in range(NQ//BQ):
        q0=i*BQ
        r=st_ref[0,0:1,q0:q0+BQ]
        delta=st_ref[0,1:2,q0:q0+BQ]
        doT=do_ref[0,:,q0:q0+BQ].astype(f32)*r
        bwd_block(kv_ref,kt_ref,q_ref,doT,delta,p_ref,i,q0+BQ,q0,dkv_ref,dq_ref,first=q0)
def local_bwd(qkv,p,do,st,heads=4):
    return pl.pallas_call(local_bwd_kernel, grid=(heads,),
        in_specs=[pl.BlockSpec((NQ,128),lambda h:(0,2*h)),pl.BlockSpec((NK,128),lambda h:(0,2*h+1)),
                  pl.BlockSpec((1,NQ//BQ,NK,BQ),lambda h:(h,0,0,0)),pl.BlockSpec((1,64,NQ),lambda h:(h,0,0)),pl.BlockSpec((1,8,NQ),lambda h:(h,0,0))],
        out_specs=[pl.BlockSpec((1,NK,128),lambda h:(h,0,0)),pl.BlockSpec((1,64,NQ),lambda h:(h,0,0))],
        out_shape=[jax.ShapeDtypeStruct((heads,NK,128),f32),jax.ShapeDtypeStruct((heads,64,NQ),bf)],
        scratch_shapes=[pltpu.VMEM((64,NK),bf)],
        compiler_params=pltpu.CompilerParams(vmem_limit_bytes=56*2**20))(qkv,qkv,p,do,st)
def cross_bwd_kernel(q_ref, kv_ref, p_ref, do_ref, st_ref, dkv_ref, dq_ref, kt_ref):
    kt_ref[...]=kv_ref[...].T[0:64,:]
    for i in range(NQ//BQ):
        q0=i*BQ
        r=st_ref[0,0:1,q0:q0+BQ]
        delta=st_ref[0,1:2,q0:q0+BQ]
        doT=do_ref[0,:,q0:q0+BQ].astype(f32)*r
        bwd_block(kv_ref,kt_ref,q_ref,doT,delta,p_ref,i,NK,q0,dkv_ref,dq_ref)
def cross_bwd(q,kv,p,do,st):
    return pl.pallas_call(cross_bwd_kernel, grid=(1,),
        in_specs=[pl.BlockSpec((NQ,128),lambda h:(0,0)),pl.BlockSpec((NK,128),lambda h:(0,0)),
                  pl.BlockSpec((1,NQ//BQ,NK,BQ),lambda h:(h,0,0,0)),pl.BlockSpec((1,64,NQ),lambda h:(h,0,0)),pl.BlockSpec((1,8,NQ),lambda h:(h,0,0))],
        out_specs=[pl.BlockSpec((1,NK,128),lambda h:(h,0,0)),pl.BlockSpec((1,64,NQ),lambda h:(h,0,0))],
        out_shape=[jax.ShapeDtypeStruct((1,NK,128),f32),jax.ShapeDtypeStruct((1,64,NQ),bf)],
        scratch_shapes=[pltpu.VMEM((64,NK),bf)],
        compiler_params=pltpu.CompilerParams(vmem_limit_bytes=56*2**20))(q,kv,p,do,st)


def rms_norm(values, gain):
    inverse = lax.rsqrt(jnp.mean(values * values, axis=-1, keepdims=True) + EPSILON)
    return values * inverse * gain


def gelu_exact(values):
    return jax.nn.gelu(values, approximate=False)


def cluster_blend_shares(logit_vals, cluster_assignment):
    spread_mask = cluster_assignment[:, :, None]
    masked_vals = jnp.where(spread_mask, logit_vals[None, :, :], -jnp.inf)
    group_peak = jnp.max(masked_vals, axis=1)
    token_peak = jnp.sum(jnp.where(spread_mask, group_peak[:, None, :], 0.0), axis=0)
    raised = jnp.exp(logit_vals - token_peak)
    group_total = jnp.sum(jnp.where(spread_mask, raised[None, :, :], 0.0), axis=1)
    token_total = jnp.sum(jnp.where(spread_mask, group_total[:, None, :], 0.0), axis=0)
    return raised / token_total


def body(
    layer_activations,
    sequence_extents,
    position_cluster_label,
    cluster_sharpness,
    heed_scale_factor,
    triple_entry_matrix,
    heed_exit_matrix,
    blend_scale_factor,
    router_matrix,
    specialist_entry_matrix,
    specialist_exit_matrix,
    upstream_derivative,
):
    seq_count, pos_count, model_width = layer_activations.shape
    tok_count = seq_count * pos_count
    groups = tok_count // GROUP
    place = lax.axis_index("seq")
    chip = place // 2
    core = place % 2
    first = core == 0
    upper = chip == 1
    half = model_width // 2

    def ordered(mine, other, axis):
        return jnp.where(first, jnp.concatenate([mine, other], axis), jnp.concatenate([other, mine], axis))

    def pick(whole, own, axis):
        size = whole.shape[axis] // 2
        low = lax.slice_in_dim(whole, 0, size, axis=axis)
        high = lax.slice_in_dim(whole, size, 2 * size, axis=axis)
        return jnp.where(first == own, low, high)

    rows_low = layer_activations.reshape(tok_count, model_width)
    flat_rows = rows_low.astype(f32)
    pair_rows = ordered(rows_low, lax.ppermute(rows_low, "seq", CORE), 0).astype(f32)
    normed_attn, norm_attn_back = jax.vjp(rms_norm, flat_rows, heed_scale_factor.astype(f32))
    pair_normed = rms_norm(pair_rows, heed_scale_factor.astype(f32)).astype(bf)
    by_head = triple_entry_matrix.reshape(model_width, 3, HEADS, HEAD)
    own = lax.dynamic_slice_in_dim(by_head, core * 4, 4, axis=2)
    packed = jnp.stack([own[:, 0], jnp.zeros_like(own[:, 0]), own[:, 1], own[:, 2]], axis=2)
    packed = packed.reshape(model_width, 4 * 256)
    qkv = jnp.dot(pair_normed, packed, preferred_element_type=f32).astype(bf)
    payload = jnp.where(upper, jnp.concatenate([qkv[:, 512:576], qkv[:, 768:832]], 1), qkv[:, 128:256])
    got_a = lax.ppermute(payload, "seq", CHIP)
    got_b = lax.ppermute(qkv[:, 384:512], "seq", UP)
    limit = (sequence_extents - chip * 2 * pos_count).astype(jnp.int32)
    probs_near, out_near, stat_near = local_fwd(limit, qkv)
    blank = jnp.zeros((2 * pos_count, HEAD), bf)
    far_q, far_kv, far = [], [], []
    for j, got in ((0, got_a), (1, got_b)):
        far_q.append(jnp.where(upper, qkv[:, 256 * j : 256 * j + 128], jnp.concatenate([got_a[:, 64 * j : 64 * j + 64], blank], 1)))
        far_kv.append(jnp.where(upper, got, qkv[:, 256 * j + 640 : 256 * j + 768]))
        far.append(cross_fwd(far_q[j], far_kv[j]))
    out_far = jnp.concatenate([far[0][1], far[1][1]], 0)
    peak_far = jnp.concatenate([far[0][2], far[1][2]], 0)[:, 0]
    total_far = jnp.concatenate([far[0][2], far[1][2]], 0)[:, 1]
    log_far = peak_far + jnp.log2(total_far)
    got_out = lax.ppermute(out_far, "seq", UP)
    got_log = lax.ppermute(log_far, "seq", UP)
    peak_near, total_near = stat_near[:, 0], stat_near[:, 1]
    log_near = peak_near + jnp.log2(total_near)
    all_far = jnp.concatenate([out_far, got_out], 0)
    all_log = jnp.where(upper, jnp.concatenate([log_far, got_log], 0), -1e30)
    top = jnp.maximum(log_near, all_log)
    whole_log = top + jnp.log2(jnp.exp2(log_near - top) + jnp.exp2(all_log - top))
    share_near = jnp.exp2(log_near - whole_log)
    share_far = jnp.where(upper, jnp.exp2(all_log - whole_log), 0.0)
    joined = (out_near.astype(f32) * share_near[:, None, :] + jnp.where(upper, all_far.astype(f32), 0.0) * share_far[:, None, :]).astype(bf)
    flat_join = joined.reshape(half, 2 * pos_count)
    other_out = lax.ppermute(pick(flat_join, False, 1), "seq", CORE)
    attended_low = ordered(pick(flat_join, True, 1), other_out, 0).T
    branch = jnp.dot(attended_low, heed_exit_matrix, preferred_element_type=jnp.float32)
    resid = flat_rows + branch
    mix_normed, norm_mix_back = jax.vjp(rms_norm, resid, blend_scale_factor.astype(jnp.float32))
    mix_low = mix_normed.astype(jnp.bfloat16)
    logit_vals = jnp.dot(mix_low, router_matrix, preferred_element_type=jnp.float32)
    cluster_assignment = (
        position_cluster_label.reshape(tok_count)[None, :]
        == jnp.arange(groups, dtype=jnp.int32)[:, None]
    )

    def weigh(router_scores):
        return cluster_blend_shares(router_scores / cluster_sharpness[0], cluster_assignment)

    blend_coefficients, weigh_back = jax.vjp(weigh, logit_vals)
    weight_low = blend_coefficients.astype(jnp.bfloat16)
    mixing = jnp.where(
        cluster_assignment[None, :, :], weight_low.T[:, None, :], jnp.zeros((), jnp.bfloat16)
    )
    mixed_low = jnp.einsum(
        "egt,td->egd", mixing, mix_low, preferred_element_type=jnp.float32
    ).astype(jnp.bfloat16)
    inner = jnp.einsum(
        "egd,edh->egh", mixed_low, specialist_entry_matrix, preferred_element_type=jnp.float32
    )
    active, gelu_back = jax.vjp(gelu_exact, inner)
    active_low = active.astype(jnp.bfloat16)
    expert_low = jnp.einsum(
        "egh,ehd->egd", active_low, specialist_exit_matrix, preferred_element_type=jnp.float32
    ).astype(jnp.bfloat16)
    spread = jnp.einsum("egt,egd->td", mixing, expert_low, preferred_element_type=jnp.float32)
    block_out = (resid + spread).astype(jnp.bfloat16).reshape(layer_activations.shape)
    cot_low = upstream_derivative.reshape(tok_count, model_width)
    cot_full = cot_low.astype(jnp.float32)
    back_expert = jnp.einsum(
        "egt,td->egd", mixing, cot_low, preferred_element_type=jnp.float32
    ).astype(jnp.bfloat16)
    grad_down = jnp.einsum(
        "egh,egd->ehd", active_low, back_expert, preferred_element_type=jnp.float32
    )
    back_active = jnp.einsum(
        "egd,ehd->egh", back_expert, specialist_exit_matrix, preferred_element_type=jnp.float32
    )
    back_inner = gelu_back(back_active)[0].astype(jnp.bfloat16)
    grad_in = jnp.einsum("egd,egh->edh", mixed_low, back_inner, preferred_element_type=jnp.float32)
    back_mixed = jnp.einsum(
        "egh,edh->egd", back_inner, specialist_entry_matrix, preferred_element_type=jnp.float32
    ).astype(jnp.bfloat16)
    back_mixing = jnp.einsum("td,egd->egt", cot_low, expert_low, preferred_element_type=jnp.float32)
    back_mixing = back_mixing + jnp.einsum(
        "td,egd->egt", mix_low, back_mixed, preferred_element_type=jnp.float32
    )
    back_weight = jnp.sum(jnp.where(cluster_assignment[None, :, :], back_mixing, 0.0), axis=1).T
    back_logits = weigh_back(back_weight)[0].astype(jnp.bfloat16)
    grad_ctrl = jnp.einsum("td,te->de", mix_low, back_logits, preferred_element_type=jnp.float32)
    back_mix = jnp.einsum("egt,egd->td", mixing, back_mixed, preferred_element_type=jnp.float32)
    back_mix = back_mix + jnp.einsum(
        "te,de->td", back_logits, router_matrix, preferred_element_type=jnp.float32
    )
    back_resid_norm, grad_gain_mix = norm_mix_back(back_mix)
    back_resid = cot_full + back_resid_norm
    back_branch = back_resid.astype(jnp.bfloat16)
    grad_out = jnp.einsum(
        "td,te->de", attended_low, back_branch, preferred_element_type=jnp.float32
    )
    back_attended = jnp.einsum("de,te->dt", heed_exit_matrix, back_branch, preferred_element_type=f32).astype(bf)
    other_grad = lax.ppermute(pick(back_attended, False, 0), "seq", CORE)
    grads_out = ordered(pick(back_attended, True, 0), other_grad, 1).reshape(4, HEAD, 2 * pos_count)
    inner_rows = jnp.sum(grads_out.astype(f32) * joined.astype(f32), axis=1)
    got_grad = lax.ppermute(grads_out[2:4], "seq", DOWN)
    got_stat = lax.ppermute(jnp.stack([whole_log[2:4], inner_rows[2:4]]), "seq", DOWN)

    def scaled(peak, whole, inner):
        ratio = jnp.exp2(peak - whole)
        return jnp.stack([ratio, inner * ratio] + [jnp.zeros_like(ratio)] * 6, axis=1)

    near_kv, near_q = local_bwd(qkv, probs_near, grads_out, scaled(peak_near, whole_log, inner_rows))
    far_grad = jnp.where(upper, grads_out[0:2], got_grad)
    far_log = jnp.where(upper, whole_log[0:2], got_stat[0])
    far_inner = jnp.where(upper, inner_rows[0:2], got_stat[1])
    far_stat = scaled(peak_far, far_log, far_inner)
    far_back = [cross_bwd(far_q[j], far_kv[j], far[j][0], far_grad[j : j + 1], far_stat[j : j + 1]) for j in range(2)]
    far_kv_grad = jnp.concatenate([far_back[0][0], far_back[1][0]], 0)
    far_q_grad = jnp.concatenate([far_back[0][1], far_back[1][1]], 0)
    got_kv = lax.ppermute(far_kv_grad.astype(bf), "seq", DOWN)
    got_q = lax.ppermute(far_q_grad, "seq", UP)
    sum_q = near_q.astype(f32) + jnp.where(upper, jnp.concatenate([far_q_grad, got_q], 0).astype(f32), 0.0)
    sum_kv = near_kv + jnp.where(upper, 0.0, jnp.concatenate([got_kv.astype(f32), far_kv_grad], 0))
    sum_q = sum_q.astype(bf).reshape(half, 2 * pos_count).T
    sum_k = (sum_kv[:, :, :HEAD] * 0.125).astype(bf).transpose(1, 0, 2).reshape(2 * pos_count, half)
    sum_v = sum_kv[:, :, HEAD:].astype(bf).transpose(1, 0, 2).reshape(2 * pos_count, half)
    own_qkv = jnp.stack([sum_q, sum_k, sum_v], axis=1)
    own_grad = jnp.einsum("td,tjf->djf", pair_normed, own_qkv, preferred_element_type=f32)
    empty = jnp.zeros_like(own_grad)
    grad_qkv = ordered(own_grad, empty, 2).reshape(model_width, 3 * model_width)
    other_qkv = lax.ppermute(pick(own_qkv, False, 0), "seq", CORE)
    back_qkv = ordered(pick(own_qkv, True, 0), other_qkv, 2).reshape(tok_count, 3 * model_width)
    back_normed = jnp.einsum("tf,df->td", back_qkv, triple_entry_matrix, preferred_element_type=f32)
    back_rows_norm, grad_gain_attn = norm_attn_back(back_normed)
    tokens_grad = (
        (back_resid + back_rows_norm).astype(jnp.bfloat16).reshape(layer_activations.shape)
    )
    local_grads = (grad_gain_attn, grad_qkv, grad_out, grad_gain_mix, grad_ctrl, grad_in, grad_down)
    summed = lax.psum(
        (
            local_grads[0],
            local_grads[1],
            local_grads[2],
            local_grads[3],
            local_grads[4],
            local_grads[5],
            local_grads[6],
        ),
        ("batch", "seq"),
    )
    return (
        block_out,
        tokens_grad,
        summed[0],
        summed[1],
        summed[2],
        summed[3],
        summed[4],
        summed[5],
        summed[6],
    )


def solution(mesh):
    placed = (
        P("batch", "seq", None),
        P("batch"),
        P("batch", "seq"),
        P(),
        P(),
        P(),
        P(),
        P(),
        P(),
        P(),
        P(),
        P("batch", "seq", None),
    )
    return jax.shard_map(
        body,
        mesh=mesh,
        in_specs=placed,
        out_specs=(
            P("batch", "seq", None),
            P("batch", "seq", None),
            P(),
            P(),
            P(),
            P(),
            P(),
            P(),
            P(),
        ),
        check_vma=False,
    )
```

```python
import jax
import jax.numpy as jnp
from jax import lax
from jax.experimental import pallas as pl
from jax.experimental.pallas import tpu as pltpu
from jax.sharding import PartitionSpec as P

HEADS = 8
HEAD = 64
GROUP = 32
EPSILON = 1e-06
LOG2E = 1.4426950408889634
SC = 0.125 * LOG2E
MASKED = -1e30
BQ = 512
CH = 512
bf = jnp.bfloat16
f32 = jnp.float32
AXES = ("batch", "seq")
NT = (((1,), (1,)), ((), ()))
TN = (((0,), (0,)), ((), ()))


def nt(a, b):
    return lax.dot_general(a, b, NT, preferred_element_type=f32)


def tn(a, b):
    return lax.dot_general(a, b, TN, preferred_element_type=f32)


def nn(a, b):
    return jnp.dot(a, b, preferred_element_type=f32)


def rows_of(shape):
    return lax.broadcasted_iota(jnp.int32, shape, 0)


def lanes_of(shape):
    return lax.broadcasted_iota(jnp.int32, shape, 1)


def vmem():
    return pl.BlockSpec(memory_space=pltpu.VMEM)


def smem():
    return pl.BlockSpec(memory_space=pltpu.SMEM)


def params(mib):
    return pltpu.CompilerParams(vmem_limit_bytes=mib * 2**20)


def cost(us):
    return pl.CostEstimate(flops=int(us * 1e9), bytes_accessed=2**20, transcendentals=0)


def shift_lanes(value):
    return pltpu.roll(value.astype(f32), 64, axis=1).astype(bf)


def left(first, second):
    return jnp.where(lanes_of(first.shape) < 64, first, shift_lanes(second))


def right(first, second):
    return jnp.where(lanes_of(first.shape) < 64, shift_lanes(first), second)


def project_kernel(place, x_own, x_other, gain, w, normed, qkv, send_a, send_b, packs, w_own):
    core, chip = place[0], place[1]
    block = pl.program_id(0)

    @pl.when(block == 0)
    def _():
        for c in range(2):
            q = w[:, 256 * c : 256 * c + 256]
            packs[c, :, 0:256] = q
            for h in range(4):
                at = 256 * c + 128 * (h // 2)
                k = w[:, 512 + at : 640 + at]
                v = w[:, 1024 + at : 1152 + at]
                pair = left(k, v) if h % 2 == 0 else right(k, v)
                packs[c, :, 256 + 128 * h : 384 + 128 * h] = pair
        for h in range(4):
            q = packs[core, :, 128 * (h // 2) : 128 * (h // 2) + 128]
            q = q if h % 2 == 0 else shift_lanes(q)
            w_own[:, 256 * h : 256 * h + 128] = jnp.where(lanes_of(q.shape) < 64, q, jnp.zeros((), bf))
            w_own[:, 256 * h + 128 : 256 * h + 256] = packs[core, :, 256 + 128 * h : 384 + 128 * h]

    def go(x_ref):
        x = x_ref[...].astype(f32)
        inverse = lax.rsqrt(jnp.mean(x * x, axis=1, keepdims=True) + EPSILON)
        low = (x * inverse * gain[...]).astype(bf)
        normed[...] = low
        out = nn(low, w_own[...]).astype(bf)
        qkv[...] = out
        send_b[...] = out[:, 384:512]

        @pl.when(chip == 0)
        def _():
            send_a[...] = out[:, 128:256]

        @pl.when(chip == 1)
        def _():
            send_a[...] = left(out[:, 512:640], out[:, 768:896])

    @pl.when(block // 2 == core)
    def _():
        go(x_own)

    @pl.when(block // 2 != core)
    def _():
        go(x_other)


def project(place, x_own, x_other, gain, w):
    rows, width = x_own.shape

    def own(b, p):
        return (jnp.where(b // 2 == p[0], b % 2, jnp.where(b // 2 > p[0], 1, 0)), 0)

    def other(b, p):
        return (jnp.where(b // 2 != p[0], b % 2, jnp.where(b // 2 > 1 - p[0], 1, 0)), 0)

    half = rows // 2
    return pl.pallas_call(
        project_kernel,
        grid_spec=pltpu.PrefetchScalarGridSpec(
            num_scalar_prefetch=1,
            grid=(4,),
            in_specs=[
                pl.BlockSpec((half, width), own),
                pl.BlockSpec((half, width), other),
                pl.BlockSpec((1, width), lambda b, p: (0, 0)),
                pl.BlockSpec((width, 3 * width), lambda b, p: (0, 0)),
            ],
            out_specs=[
                pl.BlockSpec((half, width), lambda b, p: (b, 0)),
                pl.BlockSpec((half, 1024), lambda b, p: (b, 0)),
                pl.BlockSpec((half, 128), lambda b, p: (b, 0)),
                pl.BlockSpec((half, 128), lambda b, p: (b, 0)),
                pl.BlockSpec((2, width, 768), lambda b, p: (0, 0, 0)),
            ],
            scratch_shapes=[pltpu.VMEM((width, 1024), bf)],
        ),
        out_shape=[
            jax.ShapeDtypeStruct((2 * rows, width), bf),
            jax.ShapeDtypeStruct((2 * rows, 1024), bf),
            jax.ShapeDtypeStruct((2 * rows, 128), bf),
            jax.ShapeDtypeStruct((2 * rows, 128), bf),
            jax.ShapeDtypeStruct((2, width, 768), bf),
        ],
        compiler_params=params(40),
        cost_estimate=cost(4),
    )(place, x_own, x_other, gain, w)


def scores(kv, q, s_ref, slot, kmax, q0, limit, causal):
    peak = None
    for k0 in range(0, kmax, CH):
        s = nt(kv[k0 : k0 + CH, :], q)
        if causal:
            if k0 >= 1024:
                s = jnp.where(rows_of(s.shape) + k0 < limit, s, MASKED)
            if k0 + CH > q0:
                s = jnp.where(rows_of(s.shape) + (k0 - q0) <= lanes_of(s.shape), s, MASKED)
        s_ref[slot, k0 : k0 + CH, :] = s
        m = jnp.max(s, axis=0, keepdims=True)
        peak = m if peak is None else jnp.maximum(peak, m)
    return peak


def weigh(vt, s_ref, slot, peak, kmax, p_ref, i):
    scaled = peak * SC
    acc = None
    for k0 in range(0, kmax, CH):
        p = jnp.exp2(s_ref[slot, k0 : k0 + CH, :] * SC - scaled).astype(bf)
        p_ref[0, i, k0 : k0 + CH, :] = p
        d = nn(vt[:, k0 : k0 + CH], p)
        acc = d if acc is None else acc + d
    total = acc[0:1, :]
    return acc[64:128, :] * (1.0 / total), scaled, total


def ones_and_values(kv):
    vt = kv.T
    return jnp.where(rows_of(vt.shape) < 64, jnp.ones((), bf), vt)


def near_forward_kernel(limit_ref, q_ref, kv_ref, p_ref, o_ref, st_ref, s_ref, vt_ref):
    limit = limit_ref[0]
    vt_ref[...] = ones_and_values(kv_ref[...])
    count = q_ref.shape[0] // BQ
    peak = scores(kv_ref, q_ref[0:BQ, :], s_ref, 0, BQ, 0, limit, True)
    for i in range(count):
        later = None
        if i + 1 < count:
            later = scores(kv_ref, q_ref[(i + 1) * BQ : (i + 2) * BQ, :], s_ref, (i + 1) % 2, (i + 2) * BQ, (i + 1) * BQ, limit, True)
        out, scaled, total = weigh(vt_ref, s_ref, i % 2, peak, (i + 1) * BQ, p_ref, i)
        o_ref[0, :, i * BQ : (i + 1) * BQ] = out.astype(bf)
        st_ref[0, 0:1, i * BQ : (i + 1) * BQ] = scaled
        st_ref[0, 1:2, i * BQ : (i + 1) * BQ] = total
        peak = later


def near_forward(limit, qkv):
    n = qkv.shape[0]
    return pl.pallas_call(
        near_forward_kernel,
        grid=(4,),
        in_specs=[smem(), pl.BlockSpec((n, 128), lambda h: (0, 2 * h)), pl.BlockSpec((n, 128), lambda h: (0, 2 * h + 1))],
        out_specs=[
            pl.BlockSpec((1, n // BQ, n, BQ), lambda h: (h, 0, 0, 0)),
            pl.BlockSpec((1, 64, n), lambda h: (h, 0, 0)),
            pl.BlockSpec((1, 8, n), lambda h: (h, 0, 0)),
        ],
        out_shape=[
            jax.ShapeDtypeStruct((4, n // BQ, n, BQ), bf),
            jax.ShapeDtypeStruct((4, 64, n), bf),
            jax.ShapeDtypeStruct((4, 8, n), f32),
        ],
        scratch_shapes=[pltpu.VMEM((2, n, BQ), f32), pltpu.VMEM((128, n), bf)],
        compiler_params=params(56),
        cost_estimate=cost(20),
    )(limit, qkv, qkv)


def three(value):
    high = value.astype(bf)
    rest = value - high.astype(f32)
    mid = rest.astype(bf)
    return high, mid, (rest - mid.astype(f32)).astype(bf)


def far_forward_kernel(j, place, q_own, q_got, kv_own, kv_got, p_ref, o_ref, st_ref, q_ref, kv_ref, s_ref, vt_ref):
    n = q_own.shape[0]

    @pl.when(place[1] == 1)
    def _():
        q_ref[...] = q_own[...]
        kv_ref[...] = kv_got[...]

    @pl.when(place[1] == 0)
    def _():
        q = q_got[...] if j == 0 else shift_lanes(q_got[...])
        q_ref[...] = jnp.where(lanes_of(q.shape) < 64, q, jnp.zeros((), bf))
        kv_ref[...] = kv_own[...]

    vt_ref[...] = ones_and_values(kv_ref[...])
    count = n // BQ
    peak = scores(kv_ref, q_ref[0:BQ, :], s_ref, 0, n, 0, None, False)
    for i in range(count):
        later = None
        at = slice(i * BQ, (i + 1) * BQ)
        if i + 1 < count:
            later = scores(kv_ref, q_ref[(i + 1) * BQ : (i + 2) * BQ, :], s_ref, (i + 1) % 2, n, 0, None, False)
        out, scaled, total = weigh(vt_ref, s_ref, i % 2, peak, n, p_ref, i)
        o_ref[0:64, at] = out.astype(bf)
        high, mid, low = three(scaled + jnp.log(total) * LOG2E)
        tail = jnp.concatenate([high.astype(f32), mid.astype(f32), low.astype(f32), jnp.zeros((13, BQ), f32)], 0)
        o_ref[64:80, at] = tail.astype(bf)
        st_ref[0:1, at] = scaled
        peak = later


def far_forward(j, place, qkv, q_got, kv_got):
    n = qkv.shape[0]
    whole = pl.BlockSpec((n, 128), lambda h: (0, 0))
    return pl.pallas_call(
        lambda *refs: far_forward_kernel(j, *refs),
        grid=(1,),
        in_specs=[
            smem(),
            pl.BlockSpec((n, 128), lambda h: (0, 2 * j)),
            whole,
            pl.BlockSpec((n, 128), lambda h: (0, 2 * j + 5)),
            whole,
        ],
        out_specs=[
            pl.BlockSpec((1, n // BQ, n, BQ), lambda h: (0, 0, 0, 0)),
            pl.BlockSpec((80, n), lambda h: (0, 0)),
            pl.BlockSpec((8, n), lambda h: (0, 0)),
            whole,
            whole,
        ],
        out_shape=[
            jax.ShapeDtypeStruct((1, n // BQ, n, BQ), bf),
            jax.ShapeDtypeStruct((80, n), bf),
            jax.ShapeDtypeStruct((8, n), f32),
            jax.ShapeDtypeStruct((n, 128), bf),
            jax.ShapeDtypeStruct((n, 128), bf),
        ],
        scratch_shapes=[pltpu.VMEM((2, n, BQ), f32), pltpu.VMEM((128, n), bf)],
        compiler_params=params(56),
        cost_estimate=cost(11),
    )(place, qkv, q_got, qkv, kv_got)


def unsplit(ref, at):
    return ref[at : at + 1, :].astype(f32) + ref[at + 1 : at + 2, :].astype(f32) + ref[at + 2 : at + 3, :].astype(f32)


def join_kernel(place, near, stat, far_a, far_b, got_a, got_b, mine, other, log_ref):
    core, chip = place[0], place[1]
    half = mine.shape[1]
    for h in range(4):
        far = (far_a, far_b, got_a, got_b)[h]
        log_near = stat[h, 0:1, :] + jnp.log(stat[h, 1:2, :]) * LOG2E
        log_far = jnp.where(chip == 1, unsplit(far, 64), MASKED)
        top = jnp.maximum(log_near, log_far)
        e_near, e_far = jnp.exp2(log_near - top), jnp.exp2(log_far - top)
        both = e_near + e_far
        log_ref[h] = jnp.broadcast_to(top + jnp.log(both) * LOG2E, log_ref.shape[1:])
        far_out = jnp.where(chip == 1, far[0:64, :].astype(f32), 0.0)
        joined = ((near[h].astype(f32) * e_near + far_out * e_far) * (1.0 / both)).astype(bf)
        at = slice(64 * h, 64 * h + 64)

        @pl.when(core == 0)
        def _():
            mine[at, :] = joined[:, :half]
            other[at, :] = joined[:, half:]

        @pl.when(core == 1)
        def _():
            mine[at, :] = joined[:, half:]
            other[at, :] = joined[:, :half]


def join(place, near, stat, far_a, far_b, got_a, got_b):
    n = near.shape[2]
    return pl.pallas_call(
        join_kernel,
        in_specs=[smem()] + [vmem()] * 6,
        out_specs=[vmem()] * 3,
        out_shape=[
            jax.ShapeDtypeStruct((256, n // 2), bf),
            jax.ShapeDtypeStruct((256, n // 2), bf),
            jax.ShapeDtypeStruct((4, 8, n), f32),
        ],
        compiler_params=params(40),
        cost_estimate=cost(2),
    )(place, near, stat, far_a, far_b, got_a, got_b)


def mixture_kernel(
    place, sharp, x, att_own, att_got, wout, gain, router, labels, gy, w1_hbm, w2_hbm,
    block_out, fac, gout, tiny, back_resid, ba_own, ba_other, w1, w2, sems,
):
    core = place[0]
    copy1 = pltpu.make_async_copy(w1_hbm, w1, sems.at[0])
    copy2 = pltpu.make_async_copy(w2_hbm, w2, sems.at[1])
    copy1.start()
    copy2.start()
    own_rows = pl.ds(pl.multiple_of(core * 256, 256), 256)
    other_rows = pl.ds(pl.multiple_of(256 - core * 256, 256), 256)
    wo_own, wo_other = wout[own_rows, :], wout[other_rows, :]
    resid = x[...].astype(f32) + tn(att_own[...], wo_own) + tn(att_got[...], wo_other)
    inverse = lax.rsqrt(jnp.mean(resid * resid, axis=1, keepdims=True) + EPSILON)
    unit = resid * inverse
    mix = (unit * gain[...]).astype(bf)
    temper = 1.0 / sharp[0]
    logits = nt(router[...], mix) * temper
    tokens = mix.shape[0]
    groups = tokens // GROUP
    member = labels[...] == rows_of((groups, tokens))
    weights, mixing = [], []
    for e in range(2):
        row = logits[e : e + 1, :]
        peak = jnp.max(jnp.where(member, row, -jnp.inf), axis=1, keepdims=True)
        token_peak = jnp.sum(jnp.where(member, peak, 0.0), axis=0, keepdims=True)
        raised = jnp.exp(row - token_peak)
        total = jnp.sum(jnp.where(member, raised, 0.0), axis=1, keepdims=True)
        token_total = jnp.sum(jnp.where(member, total, 0.0), axis=0, keepdims=True)
        w = raised / token_total
        weights.append(w)
        mixing.append(jnp.where(member, w, 0.0))
    mixing = jnp.concatenate(mixing, 0).astype(bf)
    mixed = nn(mixing, mix).astype(bf)
    back_expert = nn(mixing, gy[...]).astype(bf)
    copy1.wait()
    copy2.wait()
    expert_out, back_mixed = [], []
    quarter = w1.shape[2] // 4
    width = mix.shape[1]
    for e in range(2):
        at = slice(groups * e, groups * (e + 1))
        inner = nn(mixed[at], w1[e])
        cdf = 0.5 * (1.0 + lax.erf(inner * 0.7071067811865476))
        active = (inner * cdf).astype(bf)
        slope = cdf + inner * (jnp.exp(-0.5 * inner * inner) * 0.3989422804014327)
        expert_out.append(nn(active, w2[e]))
        back_inner = (slope * nt(back_expert[at], w2[e])).astype(bf)
        back_mixed.append(nt(back_inner, w1[e]))
        fac[e, :, 0:width] = mixed[at]
        fac[e, :, width : 2 * width] = back_expert[at]
        for q in range(4):
            base = 2 * width + 2 * quarter * q
            fac[e, :, base : base + quarter] = back_inner[:, quarter * q : quarter * (q + 1)]
            fac[e, :, base + quarter : base + 2 * quarter] = active[:, quarter * q : quarter * (q + 1)]
    expert_out = jnp.concatenate(expert_out, 0).astype(bf)
    back_mixed = jnp.concatenate(back_mixed, 0).astype(bf)
    block_out[...] = (resid + tn(mixing, expert_out)).astype(bf)
    spread = nt(expert_out, gy[...]) + nt(back_mixed, mix)
    rows16 = rows_of((16, tokens))
    back_logits = jnp.zeros((16, tokens), f32)
    for e in range(2):
        back_weight = jnp.sum(jnp.where(member, spread[groups * e : groups * (e + 1)], 0.0), axis=0, keepdims=True)
        w = weights[e]
        inner = jnp.sum(jnp.where(member, w * back_weight, 0.0), axis=1, keepdims=True)
        token_inner = jnp.sum(jnp.where(member, inner, 0.0), axis=0, keepdims=True)
        back_logits = jnp.where(rows16 == e, w * (back_weight - token_inner) * temper, back_logits)
    back_logits = back_logits.astype(bf)
    ctrl = nn(back_logits, mix)
    back_mix = tn(mixing, back_mixed) + tn(back_logits, router[...])
    tiny[...] = jnp.zeros_like(tiny)
    tiny[0:2, :] = ctrl[0:2, :]
    tiny[2:3, :] = jnp.sum(back_mix * unit, axis=0, keepdims=True)
    n = back_mix * gain[...]
    mean = jnp.mean(n * resid, axis=1, keepdims=True)
    back = gy[...].astype(f32) + inverse * n - resid * (inverse * inverse * inverse * mean)
    back_resid[...] = back
    branch = back.astype(bf)
    gout[core] = nn(att_own[...], branch).astype(bf)
    gout[1 - core] = nn(att_got[...], branch).astype(bf)
    ba_own[...] = nt(wo_own, branch).astype(bf)
    ba_other[...] = nt(wo_other, branch).astype(bf)


def mixture(place, sharp, x, att_own, att_got, wout, gain, router, labels, gy, w1, w2):
    tokens, width = x.shape
    hidden = w1.shape[2]
    groups = tokens // GROUP
    return pl.pallas_call(
        mixture_kernel,
        in_specs=[smem(), smem()] + [vmem()] * 8 + [pl.BlockSpec(memory_space=pl.ANY)] * 2,
        out_specs=[vmem()] * 7,
        out_shape=[
            jax.ShapeDtypeStruct((tokens, width), bf),
            jax.ShapeDtypeStruct((2, groups, 2 * width + 2 * hidden), bf),
            jax.ShapeDtypeStruct((2, width // 2, width), bf),
            jax.ShapeDtypeStruct((8, width), f32),
            jax.ShapeDtypeStruct((tokens, width), f32),
            jax.ShapeDtypeStruct((width // 2, tokens), bf),
            jax.ShapeDtypeStruct((width // 2, tokens), bf),
        ],
        scratch_shapes=[pltpu.VMEM(w1.shape, bf), pltpu.VMEM(w2.shape, bf), pltpu.SemaphoreType.DMA((2,))],
        compiler_params=params(60),
        cost_estimate=cost(15),
    )(place, sharp, x, att_own, att_got, wout, gain, router, labels, gy, w1, w2)


def ready_kernel(place, ba_own, ba_got, mine, other, log_ref, grads, inner, payload):
    core = place[0]
    half = mine.shape[1]
    for h in range(4):
        at = slice(64 * h, 64 * h + 64)
        g_own, g_got = ba_own[at, :], ba_got[at, :]
        d_own = jnp.sum(g_own.astype(f32) * mine[at, :].astype(f32), axis=0, keepdims=True)
        d_got = jnp.sum(g_got.astype(f32) * other[at, :].astype(f32), axis=0, keepdims=True)

        def put(g0, g1, d0, d1):
            grads[h, :, :half] = g0
            grads[h, :, half:] = g1
            inner[h, :, :half] = jnp.broadcast_to(d0, (8, half))
            inner[h, :, half:] = jnp.broadcast_to(d1, (8, half))
            if h >= 2:
                for g, d, s in ((g0, d0, slice(0, half)), (g1, d1, slice(half, 2 * half))):
                    payload[h - 2, 0:64, s] = g
                    parts = three(log_ref[h, 0:1, s]) + three(d)
                    tail = jnp.concatenate([part.astype(f32) for part in parts] + [jnp.zeros((10, half), f32)], 0)
                    payload[h - 2, 64:80, s] = tail.astype(bf)

        @pl.when(core == 0)
        def _():
            put(g_own, g_got, d_own, d_got)

        @pl.when(core == 1)
        def _():
            put(g_got, g_own, d_got, d_own)


def ready(place, ba_own, ba_got, mine, other, log):
    half = mine.shape[1]
    return pl.pallas_call(
        ready_kernel,
        in_specs=[smem()] + [vmem()] * 5,
        out_specs=[vmem()] * 3,
        out_shape=[
            jax.ShapeDtypeStruct((4, 64, 2 * half), bf),
            jax.ShapeDtypeStruct((4, 8, 2 * half), f32),
            jax.ShapeDtypeStruct((2, 80, 2 * half), bf),
        ],
        compiler_params=params(40),
        cost_estimate=cost(2),
    )(place, ba_own, ba_got, mine, other, log)


def back_block(kv_ref, kt_ref, q_ref, grad, ratio, inner, p_ref, i, kmax, first, put_kv):
    low = (grad.astype(f32) * ratio).astype(bf)
    rhs = jnp.concatenate([jnp.zeros((64, BQ), bf), low], axis=0)
    shift = inner * ratio
    q = q_ref[i * BQ : (i + 1) * BQ, :]
    natural = rhs.T
    acc = None
    for k0 in range(0, kmax, CH):
        dp = nn(kv_ref[k0 : k0 + CH, :], rhs)
        p = p_ref[0, i, k0 : k0 + CH, :]
        ds = (p.astype(f32) * (dp - shift)).astype(bf)
        d = nn(kt_ref[:, k0 : k0 + CH], ds)
        acc = d if acc is None else acc + d
        put_kv(k0, k0 >= first, nn(ds, q) + nn(p, natural))
    return (acc * 0.125).astype(bf)


def near_backward_kernel(q_ref, kv_ref, p_ref, grad_ref, stat, log_ref, inner_ref, dep, dkv_ref, dq_ref, kt_ref):
    kt_ref[...] = kv_ref[...].T[0:64, :]

    def put(k0, fresh, value):
        if fresh:
            dkv_ref[0, k0 : k0 + CH, :] = value
        else:
            dkv_ref[0, k0 : k0 + CH, :] += value

    for i in range(q_ref.shape[0] // BQ):
        at = slice(i * BQ, (i + 1) * BQ)
        ratio = jnp.exp2(stat[0, 0:1, at] - log_ref[0, 0:1, at])
        dq_ref[0, :, at] = back_block(
            kv_ref, kt_ref, q_ref, grad_ref[0, :, at], ratio, inner_ref[0, 0:1, at], p_ref, i, (i + 1) * BQ, i * BQ, put
        )


def near_backward(h0, heads, qkv, p, grads, stat, log, inner, dep):
    n = qkv.shape[0]
    row = pl.BlockSpec((1, 8, n), lambda h: (h + h0, 0, 0))
    return pl.pallas_call(
        near_backward_kernel,
        grid=(heads,),
        in_specs=[
            pl.BlockSpec((n, 128), lambda h: (0, 2 * (h + h0))),
            pl.BlockSpec((n, 128), lambda h: (0, 2 * (h + h0) + 1)),
            pl.BlockSpec((1, n // BQ, n, BQ), lambda h: (h + h0, 0, 0, 0)),
            pl.BlockSpec((1, 64, n), lambda h: (h + h0, 0, 0)),
            row,
            row,
            row,
            pl.BlockSpec(memory_space=pl.ANY),
        ],
        out_specs=[pl.BlockSpec((1, n, 128), lambda h: (h, 0, 0)), pl.BlockSpec((1, 64, n), lambda h: (h, 0, 0))],
        out_shape=[jax.ShapeDtypeStruct((heads, n, 128), f32), jax.ShapeDtypeStruct((heads, 64, n), bf)],
        scratch_shapes=[pltpu.VMEM((64, n), bf)],
        compiler_params=params(56),
        cost_estimate=cost(6.5 * heads),
    )(qkv, qkv, p, grads, stat, log, inner, dep)


def far_backward_kernel(
    place, q_ref, kv_ref, p_ref, stat, grad_own, log_own, inner_own, got, dep, send_ref, keep_ref, kt_ref, sum_ref, dq_ref
):
    kt_ref[...] = kv_ref[...].T[0:64, :]
    upper = place[1] == 1
    n = q_ref.shape[0]

    def put(k0, fresh, value):
        if fresh:
            sum_ref[k0 : k0 + CH, :] = value
        else:
            sum_ref[k0 : k0 + CH, :] += value

    for i in range(n // BQ):
        at = slice(i * BQ, (i + 1) * BQ)
        got_log = got[0, 64:67, at].astype(f32)
        got_inner = got[0, 67:70, at].astype(f32)
        log = jnp.where(upper, log_own[0, 0:1, at], jnp.sum(got_log, axis=0, keepdims=True))
        inner = jnp.where(upper, inner_own[0, 0:1, at], jnp.sum(got_inner, axis=0, keepdims=True))
        grad = jnp.where(upper, grad_own[0, :, at], got[0, 0:64, at])
        ratio = jnp.exp2(stat[0:1, at] - log)
        dq = back_block(kv_ref, kt_ref, q_ref, grad, ratio, inner, p_ref, i, n, 0 if i == 0 else n, put)
        dq_ref[at, :] = jnp.concatenate([dq, jnp.zeros((64, BQ), bf)], 0).T

    @pl.when(upper)
    def _():
        send_ref[...] = sum_ref[...].astype(bf)
        keep_ref[...] = dq_ref[...]

    @pl.when(jnp.logical_not(upper))
    def _():
        send_ref[...] = dq_ref[...]
        keep_ref[...] = sum_ref[...].astype(bf)


def far_backward(j, place, q, kv, p, stat, grads, log, inner, got, dep):
    n = q.shape[0]
    row = pl.BlockSpec((1, 8, n), lambda h: (j, 0, 0))
    whole = pl.BlockSpec((n, 128), lambda h: (0, 0))
    return pl.pallas_call(
        far_backward_kernel,
        grid=(1,),
        in_specs=[
            smem(),
            whole,
            whole,
            pl.BlockSpec((1, n // BQ, n, BQ), lambda h: (0, 0, 0, 0)),
            pl.BlockSpec((8, n), lambda h: (0, 0)),
            pl.BlockSpec((1, 64, n), lambda h: (j, 0, 0)),
            row,
            row,
            pl.BlockSpec((1, 80, n), lambda h: (j, 0, 0)),
            pl.BlockSpec(memory_space=pl.ANY),
        ],
        out_specs=[whole, whole],
        out_shape=[jax.ShapeDtypeStruct((n, 128), bf)] * 2,
        scratch_shapes=[pltpu.VMEM((64, n), bf), pltpu.VMEM((n, 128), f32), pltpu.VMEM((n, 128), bf)],
        compiler_params=params(56),
        cost_estimate=cost(13),
    )(place, q, kv, p, stat, grads, log, inner, got, dep)


def swap(value, bits):
    count = lax.axis_size("batch") * lax.axis_size("seq")
    return lax.ppermute(value, AXES, [(i, i ^ bits) for i in range(count)])


def take(value, index, axis=0):
    return lax.dynamic_index_in_dim(value, index, axis, keepdims=False)


def reorder(value, line, count):
    bit = 1
    while bit < count:
        shape = value.shape
        split = value.reshape((count // (2 * bit), 2, bit) + shape[1:])
        value = jnp.where((line // bit) % 2 == 1, split[:, ::-1], split).reshape(shape)
        bit *= 2
    return value


MOVES = ((0, 0), (1, 0), (0, 1), (1, 1))


def factors_kernel(place, fac, got, gout, got_out, *outs):
    core, chip, side = place[0], place[1], place[2]
    groups = got.shape[0]
    width = gout.shape[2]
    part = (got.shape[1] - 2 * width) // 4
    rows = gout.shape[1] // 4
    for (x, y), out in zip(MOVES, outs):
        index = 2 * (chip ^ x) + (side ^ y)
        lanes = pl.ds(pl.multiple_of(2 * width + index * part, 128), part)
        at = pl.ds(pl.multiple_of(index * rows, rows), rows)
        out[0:groups, 0 : 2 * width] = fac[core, :, 0 : 2 * width]
        out[groups:, 0 : 2 * width] = got[:, 0 : 2 * width]
        out[0:groups, 2 * width : 2 * width + part] = fac[core, :, lanes]
        out[groups:, 2 * width : 2 * width + part] = got[:, lanes]
        out[:, 2 * width + part :] = (gout[core, at, :].astype(f32) + got_out[at, :].astype(f32)).astype(bf)


def factors(place, fac, got, gout, got_out):
    groups, per = got.shape
    width = gout.shape[2]
    shape = jax.ShapeDtypeStruct((2 * groups, 2 * width + (per - 2 * width) // 4 + width), bf)
    return pl.pallas_call(
        factors_kernel,
        in_specs=[smem()] + [vmem()] * 4,
        out_specs=[vmem()] * 4,
        out_shape=[shape] * 4,
        compiler_params=params(32),
        cost_estimate=cost(2),
    )(place, fac, got, gout, got_out)


def slab_kernel(dep, a, b, c, d, in_ref, down_ref, out_ref):
    width = out_ref.shape[1]
    quarter = in_ref.shape[1]

    def lanes(start, size):
        return jnp.concatenate([ref[:, start : start + size] for ref in (a, b, c, d)], 0)

    in_ref[...] = tn(lanes(0, width), lanes(2 * width, quarter)).astype(bf)
    down_ref[...] = tn(lanes(2 * width + quarter, quarter), lanes(width, width)).astype(bf)
    total = a[:, 2 * width + 2 * quarter :].astype(f32)
    for ref in (b, c, d):
        total = total + ref[:, 2 * width + 2 * quarter :].astype(f32)
    out_ref[...] = total.astype(bf)


def slabs(dep, payloads, width, quarter):
    rows = payloads[0].shape[0]
    return pl.pallas_call(
        slab_kernel,
        in_specs=[pl.BlockSpec(memory_space=pl.ANY)] + [vmem()] * 4,
        out_specs=[vmem()] * 3,
        out_shape=[
            jax.ShapeDtypeStruct((width, quarter), bf),
            jax.ShapeDtypeStruct((quarter, width), bf),
            jax.ShapeDtypeStruct((rows, width), bf),
        ],
        compiler_params=params(32),
        cost_estimate=cost(2),
    )(dep, *payloads)


def add_kernel(dep, *refs):
    total = refs[0][...].astype(f32)
    for ref in refs[1:-1]:
        total = total + ref[...].astype(f32)
    refs[-1][...] = total.astype(bf)


def add(dep, values):
    return pl.pallas_call(
        add_kernel,
        in_specs=[pl.BlockSpec(memory_space=pl.ANY)] + [vmem()] * len(values),
        out_specs=vmem(),
        out_shape=jax.ShapeDtypeStruct(values[0].shape, bf),
        compiler_params=params(32),
        cost_estimate=cost(1),
    )(dep, *values)


def spread_kernel(place, near_in, far_in, near_down, far_down, in_ref, down_ref):
    expert = pl.program_id(0)
    line = place[3]
    count, rows = near_in.shape[1], near_in.shape[2]

    def put(source_in, source_down):
        for k in range(count):
            start = pl.multiple_of((line ^ k) * rows, rows)
            in_ref[0, pl.ds(start, rows), :] = source_in[0, k].astype(f32)
            down_ref[0, pl.ds(start, rows), :] = source_down[0, k].astype(f32)

    @pl.when(expert == place[0])
    def _():
        put(near_in, near_down)

    @pl.when(expert != place[0])
    def _():
        put(far_in, far_down)


def spread_experts(place, near_in, far_in, near_down, far_down, hidden, width):
    block = near_in.shape[1:]

    def x_inner(q, p):
        return ((q ^ p[2]) % 2) * 2 + ((q // 2) ^ p[1])

    def y_inner(q, p):
        return q ^ (2 * p[1] + p[2])

    def spec(order, near):
        def index(e, q, p):
            wanted = (e == p[0]) == near
            return (order(jnp.where(wanted, q, jnp.where(e == 0, 0, 3)), p), 0, 0, 0)

        return pl.BlockSpec((1,) + block, index)

    return pl.pallas_call(
        spread_kernel,
        grid_spec=pltpu.PrefetchScalarGridSpec(
            num_scalar_prefetch=1,
            grid=(2, 4),
            in_specs=[spec(x_inner, True), spec(x_inner, False), spec(y_inner, True), spec(y_inner, False)],
            out_specs=[
                pl.BlockSpec((1, width, hidden // 4), lambda e, q, p: (e, 0, q)),
                pl.BlockSpec((1, hidden // 4, width), lambda e, q, p: (e, q, 0)),
            ],
        ),
        out_shape=[jax.ShapeDtypeStruct((2, width, hidden), f32), jax.ShapeDtypeStruct((2, hidden, width), f32)],
        compiler_params=params(40),
        cost_estimate=cost(8),
    )(place, near_in, far_in, near_down, far_down)


def own_block(b, p):
    return jnp.where(b // 2 == p[0], b % 2, jnp.where(b // 2 > p[0], 1, 0))


def other_block(b, p):
    return jnp.where(b // 2 != p[0], b % 2, jnp.where(b // 2 > 1 - p[0], 1, 0))


def collect_kernel(
    place, normed, kv_a, kv_b, q_a, q_b, keep_a, keep_b, got_a, got_b, packs, gain, tiny, mine, other, slabs_ref, sum_ref
):
    block = pl.program_id(0)
    upper = place[1] == 1
    dq = jnp.concatenate([q_a[0], q_a[1], q_b[0], q_b[1]], 0).T.astype(f32)
    far = jnp.concatenate([left(keep_a[...], keep_b[...]), left(got_a[...], got_b[...])], 1).astype(f32)
    pieces = [(dq + jnp.where(upper, far, 0.0)).astype(bf)]
    for near, h, extra in ((kv_a, 0, got_a), (kv_a, 1, got_b), (kv_b, 0, keep_a), (kv_b, 1, keep_b)):
        value = near[h] + jnp.where(upper, 0.0, extra[...].astype(f32))
        pieces.append(jnp.where(lanes_of(value.shape) < 64, value * 0.125, value).astype(bf))
    back = jnp.concatenate(pieces, 1)

    @pl.when(block // 2 == place[0])
    def _():
        mine[...] = back

    @pl.when(block // 2 != place[0])
    def _():
        other[...] = back

    part = tn(normed[...], back)

    @pl.when(block == 0)
    def _():
        sum_ref[...] = part

    @pl.when(block > 0)
    def _():
        sum_ref[...] += part

    @pl.when(block == 3)
    def _():
        total = sum_ref[...]
        width = total.shape[0]
        product = total * packs[place[0]].astype(f32)
        ones = jnp.ones((8, total.shape[1]), f32)
        summed = lax.dot_general(ones, product, NT, precision=lax.Precision.HIGHEST, preferred_element_type=f32)
        values = [summed[0:1, :] / gain[...], tiny[0:1, :], tiny[1:2, :], tiny[2:3, :]]
        rows = rows_of((16, width))
        small = jnp.zeros((16, width), f32)
        for r, value in enumerate(values):
            high = value.astype(bf).astype(f32)
            small = jnp.where(rows == r, high, jnp.where(rows == r + 4, value - high, small))
        small = jnp.concatenate([small.astype(bf), jnp.zeros((16, total.shape[1] - width), bf)], 1)
        for q in range(4):
            slabs_ref[q, 0 : width // 4, :] = total[q * width // 4 : (q + 1) * width // 4, :].astype(bf)
            slabs_ref[q, width // 4 :, :] = small


def collect(place, normed, kv_a, kv_b, q_a, q_b, keep_a, keep_b, got_a, got_b, packs, gain, tiny):
    n, width = normed.shape
    rows = n // 4
    kv = pl.BlockSpec((2, rows, 128), lambda b, p: (0, b, 0))
    dq = pl.BlockSpec((2, 64, rows), lambda b, p: (0, 0, b))
    flat = pl.BlockSpec((rows, 128), lambda b, p: (b, 0))
    return pl.pallas_call(
        collect_kernel,
        grid_spec=pltpu.PrefetchScalarGridSpec(
            num_scalar_prefetch=1,
            grid=(4,),
            in_specs=[
                pl.BlockSpec((rows, width), lambda b, p: (b, 0)),
                kv, kv, dq, dq, flat, flat, flat, flat,
                pl.BlockSpec(packs.shape, lambda b, p: (0, 0, 0)),
                pl.BlockSpec((1, width), lambda b, p: (0, 0)),
                pl.BlockSpec(tiny.shape, lambda b, p: (0, 0)),
            ],
            out_specs=[
                pl.BlockSpec((rows, 768), lambda b, p: (own_block(b, p), 0)),
                pl.BlockSpec((rows, 768), lambda b, p: (other_block(b, p), 0)),
                pl.BlockSpec((4, width // 4 + 16, 768), lambda b, p: (0, 0, 0)),
            ],
            scratch_shapes=[pltpu.VMEM((width, 768), f32)],
        ),
        out_shape=[
            jax.ShapeDtypeStruct((n // 2, 768), bf),
            jax.ShapeDtypeStruct((n // 2, 768), bf),
            jax.ShapeDtypeStruct((4, width // 4 + 16, 768), bf),
        ],
        compiler_params=params(40),
        cost_estimate=cost(5),
    )(place, normed, kv_a, kv_b, q_a, q_b, keep_a, keep_b, got_a, got_b, packs, gain, tiny)


def tokens_kernel(place, mine, got, packs, x_ref, back_resid, gain, out):
    core = place[0]
    back = nt(mine[...], packs[core]) + nt(got[...], packs[1 - core])
    x = x_ref[...].astype(f32)
    inverse = lax.rsqrt(jnp.mean(x * x, axis=1, keepdims=True) + EPSILON)
    k = back * gain[...]
    mean = jnp.mean(k * x, axis=1, keepdims=True)
    out[...] = (back_resid[...] + inverse * k - x * (inverse * inverse * inverse * mean)).astype(bf)


def tokens_back(place, mine, got, packs, x, back_resid, gain):
    n, width = x.shape
    rows = n // 4
    wide = pl.BlockSpec((rows, 768), lambda b, p: (b, 0))
    block = pl.BlockSpec((rows, width), lambda b, p: (b, 0))
    return pl.pallas_call(
        tokens_kernel,
        grid_spec=pltpu.PrefetchScalarGridSpec(
            num_scalar_prefetch=1,
            grid=(4,),
            in_specs=[wide, wide, pl.BlockSpec(packs.shape, lambda b, p: (0, 0, 0)), block, block, pl.BlockSpec((1, width), lambda b, p: (0, 0))],
            out_specs=block,
        ),
        out_shape=jax.ShapeDtypeStruct((n, width), bf),
        compiler_params=params(40),
        cost_estimate=cost(4),
    )(place, mine, got, packs, x, back_resid, gain)


def unfold_kernel(place, near, far, out):
    line = place[3]
    count, rows = near.shape[1], near.shape[2]
    for source, c in ((near, place[0]), (far, 1 - place[0])):
        for k in range(count):
            at = pl.ds(pl.multiple_of((line ^ k) * rows, rows), rows)
            value = source[0, k]
            base = c * 256
            out[at, pl.ds(pl.multiple_of(base, 128), 256)] = value[:, 0:256].astype(f32)
            for pair in range(2):
                a = value[:, 256 + 256 * pair : 384 + 256 * pair]
                b = value[:, 384 + 256 * pair : 512 + 256 * pair]
                out[at, pl.ds(pl.multiple_of(512 + base + 128 * pair, 128), 128)] = left(a, b).astype(f32)
                out[at, pl.ds(pl.multiple_of(1024 + base + 128 * pair, 128), 128)] = right(a, b).astype(f32)


def unfold(place, near, far, width):
    block = near.shape[1:]
    piece = pl.BlockSpec((1,) + block, lambda q, p: (q ^ (2 * p[1] + p[2]), 0, 0, 0))
    return pl.pallas_call(
        unfold_kernel,
        grid_spec=pltpu.PrefetchScalarGridSpec(
            num_scalar_prefetch=1,
            grid=(4,),
            in_specs=[piece, piece],
            out_specs=pl.BlockSpec((width // 4, 3 * width), lambda q, p: (q, 0)),
        ),
        out_shape=jax.ShapeDtypeStruct((width, 3 * width), f32),
        compiler_params=params(40),
        cost_estimate=cost(3),
    )(place, near, far)


def body(
    layer_activations,
    sequence_extents,
    position_cluster_label,
    cluster_sharpness,
    heed_scale_factor,
    triple_entry_matrix,
    heed_exit_matrix,
    blend_scale_factor,
    router_matrix,
    specialist_entry_matrix,
    specialist_exit_matrix,
    upstream_derivative,
):
    seq_count, pos_count, width = layer_activations.shape
    tokens = seq_count * pos_count
    hidden = specialist_entry_matrix.shape[2]
    spot = lax.axis_index("seq")
    row = lax.axis_index("batch")
    core, chip, side, line = spot % 2, spot // 2, row % 2, row // 2
    lines = lax.axis_size("batch") // 2
    place = jnp.stack([core, chip, side, line]).astype(jnp.int32)
    core_pairs, chip_pairs = [(0, 1), (1, 0), (2, 3), (3, 2)], [(0, 2), (1, 3), (2, 0), (3, 1)]
    up, down = chip_pairs[:2], chip_pairs[2:]

    x = layer_activations.reshape(tokens, width)
    x_other = lax.ppermute(x, "seq", core_pairs)
    gain_a = heed_scale_factor.astype(f32).reshape(1, width)
    normed, qkv, send_a, send_b, packs = project(place, x, x_other, gain_a, triple_entry_matrix)
    got_a = lax.ppermute(send_a, "seq", chip_pairs)
    got_b = lax.ppermute(send_b, "seq", up)
    limit = (sequence_extents - chip * 2 * pos_count).astype(jnp.int32)
    probs, near_out, near_stat = near_forward(limit, qkv)
    p_a, o_a, st_a, q_a, kv_a = far_forward(0, place, qkv, got_a, got_a)
    got_oa = lax.ppermute(o_a, "seq", up)
    p_b, o_b, st_b, q_b, kv_b = far_forward(1, place, qkv, got_a, got_b)
    got_ob = lax.ppermute(o_b, "seq", up)
    att_mine, att_send, log = join(place, near_out, near_stat, o_a, o_b, got_oa, got_ob)
    att_got = lax.ppermute(att_send, "seq", core_pairs)

    router = jnp.zeros((16, width), bf).at[:2].set(router_matrix.T)
    block_out, fac, gout, tiny, back_resid, ba_own, ba_send = mixture(
        place,
        cluster_sharpness,
        x,
        att_mine,
        att_got,
        heed_exit_matrix,
        blend_scale_factor.astype(f32).reshape(1, width),
        router,
        position_cluster_label.reshape(1, tokens),
        upstream_derivative.reshape(tokens, width),
        specialist_entry_matrix,
        specialist_exit_matrix,
    )

    ba_got = lax.ppermute(ba_send, "seq", core_pairs)
    fac_got = swap(take(fac, 1 - core), 1)
    gout_got = swap(take(gout, 1 - core), 1)
    grads, inner, payload = ready(place, ba_own, ba_got, att_mine, att_send, log)
    got_grad = lax.ppermute(payload, "seq", down)
    pay = factors(place, fac, fac_got, gout, gout_got)
    pays = [pay[0]] + [swap(pay[i], 2 * m[0] + 4 * m[1]) for i, m in list(enumerate(MOVES))[1:]]
    dkv_a, dq_a = near_backward(0, 2, qkv, probs, grads, near_stat, log, inner, pay[0])
    g_in, g_down, g_out = slabs(dkv_a, pays, width, hidden // 4)
    slab = jnp.concatenate([g.reshape(lines, g.shape[0] // lines, width) for g in (g_in, g_down, g_out)], 1)
    kept = [take(slab, line)] + [swap(take(slab, line ^ k), 8 * k) for k in range(1, lines)]
    send_fa, keep_fa = far_backward(0, place, q_a, kv_a, p_a, st_a, grads, log, inner, got_grad, slab)
    got_fa = lax.ppermute(send_fa, "seq", chip_pairs)
    send_fb, keep_fb = far_backward(1, place, q_b, kv_b, p_b, st_b, grads, log, inner, got_grad, slab)
    got_fb = lax.ppermute(send_fb, "seq", chip_pairs)
    kept = add(keep_fb, kept)
    whole = jnp.stack([kept] + [swap(kept, 8 * k) for k in range(1, lines)])
    dkv_b, dq_b = near_backward(2, 2, qkv, probs, grads, near_stat, log, inner, kept)
    d_mine, d_send, q_slabs = collect(
        place, normed, dkv_a, dkv_b, dq_a, dq_b, keep_fa, keep_fb, got_fa, got_fb, packs, gain_a, tiny
    )

    d_got = lax.ppermute(d_send, "seq", core_pairs)
    mine = 2 * chip + side
    parts = [take(q_slabs, mine)] + [swap(take(q_slabs, mine ^ (2 * m[0] + m[1])), 2 * m[0] + 4 * m[1]) for m in MOVES[1:]]
    tokens_grad = tokens_back(place, d_mine, d_got, packs, x, back_resid, gain_a)
    rows = width // 4
    part = add(q_slabs, parts)
    by_line = part[:rows].reshape(lines, rows // lines, 768)
    small = jnp.broadcast_to(part[rows:], (lines, 16, 768))
    by_line = jnp.concatenate([by_line, small], 1)
    part = add(part, [take(by_line, line)] + [swap(take(by_line, line ^ k), 8 * k) for k in range(1, lines)])
    small = part[rows // lines :]
    part = part[: rows // lines]
    zs = jnp.stack([part] + [swap(part, 8 * k) for k in range(1, lines)])
    near = jnp.stack([zs, swap(zs, 4), swap(zs, 2), swap(zs, 6)])
    far = swap(near, 1)
    small_far = swap(small, 1)
    small = small.astype(f32) + small_far.astype(f32)
    small = (small[0:4] + small[4:8])[:, :width]
    grad_qkv = unfold(place, near, far, width)

    piece = width // lines
    lane_in = whole[:, :piece]
    lane_down = whole[:, piece:]
    lane_in, lane_down = jnp.stack([lane_in, swap(lane_in, 2)]), jnp.stack([lane_down, swap(lane_down, 4)])
    lane_in, lane_down = jnp.concatenate([lane_in, swap(lane_in, 4)]), jnp.concatenate([lane_down, swap(lane_down, 2)])
    far_in, far_down = swap(lane_in, 1), swap(lane_down, 1)
    cut = hidden // 4 // lines
    grad_in, grad_down = spread_experts(place, lane_in, far_in, lane_down[:, :, :cut], far_down[:, :, :cut], hidden, width)
    outs = jnp.stack([lane_down[:, :, cut:], far_down[:, :, cut:]])
    outs = reorder(outs, core, 2)
    outs = reorder(jnp.moveaxis(outs, 1, 0), mine, 4)
    outs = reorder(jnp.moveaxis(outs, 2, 0), line, lines)
    grad_out = outs.transpose(2, 1, 0, 3, 4).reshape(width, width).astype(f32)
    return (
        block_out.reshape(layer_activations.shape),
        tokens_grad.reshape(layer_activations.shape),
        small[0],
        grad_qkv,
        grad_out,
        small[3],
        small[1:3].T,
        grad_in,
        grad_down,
    )


def solution(mesh):
    rows = P("batch", "seq", None)
    placed = (rows, P("batch"), P("batch", "seq")) + (P(),) * 8 + (rows,)
    return jax.shard_map(body, mesh=mesh, in_specs=placed, out_specs=(rows, rows) + (P(),) * 7, check_vma=False)
```

```python
import jax
import jax.numpy as jnp
from jax import lax
from jax.experimental import pallas as pl
from jax.experimental.pallas import tpu as pltpu
from jax.sharding import PartitionSpec as P

HEADS = 8
HEAD = 64
GROUP = 32
EPSILON = 1e-06
LOG2E = 1.4426950408889634
SC = 0.125 * LOG2E
MASKED = -1e30
BQ = 512
CH = 512
bf = jnp.bfloat16
f32 = jnp.float32
AXES = ("batch", "seq")
NT = (((1,), (1,)), ((), ()))
TN = (((0,), (0,)), ((), ()))


def nt(a, b):
    return lax.dot_general(a, b, NT, preferred_element_type=f32)


def tn(a, b):
    return lax.dot_general(a, b, TN, preferred_element_type=f32)


def nn(a, b):
    return jnp.dot(a, b, preferred_element_type=f32)


def rows_of(shape):
    return lax.broadcasted_iota(jnp.int32, shape, 0)


def lanes_of(shape):
    return lax.broadcasted_iota(jnp.int32, shape, 1)


def vmem():
    return pl.BlockSpec(memory_space=pltpu.VMEM)


def smem():
    return pl.BlockSpec(memory_space=pltpu.SMEM)


def params():
    return pltpu.CompilerParams(vmem_limit_bytes=60 * 2**20)


def anywhere():
    return pl.BlockSpec(memory_space=pl.ANY)


def cost(us):
    return pl.CostEstimate(flops=int(us * 1e9), bytes_accessed=2**20, transcendentals=0)


def shift_lanes(value):
    return pltpu.roll(value.astype(f32), 64, axis=1).astype(bf)


def left(first, second):
    return jnp.where(lanes_of(first.shape) < 64, first, shift_lanes(second))


def right(first, second):
    return jnp.where(lanes_of(first.shape) < 64, shift_lanes(first), second)


def project_kernel(place, x_own, x_other, gain, w, normed, qkv, send_a, send_b, packs, w_own):
    core, chip = place[0], place[1]
    block = pl.program_id(0)

    @pl.when(block == 0)
    def _():
        for c in range(2):
            q = w[:, 256 * c : 256 * c + 256]
            packs[c, :, 0:256] = q
            for h in range(4):
                at = 256 * c + 128 * (h // 2)
                k = w[:, 512 + at : 640 + at]
                v = w[:, 1024 + at : 1152 + at]
                pair = left(k, v) if h % 2 == 0 else right(k, v)
                packs[c, :, 256 + 128 * h : 384 + 128 * h] = pair
        for h in range(4):
            q = packs[core, :, 128 * (h // 2) : 128 * (h // 2) + 128]
            q = q if h % 2 == 0 else shift_lanes(q)
            w_own[:, 256 * h : 256 * h + 128] = jnp.where(lanes_of(q.shape) < 64, q, jnp.zeros((), bf))
            w_own[:, 256 * h + 128 : 256 * h + 256] = packs[core, :, 256 + 128 * h : 384 + 128 * h]

    def go(x_ref):
        x = x_ref[...].astype(f32)
        inverse = lax.rsqrt(jnp.mean(x * x, axis=1, keepdims=True) + EPSILON)
        low = (x * inverse * gain[...]).astype(bf)
        normed[...] = low
        out = nn(low, w_own[...]).astype(bf)
        qkv[...] = out
        send_b[...] = out[:, 384:512]

        @pl.when(chip == 0)
        def _():
            send_a[...] = out[:, 128:256]

        @pl.when(chip == 1)
        def _():
            send_a[...] = left(out[:, 512:640], out[:, 768:896])

    @pl.when(block // 2 == core)
    def _():
        go(x_own)

    @pl.when(block // 2 != core)
    def _():
        go(x_other)


def project(place, x_own, x_other, gain, w):
    rows, width = x_own.shape

    def own(b, p):
        return (jnp.where(b // 2 == p[0], b % 2, jnp.where(b // 2 > p[0], 1, 0)), 0)

    def other(b, p):
        return (jnp.where(b // 2 != p[0], b % 2, jnp.where(b // 2 > 1 - p[0], 1, 0)), 0)

    half = rows // 2
    return pl.pallas_call(
        project_kernel,
        grid_spec=pltpu.PrefetchScalarGridSpec(
            num_scalar_prefetch=1,
            grid=(4,),
            in_specs=[
                pl.BlockSpec((half, width), own),
                pl.BlockSpec((half, width), other),
                pl.BlockSpec((1, width), lambda b, p: (0, 0)),
                pl.BlockSpec((width, 3 * width), lambda b, p: (0, 0)),
            ],
            out_specs=[
                pl.BlockSpec((half, width), lambda b, p: (b, 0)),
                pl.BlockSpec((half, 1024), lambda b, p: (b, 0)),
                pl.BlockSpec((half, 128), lambda b, p: (b, 0)),
                pl.BlockSpec((half, 128), lambda b, p: (b, 0)),
                pl.BlockSpec((2, width, 768), lambda b, p: (0, 0, 0)),
            ],
            scratch_shapes=[pltpu.VMEM((width, 1024), bf)],
        ),
        out_shape=[
            jax.ShapeDtypeStruct((2 * rows, width), bf),
            jax.ShapeDtypeStruct((2 * rows, 1024), bf),
            jax.ShapeDtypeStruct((2 * rows, 128), bf),
            jax.ShapeDtypeStruct((2 * rows, 128), bf),
            jax.ShapeDtypeStruct((2, width, 768), bf),
        ],
        compiler_params=params(),
        cost_estimate=cost(4),
    )(place, x_own, x_other, gain, w)


def scores(kv, q, s_ref, slot, kmax, q0, limit, causal):
    peak = None
    for k0 in range(0, kmax, CH):
        s = nt(kv[k0 : k0 + CH, :], q)
        if causal:
            if k0 >= 1024:
                s = jnp.where(rows_of(s.shape) + k0 < limit, s, MASKED)
            if k0 + CH > q0:
                s = jnp.where(rows_of(s.shape) + (k0 - q0) <= lanes_of(s.shape), s, MASKED)
        s_ref[slot, k0 : k0 + CH, :] = s
        m = jnp.max(s, axis=0, keepdims=True)
        peak = m if peak is None else jnp.maximum(peak, m)
    return peak


def weigh(vt, s_ref, slot, peak, kmax, put):
    scaled = peak * SC
    acc = None
    for k0 in range(0, kmax, CH):
        p = jnp.exp2(s_ref[slot, k0 : k0 + CH, :] * SC - scaled).astype(bf)
        put(k0 // CH, p)
        d = nn(vt[:, k0 : k0 + CH], p)
        acc = d if acc is None else acc + d
    total = acc[0:1, :]
    return acc[64:128, :] * (1.0 / total), scaled, total


def ones_and_values(kv):
    vt = kv.T
    return jnp.where(rows_of(vt.shape) < 64, jnp.ones((), bf), vt)


def near_forward_kernel(limit_ref, qkv, dep, p_ref, o_ref, st_ref, s_ref, vt_ref, buf, sems):
    limit = limit_ref[0]
    count = qkv.shape[0] // BQ
    tasks = [(h, i) for h in range(2) for i in range(count)]

    def start_scores(at):
        h, i = tasks[at]
        kv = qkv.at[:, 256 * h + 128 : 256 * h + 256]
        q = qkv[i * BQ : (i + 1) * BQ, 256 * h : 256 * h + 128]
        return scores(kv, q, s_ref, at % 2, (i + 1) * BQ, i * BQ, limit, True)

    copies = []
    peak = start_scores(0)
    for at, (h, i) in enumerate(tasks):
        if i == 0:
            vt_ref[h] = ones_and_values(qkv[:, 256 * h + 128 : 256 * h + 256])
        later = start_scores(at + 1) if at + 1 < len(tasks) else None
        base = i * (i + 1) // 2

        def put(k, p):
            buf[h, base + k] = p

        out, scaled, total = weigh(vt_ref.at[h], s_ref, at % 2, peak, (i + 1) * BQ, put)
        copies.append(pltpu.make_async_copy(buf.at[h, base : base + i + 1], p_ref.at[h, base : base + i + 1], sems.at[h, i]))
        copies[-1].start()
        o_ref[h, :, i * BQ : (i + 1) * BQ] = out.astype(bf)
        st_ref[h, 0:1, i * BQ : (i + 1) * BQ] = scaled
        st_ref[h, 1:2, i * BQ : (i + 1) * BQ] = total
        peak = later
    for copy in copies:
        copy.wait()


def near_forward(pair, limit, qkv, dep):
    n = qkv.shape[0]
    count = n // BQ
    shape = (2, count * (count + 1) // 2, CH, BQ)
    return pl.pallas_call(
        near_forward_kernel,
        grid=(1,),
        in_specs=[smem(), pl.BlockSpec((n, 512), lambda g: (0, pair)), anywhere()],
        out_specs=[
            anywhere(),
            pl.BlockSpec((2, 64, n), lambda g: (0, 0, 0)),
            pl.BlockSpec((2, 8, n), lambda g: (0, 0, 0)),
        ],
        out_shape=[
            jax.ShapeDtypeStruct(shape, bf),
            jax.ShapeDtypeStruct((2, 64, n), bf),
            jax.ShapeDtypeStruct((2, 8, n), f32),
        ],
        scratch_shapes=[
            pltpu.VMEM((2, n, BQ), f32),
            pltpu.VMEM((2, 128, n), bf),
            pltpu.VMEM(shape, bf),
            pltpu.SemaphoreType.DMA((2, count)),
        ],
        compiler_params=params(),
        cost_estimate=cost(9),
    )(limit, qkv, dep)


def three(value):
    high = value.astype(bf)
    rest = value - high.astype(f32)
    mid = rest.astype(bf)
    return high, mid, (rest - mid.astype(f32)).astype(bf)


def far_forward_kernel(j, place, q_own, q_got, kv_own, kv_got, dep, p_ref, o_ref, st_ref, q_ref, kv_ref, s_ref, vt_ref, buf, sems):
    n = q_own.shape[0]

    @pl.when(place[1] == 1)
    def _():
        q_ref[...] = q_own[...]
        kv_ref[...] = kv_got[...]

    @pl.when(place[1] == 0)
    def _():
        q = q_got[...] if j == 0 else shift_lanes(q_got[...])
        q_ref[...] = jnp.where(lanes_of(q.shape) < 64, q, jnp.zeros((), bf))
        kv_ref[...] = kv_own[...]

    vt_ref[...] = ones_and_values(kv_ref[...])
    count = n // BQ
    copies = []
    peak = scores(kv_ref, q_ref[0:BQ, :], s_ref, 0, n, 0, None, False)
    for i in range(count):
        later = None
        at = slice(i * BQ, (i + 1) * BQ)
        if i + 1 < count:
            later = scores(kv_ref, q_ref[(i + 1) * BQ : (i + 2) * BQ, :], s_ref, (i + 1) % 2, n, 0, None, False)

        def put(k, p):
            buf[i, k] = p

        out, scaled, total = weigh(vt_ref, s_ref, i % 2, peak, n, put)
        copies.append(pltpu.make_async_copy(buf.at[i], p_ref.at[i], sems.at[i]))
        copies[-1].start()
        o_ref[0:64, at] = out.astype(bf)
        high, mid, low = three(scaled + jnp.log(total) * LOG2E)
        tail = jnp.concatenate([high.astype(f32), mid.astype(f32), low.astype(f32), jnp.zeros((13, BQ), f32)], 0)
        o_ref[64:80, at] = tail.astype(bf)
        st_ref[0:1, at] = scaled
        peak = later
    for copy in copies:
        copy.wait()


def far_forward(j, place, qkv, q_got, kv_got, dep):
    n = qkv.shape[0]
    whole = pl.BlockSpec((n, 128), lambda h: (0, 0))
    shape = (n // BQ, n // CH, CH, BQ)
    return pl.pallas_call(
        lambda *refs: far_forward_kernel(j, *refs),
        grid=(1,),
        in_specs=[
            smem(),
            pl.BlockSpec((n, 128), lambda h: (0, 2 * j)),
            whole,
            pl.BlockSpec((n, 128), lambda h: (0, 2 * j + 5)),
            whole,
            anywhere(),
        ],
        out_specs=[
            anywhere(),
            pl.BlockSpec((80, n), lambda h: (0, 0)),
            pl.BlockSpec((8, n), lambda h: (0, 0)),
            whole,
            whole,
        ],
        out_shape=[
            jax.ShapeDtypeStruct(shape, bf),
            jax.ShapeDtypeStruct((80, n), bf),
            jax.ShapeDtypeStruct((8, n), f32),
            jax.ShapeDtypeStruct((n, 128), bf),
            jax.ShapeDtypeStruct((n, 128), bf),
        ],
        scratch_shapes=[
            pltpu.VMEM((2, n, BQ), f32),
            pltpu.VMEM((128, n), bf),
            pltpu.VMEM(shape, bf),
            pltpu.SemaphoreType.DMA((n // BQ,)),
        ],
        compiler_params=params(),
        cost_estimate=cost(10),
    )(place, qkv, q_got, qkv, kv_got, dep)


def unsplit(ref, at):
    return ref[at : at + 1, :].astype(f32) + ref[at + 1 : at + 2, :].astype(f32) + ref[at + 2 : at + 3, :].astype(f32)


def join_kernel(place, near_a, near_b, stat_a, stat_b, far_a, far_b, got_a, got_b, mine, other, log_ref):
    core, chip = place[0], place[1]
    half = mine.shape[1]
    for h in range(4):
        far = (far_a, far_b, got_a, got_b)[h]
        near, stat = (near_a, near_b)[h // 2], (stat_a, stat_b)[h // 2]
        log_near = stat[h % 2, 0:1, :] + jnp.log(stat[h % 2, 1:2, :]) * LOG2E
        log_far = jnp.where(chip == 1, unsplit(far, 64), MASKED)
        top = jnp.maximum(log_near, log_far)
        e_near, e_far = jnp.exp2(log_near - top), jnp.exp2(log_far - top)
        both = e_near + e_far
        log_ref[h] = jnp.broadcast_to(top + jnp.log(both) * LOG2E, log_ref.shape[1:])
        far_out = jnp.where(chip == 1, far[0:64, :].astype(f32), 0.0)
        joined = ((near[h % 2].astype(f32) * e_near + far_out * e_far) * (1.0 / both)).astype(bf)
        at = slice(64 * h, 64 * h + 64)

        @pl.when(core == 0)
        def _():
            mine[at, :] = joined[:, :half]
            other[at, :] = joined[:, half:]

        @pl.when(core == 1)
        def _():
            mine[at, :] = joined[:, half:]
            other[at, :] = joined[:, :half]


def join(place, near_a, near_b, stat_a, stat_b, far_a, far_b, got_a, got_b):
    n = near_a.shape[2]
    return pl.pallas_call(
        join_kernel,
        in_specs=[smem()] + [vmem()] * 8,
        out_specs=[vmem()] * 3,
        out_shape=[
            jax.ShapeDtypeStruct((256, n // 2), bf),
            jax.ShapeDtypeStruct((256, n // 2), bf),
            jax.ShapeDtypeStruct((4, 8, n), f32),
        ],
        compiler_params=params(),
        cost_estimate=cost(2),
    )(place, near_a, near_b, stat_a, stat_b, far_a, far_b, got_a, got_b)


def mixture_kernel(
    place, sharp, x, att_own, att_got, wout, gain, router, labels, gy, w1_hbm, w2_hbm,
    block_out, fac, gout, tiny, back_resid, ba_own, ba_other, w1, w2, sems,
):
    core = place[0]
    copy1 = pltpu.make_async_copy(w1_hbm, w1, sems.at[0])
    copy2 = pltpu.make_async_copy(w2_hbm, w2, sems.at[1])
    copy1.start()
    copy2.start()
    own_rows = pl.ds(pl.multiple_of(core * 256, 256), 256)
    other_rows = pl.ds(pl.multiple_of(256 - core * 256, 256), 256)
    wo_own, wo_other = wout[own_rows, :], wout[other_rows, :]
    resid = x[...].astype(f32) + tn(att_own[...], wo_own) + tn(att_got[...], wo_other)
    inverse = lax.rsqrt(jnp.mean(resid * resid, axis=1, keepdims=True) + EPSILON)
    unit = resid * inverse
    mix = (unit * gain[...]).astype(bf)
    temper = 1.0 / sharp[0]
    logits = nt(router[...], mix) * temper
    tokens = mix.shape[0]
    groups = tokens // GROUP
    member = labels[...] == rows_of((groups, tokens))
    weights, mixing = [], []
    for e in range(2):
        row = logits[e : e + 1, :]
        peak = jnp.max(jnp.where(member, row, -jnp.inf), axis=1, keepdims=True)
        token_peak = jnp.sum(jnp.where(member, peak, 0.0), axis=0, keepdims=True)
        raised = jnp.exp(row - token_peak)
        total = jnp.sum(jnp.where(member, raised, 0.0), axis=1, keepdims=True)
        token_total = jnp.sum(jnp.where(member, total, 0.0), axis=0, keepdims=True)
        w = raised / token_total
        weights.append(w)
        mixing.append(jnp.where(member, w, 0.0))
    mixing = jnp.concatenate(mixing, 0).astype(bf)
    mixed = nn(mixing, mix).astype(bf)
    back_expert = nn(mixing, gy[...]).astype(bf)
    copy1.wait()
    copy2.wait()
    expert_out, back_mixed = [], []
    quarter = w1.shape[2] // 4
    width = mix.shape[1]
    for e in range(2):
        at = slice(groups * e, groups * (e + 1))
        inner = nn(mixed[at], w1[e])
        cdf = 0.5 * (1.0 + lax.erf(inner * 0.7071067811865476))
        active = (inner * cdf).astype(bf)
        slope = cdf + inner * (jnp.exp(-0.5 * inner * inner) * 0.3989422804014327)
        expert_out.append(nn(active, w2[e]))
        back_inner = (slope * nt(back_expert[at], w2[e])).astype(bf)
        back_mixed.append(nt(back_inner, w1[e]))
        fac[e, :, 0:width] = mixed[at]
        fac[e, :, width : 2 * width] = back_expert[at]
        for q in range(4):
            base = 2 * width + 2 * quarter * q
            fac[e, :, base : base + quarter] = back_inner[:, quarter * q : quarter * (q + 1)]
            fac[e, :, base + quarter : base + 2 * quarter] = active[:, quarter * q : quarter * (q + 1)]
    expert_out = jnp.concatenate(expert_out, 0).astype(bf)
    back_mixed = jnp.concatenate(back_mixed, 0).astype(bf)
    block_out[...] = (resid + tn(mixing, expert_out)).astype(bf)
    spread = nt(expert_out, gy[...]) + nt(back_mixed, mix)
    rows16 = rows_of((16, tokens))
    back_logits = jnp.zeros((16, tokens), f32)
    for e in range(2):
        back_weight = jnp.sum(jnp.where(member, spread[groups * e : groups * (e + 1)], 0.0), axis=0, keepdims=True)
        w = weights[e]
        inner = jnp.sum(jnp.where(member, w * back_weight, 0.0), axis=1, keepdims=True)
        token_inner = jnp.sum(jnp.where(member, inner, 0.0), axis=0, keepdims=True)
        back_logits = jnp.where(rows16 == e, w * (back_weight - token_inner) * temper, back_logits)
    back_logits = back_logits.astype(bf)
    ctrl = nn(back_logits, mix)
    back_mix = tn(mixing, back_mixed) + tn(back_logits, router[...])
    tiny[...] = jnp.zeros_like(tiny)
    tiny[0:2, :] = ctrl[0:2, :]
    tiny[2:3, :] = jnp.sum(back_mix * unit, axis=0, keepdims=True)
    n = back_mix * gain[...]
    mean = jnp.mean(n * resid, axis=1, keepdims=True)
    back = gy[...].astype(f32) + inverse * n - resid * (inverse * inverse * inverse * mean)
    back_resid[...] = back
    branch = back.astype(bf)
    gout[core] = nn(att_own[...], branch).astype(bf)
    gout[1 - core] = nn(att_got[...], branch).astype(bf)
    ba_own[...] = nt(wo_own, branch).astype(bf)
    ba_other[...] = nt(wo_other, branch).astype(bf)


def mixture(place, sharp, x, att_own, att_got, wout, gain, router, labels, gy, w1, w2):
    tokens, width = x.shape
    hidden = w1.shape[2]
    groups = tokens // GROUP
    return pl.pallas_call(
        mixture_kernel,
        in_specs=[smem(), smem()] + [vmem()] * 8 + [pl.BlockSpec(memory_space=pl.ANY)] * 2,
        out_specs=[vmem()] * 7,
        out_shape=[
            jax.ShapeDtypeStruct((tokens, width), bf),
            jax.ShapeDtypeStruct((2, groups, 2 * width + 2 * hidden), bf),
            jax.ShapeDtypeStruct((2, width // 2, width), bf),
            jax.ShapeDtypeStruct((8, width), f32),
            jax.ShapeDtypeStruct((tokens, width), f32),
            jax.ShapeDtypeStruct((width // 2, tokens), bf),
            jax.ShapeDtypeStruct((width // 2, tokens), bf),
        ],
        scratch_shapes=[pltpu.VMEM(w1.shape, bf), pltpu.VMEM(w2.shape, bf), pltpu.SemaphoreType.DMA((2,))],
        compiler_params=params(),
        cost_estimate=cost(15),
    )(place, sharp, x, att_own, att_got, wout, gain, router, labels, gy, w1, w2)


def ready_kernel(place, ba_own, ba_got, mine, other, log_ref, grads, inner, payload):
    core = place[0]
    half = mine.shape[1]
    for h in range(4):
        at = slice(64 * h, 64 * h + 64)
        g_own, g_got = ba_own[at, :], ba_got[at, :]
        d_own = jnp.sum(g_own.astype(f32) * mine[at, :].astype(f32), axis=0, keepdims=True)
        d_got = jnp.sum(g_got.astype(f32) * other[at, :].astype(f32), axis=0, keepdims=True)

        def put(g0, g1, d0, d1):
            grads[h, :, :half] = g0
            grads[h, :, half:] = g1
            inner[h, :, :half] = jnp.broadcast_to(d0, (8, half))
            inner[h, :, half:] = jnp.broadcast_to(d1, (8, half))
            if h >= 2:
                for g, d, s in ((g0, d0, slice(0, half)), (g1, d1, slice(half, 2 * half))):
                    payload[h - 2, 0:64, s] = g
                    parts = three(log_ref[h, 0:1, s]) + three(d)
                    tail = jnp.concatenate([part.astype(f32) for part in parts] + [jnp.zeros((10, half), f32)], 0)
                    payload[h - 2, 64:80, s] = tail.astype(bf)

        @pl.when(core == 0)
        def _():
            put(g_own, g_got, d_own, d_got)

        @pl.when(core == 1)
        def _():
            put(g_got, g_own, d_got, d_own)


def ready(place, ba_own, ba_got, mine, other, log):
    half = mine.shape[1]
    return pl.pallas_call(
        ready_kernel,
        in_specs=[smem()] + [vmem()] * 5,
        out_specs=[vmem()] * 3,
        out_shape=[
            jax.ShapeDtypeStruct((4, 64, 2 * half), bf),
            jax.ShapeDtypeStruct((4, 8, 2 * half), f32),
            jax.ShapeDtypeStruct((2, 80, 2 * half), bf),
        ],
        compiler_params=params(),
        cost_estimate=cost(2),
    )(place, ba_own, ba_got, mine, other, log)


def back_block(kv_ref, kt_ref, q, grad, ratio, inner, block, kmax, first, put_kv):
    low = (grad.astype(f32) * ratio).astype(bf)
    rhs = jnp.concatenate([jnp.zeros((64, BQ), bf), low], axis=0)
    shift = inner * ratio
    natural = rhs.T
    acc = None
    for k0 in range(0, kmax, CH):
        dp = nn(kv_ref[k0 : k0 + CH, :], rhs)
        p = block(k0 // CH)
        ds = (p.astype(f32) * (dp - shift)).astype(bf)
        d = nn(kt_ref[:, k0 : k0 + CH], ds)
        acc = d if acc is None else acc + d
        put_kv(k0, k0 >= first, nn(ds, q) + nn(p, natural))
    return (acc * 0.125).astype(bf)


def near_backward_kernel(qkv, p_ref, grad_ref, stat, log_ref, inner_ref, dep, dkv_ref, dq_ref, kt_ref, buf, sems):
    count = qkv.shape[0] // BQ
    copies = {}
    for h in range(2):
        for i in range(count):
            at = slice(i * (i + 1) // 2, (i + 1) * (i + 2) // 2)
            copies[h, i] = pltpu.make_async_copy(p_ref.at[h, at], buf.at[h, at], sems.at[h, i])
            copies[h, i].start()
    for h in range(2):
        kv_ref = qkv.at[:, 256 * h + 128 : 256 * h + 256]
        kt_ref[h] = kv_ref[...].T[0:64, :]

        def put(k0, fresh, value):
            if fresh:
                dkv_ref[h, k0 : k0 + CH, :] = value
            else:
                dkv_ref[h, k0 : k0 + CH, :] += value

        for i in range(count):
            at = slice(i * BQ, (i + 1) * BQ)
            base = i * (i + 1) // 2
            copies[h, i].wait()
            ratio = jnp.exp2(stat[h, 0:1, at] - log_ref[h, 0:1, at])
            q = qkv[at, 256 * h : 256 * h + 128]

            def block(k):
                return buf[h, base + k]

            dq_ref[h, :, at] = back_block(
                kv_ref, kt_ref.at[h], q, grad_ref[h, :, at], ratio, inner_ref[h, 0:1, at], block, (i + 1) * BQ, i * BQ, put
            )


def near_backward(pair, qkv, p, grads, stat, log, inner, dep):
    n = qkv.shape[0]
    row = pl.BlockSpec((2, 8, n), lambda g: (pair, 0, 0))
    return pl.pallas_call(
        near_backward_kernel,
        grid=(1,),
        in_specs=[
            pl.BlockSpec((n, 512), lambda g: (0, pair)),
            anywhere(),
            pl.BlockSpec((2, 64, n), lambda g: (pair, 0, 0)),
            pl.BlockSpec((2, 8, n), lambda g: (0, 0, 0)),
            row,
            row,
            anywhere(),
        ],
        out_specs=[pl.BlockSpec((2, n, 128), lambda g: (0, 0, 0)), pl.BlockSpec((2, 64, n), lambda g: (0, 0, 0))],
        out_shape=[jax.ShapeDtypeStruct((2, n, 128), f32), jax.ShapeDtypeStruct((2, 64, n), bf)],
        scratch_shapes=[pltpu.VMEM((2, 64, n), bf), pltpu.VMEM(p.shape, bf), pltpu.SemaphoreType.DMA((2, n // BQ))],
        compiler_params=params(),
        cost_estimate=cost(13),
    )(qkv, p, grads, stat, log, inner, dep)


def far_backward_kernel(
    place, q_ref, kv_ref, p_ref, stat, grad_own, log_own, inner_own, got, dep, send_ref, keep_ref, kt_ref, sum_ref, dq_ref, buf, sems
):
    kt_ref[...] = kv_ref[...].T[0:64, :]
    upper = place[1] == 1
    n = q_ref.shape[0]
    copies = [pltpu.make_async_copy(p_ref.at[i], buf.at[i], sems.at[i]) for i in range(n // BQ)]
    for copy in copies:
        copy.start()

    def put(k0, fresh, value):
        if fresh:
            sum_ref[k0 : k0 + CH, :] = value
        else:
            sum_ref[k0 : k0 + CH, :] += value

    for i in range(n // BQ):
        at = slice(i * BQ, (i + 1) * BQ)
        got_log = got[0, 64:67, at].astype(f32)
        got_inner = got[0, 67:70, at].astype(f32)
        log = jnp.where(upper, log_own[0, 0:1, at], jnp.sum(got_log, axis=0, keepdims=True))
        inner = jnp.where(upper, inner_own[0, 0:1, at], jnp.sum(got_inner, axis=0, keepdims=True))
        grad = jnp.where(upper, grad_own[0, :, at], got[0, 0:64, at])
        ratio = jnp.exp2(stat[0:1, at] - log)
        copies[i].wait()

        def block(k):
            return buf[i, k]

        dq = back_block(kv_ref, kt_ref, q_ref[at, :], grad, ratio, inner, block, n, 0 if i == 0 else n, put)
        dq_ref[at, :] = jnp.concatenate([dq, jnp.zeros((64, BQ), bf)], 0).T

    @pl.when(upper)
    def _():
        send_ref[...] = sum_ref[...].astype(bf)
        keep_ref[...] = dq_ref[...]

    @pl.when(jnp.logical_not(upper))
    def _():
        send_ref[...] = dq_ref[...]
        keep_ref[...] = sum_ref[...].astype(bf)


def far_backward(j, place, q, kv, p, stat, grads, log, inner, got, dep):
    n = q.shape[0]
    row = pl.BlockSpec((1, 8, n), lambda h: (j, 0, 0))
    whole = pl.BlockSpec((n, 128), lambda h: (0, 0))
    return pl.pallas_call(
        far_backward_kernel,
        grid=(1,),
        in_specs=[
            smem(),
            whole,
            whole,
            anywhere(),
            pl.BlockSpec((8, n), lambda h: (0, 0)),
            pl.BlockSpec((1, 64, n), lambda h: (j, 0, 0)),
            row,
            row,
            pl.BlockSpec((1, 80, n), lambda h: (j, 0, 0)),
            pl.BlockSpec(memory_space=pl.ANY),
        ],
        out_specs=[whole, whole],
        out_shape=[jax.ShapeDtypeStruct((n, 128), bf)] * 2,
        scratch_shapes=[
            pltpu.VMEM((64, n), bf),
            pltpu.VMEM((n, 128), f32),
            pltpu.VMEM((n, 128), bf),
            pltpu.VMEM(p.shape, bf),
            pltpu.SemaphoreType.DMA((n // BQ,)),
        ],
        compiler_params=params(),
        cost_estimate=cost(13),
    )(place, q, kv, p, stat, grads, log, inner, got, dep)


def swap(value, bits):
    count = lax.axis_size("batch") * lax.axis_size("seq")
    return lax.ppermute(value, AXES, [(i, i ^ bits) for i in range(count)])


def turns():
    bits = (lax.axis_size("batch") // 2).bit_length() - 1
    return [(t, bits - 1 - t) for t in range(bits)]


def swap_by_core(value, bits):
    count = lax.axis_size("batch") * lax.axis_size("seq")
    return lax.ppermute(value, AXES, [(i, i ^ bits[i % 2]) for i in range(count)])


def bit_of(line, core, pair):
    return (line >> jnp.where(core == 0, pair[0], pair[1])) & 1


def take(value, index, axis=0):
    return lax.dynamic_index_in_dim(value, index, axis, keepdims=False)


MOVES = ((0, 0), (1, 0), (0, 1), (1, 1))


def factors_kernel(place, fac, got, gout, got_out, *outs):
    core, chip, side = place[0], place[1], place[2]
    groups = got.shape[0]
    width = gout.shape[2]
    part = (got.shape[1] - 2 * width) // 4
    rows = gout.shape[1] // 4
    for (x, y), out in zip(MOVES, outs):
        index = 2 * (chip ^ x) + (side ^ y)
        lanes = pl.ds(pl.multiple_of(2 * width + index * part, 128), part)
        at = pl.ds(pl.multiple_of(index * rows, rows), rows)
        out[0:groups, 0 : 2 * width] = fac[core, :, 0 : 2 * width]
        out[groups:, 0 : 2 * width] = got[:, 0 : 2 * width]
        out[0:groups, 2 * width : 2 * width + part] = fac[core, :, lanes]
        out[groups:, 2 * width : 2 * width + part] = got[:, lanes]
        out[:, 2 * width + part :] = (gout[core, at, :].astype(f32) + got_out[at, :].astype(f32)).astype(bf)


def factors(place, fac, got, gout, got_out):
    groups, per = got.shape
    width = gout.shape[2]
    shape = jax.ShapeDtypeStruct((2 * groups, 2 * width + (per - 2 * width) // 4 + width), bf)
    return pl.pallas_call(
        factors_kernel,
        in_specs=[smem()] + [vmem()] * 4,
        out_specs=[vmem()] * 4,
        out_shape=[shape] * 4,
        compiler_params=params(),
        cost_estimate=cost(2),
    )(place, fac, got, gout, got_out)


def slab_kernel(turn, lines, place, dep, a, b, c, d, keep, send):
    core, line = place[0], place[3]
    width = keep.shape[2]
    quarter = (a.shape[1] - 3 * width) // 2

    def lanes(start, size):
        return jnp.concatenate([ref[:, start : start + size] for ref in (a, b, c, d)], 0)

    g_in = tn(lanes(0, width), lanes(2 * width, quarter)).astype(bf)
    g_down = tn(lanes(2 * width + quarter, quarter), lanes(width, width)).astype(bf)
    total = a[:, 2 * width + 2 * quarter :].astype(f32)
    for ref in (b, c, d):
        total = total + ref[:, 2 * width + 2 * quarter :].astype(f32)
    pieces = [total.astype(bf), g_in, g_down]
    bits = lines.bit_length() - 1
    for z in range(lines):
        flipped = sum(((z >> t) & 1) << (bits - 1 - t) for t in range(bits))
        spot = jnp.where(core == 0, flipped, z)
        chosen = bit_of(z, core, turn) == bit_of(line, core, turn)

        def put(ref):
            start = 0
            for piece in pieces[1:] + pieces[:1]:
                rows = piece.shape[0] // lines
                ref[spot % (lines // 2), start : start + rows, :] = piece[z * rows : (z + 1) * rows, :]
                start += rows

        @pl.when(chosen)
        def _():
            put(keep)

        @pl.when(jnp.logical_not(chosen))
        def _():
            put(send)


def slabs(place, dep, payloads, width, quarter, lines):
    rows = (width + quarter + payloads[0].shape[0]) // lines
    shape = jax.ShapeDtypeStruct((lines // 2, rows, width), bf)
    turn = turns()[0]
    return pl.pallas_call(
        lambda *refs: slab_kernel(turn, lines, *refs),
        in_specs=[smem(), anywhere()] + [vmem()] * 4,
        out_specs=[vmem()] * 2,
        out_shape=[shape] * 2,
        compiler_params=params(),
        cost_estimate=cost(2),
    )(place, dep, *payloads)


def fold_kernel(turn, place, dep, kept, got, keep, *send):
    if turn is None:
        keep[...] = (kept[...].astype(f32) + got[...].astype(f32)).astype(bf)
        return
    half = keep.shape[0]
    mine = bit_of(place[3], place[0], turn)
    at = pl.ds(mine * half, half)
    keep[...] = (kept[at].astype(f32) + got[at].astype(f32)).astype(bf)
    at = pl.ds((1 - mine) * half, half)
    send[0][...] = (kept[at].astype(f32) + got[at].astype(f32)).astype(bf)


def fold(turn, place, dep, kept, got):
    count = kept.shape[0] if turn is None else kept.shape[0] // 2
    shape = jax.ShapeDtypeStruct((count,) + kept.shape[1:], bf)
    outs = 1 if turn is None else 2
    return pl.pallas_call(
        lambda *refs: fold_kernel(turn, *refs),
        in_specs=[smem(), anywhere(), vmem(), vmem()],
        out_specs=[vmem()] * outs,
        out_shape=[shape] * outs,
        compiler_params=params(),
        cost_estimate=cost(1),
    )(place, dep, kept, got)


def pile_kernel(dep, a, b, out):
    half = out.shape[0] // 2
    out[:half] = a[...]
    out[half:] = b[...]


def pile(dep, a, b):
    return pl.pallas_call(
        pile_kernel,
        in_specs=[anywhere(), vmem(), vmem()],
        out_specs=vmem(),
        out_shape=jax.ShapeDtypeStruct((2 * a.shape[0],) + a.shape[1:], bf),
        compiler_params=params(),
        cost_estimate=cost(1),
    )(dep, a, b)


def add_kernel(dep, *refs):
    total = refs[0][...].astype(f32)
    for ref in refs[1:-1]:
        total = total + ref[...].astype(f32)
    refs[-1][...] = total.astype(bf)


def add(dep, values):
    return pl.pallas_call(
        add_kernel,
        in_specs=[pl.BlockSpec(memory_space=pl.ANY)] + [vmem()] * len(values),
        out_specs=vmem(),
        out_shape=jax.ShapeDtypeStruct(values[0].shape, bf),
        compiler_params=params(),
        cost_estimate=cost(1),
    )(dep, *values)


def spread_kernel(place, near_a, near_b, far_a, far_b, in_ref, down_ref, out_ref):
    expert, q = pl.program_id(0), pl.program_id(1)
    line = place[3]
    lines = near_a.shape[1]
    width = in_ref.shape[1]
    cut_in = width // lines
    cut_down = down_ref.shape[1] // lines
    bits = lines.bit_length() - 1
    move_x, move_y = (q // 2) ^ place[1], (q % 2) ^ place[2]
    outer = jnp.where(expert == 0, move_y, move_x)

    def put(ref):
        for k in range(lines):
            flipped = sum(((k >> t) & 1) << (bits - 1 - t) for t in range(bits))
            z = line ^ jnp.where(expert == 0, flipped, k)
            in_ref[0, pl.ds(pl.multiple_of(z * cut_in, cut_in), cut_in), :] = ref[0, k, :cut_in].astype(f32)
            down_ref[0, pl.ds(pl.multiple_of(z * cut_down, cut_down), cut_down), :] = ref[0, k, cut_in : cut_in + cut_down].astype(f32)
            out_ref[0, z] = ref[0, k, cut_in + cut_down :].astype(f32)

    for near, pair in ((True, (near_a, near_b)), (False, (far_a, far_b))):
        for side in range(2):

            @pl.when(((expert == place[0]) == near) & (outer == side))
            def _():
                put(pair[side])


def spread_experts(place, near_a, near_b, far_a, far_b, hidden, width):
    block = near_a.shape[1:]
    lines = block[0]

    def spec(near):
        def index(e, q, p):
            move_x, move_y = (q // 2) ^ p[1], (q % 2) ^ p[2]
            inner = jnp.where(e == 0, move_x, move_y)
            return (jnp.where((e == p[0]) == near, inner, 0), 0, 0, 0)

        return pl.BlockSpec((1,) + block, index)

    return pl.pallas_call(
        spread_kernel,
        grid_spec=pltpu.PrefetchScalarGridSpec(
            num_scalar_prefetch=1,
            grid=(2, 4),
            in_specs=[spec(True), spec(True), spec(False), spec(False)],
            out_specs=[
                pl.BlockSpec((1, width, hidden // 4), lambda e, q, p: (e, 0, q)),
                pl.BlockSpec((1, hidden // 4, width), lambda e, q, p: (e, q, 0)),
                pl.BlockSpec((1, lines, width // 8 // lines, width), lambda e, q, p: (e * 4 + q, 0, 0, 0)),
            ],
        ),
        out_shape=[
            jax.ShapeDtypeStruct((2, width, hidden), f32),
            jax.ShapeDtypeStruct((2, hidden, width), f32),
            jax.ShapeDtypeStruct((8, lines, width // 8 // lines, width), f32),
        ],
        compiler_params=params(),
        cost_estimate=cost(8),
    )(place, near_a, near_b, far_a, far_b)


def own_block(b, p):
    return jnp.where(b // 2 == p[0], b % 2, jnp.where(b // 2 > p[0], 1, 0))


def other_block(b, p):
    return jnp.where(b // 2 != p[0], b % 2, jnp.where(b // 2 > 1 - p[0], 1, 0))


def collect_kernel(
    place, normed, kv_a, kv_b, q_a, q_b, keep_a, keep_b, got_a, got_b, packs, gain, tiny, dep, mine, other, slabs_ref, sum_ref
):
    block = pl.program_id(0)
    upper = place[1] == 1
    dq = jnp.concatenate([q_a[0], q_a[1], q_b[0], q_b[1]], 0).T.astype(f32)
    far = jnp.concatenate([left(keep_a[...], keep_b[...]), left(got_a[...], got_b[...])], 1).astype(f32)
    pieces = [(dq + jnp.where(upper, far, 0.0)).astype(bf)]
    for near, h, extra in ((kv_a, 0, got_a), (kv_a, 1, got_b), (kv_b, 0, keep_a), (kv_b, 1, keep_b)):
        value = near[h] + jnp.where(upper, 0.0, extra[...].astype(f32))
        pieces.append(jnp.where(lanes_of(value.shape) < 64, value * 0.125, value).astype(bf))
    back = jnp.concatenate(pieces, 1)

    @pl.when(block // 2 == place[0])
    def _():
        mine[...] = back

    @pl.when(block // 2 != place[0])
    def _():
        other[...] = back

    part = tn(normed[...], back)

    @pl.when(block == 0)
    def _():
        sum_ref[...] = part

    @pl.when(block > 0)
    def _():
        sum_ref[...] += part

    @pl.when(block == 3)
    def _():
        total = sum_ref[...]
        width = total.shape[0]
        product = total * packs[place[0]].astype(f32)
        ones = jnp.ones((8, total.shape[1]), f32)
        summed = lax.dot_general(ones, product, NT, precision=lax.Precision.HIGHEST, preferred_element_type=f32)
        values = [summed[0:1, :] / gain[...], tiny[0:1, :], tiny[1:2, :], tiny[2:3, :]]
        rows = rows_of((16, width))
        small = jnp.zeros((16, width), f32)
        for r, value in enumerate(values):
            high = value.astype(bf).astype(f32)
            small = jnp.where(rows == r, high, jnp.where(rows == r + 4, value - high, small))
        small = jnp.concatenate([small.astype(bf), jnp.zeros((16, total.shape[1] - width), bf)], 1)
        for q in range(4):
            slabs_ref[q, 0 : width // 4, :] = total[q * width // 4 : (q + 1) * width // 4, :].astype(bf)
            slabs_ref[q, width // 4 :, :] = small


def collect(place, normed, kv_a, kv_b, q_a, q_b, keep_a, keep_b, got_a, got_b, packs, gain, tiny, dep):
    n, width = normed.shape
    rows = n // 4
    kv = pl.BlockSpec((2, rows, 128), lambda b, p: (0, b, 0))
    dq = pl.BlockSpec((2, 64, rows), lambda b, p: (0, 0, b))
    flat = pl.BlockSpec((rows, 128), lambda b, p: (b, 0))
    return pl.pallas_call(
        collect_kernel,
        grid_spec=pltpu.PrefetchScalarGridSpec(
            num_scalar_prefetch=1,
            grid=(4,),
            in_specs=[
                pl.BlockSpec((rows, width), lambda b, p: (b, 0)),
                kv, kv, dq, dq, flat, flat, flat, flat,
                pl.BlockSpec(packs.shape, lambda b, p: (0, 0, 0)),
                pl.BlockSpec((1, width), lambda b, p: (0, 0)),
                pl.BlockSpec(tiny.shape, lambda b, p: (0, 0)),
                anywhere(),
            ],
            out_specs=[
                pl.BlockSpec((rows, 768), lambda b, p: (own_block(b, p), 0)),
                pl.BlockSpec((rows, 768), lambda b, p: (other_block(b, p), 0)),
                pl.BlockSpec((4, width // 4 + 16, 768), lambda b, p: (0, 0, 0)),
            ],
            scratch_shapes=[pltpu.VMEM((width, 768), f32)],
        ),
        out_shape=[
            jax.ShapeDtypeStruct((n // 2, 768), bf),
            jax.ShapeDtypeStruct((n // 2, 768), bf),
            jax.ShapeDtypeStruct((4, width // 4 + 16, 768), bf),
        ],
        compiler_params=params(),
        cost_estimate=cost(5),
    )(place, normed, kv_a, kv_b, q_a, q_b, keep_a, keep_b, got_a, got_b, packs, gain, tiny, dep)


def tokens_kernel(place, mine, got, packs, x_ref, back_resid, gain, dep, out):
    core = place[0]
    back = nt(mine[...], packs[core]) + nt(got[...], packs[1 - core])
    x = x_ref[...].astype(f32)
    inverse = lax.rsqrt(jnp.mean(x * x, axis=1, keepdims=True) + EPSILON)
    k = back * gain[...]
    mean = jnp.mean(k * x, axis=1, keepdims=True)
    out[...] = (back_resid[...] + inverse * k - x * (inverse * inverse * inverse * mean)).astype(bf)


def tokens_back(place, mine, got, packs, x, back_resid, gain, dep):
    n, width = x.shape
    rows = n // 4
    wide = pl.BlockSpec((rows, 768), lambda b, p: (b, 0))
    block = pl.BlockSpec((rows, width), lambda b, p: (b, 0))
    return pl.pallas_call(
        tokens_kernel,
        grid_spec=pltpu.PrefetchScalarGridSpec(
            num_scalar_prefetch=1,
            grid=(4,),
            in_specs=[wide, wide, pl.BlockSpec(packs.shape, lambda b, p: (0, 0, 0)), block, block, pl.BlockSpec((1, width), lambda b, p: (0, 0)), anywhere()],
            out_specs=block,
        ),
        out_shape=jax.ShapeDtypeStruct((n, width), bf),
        compiler_params=params(),
        cost_estimate=cost(4),
    )(place, mine, got, packs, x, back_resid, gain, dep)


def unfold_kernel(place, near, far, small, small_far, out, rows_out):
    line = place[3]
    width = rows_out.shape[1]
    both = small[0:8, :width].astype(f32) + small_far[0:8, :width].astype(f32)
    rows_out[...] = both + pltpu.roll(both, 4, axis=0)
    count, rows = near.shape[1], near.shape[2]
    for source, c in ((near, place[0]), (far, 1 - place[0])):
        for k in range(count):
            at = pl.ds(pl.multiple_of((line ^ k) * rows, rows), rows)
            value = source[0, k]
            base = c * 256
            out[at, pl.ds(pl.multiple_of(base, 128), 256)] = value[:, 0:256].astype(f32)
            for pair in range(2):
                a = value[:, 256 + 256 * pair : 384 + 256 * pair]
                b = value[:, 384 + 256 * pair : 512 + 256 * pair]
                out[at, pl.ds(pl.multiple_of(512 + base + 128 * pair, 128), 128)] = left(a, b).astype(f32)
                out[at, pl.ds(pl.multiple_of(1024 + base + 128 * pair, 128), 128)] = right(a, b).astype(f32)


def unfold(place, near, far, small, small_far, width):
    block = near.shape[1:]
    piece = pl.BlockSpec((1,) + block, lambda q, p: (q ^ (2 * p[1] + p[2]), 0, 0, 0))
    tail = pl.BlockSpec(small.shape, lambda q, p: (0, 0))
    return pl.pallas_call(
        unfold_kernel,
        grid_spec=pltpu.PrefetchScalarGridSpec(
            num_scalar_prefetch=1,
            grid=(4,),
            in_specs=[piece, piece, tail, tail],
            out_specs=[pl.BlockSpec((width // 4, 3 * width), lambda q, p: (q, 0)), pl.BlockSpec((8, width), lambda q, p: (0, 0))],
        ),
        out_shape=[jax.ShapeDtypeStruct((width, 3 * width), f32), jax.ShapeDtypeStruct((8, width), f32)],
        compiler_params=params(),
        cost_estimate=cost(3),
    )(place, near, far, small, small_far)


def body(
    layer_activations,
    sequence_extents,
    position_cluster_label,
    cluster_sharpness,
    heed_scale_factor,
    triple_entry_matrix,
    heed_exit_matrix,
    blend_scale_factor,
    router_matrix,
    specialist_entry_matrix,
    specialist_exit_matrix,
    upstream_derivative,
):
    seq_count, pos_count, width = layer_activations.shape
    tokens = seq_count * pos_count
    hidden = specialist_entry_matrix.shape[2]
    spot = lax.axis_index("seq")
    row = lax.axis_index("batch")
    core, chip, side, line = spot % 2, spot // 2, row % 2, row // 2
    lines = lax.axis_size("batch") // 2
    place = jnp.stack([core, chip, side, line]).astype(jnp.int32)
    core_pairs, chip_pairs = [(0, 1), (1, 0), (2, 3), (3, 2)], [(0, 2), (1, 3), (2, 0), (3, 1)]
    up, down = chip_pairs[:2], chip_pairs[2:]

    x = layer_activations.reshape(tokens, width)
    x_other = lax.ppermute(x, "seq", core_pairs)
    gain_a = heed_scale_factor.astype(f32).reshape(1, width)
    normed, qkv, send_a, send_b, packs = project(place, x, x_other, gain_a, triple_entry_matrix)
    got_a = lax.ppermute(send_a, "seq", chip_pairs)
    got_b = lax.ppermute(send_b, "seq", up)
    limit = (sequence_extents - chip * 2 * pos_count).astype(jnp.int32)
    p_na, o_na, st_na = near_forward(0, limit, qkv, qkv)
    p_a, o_a, st_a, q_a, kv_a = far_forward(0, place, qkv, got_a, got_a, o_na)
    got_oa = lax.ppermute(o_a, "seq", up)
    p_b, o_b, st_b, q_b, kv_b = far_forward(1, place, qkv, got_a, got_b, o_a)
    got_ob = lax.ppermute(o_b, "seq", up)
    p_nb, o_nb, st_nb = near_forward(1, limit, qkv, o_b)
    att_mine, att_send, log = join(place, o_na, o_nb, st_na, st_nb, o_a, o_b, got_oa, got_ob)
    att_got = lax.ppermute(att_send, "seq", core_pairs)

    router = jnp.zeros((16, width), bf).at[:2].set(router_matrix.T)
    block_out, fac, gout, tiny, back_resid, ba_own, ba_send = mixture(
        place,
        cluster_sharpness,
        x,
        att_mine,
        att_got,
        heed_exit_matrix,
        blend_scale_factor.astype(f32).reshape(1, width),
        router,
        position_cluster_label.reshape(1, tokens),
        upstream_derivative.reshape(tokens, width),
        specialist_entry_matrix,
        specialist_exit_matrix,
    )

    ba_got = lax.ppermute(ba_send, "seq", core_pairs)
    fac_got = swap(take(fac, 1 - core), 1)
    gout_got = swap(take(gout, 1 - core), 1)
    grads, inner, payload = ready(place, ba_own, ba_got, att_mine, att_send, log)
    got_grad = lax.ppermute(payload, "seq", down)
    pay = factors(place, fac, fac_got, gout, gout_got)
    pays = [pay[0]] + [swap(pay[i], 2 * m[0] + 4 * m[1]) for i, m in list(enumerate(MOVES))[1:]]
    dkv_a, dq_a = near_backward(0, qkv, p_na, grads, st_na, log, inner, pay[0])
    stages = turns()
    kept, sent = slabs(place, dkv_a, pays, width, hidden // 4, lines)
    send_fa, keep_fa = far_backward(0, place, q_a, kv_a, p_a, st_a, grads, log, inner, got_grad, kept)
    got_fa = lax.ppermute(send_fa, "seq", chip_pairs)
    for t, turn in enumerate(stages):
        got = swap_by_core(sent, (8 << turn[0], 8 << turn[1]))
        after = stages[t + 1] if t + 1 < len(stages) else None
        if t == len(stages) - 1:
            send_fb, keep_fb = far_backward(1, place, q_b, kv_b, p_b, st_b, grads, log, inner, got_grad, kept)
            got_fb = lax.ppermute(send_fb, "seq", chip_pairs)
            kept = fold(None, place, keep_fb, kept, got)[0]
        else:
            kept, sent = fold(after, place, keep_fa, kept, got)
    dkv_b, dq_b = near_backward(1, qkv, p_nb, grads, st_nb, log, inner, kept)
    last = dkv_b
    whole = kept
    for turn in stages[:0:-1]:
        whole = pile(last, whole, swap_by_core(whole, (8 << turn[0], 8 << turn[1])))
    got_z = swap_by_core(whole, (8 << stages[0][0], 8 << stages[0][1]))
    d_mine, d_send, q_slabs = collect(
        place, normed, dkv_a, dkv_b, dq_a, dq_b, keep_fa, keep_fb, got_fa, got_fb, packs, gain_a, tiny, whole
    )

    d_got = lax.ppermute(d_send, "seq", core_pairs)
    mine = 2 * chip + side
    parts = [take(q_slabs, mine)] + [swap(take(q_slabs, mine ^ (2 * m[0] + m[1])), 2 * m[0] + 4 * m[1]) for m in MOVES[1:]]
    whole = pile(q_slabs, whole, got_z)
    got_first = swap_by_core(whole, (2, 4))
    tokens_grad = tokens_back(place, d_mine, d_got, packs, x, back_resid, gain_a, whole)
    rows = width // 4
    part = add(tokens_grad, parts)
    by_line = part[:rows].reshape(lines, rows // lines, 768)
    small = jnp.broadcast_to(part[rows:], (lines, 16, 768))
    by_line = jnp.concatenate([by_line, small], 1)
    z_parts = [take(by_line, line)] + [swap(take(by_line, line ^ k), 8 * k) for k in range(1, lines)]
    whole = pile(part, whole, got_first)
    got_second = swap_by_core(whole, (4, 2))
    far_first = swap(whole, 1)
    part = add(whole, z_parts)
    small = part[rows // lines :]
    part = part[: rows // lines]
    zs = jnp.stack([part] + [swap(part, 8 * k) for k in range(1, lines)])
    near = jnp.stack([zs, swap(zs, 4), swap(zs, 2), swap(zs, 6)])
    far = swap(near, 1)
    grad_qkv, small = unfold(place, near, far, small, swap(small, 1), width)
    far_second = swap(got_second, 1)
    block = (2, lines) + whole.shape[1:]
    grad_in, grad_down, grad_out = spread_experts(
        place, whole.reshape(block), got_second.reshape(block), far_first.reshape(block), far_second.reshape(block), hidden, width
    )
    return (
        block_out.reshape(layer_activations.shape),
        tokens_grad.reshape(layer_activations.shape),
        small[0],
        grad_qkv,
        grad_out.reshape(width, width),
        small[3],
        small[1:3].T,
        grad_in,
        grad_down,
    )


def solution(mesh):
    rows = P("batch", "seq", None)
    placed = (rows, P("batch"), P("batch", "seq")) + (P(),) * 8 + (rows,)
    return jax.shard_map(body, mesh=mesh, in_specs=placed, out_specs=(rows, rows) + (P(),) * 7, check_vma=False)
```

```python
import jax
import jax.numpy as jnp
from jax import lax
from jax.experimental import pallas as pl
from jax.experimental.pallas import tpu as pltpu
from jax.sharding import PartitionSpec as P

HEADS = 8
HEAD = 64
GROUP = 32
EPSILON = 1e-06
LOG2E = 1.4426950408889634
SC = 0.125 * LOG2E
MASKED = -1e30
BQ = 512
CH = 512
bf = jnp.bfloat16
f32 = jnp.float32
AXES = ("batch", "seq")
NT = (((1,), (1,)), ((), ()))
TN = (((0,), (0,)), ((), ()))


def nt(a, b):
    return lax.dot_general(a, b, NT, preferred_element_type=f32)


def tn(a, b):
    return lax.dot_general(a, b, TN, preferred_element_type=f32)


def nn(a, b):
    return jnp.dot(a, b, preferred_element_type=f32)


def rows_of(shape):
    return lax.broadcasted_iota(jnp.int32, shape, 0)


def lanes_of(shape):
    return lax.broadcasted_iota(jnp.int32, shape, 1)


def vmem():
    return pl.BlockSpec(memory_space=pltpu.VMEM)


def smem():
    return pl.BlockSpec(memory_space=pltpu.SMEM)


def params(mib=16):
    return pltpu.CompilerParams(vmem_limit_bytes=mib * 2**20)


def anywhere():
    return pl.BlockSpec(memory_space=pl.ANY)


def hbm():
    return pl.BlockSpec(memory_space=pltpu.HBM)


def cost(us):
    return pl.CostEstimate(flops=int(us * 1e6), bytes_accessed=2**10, transcendentals=0)


def stay(value):
    return pltpu.with_memory_space_constraint(value, pltpu.HBM)


def kept_out(shape, dtype):
    return pltpu.HBM(shape, dtype)


def shift_lanes(value):
    return pltpu.roll(value.astype(f32), 64, axis=1).astype(bf)


def left(first, second):
    return jnp.where(lanes_of(first.shape) < 64, first, shift_lanes(second))


def right(first, second):
    return jnp.where(lanes_of(first.shape) < 64, shift_lanes(first), second)


def pack_kernel(place, w, packs, w_own):
    core = place[0]
    for c in range(2):
        packs[c, :, 0:256] = w[:, 256 * c : 256 * c + 256]
        for h in range(4):
            at = 256 * c + 128 * (h // 2)
            k = w[:, 512 + at : 640 + at]
            v = w[:, 1024 + at : 1152 + at]
            packs[c, :, 256 + 128 * h : 384 + 128 * h] = left(k, v) if h % 2 == 0 else right(k, v)
    for h in range(4):
        q = packs[core, :, 128 * (h // 2) : 128 * (h // 2) + 128]
        q = q if h % 2 == 0 else shift_lanes(q)
        w_own[:, 256 * h : 256 * h + 128] = jnp.where(lanes_of(q.shape) < 64, q, jnp.zeros((), bf))
        w_own[:, 256 * h + 128 : 256 * h + 256] = packs[core, :, 256 + 128 * h : 384 + 128 * h]


def pack(place, w):
    width = w.shape[0]
    return pl.pallas_call(
        pack_kernel,
        in_specs=[smem(), vmem()],
        out_specs=[vmem()] * 2,
        out_shape=[jax.ShapeDtypeStruct((2, width, 768), bf), jax.ShapeDtypeStruct((width, 1024), bf)],
        compiler_params=params(16),
        cost_estimate=cost(3),
    )(place, w)


def project_kernel(place, x_own, x_other, gain, w_own, normed, qkv, send_a, send_b):
    core, chip = place[0], place[1]
    block = pl.program_id(0)

    def go(x_ref):
        x = x_ref[...].astype(f32)
        inverse = lax.rsqrt(jnp.mean(x * x, axis=1, keepdims=True) + EPSILON)
        low = (x * inverse * gain[...]).astype(bf)
        normed[...] = low
        out = nn(low, w_own[...]).astype(bf)
        qkv[...] = out
        send_b[...] = out[:, 384:512]

        @pl.when(chip == 0)
        def _():
            send_a[...] = out[:, 128:256]

        @pl.when(chip == 1)
        def _():
            send_a[...] = left(out[:, 512:640], out[:, 768:896])

    @pl.when(block // 2 == core)
    def _():
        go(x_own)

    @pl.when(block // 2 != core)
    def _():
        go(x_other)


def project(place, x_own, x_other, gain, w_own):
    rows, width = x_own.shape

    def own(b, p):
        return (jnp.where(b // 2 == p[0], b % 2, jnp.where(b // 2 > p[0], 1, 0)), 0)

    def other(b, p):
        return (jnp.where(b // 2 != p[0], b % 2, jnp.where(b // 2 > 1 - p[0], 1, 0)), 0)

    half = rows // 2
    return pl.pallas_call(
        project_kernel,
        grid_spec=pltpu.PrefetchScalarGridSpec(
            num_scalar_prefetch=1,
            grid=(4,),
            in_specs=[
                pl.BlockSpec((half, width), own),
                pl.BlockSpec((half, width), other),
                pl.BlockSpec((1, width), lambda b, p: (0, 0)),
                pl.BlockSpec((width, 1024), lambda b, p: (0, 0)),
            ],
            out_specs=[
                pl.BlockSpec((half, width), lambda b, p: (b, 0)),
                pl.BlockSpec((half, 1024), lambda b, p: (b, 0)),
                pl.BlockSpec((half, 128), lambda b, p: (b, 0)),
                pl.BlockSpec((half, 128), lambda b, p: (b, 0)),
            ],
        ),
        out_shape=[
            kept_out((2 * rows, width), bf),
            kept_out((2 * rows, 1024), bf),
            jax.ShapeDtypeStruct((2 * rows, 128), bf),
            jax.ShapeDtypeStruct((2 * rows, 128), bf),
        ],
        compiler_params=params(20),
        cost_estimate=cost(4),
    )(place, x_own, x_other, gain, w_own)


def scores(kv, q, s_ref, slot, kmax, q0, limit, causal):
    peak = None
    for k0 in range(0, kmax, CH):
        s = nt(kv[k0 : k0 + CH, :], q)
        if causal:
            if k0 >= 1024:
                s = jnp.where(rows_of(s.shape) + k0 < limit, s, MASKED)
            if k0 + CH > q0:
                s = jnp.where(rows_of(s.shape) + (k0 - q0) <= lanes_of(s.shape), s, MASKED)
        s_ref[slot, k0 : k0 + CH, :] = s
        m = jnp.max(s, axis=0, keepdims=True)
        peak = m if peak is None else jnp.maximum(peak, m)
    return peak


def weigh(vt, s_ref, slot, peak, kmax, put):
    scaled = peak * SC
    acc = None
    for k0 in range(0, kmax, CH):
        p = jnp.exp2(s_ref[slot, k0 : k0 + CH, :] * SC - scaled).astype(bf)
        put(k0 // CH, p)
        d = nn(vt[:, k0 : k0 + CH], p)
        acc = d if acc is None else acc + d
    total = acc[0:1, :]
    return acc[64:128, :] * (1.0 / total), scaled, total


def ones_and_values(kv):
    vt = kv.T
    return jnp.where(rows_of(vt.shape) < 64, jnp.ones((), bf), vt)


def near_forward_kernel(limit_ref, qkv, dep, p_ref, o_ref, st_ref, s_ref, vt_ref, buf, sems):
    limit = limit_ref[0]
    count = qkv.shape[0] // BQ
    tasks = [(h, i) for h in range(2) for i in range(count)]

    def start_scores(at):
        h, i = tasks[at]
        kv = qkv.at[:, 256 * h + 128 : 256 * h + 256]
        q = qkv[i * BQ : (i + 1) * BQ, 256 * h : 256 * h + 128]
        return scores(kv, q, s_ref, at % 2, (i + 1) * BQ, i * BQ, limit, True)

    copies = []
    peak = start_scores(0)
    for at, (h, i) in enumerate(tasks):
        if i == 0:
            vt_ref[h] = ones_and_values(qkv[:, 256 * h + 128 : 256 * h + 256])
        later = start_scores(at + 1) if at + 1 < len(tasks) else None
        base = i * (i + 1) // 2

        def put(k, p):
            buf[h, base + k] = p

        out, scaled, total = weigh(vt_ref.at[h], s_ref, at % 2, peak, (i + 1) * BQ, put)
        copies.append(pltpu.make_async_copy(buf.at[h, base : base + i + 1], p_ref.at[h, base : base + i + 1], sems.at[h, i]))
        copies[-1].start()
        o_ref[h, :, i * BQ : (i + 1) * BQ] = out.astype(bf)
        st_ref[h, 0:1, i * BQ : (i + 1) * BQ] = scaled
        st_ref[h, 1:2, i * BQ : (i + 1) * BQ] = total
        peak = later
    for copy in copies:
        copy.wait()


def near_forward(pair, limit, qkv, dep):
    n = qkv.shape[0]
    count = n // BQ
    shape = (2, count * (count + 1) // 2, CH, BQ)
    return pl.pallas_call(
        near_forward_kernel,
        grid=(1,),
        in_specs=[smem(), pl.BlockSpec((n, 512), lambda g: (0, pair)), anywhere()],
        out_specs=[
            anywhere(),
            pl.BlockSpec((2, 64, n), lambda g: (0, 0, 0)),
            pl.BlockSpec((2, 8, n), lambda g: (0, 0, 0)),
        ],
        out_shape=[
            kept_out(shape, bf),
            jax.ShapeDtypeStruct((2, 64, n), bf),
            jax.ShapeDtypeStruct((2, 8, n), f32),
        ],
        scratch_shapes=[
            pltpu.VMEM((2, n, BQ), f32),
            pltpu.VMEM((2, 128, n), bf),
            pltpu.VMEM(shape, bf),
            pltpu.SemaphoreType.DMA((2, count)),
        ],
        compiler_params=params(34),
        cost_estimate=cost(9),
    )(limit, qkv, dep)


def three(value):
    high = value.astype(bf)
    rest = value - high.astype(f32)
    mid = rest.astype(bf)
    return high, mid, (rest - mid.astype(f32)).astype(bf)


def far_forward_kernel(j, place, q_own, q_got, kv_own, kv_got, dep, p_ref, o_ref, st_ref, q_ref, kv_ref, s_ref, vt_ref, buf, sems):
    n = q_own.shape[0]

    @pl.when(place[1] == 1)
    def _():
        q_ref[...] = q_own[...]
        kv_ref[...] = kv_got[...]

    @pl.when(place[1] == 0)
    def _():
        q = q_got[...] if j == 0 else shift_lanes(q_got[...])
        q_ref[...] = jnp.where(lanes_of(q.shape) < 64, q, jnp.zeros((), bf))
        kv_ref[...] = kv_own[...]

    vt_ref[...] = ones_and_values(kv_ref[...])
    count = n // BQ
    copies = []
    peak = scores(kv_ref, q_ref[0:BQ, :], s_ref, 0, n, 0, None, False)
    for i in range(count):
        later = None
        at = slice(i * BQ, (i + 1) * BQ)
        if i + 1 < count:
            later = scores(kv_ref, q_ref[(i + 1) * BQ : (i + 2) * BQ, :], s_ref, (i + 1) % 2, n, 0, None, False)

        def put(k, p):
            buf[i, k] = p

        out, scaled, total = weigh(vt_ref, s_ref, i % 2, peak, n, put)
        copies.append(pltpu.make_async_copy(buf.at[i], p_ref.at[i], sems.at[i]))
        copies[-1].start()
        o_ref[0:64, at] = out.astype(bf)
        high, mid, low = three(scaled + jnp.log(total) * LOG2E)
        tail = jnp.concatenate([high.astype(f32), mid.astype(f32), low.astype(f32), jnp.zeros((13, BQ), f32)], 0)
        o_ref[64:80, at] = tail.astype(bf)
        st_ref[0:1, at] = scaled
        peak = later
    for copy in copies:
        copy.wait()


def far_forward(j, place, qkv, q_got, kv_got, dep):
    n = qkv.shape[0]
    whole = pl.BlockSpec((n, 128), lambda h: (0, 0))
    shape = (n // BQ, n // CH, CH, BQ)
    return pl.pallas_call(
        lambda *refs: far_forward_kernel(j, *refs),
        grid=(1,),
        in_specs=[
            smem(),
            pl.BlockSpec((n, 128), lambda h: (0, 2 * j)),
            whole,
            pl.BlockSpec((n, 128), lambda h: (0, 2 * j + 5)),
            whole,
            anywhere(),
        ],
        out_specs=[
            anywhere(),
            pl.BlockSpec((80, n), lambda h: (0, 0)),
            pl.BlockSpec((8, n), lambda h: (0, 0)),
            whole,
            whole,
        ],
        out_shape=[
            kept_out(shape, bf),
            jax.ShapeDtypeStruct((80, n), bf),
            jax.ShapeDtypeStruct((8, n), f32),
            kept_out((n, 128), bf),
            kept_out((n, 128), bf),
        ],
        scratch_shapes=[
            pltpu.VMEM((2, n, BQ), f32),
            pltpu.VMEM((128, n), bf),
            pltpu.VMEM(shape, bf),
            pltpu.SemaphoreType.DMA((n // BQ,)),
        ],
        compiler_params=params(34),
        cost_estimate=cost(10),
    )(place, qkv, q_got, qkv, kv_got, dep)


def unsplit(ref, at):
    return ref[at : at + 1, :].astype(f32) + ref[at + 1 : at + 2, :].astype(f32) + ref[at + 2 : at + 3, :].astype(f32)


def join_kernel(place, near_a, near_b, stat_a, stat_b, far_a, far_b, got_a, got_b, mine, other, log_ref):
    core, chip = place[0], place[1]
    half = mine.shape[1]
    for h in range(4):
        far = (far_a, far_b, got_a, got_b)[h]
        near, stat = (near_a, near_b)[h // 2], (stat_a, stat_b)[h // 2]
        log_near = stat[h % 2, 0:1, :] + jnp.log(stat[h % 2, 1:2, :]) * LOG2E
        log_far = jnp.where(chip == 1, unsplit(far, 64), MASKED)
        top = jnp.maximum(log_near, log_far)
        e_near, e_far = jnp.exp2(log_near - top), jnp.exp2(log_far - top)
        both = e_near + e_far
        log_ref[h] = jnp.broadcast_to(top + jnp.log(both) * LOG2E, log_ref.shape[1:])
        far_out = jnp.where(chip == 1, far[0:64, :].astype(f32), 0.0)
        joined = ((near[h % 2].astype(f32) * e_near + far_out * e_far) * (1.0 / both)).astype(bf)
        at = slice(64 * h, 64 * h + 64)

        @pl.when(core == 0)
        def _():
            mine[at, :] = joined[:, :half]
            other[at, :] = joined[:, half:]

        @pl.when(core == 1)
        def _():
            mine[at, :] = joined[:, half:]
            other[at, :] = joined[:, :half]


def join(place, near_a, near_b, stat_a, stat_b, far_a, far_b, got_a, got_b):
    n = near_a.shape[2]
    return pl.pallas_call(
        join_kernel,
        in_specs=[smem()] + [vmem()] * 8,
        out_specs=[vmem()] * 3,
        out_shape=[
            jax.ShapeDtypeStruct((256, n // 2), bf),
            jax.ShapeDtypeStruct((256, n // 2), bf),
            jax.ShapeDtypeStruct((4, 8, n), f32),
        ],
        compiler_params=params(),
        cost_estimate=cost(2),
    )(place, near_a, near_b, stat_a, stat_b, far_a, far_b, got_a, got_b)


def mixture_kernel(
    place, sharp, x, att_own, att_got, wout, gain, router, labels, gy, w1_hbm, w2_hbm,
    block_out, fac, gout, tiny, back_resid, ba_own, ba_other, w1, w2, sems,
):
    core = place[0]
    copy1 = pltpu.make_async_copy(w1_hbm, w1, sems.at[0])
    copy2 = pltpu.make_async_copy(w2_hbm, w2, sems.at[1])
    copy1.start()
    copy2.start()
    own_rows = pl.ds(pl.multiple_of(core * 256, 256), 256)
    other_rows = pl.ds(pl.multiple_of(256 - core * 256, 256), 256)
    wo_own, wo_other = wout[own_rows, :], wout[other_rows, :]
    resid = x[...].astype(f32) + tn(att_own[...], wo_own) + tn(att_got[...], wo_other)
    inverse = lax.rsqrt(jnp.mean(resid * resid, axis=1, keepdims=True) + EPSILON)
    unit = resid * inverse
    mix = (unit * gain[...]).astype(bf)
    temper = 1.0 / sharp[0]
    logits = nt(router[...], mix) * temper
    tokens = mix.shape[0]
    groups = tokens // GROUP
    member = labels[...] == rows_of((groups, tokens))
    weights, mixing = [], []
    for e in range(2):
        row = logits[e : e + 1, :]
        peak = jnp.max(jnp.where(member, row, -jnp.inf), axis=1, keepdims=True)
        token_peak = jnp.sum(jnp.where(member, peak, 0.0), axis=0, keepdims=True)
        raised = jnp.exp(row - token_peak)
        total = jnp.sum(jnp.where(member, raised, 0.0), axis=1, keepdims=True)
        token_total = jnp.sum(jnp.where(member, total, 0.0), axis=0, keepdims=True)
        w = raised / token_total
        weights.append(w)
        mixing.append(jnp.where(member, w, 0.0))
    mixing = jnp.concatenate(mixing, 0).astype(bf)
    mixed = nn(mixing, mix).astype(bf)
    back_expert = nn(mixing, gy[...]).astype(bf)
    copy1.wait()
    copy2.wait()
    expert_out, back_mixed = [], []
    quarter = w1.shape[2] // 4
    width = mix.shape[1]
    for e in range(2):
        at = slice(groups * e, groups * (e + 1))
        inner = nn(mixed[at], w1[e])
        cdf = 0.5 * (1.0 + lax.erf(inner * 0.7071067811865476))
        active = (inner * cdf).astype(bf)
        slope = cdf + inner * (jnp.exp(-0.5 * inner * inner) * 0.3989422804014327)
        expert_out.append(nn(active, w2[e]))
        back_inner = (slope * nt(back_expert[at], w2[e])).astype(bf)
        back_mixed.append(nt(back_inner, w1[e]))
        fac[e, :, 0:width] = mixed[at]
        fac[e, :, width : 2 * width] = back_expert[at]
        for q in range(4):
            base = 2 * width + 2 * quarter * q
            fac[e, :, base : base + quarter] = back_inner[:, quarter * q : quarter * (q + 1)]
            fac[e, :, base + quarter : base + 2 * quarter] = active[:, quarter * q : quarter * (q + 1)]
    expert_out = jnp.concatenate(expert_out, 0).astype(bf)
    back_mixed = jnp.concatenate(back_mixed, 0).astype(bf)
    block_out[...] = (resid + tn(mixing, expert_out)).astype(bf)
    spread = nt(expert_out, gy[...]) + nt(back_mixed, mix)
    rows16 = rows_of((16, tokens))
    back_logits = jnp.zeros((16, tokens), f32)
    for e in range(2):
        back_weight = jnp.sum(jnp.where(member, spread[groups * e : groups * (e + 1)], 0.0), axis=0, keepdims=True)
        w = weights[e]
        inner = jnp.sum(jnp.where(member, w * back_weight, 0.0), axis=1, keepdims=True)
        token_inner = jnp.sum(jnp.where(member, inner, 0.0), axis=0, keepdims=True)
        back_logits = jnp.where(rows16 == e, w * (back_weight - token_inner) * temper, back_logits)
    back_logits = back_logits.astype(bf)
    ctrl = nn(back_logits, mix)
    back_mix = tn(mixing, back_mixed) + tn(back_logits, router[...])
    tiny[...] = jnp.zeros_like(tiny)
    tiny[0:2, :] = ctrl[0:2, :]
    tiny[2:3, :] = jnp.sum(back_mix * unit, axis=0, keepdims=True)
    n = back_mix * gain[...]
    mean = jnp.mean(n * resid, axis=1, keepdims=True)
    back = gy[...].astype(f32) + inverse * n - resid * (inverse * inverse * inverse * mean)
    back_resid[...] = back
    branch = back.astype(bf)
    gout[core] = nn(att_own[...], branch).astype(bf)
    gout[1 - core] = nn(att_got[...], branch).astype(bf)
    ba_own[...] = nt(wo_own, branch).astype(bf)
    ba_other[...] = nt(wo_other, branch).astype(bf)


def mixture(place, sharp, x, att_own, att_got, wout, gain, router, labels, gy, w1, w2):
    tokens, width = x.shape
    hidden = w1.shape[2]
    groups = tokens // GROUP
    return pl.pallas_call(
        mixture_kernel,
        in_specs=[smem(), smem()] + [vmem()] * 8 + [pl.BlockSpec(memory_space=pl.ANY)] * 2,
        out_specs=[vmem()] * 7,
        out_shape=[
            kept_out((tokens, width), bf),
            jax.ShapeDtypeStruct((2, groups, 2 * width + 2 * hidden), bf),
            jax.ShapeDtypeStruct((2, width // 2, width), bf),
            jax.ShapeDtypeStruct((8, width), f32),
            kept_out((tokens, width), f32),
            jax.ShapeDtypeStruct((width // 2, tokens), bf),
            jax.ShapeDtypeStruct((width // 2, tokens), bf),
        ],
        scratch_shapes=[pltpu.VMEM(w1.shape, bf), pltpu.VMEM(w2.shape, bf), pltpu.SemaphoreType.DMA((2,))],
        compiler_params=params(48),
        cost_estimate=cost(15),
    )(place, sharp, x, att_own, att_got, wout, gain, router, labels, gy, w1, w2)


def ready_kernel(place, ba_own, ba_got, mine, other, log_ref, grads, inner, payload):
    core = place[0]
    half = mine.shape[1]
    for h in range(4):
        at = slice(64 * h, 64 * h + 64)
        g_own, g_got = ba_own[at, :], ba_got[at, :]
        d_own = jnp.sum(g_own.astype(f32) * mine[at, :].astype(f32), axis=0, keepdims=True)
        d_got = jnp.sum(g_got.astype(f32) * other[at, :].astype(f32), axis=0, keepdims=True)

        def put(g0, g1, d0, d1):
            grads[h, :, :half] = g0
            grads[h, :, half:] = g1
            inner[h, :, :half] = jnp.broadcast_to(d0, (8, half))
            inner[h, :, half:] = jnp.broadcast_to(d1, (8, half))
            if h >= 2:
                for g, d, s in ((g0, d0, slice(0, half)), (g1, d1, slice(half, 2 * half))):
                    payload[h - 2, 0:64, s] = g
                    parts = three(log_ref[h, 0:1, s]) + three(d)
                    tail = jnp.concatenate([part.astype(f32) for part in parts] + [jnp.zeros((10, half), f32)], 0)
                    payload[h - 2, 64:80, s] = tail.astype(bf)

        @pl.when(core == 0)
        def _():
            put(g_own, g_got, d_own, d_got)

        @pl.when(core == 1)
        def _():
            put(g_got, g_own, d_got, d_own)


def ready(place, ba_own, ba_got, mine, other, log):
    half = mine.shape[1]
    return pl.pallas_call(
        ready_kernel,
        in_specs=[smem()] + [vmem()] * 5,
        out_specs=[vmem()] * 3,
        out_shape=[
            jax.ShapeDtypeStruct((4, 64, 2 * half), bf),
            jax.ShapeDtypeStruct((4, 8, 2 * half), f32),
            jax.ShapeDtypeStruct((2, 80, 2 * half), bf),
        ],
        compiler_params=params(),
        cost_estimate=cost(2),
    )(place, ba_own, ba_got, mine, other, log)


def back_block(kv_ref, kt_ref, q, grad, ratio, inner, block, kmax, first, put_kv):
    low = (grad.astype(f32) * ratio).astype(bf)
    rhs = jnp.concatenate([jnp.zeros((64, BQ), bf), low], axis=0)
    shift = inner * ratio
    natural = rhs.T
    acc = None
    for k0 in range(0, kmax, CH):
        dp = nn(kv_ref[k0 : k0 + CH, :], rhs)
        p = block(k0 // CH)
        ds = (p.astype(f32) * (dp - shift)).astype(bf)
        d = nn(kt_ref[:, k0 : k0 + CH], ds)
        acc = d if acc is None else acc + d
        put_kv(k0, k0 >= first, nn(ds, q) + nn(p, natural))
    return (acc * 0.125).astype(bf)


def near_backward_kernel(qkv, p_ref, grad_ref, stat, log_ref, inner_ref, dep, dkv_ref, dq_ref, kt_ref, buf, sems):
    count = qkv.shape[0] // BQ
    copies = {}
    for h in range(2):
        for i in range(count):
            at = slice(i * (i + 1) // 2, (i + 1) * (i + 2) // 2)
            copies[h, i] = pltpu.make_async_copy(p_ref.at[h, at], buf.at[h, at], sems.at[h, i])
            copies[h, i].start()
    for h in range(2):
        kv_ref = qkv.at[:, 256 * h + 128 : 256 * h + 256]
        kt_ref[h] = kv_ref[...].T[0:64, :]

        def put(k0, fresh, value):
            if fresh:
                dkv_ref[h, k0 : k0 + CH, :] = value
            else:
                dkv_ref[h, k0 : k0 + CH, :] += value

        for i in range(count):
            at = slice(i * BQ, (i + 1) * BQ)
            base = i * (i + 1) // 2
            copies[h, i].wait()
            ratio = jnp.exp2(stat[h, 0:1, at] - log_ref[h, 0:1, at])
            q = qkv[at, 256 * h : 256 * h + 128]

            def block(k):
                return buf[h, base + k]

            dq_ref[h, :, at] = back_block(
                kv_ref, kt_ref.at[h], q, grad_ref[h, :, at], ratio, inner_ref[h, 0:1, at], block, (i + 1) * BQ, i * BQ, put
            )


def near_backward(pair, qkv, p, grads, stat, log, inner, dep):
    n = qkv.shape[0]
    row = pl.BlockSpec((2, 8, n), lambda g: (pair, 0, 0))
    return pl.pallas_call(
        near_backward_kernel,
        grid=(1,),
        in_specs=[
            pl.BlockSpec((n, 512), lambda g: (0, pair)),
            hbm(),
            pl.BlockSpec((2, 64, n), lambda g: (pair, 0, 0)),
            pl.BlockSpec((2, 8, n), lambda g: (0, 0, 0)),
            row,
            row,
            anywhere(),
        ],
        out_specs=[pl.BlockSpec((2, n, 128), lambda g: (0, 0, 0)), pl.BlockSpec((2, 64, n), lambda g: (0, 0, 0))],
        out_shape=[kept_out((2, n, 128), f32), kept_out((2, 64, n), bf)],
        scratch_shapes=[pltpu.VMEM((2, 64, n), bf), pltpu.VMEM(p.shape, bf), pltpu.SemaphoreType.DMA((2, n // BQ))],
        compiler_params=params(34),
        cost_estimate=cost(13),
    )(qkv, stay(p), grads, stat, log, inner, dep)


def far_backward_kernel(
    place, q_ref, kv_ref, p_ref, stat, grad_own, log_own, inner_own, got, dep, send_ref, keep_ref, kt_ref, sum_ref, dq_ref, buf, sems
):
    kt_ref[...] = kv_ref[...].T[0:64, :]
    upper = place[1] == 1
    n = q_ref.shape[0]
    copies = [pltpu.make_async_copy(p_ref.at[i], buf.at[i], sems.at[i]) for i in range(n // BQ)]
    for copy in copies:
        copy.start()

    def put(k0, fresh, value):
        if fresh:
            sum_ref[k0 : k0 + CH, :] = value
        else:
            sum_ref[k0 : k0 + CH, :] += value

    for i in range(n // BQ):
        at = slice(i * BQ, (i + 1) * BQ)
        got_log = got[0, 64:67, at].astype(f32)
        got_inner = got[0, 67:70, at].astype(f32)
        log = jnp.where(upper, log_own[0, 0:1, at], jnp.sum(got_log, axis=0, keepdims=True))
        inner = jnp.where(upper, inner_own[0, 0:1, at], jnp.sum(got_inner, axis=0, keepdims=True))
        grad = jnp.where(upper, grad_own[0, :, at], got[0, 0:64, at])
        ratio = jnp.exp2(stat[0:1, at] - log)
        copies[i].wait()

        def block(k):
            return buf[i, k]

        dq = back_block(kv_ref, kt_ref, q_ref[at, :], grad, ratio, inner, block, n, 0 if i == 0 else n, put)
        dq_ref[at, :] = jnp.concatenate([dq, jnp.zeros((64, BQ), bf)], 0).T

    @pl.when(upper)
    def _():
        send_ref[...] = sum_ref[...].astype(bf)
        keep_ref[...] = dq_ref[...]

    @pl.when(jnp.logical_not(upper))
    def _():
        send_ref[...] = dq_ref[...]
        keep_ref[...] = sum_ref[...].astype(bf)


def far_backward(j, place, q, kv, p, stat, grads, log, inner, got, dep):
    n = q.shape[0]
    row = pl.BlockSpec((1, 8, n), lambda h: (j, 0, 0))
    whole = pl.BlockSpec((n, 128), lambda h: (0, 0))
    return pl.pallas_call(
        far_backward_kernel,
        grid=(1,),
        in_specs=[
            smem(),
            whole,
            whole,
            hbm(),
            pl.BlockSpec((8, n), lambda h: (0, 0)),
            pl.BlockSpec((1, 64, n), lambda h: (j, 0, 0)),
            row,
            row,
            pl.BlockSpec((1, 80, n), lambda h: (j, 0, 0)),
            pl.BlockSpec(memory_space=pl.ANY),
        ],
        out_specs=[whole, whole],
        out_shape=[jax.ShapeDtypeStruct((n, 128), bf)] * 2,
        scratch_shapes=[
            pltpu.VMEM((64, n), bf),
            pltpu.VMEM((n, 128), f32),
            pltpu.VMEM((n, 128), bf),
            pltpu.VMEM(p.shape, bf),
            pltpu.SemaphoreType.DMA((n // BQ,)),
        ],
        compiler_params=params(30),
        cost_estimate=cost(13),
    )(place, q, kv, stay(p), stat, grads, log, inner, got, dep)


def swap(value, bits):
    count = lax.axis_size("batch") * lax.axis_size("seq")
    return lax.ppermute(value, AXES, [(i, i ^ bits) for i in range(count)])


def turns():
    bits = (lax.axis_size("batch") // 2).bit_length() - 1
    return [(t, bits - 1 - t) for t in range(bits)]


def swap_by_core(value, bits):
    count = lax.axis_size("batch") * lax.axis_size("seq")
    return lax.ppermute(value, AXES, [(i, i ^ bits[i % 2]) for i in range(count)])


def bit_of(line, core, pair):
    return (line >> jnp.where(core == 0, pair[0], pair[1])) & 1


def take(value, index, axis=0):
    return lax.dynamic_index_in_dim(value, index, axis, keepdims=False)


MOVES = ((0, 0), (1, 0), (0, 1), (1, 1))


def factors_kernel(place, fac, got, gout, got_out, *outs):
    core, chip, side = place[0], place[1], place[2]
    groups = got.shape[0]
    width = gout.shape[2]
    part = (got.shape[1] - 2 * width) // 4
    rows = gout.shape[1] // 4
    for (x, y), out in zip(MOVES, outs):
        index = 2 * (chip ^ x) + (side ^ y)
        lanes = pl.ds(pl.multiple_of(2 * width + index * part, 128), part)
        at = pl.ds(pl.multiple_of(index * rows, rows), rows)
        out[0:groups, 0 : 2 * width] = fac[core, :, 0 : 2 * width]
        out[groups:, 0 : 2 * width] = got[:, 0 : 2 * width]
        out[0:groups, 2 * width : 2 * width + part] = fac[core, :, lanes]
        out[groups:, 2 * width : 2 * width + part] = got[:, lanes]
        out[:, 2 * width + part :] = (gout[core, at, :].astype(f32) + got_out[at, :].astype(f32)).astype(bf)


def factors(place, fac, got, gout, got_out):
    groups, per = got.shape
    width = gout.shape[2]
    shape = jax.ShapeDtypeStruct((2 * groups, 2 * width + (per - 2 * width) // 4 + width), bf)
    return pl.pallas_call(
        factors_kernel,
        in_specs=[smem()] + [vmem()] * 4,
        out_specs=[vmem()] * 4,
        out_shape=[shape] * 4,
        compiler_params=params(),
        cost_estimate=cost(2),
    )(place, fac, got, gout, got_out)


def slab_kernel(turn, lines, place, dep, a, b, c, d, keep, send):
    core, line = place[0], place[3]
    width = keep.shape[2]
    quarter = (a.shape[1] - 3 * width) // 2

    def lanes(start, size):
        return jnp.concatenate([ref[:, start : start + size] for ref in (a, b, c, d)], 0)

    g_in = tn(lanes(0, width), lanes(2 * width, quarter)).astype(bf)
    g_down = tn(lanes(2 * width + quarter, quarter), lanes(width, width)).astype(bf)
    total = a[:, 2 * width + 2 * quarter :].astype(f32)
    for ref in (b, c, d):
        total = total + ref[:, 2 * width + 2 * quarter :].astype(f32)
    pieces = [total.astype(bf), g_in, g_down]
    bits = lines.bit_length() - 1
    for z in range(lines):
        flipped = sum(((z >> t) & 1) << (bits - 1 - t) for t in range(bits))
        spot = jnp.where(core == 0, flipped, z)
        chosen = bit_of(z, core, turn) == bit_of(line, core, turn)

        def put(ref):
            start = 0
            for piece in pieces[1:] + pieces[:1]:
                rows = piece.shape[0] // lines
                ref[spot % (lines // 2), start : start + rows, :] = piece[z * rows : (z + 1) * rows, :]
                start += rows

        @pl.when(chosen)
        def _():
            put(keep)

        @pl.when(jnp.logical_not(chosen))
        def _():
            put(send)


def slabs(place, dep, payloads, width, quarter, lines):
    rows = (width + quarter + payloads[0].shape[0]) // lines
    shape = jax.ShapeDtypeStruct((lines // 2, rows, width), bf)
    turn = turns()[0]
    return pl.pallas_call(
        lambda *refs: slab_kernel(turn, lines, *refs),
        in_specs=[smem(), anywhere()] + [vmem()] * 4,
        out_specs=[vmem()] * 2,
        out_shape=[shape] * 2,
        compiler_params=params(),
        cost_estimate=cost(2),
    )(place, dep, *payloads)


def fold_kernel(turn, place, dep, kept, got, keep, *send):
    if turn is None:
        keep[...] = (kept[...].astype(f32) + got[...].astype(f32)).astype(bf)
        return
    half = keep.shape[0]
    mine = bit_of(place[3], place[0], turn)
    at = pl.ds(mine * half, half)
    keep[...] = (kept[at].astype(f32) + got[at].astype(f32)).astype(bf)
    at = pl.ds((1 - mine) * half, half)
    send[0][...] = (kept[at].astype(f32) + got[at].astype(f32)).astype(bf)


def fold(turn, place, dep, kept, got):
    count = kept.shape[0] if turn is None else kept.shape[0] // 2
    shape = jax.ShapeDtypeStruct((count,) + kept.shape[1:], bf)
    outs = 1 if turn is None else 2
    return pl.pallas_call(
        lambda *refs: fold_kernel(turn, *refs),
        in_specs=[smem(), anywhere(), vmem(), vmem()],
        out_specs=[vmem()] * outs,
        out_shape=[shape] * outs,
        compiler_params=params(),
        cost_estimate=cost(1),
    )(place, dep, kept, got)


def pile_kernel(dep, a, b, out):
    half = out.shape[0] // 2
    out[:half] = a[...]
    out[half:] = b[...]


def pile(dep, a, b):
    return pl.pallas_call(
        pile_kernel,
        in_specs=[anywhere(), vmem(), vmem()],
        out_specs=vmem(),
        out_shape=jax.ShapeDtypeStruct((2 * a.shape[0],) + a.shape[1:], bf),
        compiler_params=params(),
        cost_estimate=cost(1),
    )(dep, a, b)


def add_kernel(dep, *refs):
    total = refs[0][...].astype(f32)
    for ref in refs[1:-1]:
        total = total + ref[...].astype(f32)
    refs[-1][...] = total.astype(bf)


def add(dep, values):
    return pl.pallas_call(
        add_kernel,
        in_specs=[pl.BlockSpec(memory_space=pl.ANY)] + [vmem()] * len(values),
        out_specs=vmem(),
        out_shape=jax.ShapeDtypeStruct(values[0].shape, bf),
        compiler_params=params(),
        cost_estimate=cost(1),
    )(dep, *values)


def gate_kernel(dep, value, out):
    pass


def gate(dep, value):
    return pl.pallas_call(
        gate_kernel,
        in_specs=[anywhere(), anywhere()],
        out_specs=anywhere(),
        out_shape=jax.ShapeDtypeStruct(value.shape, value.dtype),
        input_output_aliases={1: 0},
        cost_estimate=cost(1),
    )(dep, value)


def spread_kernel(place, near_a, near_b, far_a, far_b, in_ref, down_ref, out_ref):
    expert, q = pl.program_id(0), pl.program_id(1)
    line = place[3]
    lines = near_a.shape[1]
    width = in_ref.shape[1]
    cut_in = width // lines
    cut_down = down_ref.shape[1] // lines
    bits = lines.bit_length() - 1
    move_x, move_y = (q // 2) ^ place[1], (q % 2) ^ place[2]
    outer = jnp.where(expert == 0, move_y, move_x)

    def put(ref):
        for k in range(lines):
            flipped = sum(((k >> t) & 1) << (bits - 1 - t) for t in range(bits))
            z = line ^ jnp.where(expert == 0, flipped, k)
            in_ref[0, pl.ds(pl.multiple_of(z * cut_in, cut_in), cut_in), :] = ref[0, k, :cut_in].astype(f32)
            down_ref[0, pl.ds(pl.multiple_of(z * cut_down, cut_down), cut_down), :] = ref[0, k, cut_in : cut_in + cut_down].astype(f32)
            out_ref[0, z] = ref[0, k, cut_in + cut_down :].astype(f32)

    for near, pair in ((True, (near_a, near_b)), (False, (far_a, far_b))):
        for side in range(2):

            @pl.when(((expert == place[0]) == near) & (outer == side))
            def _():
                put(pair[side])


def spread_experts(place, near_a, near_b, far_a, far_b, hidden, width):
    block = near_a.shape[1:]
    lines = block[0]

    def spec(near, side):
        def index(e, q, p):
            move_x, move_y = (q // 2) ^ p[1], (q % 2) ^ p[2]
            inner = jnp.where(e == 0, move_x, move_y)
            outer = jnp.where(e == 0, move_y, move_x)
            wanted = ((e == p[0]) == near) & (outer == side)
            return (jnp.where(wanted, inner, 0), 0, 0, 0)

        return pl.BlockSpec((1,) + block, index)

    return pl.pallas_call(
        spread_kernel,
        grid_spec=pltpu.PrefetchScalarGridSpec(
            num_scalar_prefetch=1,
            grid=(2, 4),
            in_specs=[spec(True, 0), spec(True, 1), spec(False, 0), spec(False, 1)],
            out_specs=[
                pl.BlockSpec((1, width, hidden // 4), lambda e, q, p: (e, 0, q)),
                pl.BlockSpec((1, hidden // 4, width), lambda e, q, p: (e, q, 0)),
                pl.BlockSpec((1, lines, width // 8 // lines, width), lambda e, q, p: (e * 4 + q, 0, 0, 0)),
            ],
        ),
        out_shape=[
            jax.ShapeDtypeStruct((2, width, hidden), f32),
            jax.ShapeDtypeStruct((2, hidden, width), f32),
            jax.ShapeDtypeStruct((8, lines, width // 8 // lines, width), f32),
        ],
        compiler_params=params(28),
        cost_estimate=cost(8),
    )(place, near_a, near_b, far_a, far_b)


def own_block(b, p):
    return jnp.where(b // 2 == p[0], b % 2, jnp.where(b // 2 > p[0], 1, 0))


def other_block(b, p):
    return jnp.where(b // 2 != p[0], b % 2, jnp.where(b // 2 > 1 - p[0], 1, 0))


def collect_kernel(
    place, normed, kv_a, kv_b, q_a, q_b, keep_a, keep_b, got_a, got_b, packs, gain, tiny, dep, mine, other, slabs_ref, sum_ref
):
    block = pl.program_id(0)
    upper = place[1] == 1
    dq = jnp.concatenate([q_a[0], q_a[1], q_b[0], q_b[1]], 0).T.astype(f32)
    far = jnp.concatenate([left(keep_a[...], keep_b[...]), left(got_a[...], got_b[...])], 1).astype(f32)
    pieces = [(dq + jnp.where(upper, far, 0.0)).astype(bf)]
    for near, h, extra in ((kv_a, 0, got_a), (kv_a, 1, got_b), (kv_b, 0, keep_a), (kv_b, 1, keep_b)):
        value = near[h] + jnp.where(upper, 0.0, extra[...].astype(f32))
        pieces.append(jnp.where(lanes_of(value.shape) < 64, value * 0.125, value).astype(bf))
    back = jnp.concatenate(pieces, 1)

    @pl.when(block // 2 == place[0])
    def _():
        mine[...] = back

    @pl.when(block // 2 != place[0])
    def _():
        other[...] = back

    part = tn(normed[...], back)

    @pl.when(block == 0)
    def _():
        sum_ref[...] = part

    @pl.when(block > 0)
    def _():
        sum_ref[...] += part

    @pl.when(block == 3)
    def _():
        total = sum_ref[...]
        width = total.shape[0]
        product = total * packs[place[0]].astype(f32)
        ones = jnp.ones((8, total.shape[1]), f32)
        summed = lax.dot_general(ones, product, NT, precision=lax.Precision.HIGHEST, preferred_element_type=f32)
        values = [summed[0:1, :] / gain[...], tiny[0:1, :], tiny[1:2, :], tiny[2:3, :]]
        rows = rows_of((16, width))
        small = jnp.zeros((16, width), f32)
        for r, value in enumerate(values):
            high = value.astype(bf).astype(f32)
            small = jnp.where(rows == r, high, jnp.where(rows == r + 4, value - high, small))
        small = jnp.concatenate([small.astype(bf), jnp.zeros((16, total.shape[1] - width), bf)], 1)
        for q in range(4):
            slabs_ref[q, 0 : width // 4, :] = total[q * width // 4 : (q + 1) * width // 4, :].astype(bf)
            slabs_ref[q, width // 4 :, :] = small


def collect(place, normed, kv_a, kv_b, q_a, q_b, keep_a, keep_b, got_a, got_b, packs, gain, tiny, dep):
    n, width = normed.shape
    rows = n // 4
    kv = pl.BlockSpec((2, rows, 128), lambda b, p: (0, b, 0))
    dq = pl.BlockSpec((2, 64, rows), lambda b, p: (0, 0, b))
    flat = pl.BlockSpec((rows, 128), lambda b, p: (b, 0))
    return pl.pallas_call(
        collect_kernel,
        grid_spec=pltpu.PrefetchScalarGridSpec(
            num_scalar_prefetch=1,
            grid=(4,),
            in_specs=[
                pl.BlockSpec((rows, width), lambda b, p: (b, 0)),
                kv, kv, dq, dq, flat, flat, flat, flat,
                pl.BlockSpec(packs.shape, lambda b, p: (0, 0, 0)),
                pl.BlockSpec((1, width), lambda b, p: (0, 0)),
                pl.BlockSpec(tiny.shape, lambda b, p: (0, 0)),
                anywhere(),
            ],
            out_specs=[
                pl.BlockSpec((rows, 768), lambda b, p: (own_block(b, p), 0)),
                pl.BlockSpec((rows, 768), lambda b, p: (other_block(b, p), 0)),
                pl.BlockSpec((4, width // 4 + 16, 768), lambda b, p: (0, 0, 0)),
            ],
            scratch_shapes=[pltpu.VMEM((width, 768), f32)],
        ),
        out_shape=[
            jax.ShapeDtypeStruct((n // 2, 768), bf),
            jax.ShapeDtypeStruct((n // 2, 768), bf),
            jax.ShapeDtypeStruct((4, width // 4 + 16, 768), bf),
        ],
        compiler_params=params(26),
        cost_estimate=cost(5),
    )(place, normed, kv_a, kv_b, q_a, q_b, keep_a, keep_b, got_a, got_b, packs, gain, tiny, dep)


def tokens_kernel(place, mine, got, packs, x_ref, back_resid, gain, dep, out):
    core = place[0]
    back = nt(mine[...], packs[core]) + nt(got[...], packs[1 - core])
    x = x_ref[...].astype(f32)
    inverse = lax.rsqrt(jnp.mean(x * x, axis=1, keepdims=True) + EPSILON)
    k = back * gain[...]
    mean = jnp.mean(k * x, axis=1, keepdims=True)
    out[...] = (back_resid[...] + inverse * k - x * (inverse * inverse * inverse * mean)).astype(bf)


def tokens_back(place, mine, got, packs, x, back_resid, gain, dep):
    n, width = x.shape
    rows = n // 4
    wide = pl.BlockSpec((rows, 768), lambda b, p: (b, 0))
    block = pl.BlockSpec((rows, width), lambda b, p: (b, 0))
    return pl.pallas_call(
        tokens_kernel,
        grid_spec=pltpu.PrefetchScalarGridSpec(
            num_scalar_prefetch=1,
            grid=(4,),
            in_specs=[wide, wide, pl.BlockSpec(packs.shape, lambda b, p: (0, 0, 0)), block, block, pl.BlockSpec((1, width), lambda b, p: (0, 0)), anywhere()],
            out_specs=block,
        ),
        out_shape=jax.ShapeDtypeStruct((n, width), bf),
        compiler_params=params(20),
        cost_estimate=cost(4),
    )(place, mine, got, packs, x, back_resid, gain, dep)


def unfold_kernel(place, near, far, small, small_far, out, rows_out):
    line = place[3]
    width = rows_out.shape[1]
    both = small[0:8, :width].astype(f32) + small_far[0:8, :width].astype(f32)
    rows_out[...] = both + pltpu.roll(both, 4, axis=0)
    count, rows = near.shape[1], near.shape[2]
    for source, c in ((near, place[0]), (far, 1 - place[0])):
        for k in range(count):
            at = pl.ds(pl.multiple_of((line ^ k) * rows, rows), rows)
            value = source[0, k]
            base = c * 256
            out[at, pl.ds(pl.multiple_of(base, 128), 256)] = value[:, 0:256].astype(f32)
            for pair in range(2):
                a = value[:, 256 + 256 * pair : 384 + 256 * pair]
                b = value[:, 384 + 256 * pair : 512 + 256 * pair]
                out[at, pl.ds(pl.multiple_of(512 + base + 128 * pair, 128), 128)] = left(a, b).astype(f32)
                out[at, pl.ds(pl.multiple_of(1024 + base + 128 * pair, 128), 128)] = right(a, b).astype(f32)


def unfold(place, near, far, small, small_far, width):
    block = near.shape[1:]
    piece = pl.BlockSpec((1,) + block, lambda q, p: (q ^ (2 * p[1] + p[2]), 0, 0, 0))
    tail = pl.BlockSpec(small.shape, lambda q, p: (0, 0))
    return pl.pallas_call(
        unfold_kernel,
        grid_spec=pltpu.PrefetchScalarGridSpec(
            num_scalar_prefetch=1,
            grid=(4,),
            in_specs=[piece, piece, tail, tail],
            out_specs=[pl.BlockSpec((width // 4, 3 * width), lambda q, p: (q, 0)), pl.BlockSpec((8, width), lambda q, p: (0, 0))],
        ),
        out_shape=[jax.ShapeDtypeStruct((width, 3 * width), f32), jax.ShapeDtypeStruct((8, width), f32)],
        compiler_params=params(12),
        cost_estimate=cost(3),
    )(place, near, far, small, small_far)


def body(
    layer_activations,
    sequence_extents,
    position_cluster_label,
    cluster_sharpness,
    heed_scale_factor,
    triple_entry_matrix,
    heed_exit_matrix,
    blend_scale_factor,
    router_matrix,
    specialist_entry_matrix,
    specialist_exit_matrix,
    upstream_derivative,
):
    seq_count, pos_count, width = layer_activations.shape
    tokens = seq_count * pos_count
    hidden = specialist_entry_matrix.shape[2]
    spot = lax.axis_index("seq")
    row = lax.axis_index("batch")
    core, chip, side, line = spot % 2, spot // 2, row % 2, row // 2
    lines = lax.axis_size("batch") // 2
    place = jnp.stack([core, chip, side, line]).astype(jnp.int32)
    core_pairs, chip_pairs = [(0, 1), (1, 0), (2, 3), (3, 2)], [(0, 2), (1, 3), (2, 0), (3, 1)]
    up, down = chip_pairs[:2], chip_pairs[2:]

    x = layer_activations.reshape(tokens, width)
    x_other = lax.ppermute(x, "seq", core_pairs)
    gain_a = heed_scale_factor.astype(f32).reshape(1, width)
    packs, w_own = pack(place, triple_entry_matrix)
    normed, qkv, send_a, send_b = project(place, x, x_other, gain_a, w_own)
    got_a = lax.ppermute(send_a, "seq", chip_pairs)
    got_b = lax.ppermute(send_b, "seq", up)
    limit = (sequence_extents - chip * 2 * pos_count).astype(jnp.int32)
    p_na, o_na, st_na = near_forward(0, limit, qkv, qkv)
    p_a, o_a, st_a, q_a, kv_a = far_forward(0, place, qkv, got_a, got_a, o_na)
    got_oa = lax.ppermute(o_a, "seq", up)
    p_b, o_b, st_b, q_b, kv_b = far_forward(1, place, qkv, got_a, got_b, o_a)
    got_ob = lax.ppermute(o_b, "seq", up)
    p_nb, o_nb, st_nb = near_forward(1, limit, qkv, o_b)
    att_mine, att_send, log = join(place, o_na, o_nb, st_na, st_nb, o_a, o_b, got_oa, got_ob)
    att_got = lax.ppermute(att_send, "seq", core_pairs)

    router = jnp.zeros((16, width), bf).at[:2].set(router_matrix.T)
    block_out, fac, gout, tiny, back_resid, ba_own, ba_send = mixture(
        place,
        cluster_sharpness,
        x,
        att_mine,
        att_got,
        heed_exit_matrix,
        blend_scale_factor.astype(f32).reshape(1, width),
        router,
        position_cluster_label.reshape(1, tokens),
        upstream_derivative.reshape(tokens, width),
        specialist_entry_matrix,
        specialist_exit_matrix,
    )

    ba_got = lax.ppermute(ba_send, "seq", core_pairs)
    fac_got = swap(take(fac, 1 - core), 1)
    gout_got = swap(take(gout, 1 - core), 1)
    grads, inner, payload = ready(place, ba_own, ba_got, att_mine, att_send, log)
    got_grad = lax.ppermute(payload, "seq", down)
    pay = factors(place, fac, fac_got, gout, gout_got)
    pays = [pay[0]] + [swap(pay[i], 2 * m[0] + 4 * m[1]) for i, m in list(enumerate(MOVES))[1:]]
    dkv_a, dq_a = near_backward(0, qkv, p_na, grads, st_na, log, inner, pay[0])
    stages = turns()
    kept, sent = slabs(place, dkv_a, pays, width, hidden // 4, lines)
    send_fa, keep_fa = far_backward(0, place, q_a, kv_a, p_a, st_a, grads, log, inner, got_grad, kept)
    got_fa = lax.ppermute(send_fa, "seq", chip_pairs)
    for t, turn in enumerate(stages):
        got = swap_by_core(sent, (8 << turn[0], 8 << turn[1]))
        after = stages[t + 1] if t + 1 < len(stages) else None
        if t == len(stages) - 1:
            send_fb, keep_fb = far_backward(1, place, q_b, kv_b, p_b, st_b, grads, log, inner, got_grad, kept)
            got_fb = lax.ppermute(send_fb, "seq", chip_pairs)
            kept = fold(None, place, keep_fb, kept, got)[0]
        else:
            kept, sent = fold(after, place, keep_fa, kept, got)
    dkv_b, dq_b = near_backward(1, qkv, p_nb, grads, st_nb, log, inner, kept)
    last = dkv_b
    whole = kept
    for turn in stages[:0:-1]:
        whole = pile(last, whole, swap_by_core(whole, (8 << turn[0], 8 << turn[1])))
    got_z = swap_by_core(whole, (8 << stages[0][0], 8 << stages[0][1]))
    d_mine, d_send, q_slabs = collect(
        place, normed, dkv_a, dkv_b, dq_a, dq_b, keep_fa, keep_fb, got_fa, got_fb, packs, gain_a, tiny, whole
    )

    d_got = lax.ppermute(d_send, "seq", core_pairs)
    mine = 2 * chip + side
    parts = [take(q_slabs, mine)] + [swap(take(q_slabs, mine ^ (2 * m[0] + m[1])), 2 * m[0] + 4 * m[1]) for m in MOVES[1:]]
    whole = pile(q_slabs, whole, got_z)
    got_first = swap_by_core(whole, (2, 4))
    tokens_grad = tokens_back(place, d_mine, d_got, packs, x, back_resid, gain_a, whole)
    rows = width // 4
    part = add(tokens_grad, parts)
    by_line = part[:rows].reshape(lines, rows // lines, 768)
    small = jnp.broadcast_to(part[rows:], (lines, 16, 768))
    by_line = jnp.concatenate([by_line, small], 1)
    z_parts = [take(by_line, line)] + [swap(take(by_line, line ^ k), 8 * k) for k in range(1, lines)]
    whole = pile(part, whole, got_first)
    got_second = swap_by_core(whole, (4, 2))
    far_first = swap(whole, 1)
    part = add(whole, z_parts)
    small = part[rows // lines :]
    part = part[: rows // lines]
    zs = jnp.stack([part] + [swap(part, 8 * k) for k in range(1, lines)])
    near = jnp.stack([zs, swap(zs, 4), swap(zs, 2), swap(zs, 6)])
    far = swap(near, 1)
    grad_qkv, small = unfold(place, near, far, small, swap(small, 1), width)
    got_second = gate(zs, got_second)
    far_second = swap(got_second, 1)
    block = (2, lines) + whole.shape[1:]
    grad_in, grad_down, grad_out = spread_experts(
        place, whole.reshape(block), got_second.reshape(block), far_first.reshape(block), far_second.reshape(block), hidden, width
    )
    return (
        block_out.reshape(layer_activations.shape),
        tokens_grad.reshape(layer_activations.shape),
        small[0],
        grad_qkv,
        grad_out.reshape(width, width),
        small[3],
        small[1:3].T,
        grad_in,
        grad_down,
    )


def solution(mesh):
    rows = P("batch", "seq", None)
    placed = (rows, P("batch"), P("batch", "seq")) + (P(),) * 8 + (rows,)
    return jax.shard_map(body, mesh=mesh, in_specs=placed, out_specs=(rows, rows) + (P(),) * 7, check_vma=False)
```

```python
import functools

import jax
import jax.numpy as jnp
from jax import lax
from jax.experimental import pallas as pl
from jax.experimental.pallas import tpu as pltpu
from jax.sharding import PartitionSpec as P

HEADS = 8
HEAD = 64
GROUP = 32
EPSILON = 1e-06
LOG2E = 1.4426950408889634
SC = 0.125 * LOG2E
MASKED = -1e30
BQ = 512
CH = 512
bf = jnp.bfloat16
f32 = jnp.float32
AXES = ("batch", "seq")
NT = (((1,), (1,)), ((), ()))
TN = (((0,), (0,)), ((), ()))


def nt(a, b):
    return lax.dot_general(a, b, NT, preferred_element_type=f32)


def tn(a, b):
    return lax.dot_general(a, b, TN, preferred_element_type=f32)


def nn(a, b):
    return jnp.dot(a, b, preferred_element_type=f32)


def rows_of(shape):
    return lax.broadcasted_iota(jnp.int32, shape, 0)


def lanes_of(shape):
    return lax.broadcasted_iota(jnp.int32, shape, 1)


def vmem():
    return pl.BlockSpec(memory_space=pltpu.VMEM)


def smem():
    return pl.BlockSpec(memory_space=pltpu.SMEM)


def params(mib=16):
    return pltpu.CompilerParams(vmem_limit_bytes=mib * 2**20)


def anywhere():
    return pl.BlockSpec(memory_space=pl.ANY)


def hbm():
    return pl.BlockSpec(memory_space=pltpu.HBM)


def cost(us):
    return pl.CostEstimate(flops=int(us * 1e8), bytes_accessed=2**10, transcendentals=0)


def stay(value):
    return pltpu.with_memory_space_constraint(value, pltpu.HBM)


def kept_out(shape, dtype):
    return pltpu.HBM(shape, dtype)


def shift_lanes(value):
    return pltpu.roll(value.astype(f32), 64, axis=1).astype(bf)


def left(first, second):
    return jnp.where(lanes_of(first.shape) < 64, first, shift_lanes(second))


def right(first, second):
    return jnp.where(lanes_of(first.shape) < 64, shift_lanes(first), second)


def pack_kernel(place, w, router, gain_a, gain_m, packs, w_own, router_rows, gains):
    core = place[0]
    lanes = lanes_of((router.shape[0], 128))
    both = router[...].astype(f32)
    columns = jnp.where(lanes == 0, both[:, 0:1], jnp.where(lanes == 1, both[:, 1:2], 0.0))
    router_rows[...] = columns.T[0:16, :].astype(bf)
    gains[0] = gain_a[...].astype(f32)
    gains[1] = gain_m[...].astype(f32)
    for c in range(2):
        packs[c, :, 0:256] = w[:, 256 * c : 256 * c + 256]
        for h in range(4):
            at = 256 * c + 128 * (h // 2)
            k = w[:, 512 + at : 640 + at]
            v = w[:, 1024 + at : 1152 + at]
            packs[c, :, 256 + 128 * h : 384 + 128 * h] = left(k, v) if h % 2 == 0 else right(k, v)
    for h in range(4):
        q = packs[core, :, 128 * (h // 2) : 128 * (h // 2) + 128]
        q = q if h % 2 == 0 else shift_lanes(q)
        w_own[:, 256 * h : 256 * h + 128] = jnp.where(lanes_of(q.shape) < 64, q, jnp.zeros((), bf))
        w_own[:, 256 * h + 128 : 256 * h + 256] = packs[core, :, 256 + 128 * h : 384 + 128 * h]


def pack(place, w, router, gain_a, gain_m):
    width = w.shape[0]
    return pl.pallas_call(
        pack_kernel,
        in_specs=[smem()] + [vmem()] * 4,
        out_specs=[vmem()] * 4,
        out_shape=[
            kept_out((2, width, 768), bf),
            jax.ShapeDtypeStruct((width, 1024), bf),
            jax.ShapeDtypeStruct((16, width), bf),
            jax.ShapeDtypeStruct((2, 1, width), f32),
        ],
        compiler_params=params(16),
        cost_estimate=cost(3),
    )(place, w, router, gain_a, gain_m)


def project_kernel(place, x_own, x_other, gain, w_own, normed, qkv, send_a, send_b):
    core, chip = place[0], place[1]
    block = pl.program_id(0)

    def go(x_ref):
        x = x_ref[...].astype(f32)
        inverse = lax.rsqrt(jnp.mean(x * x, axis=1, keepdims=True) + EPSILON)
        low = (x * inverse * gain[...]).astype(bf)
        normed[...] = low
        out = nn(low, w_own[...]).astype(bf)
        qkv[...] = out
        send_b[...] = out[:, 384:512]

        @pl.when(chip == 0)
        def _():
            send_a[...] = out[:, 128:256]

        @pl.when(chip == 1)
        def _():
            send_a[...] = left(out[:, 512:640], out[:, 768:896])

    @pl.when(block // 2 == core)
    def _():
        go(x_own)

    @pl.when(block // 2 != core)
    def _():
        go(x_other)


def project(place, x_own, x_other, gain, w_own):
    rows, width = x_own.shape

    def own(b, p):
        return (jnp.where(b // 2 == p[0], b % 2, jnp.where(b // 2 > p[0], 1, 0)), 0)

    def other(b, p):
        return (jnp.where(b // 2 != p[0], b % 2, jnp.where(b // 2 > 1 - p[0], 1, 0)), 0)

    half = rows // 2
    return pl.pallas_call(
        project_kernel,
        grid_spec=pltpu.PrefetchScalarGridSpec(
            num_scalar_prefetch=1,
            grid=(4,),
            in_specs=[
                pl.BlockSpec((half, width), own),
                pl.BlockSpec((half, width), other),
                pl.BlockSpec((1, width), lambda b, p: (0, 0)),
                pl.BlockSpec((width, 1024), lambda b, p: (0, 0)),
            ],
            out_specs=[
                pl.BlockSpec((half, width), lambda b, p: (b, 0)),
                pl.BlockSpec((half, 1024), lambda b, p: (b, 0)),
                pl.BlockSpec((half, 128), lambda b, p: (b, 0)),
                pl.BlockSpec((half, 128), lambda b, p: (b, 0)),
            ],
        ),
        out_shape=[
            kept_out((2 * rows, width), bf),
            kept_out((2 * rows, 1024), bf),
            jax.ShapeDtypeStruct((2 * rows, 128), bf),
            jax.ShapeDtypeStruct((2 * rows, 128), bf),
        ],
        compiler_params=params(20),
        cost_estimate=cost(4),
    )(place, x_own, x_other, gain, w_own)


def scores(kv, q, s_ref, slot, kmax, q0, limit, causal):
    peak = None
    for k0 in range(0, kmax, CH):
        s = nt(kv[k0 : k0 + CH, :], q)
        if causal:
            if k0 >= 1024:
                s = jnp.where(rows_of(s.shape) + k0 < limit, s, MASKED)
            if k0 + CH > q0:
                s = jnp.where(rows_of(s.shape) + (k0 - q0) <= lanes_of(s.shape), s, MASKED)
        s_ref[slot, k0 : k0 + CH, :] = s
        m = jnp.max(s, axis=0, keepdims=True)
        peak = m if peak is None else jnp.maximum(peak, m)
    return peak


def weigh(vt, s_ref, slot, peak, kmax, put):
    scaled = peak * SC
    acc = None
    for k0 in range(0, kmax, CH):
        p = jnp.exp2(s_ref[slot, k0 : k0 + CH, :] * SC - scaled).astype(bf)
        put(k0 // CH, p)
        d = nn(vt[:, k0 : k0 + CH], p)
        acc = d if acc is None else acc + d
    total = acc[0:1, :]
    return acc[64:128, :] * (1.0 / total), scaled, total


def ones_and_values(kv):
    vt = kv.T
    return jnp.where(rows_of(vt.shape) < 64, jnp.ones((), bf), vt)


def near_forward_kernel(limit_ref, qkv, dep, p_ref, o_ref, st_ref, s_ref, vt_ref, buf, sems):
    limit = limit_ref[0]
    count = qkv.shape[0] // BQ
    tasks = [(h, i) for h in range(2) for i in range(count)]

    def start_scores(at):
        h, i = tasks[at]
        kv = qkv.at[:, 256 * h + 128 : 256 * h + 256]
        q = qkv[i * BQ : (i + 1) * BQ, 256 * h : 256 * h + 128]
        return scores(kv, q, s_ref, at % 2, (i + 1) * BQ, i * BQ, limit, True)

    copies = []
    peak = start_scores(0)
    for at, (h, i) in enumerate(tasks):
        if i == 0:
            vt_ref[h] = ones_and_values(qkv[:, 256 * h + 128 : 256 * h + 256])
        later = start_scores(at + 1) if at + 1 < len(tasks) else None
        base = i * (i + 1) // 2

        def put(k, p):
            buf[h, base + k] = p

        out, scaled, total = weigh(vt_ref.at[h], s_ref, at % 2, peak, (i + 1) * BQ, put)
        copies.append(pltpu.make_async_copy(buf.at[h, base : base + i + 1], p_ref.at[h, base : base + i + 1], sems.at[h, i]))
        copies[-1].start()
        o_ref[h, :, i * BQ : (i + 1) * BQ] = out.astype(bf)
        st_ref[h, 0:1, i * BQ : (i + 1) * BQ] = scaled
        st_ref[h, 1:2, i * BQ : (i + 1) * BQ] = total
        peak = later
    for copy in copies:
        copy.wait()


def near_forward(pair, limit, qkv, dep):
    n = qkv.shape[0]
    count = n // BQ
    shape = (2, count * (count + 1) // 2, CH, BQ)
    return pl.pallas_call(
        near_forward_kernel,
        grid=(1,),
        in_specs=[smem(), pl.BlockSpec((n, 512), lambda g: (0, pair)), anywhere()],
        out_specs=[
            anywhere(),
            pl.BlockSpec((2, 64, n), lambda g: (0, 0, 0)),
            pl.BlockSpec((2, 8, n), lambda g: (0, 0, 0)),
        ],
        out_shape=[
            kept_out(shape, bf),
            jax.ShapeDtypeStruct((2, 64, n), bf),
            jax.ShapeDtypeStruct((2, 8, n), f32),
        ],
        scratch_shapes=[
            pltpu.VMEM((2, n, BQ), f32),
            pltpu.VMEM((2, 128, n), bf),
            pltpu.VMEM(shape, bf),
            pltpu.SemaphoreType.DMA((2, count)),
        ],
        compiler_params=params(34),
        cost_estimate=cost(9),
    )(limit, qkv, dep)


def three(value):
    high = value.astype(bf)
    rest = value - high.astype(f32)
    mid = rest.astype(bf)
    return high, mid, (rest - mid.astype(f32)).astype(bf)


def far_forward_kernel(j, place, q_own, q_got, kv_own, kv_got, dep, p_ref, o_ref, st_ref, q_ref, kv_ref, s_ref, vt_ref, buf, sems):
    n = q_own.shape[0]

    @pl.when(place[1] == 1)
    def _():
        q_ref[...] = q_own[...]
        kv_ref[...] = kv_got[...]

    @pl.when(place[1] == 0)
    def _():
        q = q_got[...] if j == 0 else shift_lanes(q_got[...])
        q_ref[...] = jnp.where(lanes_of(q.shape) < 64, q, jnp.zeros((), bf))
        kv_ref[...] = kv_own[...]

    vt_ref[...] = ones_and_values(kv_ref[...])
    count = n // BQ
    copies = []
    peak = scores(kv_ref, q_ref[0:BQ, :], s_ref, 0, n, 0, None, False)
    for i in range(count):
        later = None
        at = slice(i * BQ, (i + 1) * BQ)
        if i + 1 < count:
            later = scores(kv_ref, q_ref[(i + 1) * BQ : (i + 2) * BQ, :], s_ref, (i + 1) % 2, n, 0, None, False)

        def put(k, p):
            buf[i, k] = p

        out, scaled, total = weigh(vt_ref, s_ref, i % 2, peak, n, put)
        copies.append(pltpu.make_async_copy(buf.at[i], p_ref.at[i], sems.at[i]))
        copies[-1].start()
        o_ref[0:64, at] = out.astype(bf)
        high, mid, low = three(scaled + jnp.log(total) * LOG2E)
        tail = jnp.concatenate([high.astype(f32), mid.astype(f32), low.astype(f32), jnp.zeros((13, BQ), f32)], 0)
        o_ref[64:80, at] = tail.astype(bf)
        st_ref[0:1, at] = scaled
        peak = later
    for copy in copies:
        copy.wait()


def far_forward(j, place, qkv, q_got, kv_got, dep):
    n = qkv.shape[0]
    whole = pl.BlockSpec((n, 128), lambda h: (0, 0))
    shape = (n // BQ, n // CH, CH, BQ)
    return pl.pallas_call(
        lambda *refs: far_forward_kernel(j, *refs),
        grid=(1,),
        in_specs=[
            smem(),
            pl.BlockSpec((n, 128), lambda h: (0, 2 * j)),
            whole,
            pl.BlockSpec((n, 128), lambda h: (0, 2 * j + 5)),
            whole,
            anywhere(),
        ],
        out_specs=[
            anywhere(),
            pl.BlockSpec((80, n), lambda h: (0, 0)),
            pl.BlockSpec((8, n), lambda h: (0, 0)),
            whole,
            whole,
        ],
        out_shape=[
            kept_out(shape, bf),
            jax.ShapeDtypeStruct((80, n), bf),
            jax.ShapeDtypeStruct((8, n), f32),
            kept_out((n, 128), bf),
            kept_out((n, 128), bf),
        ],
        scratch_shapes=[
            pltpu.VMEM((2, n, BQ), f32),
            pltpu.VMEM((128, n), bf),
            pltpu.VMEM(shape, bf),
            pltpu.SemaphoreType.DMA((n // BQ,)),
        ],
        compiler_params=params(34),
        cost_estimate=cost(10),
    )(place, qkv, q_got, qkv, kv_got, dep)


def unsplit(ref, at):
    return ref[at : at + 1, :].astype(f32) + ref[at + 1 : at + 2, :].astype(f32) + ref[at + 2 : at + 3, :].astype(f32)


def join_kernel(place, near_a, near_b, stat_a, stat_b, far_a, far_b, got_a, got_b, mine, other, log_ref):
    core, chip = place[0], place[1]
    half = mine.shape[1]
    for h in range(4):
        far = (far_a, far_b, got_a, got_b)[h]
        near, stat = (near_a, near_b)[h // 2], (stat_a, stat_b)[h // 2]
        log_near = stat[h % 2, 0:1, :] + jnp.log(stat[h % 2, 1:2, :]) * LOG2E
        log_far = jnp.where(chip == 1, unsplit(far, 64), MASKED)
        top = jnp.maximum(log_near, log_far)
        e_near, e_far = jnp.exp2(log_near - top), jnp.exp2(log_far - top)
        both = e_near + e_far
        log_ref[h] = jnp.broadcast_to(top + jnp.log(both) * LOG2E, log_ref.shape[1:])
        far_out = jnp.where(chip == 1, far[0:64, :].astype(f32), 0.0)
        joined = ((near[h % 2].astype(f32) * e_near + far_out * e_far) * (1.0 / both)).astype(bf)
        at = slice(64 * h, 64 * h + 64)

        @pl.when(core == 0)
        def _():
            mine[at, :] = joined[:, :half]
            other[at, :] = joined[:, half:]

        @pl.when(core == 1)
        def _():
            mine[at, :] = joined[:, half:]
            other[at, :] = joined[:, :half]


def join(place, near_a, near_b, stat_a, stat_b, far_a, far_b, got_a, got_b):
    n = near_a.shape[2]
    return pl.pallas_call(
        join_kernel,
        in_specs=[smem()] + [vmem()] * 8,
        out_specs=[vmem()] * 3,
        out_shape=[
            jax.ShapeDtypeStruct((256, n // 2), bf),
            jax.ShapeDtypeStruct((256, n // 2), bf),
            jax.ShapeDtypeStruct((4, 8, n), f32),
        ],
        compiler_params=params(),
        cost_estimate=cost(2),
    )(place, near_a, near_b, stat_a, stat_b, far_a, far_b, got_a, got_b)


def mixture_kernel(
    place, sharp, x, att_own, att_got, wout, gain, router, labels, gy, w1_hbm, w2_hbm,
    block_out, fac, gout, tiny, back_resid, ba_own, ba_other, w1, w2, sems,
):
    core = place[0]
    copy1 = pltpu.make_async_copy(w1_hbm, w1, sems.at[0])
    copy2 = pltpu.make_async_copy(w2_hbm, w2, sems.at[1])
    copy1.start()
    copy2.start()
    own_rows = pl.ds(pl.multiple_of(core * 256, 256), 256)
    other_rows = pl.ds(pl.multiple_of(256 - core * 256, 256), 256)
    wo_own, wo_other = wout[own_rows, :], wout[other_rows, :]
    resid = x[...].astype(f32) + tn(att_own[...], wo_own) + tn(att_got[...], wo_other)
    inverse = lax.rsqrt(jnp.mean(resid * resid, axis=1, keepdims=True) + EPSILON)
    unit = resid * inverse
    mix = (unit * gain[...]).astype(bf)
    temper = 1.0 / sharp[0]
    logits = nt(router[...], mix) * temper
    tokens = mix.shape[0]
    groups = tokens // GROUP
    member = labels[...] == rows_of((groups, tokens))
    weights, mixing = [], []
    for e in range(2):
        row = logits[e : e + 1, :]
        peak = jnp.max(jnp.where(member, row, -jnp.inf), axis=1, keepdims=True)
        token_peak = jnp.sum(jnp.where(member, peak, 0.0), axis=0, keepdims=True)
        raised = jnp.exp(row - token_peak)
        total = jnp.sum(jnp.where(member, raised, 0.0), axis=1, keepdims=True)
        token_total = jnp.sum(jnp.where(member, total, 0.0), axis=0, keepdims=True)
        w = raised / token_total
        weights.append(w)
        mixing.append(jnp.where(member, w, 0.0))
    mixing = jnp.concatenate(mixing, 0).astype(bf)
    mixed = nn(mixing, mix).astype(bf)
    back_expert = nn(mixing, gy[...]).astype(bf)
    copy1.wait()
    copy2.wait()
    expert_out, back_mixed = [], []
    quarter = w1.shape[2] // 4
    width = mix.shape[1]
    for e in range(2):
        at = slice(groups * e, groups * (e + 1))
        inner = nn(mixed[at], w1[e])
        cdf = 0.5 * (1.0 + lax.erf(inner * 0.7071067811865476))
        active = (inner * cdf).astype(bf)
        slope = cdf + inner * (jnp.exp(-0.5 * inner * inner) * 0.3989422804014327)
        expert_out.append(nn(active, w2[e]))
        back_inner = (slope * nt(back_expert[at], w2[e])).astype(bf)
        back_mixed.append(nt(back_inner, w1[e]))
        fac[e, :, 0:width] = mixed[at]
        fac[e, :, width : 2 * width] = back_expert[at]
        for q in range(4):
            base = 2 * width + 2 * quarter * q
            fac[e, :, base : base + quarter] = back_inner[:, quarter * q : quarter * (q + 1)]
            fac[e, :, base + quarter : base + 2 * quarter] = active[:, quarter * q : quarter * (q + 1)]
    expert_out = jnp.concatenate(expert_out, 0).astype(bf)
    back_mixed = jnp.concatenate(back_mixed, 0).astype(bf)
    block_out[...] = (resid + tn(mixing, expert_out)).astype(bf)
    spread = nt(expert_out, gy[...]) + nt(back_mixed, mix)
    rows16 = rows_of((16, tokens))
    back_logits = jnp.zeros((16, tokens), f32)
    for e in range(2):
        back_weight = jnp.sum(jnp.where(member, spread[groups * e : groups * (e + 1)], 0.0), axis=0, keepdims=True)
        w = weights[e]
        inner = jnp.sum(jnp.where(member, w * back_weight, 0.0), axis=1, keepdims=True)
        token_inner = jnp.sum(jnp.where(member, inner, 0.0), axis=0, keepdims=True)
        back_logits = jnp.where(rows16 == e, w * (back_weight - token_inner) * temper, back_logits)
    back_logits = back_logits.astype(bf)
    ctrl = nn(back_logits, mix)
    back_mix = tn(mixing, back_mixed) + tn(back_logits, router[...])
    tiny[...] = jnp.zeros_like(tiny)
    tiny[0:2, :] = ctrl[0:2, :]
    tiny[2:3, :] = jnp.sum(back_mix * unit, axis=0, keepdims=True)
    n = back_mix * gain[...]
    mean = jnp.mean(n * resid, axis=1, keepdims=True)
    back = gy[...].astype(f32) + inverse * n - resid * (inverse * inverse * inverse * mean)
    back_resid[...] = back
    branch = back.astype(bf)
    gout[core] = nn(att_own[...], branch).astype(bf)
    gout[1 - core] = nn(att_got[...], branch).astype(bf)
    ba_own[...] = nt(wo_own, branch).astype(bf)
    ba_other[...] = nt(wo_other, branch).astype(bf)


def mixture(place, sharp, x, att_own, att_got, wout, gain, router, labels, gy, w1, w2):
    tokens, width = x.shape
    hidden = w1.shape[2]
    groups = tokens // GROUP
    return pl.pallas_call(
        mixture_kernel,
        in_specs=[smem(), smem()] + [vmem()] * 8 + [pl.BlockSpec(memory_space=pl.ANY)] * 2,
        out_specs=[vmem()] * 7,
        out_shape=[
            kept_out((tokens, width), bf),
            jax.ShapeDtypeStruct((2, groups, 2 * width + 2 * hidden), bf),
            jax.ShapeDtypeStruct((2, width // 2, width), bf),
            jax.ShapeDtypeStruct((8, width), f32),
            kept_out((tokens, width), f32),
            jax.ShapeDtypeStruct((width // 2, tokens), bf),
            jax.ShapeDtypeStruct((width // 2, tokens), bf),
        ],
        scratch_shapes=[pltpu.VMEM(w1.shape, bf), pltpu.VMEM(w2.shape, bf), pltpu.SemaphoreType.DMA((2,))],
        compiler_params=params(48),
        cost_estimate=cost(15),
    )(place, sharp, x, att_own, att_got, wout, gain, router, labels, gy, w1, w2)


def ready_kernel(place, ba_own, ba_got, mine, other, log_ref, grads, inner, payload):
    core = place[0]
    half = mine.shape[1]
    for h in range(4):
        at = slice(64 * h, 64 * h + 64)
        g_own, g_got = ba_own[at, :], ba_got[at, :]
        d_own = jnp.sum(g_own.astype(f32) * mine[at, :].astype(f32), axis=0, keepdims=True)
        d_got = jnp.sum(g_got.astype(f32) * other[at, :].astype(f32), axis=0, keepdims=True)

        def put(g0, g1, d0, d1):
            grads[h, :, :half] = g0
            grads[h, :, half:] = g1
            inner[h, :, :half] = jnp.broadcast_to(d0, (8, half))
            inner[h, :, half:] = jnp.broadcast_to(d1, (8, half))
            if h >= 2:
                for g, d, s in ((g0, d0, slice(0, half)), (g1, d1, slice(half, 2 * half))):
                    payload[h - 2, 0:64, s] = g
                    parts = three(log_ref[h, 0:1, s]) + three(d)
                    tail = jnp.concatenate([part.astype(f32) for part in parts] + [jnp.zeros((10, half), f32)], 0)
                    payload[h - 2, 64:80, s] = tail.astype(bf)

        @pl.when(core == 0)
        def _():
            put(g_own, g_got, d_own, d_got)

        @pl.when(core == 1)
        def _():
            put(g_got, g_own, d_got, d_own)


def ready(place, ba_own, ba_got, mine, other, log):
    half = mine.shape[1]
    return pl.pallas_call(
        ready_kernel,
        in_specs=[smem()] + [vmem()] * 5,
        out_specs=[vmem()] * 3,
        out_shape=[
            jax.ShapeDtypeStruct((4, 64, 2 * half), bf),
            jax.ShapeDtypeStruct((4, 8, 2 * half), f32),
            jax.ShapeDtypeStruct((2, 80, 2 * half), bf),
        ],
        compiler_params=params(),
        cost_estimate=cost(2),
    )(place, ba_own, ba_got, mine, other, log)


def back_block(kv_ref, kt_ref, q, grad, ratio, inner, block, kmax, first, put_kv):
    low = (grad.astype(f32) * ratio).astype(bf)
    rhs = jnp.concatenate([jnp.zeros((64, BQ), bf), low], axis=0)
    shift = inner * ratio
    natural = rhs.T
    acc = None
    for k0 in range(0, kmax, CH):
        dp = nn(kv_ref[k0 : k0 + CH, :], rhs)
        p = block(k0 // CH)
        ds = (p.astype(f32) * (dp - shift)).astype(bf)
        d = nn(kt_ref[:, k0 : k0 + CH], ds)
        acc = d if acc is None else acc + d
        put_kv(k0, k0 >= first, nn(ds, q) + nn(p, natural))
    return (acc * 0.125).astype(bf)


def near_backward_kernel(head, q_ref, kv_ref, p_ref, grad_ref, stat, log_ref, inner_ref, *refs):
    dkv_ref, dq_ref, kt_ref, buf, sems = refs[-5:]
    count = q_ref.shape[0] // BQ
    copies = []
    for i in range(count):
        at = slice(i * (i + 1) // 2, (i + 1) * (i + 2) // 2)
        copies.append(pltpu.make_async_copy(p_ref.at[head, at], buf.at[at], sems.at[i]))
        copies[-1].start()
    kt_ref[...] = kv_ref[...].T[0:64, :]

    def put(k0, fresh, value):
        if fresh:
            dkv_ref[k0 : k0 + CH, :] = value
        else:
            dkv_ref[k0 : k0 + CH, :] += value

    for i in range(count):
        at = slice(i * BQ, (i + 1) * BQ)
        base = i * (i + 1) // 2
        copies[i].wait()
        ratio = jnp.exp2(stat[0, 0:1, at] - log_ref[0, 0:1, at])

        def block(k):
            return buf[base + k]

        dq_ref[:, at] = back_block(
            kv_ref, kt_ref, q_ref[at, :], grad_ref[0, :, at], ratio, inner_ref[0, 0:1, at], block, (i + 1) * BQ, i * BQ, put
        )


def near_backward(h, qkv, p, grads, stat, log, inner, deps):
    n = qkv.shape[0]
    row = pl.BlockSpec((1, 8, n), lambda g: (h, 0, 0))
    return pl.pallas_call(
        functools.partial(near_backward_kernel, h % 2),
        grid=(1,),
        in_specs=[
            pl.BlockSpec((n, 128), lambda g: (0, 2 * h)),
            pl.BlockSpec((n, 128), lambda g: (0, 2 * h + 1)),
            hbm(),
            pl.BlockSpec((1, 64, n), lambda g: (h, 0, 0)),
            pl.BlockSpec((1, 8, n), lambda g: (h % 2, 0, 0)),
            row,
            row,
        ]
        + [anywhere()] * len(deps),
        out_specs=[pl.BlockSpec((n, 128), lambda g: (0, 0)), pl.BlockSpec((64, n), lambda g: (0, 0))],
        out_shape=[kept_out((n, 128), f32), kept_out((64, n), bf)],
        scratch_shapes=[pltpu.VMEM((64, n), bf), pltpu.VMEM(p.shape[1:], bf), pltpu.SemaphoreType.DMA((n // BQ,))],
        compiler_params=params(24),
        cost_estimate=cost(7),
    )(qkv, qkv, stay(p), grads, stat, log, inner, *deps)


def far_backward_kernel(
    place, q_ref, kv_ref, p_ref, stat, grad_own, log_own, inner_own, got, dep, send_ref, keep_ref, kt_ref, sum_ref, dq_ref, buf, sems
):
    kt_ref[...] = kv_ref[...].T[0:64, :]
    upper = place[1] == 1
    n = q_ref.shape[0]
    copies = [pltpu.make_async_copy(p_ref.at[i], buf.at[i], sems.at[i]) for i in range(n // BQ)]
    for copy in copies:
        copy.start()

    def put(k0, fresh, value):
        if fresh:
            sum_ref[k0 : k0 + CH, :] = value
        else:
            sum_ref[k0 : k0 + CH, :] += value

    for i in range(n // BQ):
        at = slice(i * BQ, (i + 1) * BQ)
        got_log = got[0, 64:67, at].astype(f32)
        got_inner = got[0, 67:70, at].astype(f32)
        log = jnp.where(upper, log_own[0, 0:1, at], jnp.sum(got_log, axis=0, keepdims=True))
        inner = jnp.where(upper, inner_own[0, 0:1, at], jnp.sum(got_inner, axis=0, keepdims=True))
        grad = jnp.where(upper, grad_own[0, :, at], got[0, 0:64, at])
        ratio = jnp.exp2(stat[0:1, at] - log)
        copies[i].wait()

        def block(k):
            return buf[i, k]

        dq = back_block(kv_ref, kt_ref, q_ref[at, :], grad, ratio, inner, block, n, 0 if i == 0 else n, put)
        dq_ref[at, :] = jnp.concatenate([dq, jnp.zeros((64, BQ), bf)], 0).T

    @pl.when(upper)
    def _():
        send_ref[...] = sum_ref[...].astype(bf)
        keep_ref[...] = dq_ref[...]

    @pl.when(jnp.logical_not(upper))
    def _():
        send_ref[...] = dq_ref[...]
        keep_ref[...] = sum_ref[...].astype(bf)


def far_backward(j, place, q, kv, p, stat, grads, log, inner, got, dep):
    n = q.shape[0]
    row = pl.BlockSpec((1, 8, n), lambda h: (j, 0, 0))
    whole = pl.BlockSpec((n, 128), lambda h: (0, 0))
    return pl.pallas_call(
        far_backward_kernel,
        grid=(1,),
        in_specs=[
            smem(),
            whole,
            whole,
            hbm(),
            pl.BlockSpec((8, n), lambda h: (0, 0)),
            pl.BlockSpec((1, 64, n), lambda h: (j, 0, 0)),
            row,
            row,
            pl.BlockSpec((1, 80, n), lambda h: (j, 0, 0)),
            pl.BlockSpec(memory_space=pl.ANY),
        ],
        out_specs=[whole, whole],
        out_shape=[jax.ShapeDtypeStruct((n, 128), bf)] * 2,
        scratch_shapes=[
            pltpu.VMEM((64, n), bf),
            pltpu.VMEM((n, 128), f32),
            pltpu.VMEM((n, 128), bf),
            pltpu.VMEM(p.shape, bf),
            pltpu.SemaphoreType.DMA((n // BQ,)),
        ],
        compiler_params=params(30),
        cost_estimate=cost(13),
    )(place, q, kv, stay(p), stat, grads, log, inner, got, stay(dep))


def swap(value, bits):
    count = lax.axis_size("batch") * lax.axis_size("seq")
    return lax.ppermute(value, AXES, [(i, i ^ bits) for i in range(count)])


def turns():
    bits = (lax.axis_size("batch") // 2).bit_length() - 1
    return [(3 + t, 2 + bits - t) for t in range(bits)]


PLANE = [(1, 2), (2, 1)]


def swap_by_core(value, turn):
    count = lax.axis_size("batch") * lax.axis_size("seq")
    return lax.ppermute(value, AXES, [(i, i ^ (1 << turn[i % 2])) for i in range(count)])


def bit_of(number, core, turn):
    return (number >> jnp.where(core == 0, turn[0], turn[1])) & 1


def take(value, index, axis=0):
    return lax.dynamic_index_in_dim(value, index, axis, keepdims=False)


MOVES = ((0, 0), (1, 0), (0, 1), (1, 1))


def factors_kernel(place, fac, got, gout, got_out, dep, *outs):
    core, chip, side = place[0], place[1], place[2]
    groups = got.shape[0]
    width = gout.shape[2]
    part = (got.shape[1] - 2 * width) // 4
    rows = gout.shape[1] // 4
    for (x, y), out in zip(MOVES, outs):
        index = 2 * (chip ^ x) + (side ^ y)
        lanes = pl.ds(pl.multiple_of(2 * width + index * part, 128), part)
        at = pl.ds(pl.multiple_of(index * rows, rows), rows)
        out[0:groups, 0 : 2 * width] = fac[core, :, 0 : 2 * width]
        out[groups:, 0 : 2 * width] = got[:, 0 : 2 * width]
        out[0:groups, 2 * width : 2 * width + part] = fac[core, :, lanes]
        out[groups:, 2 * width : 2 * width + part] = got[:, lanes]
        out[:, 2 * width + part :] = (gout[core, at, :].astype(f32) + got_out[at, :].astype(f32)).astype(bf)


def factors(place, fac, got, gout, got_out, dep):
    groups, per = got.shape
    width = gout.shape[2]
    shape = jax.ShapeDtypeStruct((2 * groups, 2 * width + (per - 2 * width) // 4 + width), bf)
    return pl.pallas_call(
        factors_kernel,
        in_specs=[smem()] + [vmem()] * 4 + [anywhere()],
        out_specs=[vmem()] * 4,
        out_shape=[shape] * 4,
        compiler_params=params(),
        cost_estimate=cost(2),
    )(place, fac, got, gout, got_out, dep)


def slab_kernel(turn, lines, place, dep, a, b, c, d, keep, send):
    core, line = place[0], place[3]
    width = keep.shape[2]
    quarter = (a.shape[1] - 3 * width) // 2

    def lanes(start, size):
        return jnp.concatenate([ref[:, start : start + size] for ref in (a, b, c, d)], 0)

    g_in = tn(lanes(0, width), lanes(2 * width, quarter)).astype(bf)
    g_down = tn(lanes(2 * width + quarter, quarter), lanes(width, width)).astype(bf)
    total = a[:, 2 * width + 2 * quarter :].astype(f32)
    for ref in (b, c, d):
        total = total + ref[:, 2 * width + 2 * quarter :].astype(f32)
    pieces = [total.astype(bf), g_in, g_down]
    bits = lines.bit_length() - 1
    for z in range(lines):
        flipped = sum(((z >> t) & 1) << (bits - 1 - t) for t in range(bits))
        spot = jnp.where(core == 0, flipped, z)
        chosen = bit_of(8 * z, core, turn) == bit_of(8 * line, core, turn)

        def put(ref):
            start = 0
            for piece in pieces[1:] + pieces[:1]:
                rows = piece.shape[0] // lines
                ref[spot % (lines // 2), start : start + rows, :] = piece[z * rows : (z + 1) * rows, :]
                start += rows

        @pl.when(chosen)
        def _():
            put(keep)

        @pl.when(jnp.logical_not(chosen))
        def _():
            put(send)


def slabs(place, dep, payloads, width, quarter, lines):
    rows = (width + quarter + payloads[0].shape[0]) // lines
    shape = jax.ShapeDtypeStruct((lines // 2, rows, width), bf)
    turn = turns()[0]
    return pl.pallas_call(
        lambda *refs: slab_kernel(turn, lines, *refs),
        in_specs=[smem(), anywhere()] + [vmem()] * 4,
        out_specs=[vmem()] * 2,
        out_shape=[shape] * 2,
        compiler_params=params(),
        cost_estimate=cost(2),
    )(place, stay(dep), *payloads)


def fold_kernel(turn, place, dep, kept, got, keep, *send):
    if turn is None:
        keep[...] = (kept[...].astype(f32) + got[...].astype(f32)).astype(bf)
        return
    half = keep.shape[0]
    mine = bit_of(place[4], place[0], turn)
    at = pl.ds(mine * half, half)
    keep[...] = (kept[at].astype(f32) + got[at].astype(f32)).astype(bf)
    at = pl.ds((1 - mine) * half, half)
    send[0][...] = (kept[at].astype(f32) + got[at].astype(f32)).astype(bf)


def fold(turn, place, dep, kept, got):
    count = kept.shape[0] if turn is None else kept.shape[0] // 2
    shape = jax.ShapeDtypeStruct((count,) + kept.shape[1:], bf)
    outs = 1 if turn is None else 2
    return pl.pallas_call(
        lambda *refs: fold_kernel(turn, *refs),
        in_specs=[smem(), anywhere(), vmem(), vmem()],
        out_specs=[vmem()] * outs,
        out_shape=[shape] * outs,
        compiler_params=params(),
        cost_estimate=cost(1),
    )(place, dep, kept, got)


def pile_kernel(a, b, *refs):
    out = refs[-1]
    half = out.shape[0] // 2
    out[:half] = a[...]
    out[half:] = b[...]


def pile(a, b, *deps):
    return pl.pallas_call(
        pile_kernel,
        in_specs=[vmem(), vmem()] + [anywhere()] * len(deps),
        out_specs=vmem(),
        out_shape=jax.ShapeDtypeStruct((2 * a.shape[0],) + a.shape[1:], bf),
        compiler_params=params(),
        cost_estimate=cost(1),
    )(a, b, *deps)


def add_kernel(values, pieces, place, *refs):
    total = refs[0][...].astype(f32)
    for ref in refs[1:values]:
        total = total + ref[...].astype(f32)
    outs = refs[len(refs) - pieces :]
    if pieces == 1:
        outs[0][...] = total.astype(bf)
        return
    total = total.astype(bf)
    rows = outs[0].shape[0]
    for z in range(pieces):
        for k in range(pieces):

            @pl.when((place[3] ^ k) == z)
            def _():
                outs[k][...] = total[z * rows : (z + 1) * rows]


def add(place, values, pieces, *deps):
    rows, lanes = values[0].shape
    return pl.pallas_call(
        functools.partial(add_kernel, len(values), pieces),
        in_specs=[smem()] + [vmem()] * len(values) + [anywhere()] * len(deps),
        out_specs=[vmem()] * pieces,
        out_shape=[jax.ShapeDtypeStruct((rows // pieces, lanes), bf)] * pieces,
        compiler_params=params(),
        cost_estimate=cost(1),
    )(place, *values, *deps)


def stack_kernel(count, *refs):
    for k in range(count):
        refs[-1][k] = refs[k][...]


def stack(values, *deps):
    return pl.pallas_call(
        functools.partial(stack_kernel, len(values)),
        in_specs=[vmem()] * len(values) + [anywhere()] * len(deps),
        out_specs=vmem(),
        out_shape=jax.ShapeDtypeStruct((len(values),) + values[0].shape, bf),
        compiler_params=params(),
        cost_estimate=cost(1),
    )(*values, *deps)


def gate_kernel(value, *refs):
    pass


def gate(value, *deps):
    return pl.pallas_call(
        gate_kernel,
        in_specs=[anywhere()] * (1 + len(deps)),
        out_specs=anywhere(),
        out_shape=jax.ShapeDtypeStruct(value.shape, value.dtype),
        input_output_aliases={0: 0},
        cost_estimate=cost(1),
    )(value, *deps)


def spread_kernel(place, near, far, *refs):
    in_ref, down_ref, out_ref = refs[-3:]
    expert = pl.program_id(0)
    line = place[3]
    lines = near.shape[1]
    width = in_ref.shape[1]
    cut_in = width // lines
    cut_down = down_ref.shape[1] // lines
    bits = lines.bit_length() - 1

    def put(ref):
        for k in range(lines):
            flipped = sum(((k >> t) & 1) << (bits - 1 - t) for t in range(bits))
            z = line ^ jnp.where(expert == 0, flipped, k)
            in_ref[0, pl.ds(pl.multiple_of(z * cut_in, cut_in), cut_in), :] = ref[0, k, :cut_in].astype(f32)
            down_ref[0, pl.ds(pl.multiple_of(z * cut_down, cut_down), cut_down), :] = ref[0, k, cut_in : cut_in + cut_down].astype(f32)
            out_ref[0, z] = ref[0, k, cut_in + cut_down :].astype(f32)

    @pl.when(expert == place[0])
    def _():
        put(near)

    @pl.when(expert != place[0])
    def _():
        put(far)


def spread_experts(outer, place, near, far, hidden, width, earlier, *deps):
    block = near.shape[1:]
    lines = block[0]

    def spec(is_near):
        def index(e, i, p):
            return (jnp.where((e == p[0]) == is_near, i, 0), 0, 0, 0)

        return pl.BlockSpec((1,) + block, index)

    def quarter(e, i, p):
        move_x, move_y = jnp.where(e == 0, i, outer), jnp.where(e == 0, outer, i)
        return 2 * (p[1] ^ move_x) + (p[2] ^ move_y)

    return pl.pallas_call(
        spread_kernel,
        grid_spec=pltpu.PrefetchScalarGridSpec(
            num_scalar_prefetch=1,
            grid=(2, 2),
            in_specs=[spec(True), spec(False)] + [anywhere()] * (len(earlier) + len(deps)),
            out_specs=[
                pl.BlockSpec((1, width, hidden // 4), lambda e, i, p: (e, 0, quarter(e, i, p))),
                pl.BlockSpec((1, hidden // 4, width), lambda e, i, p: (e, quarter(e, i, p), 0)),
                pl.BlockSpec((1, lines, width // 8 // lines, width), lambda e, i, p: (e * 4 + quarter(e, i, p), 0, 0, 0)),
            ],
        ),
        out_shape=[
            kept_out((2, width, hidden), f32),
            kept_out((2, hidden, width), f32),
            kept_out((8, lines, width // 8 // lines, width), f32),
        ],
        input_output_aliases={3: 0, 4: 1, 5: 2} if earlier else {},
        compiler_params=params(28),
        cost_estimate=cost(6),
    )(place, near, far, *earlier, *deps)


def own_block(b, p):
    return jnp.where(b // 2 == p[0], b % 2, jnp.where(b // 2 > p[0], 1, 0))


def other_block(b, p):
    return jnp.where(b // 2 != p[0], b % 2, jnp.where(b // 2 > 1 - p[0], 1, 0))


def collect_kernel(
    place, normed, kv_a, kv_b, kv_c, kv_d, q_a, q_b, q_c, q_d, keep_a, keep_b, got_a, got_b, packs, gain, tiny, dep,
    mine, other, slab_0, slab_1, slab_2, slab_3, sum_ref,
):
    block = pl.program_id(0)
    core, chip, side = place[0], place[1], place[2]
    upper = chip == 1
    dq = jnp.concatenate([q_a[...], q_b[...], q_c[...], q_d[...]], 0).T.astype(f32)
    far = jnp.concatenate([left(keep_a[...], keep_b[...]), left(got_a[...], got_b[...])], 1).astype(f32)
    pieces = [(dq + jnp.where(upper, far, 0.0)).astype(bf)]
    for near, extra in ((kv_a, got_a), (kv_b, got_b), (kv_c, keep_a), (kv_d, keep_b)):
        value = near[...] + jnp.where(upper, 0.0, extra[...].astype(f32))
        pieces.append(jnp.where(lanes_of(value.shape) < 64, value * 0.125, value).astype(bf))
    back = jnp.concatenate(pieces, 1)

    @pl.when(block // 2 == core)
    def _():
        mine[...] = back

    @pl.when(block // 2 != core)
    def _():
        other[...] = back

    part = tn(normed[...], back)

    @pl.when(block == 0)
    def _():
        sum_ref[...] = part

    @pl.when(block > 0)
    def _():
        sum_ref[...] += part

    @pl.when(block == 3)
    def _():
        total = sum_ref[...]
        width, wide = total.shape
        product = jnp.sum(total * packs[core].astype(f32), axis=1, keepdims=True)
        small = tiny[...].T
        small = jnp.concatenate([small, jnp.zeros((width, 120), f32)], 1)
        lanes = lanes_of(small.shape)
        small = jnp.where(lanes == 3, product / gain[...].T, small)
        high = small.astype(bf)
        low = (small - high.astype(f32)).astype(bf)
        small = jnp.where(lanes < 8, high.astype(f32), pltpu.roll(low.astype(f32), 8, axis=1)).astype(bf)
        low = total.astype(bf)
        rows = width // 4
        for (move_x, move_y), ref in zip(MOVES, (slab_0, slab_1, slab_2, slab_3)):
            for q in range(4):

                @pl.when(2 * (chip ^ move_x) + (side ^ move_y) == q)
                def _():
                    ref[:, :wide] = low[q * rows : (q + 1) * rows]
                    ref[:, wide:] = small[q * rows : (q + 1) * rows]


def collect(place, normed, kvs, qs, keep_a, keep_b, got_a, got_b, packs, gain, tiny, dep):
    n, width = normed.shape
    rows = n // 4
    dq = pl.BlockSpec((64, rows), lambda b, p: (0, b))
    flat = pl.BlockSpec((rows, 128), lambda b, p: (b, 0))
    slab = (width // 4, 896)
    return pl.pallas_call(
        collect_kernel,
        grid_spec=pltpu.PrefetchScalarGridSpec(
            num_scalar_prefetch=1,
            grid=(4,),
            in_specs=[pl.BlockSpec((rows, width), lambda b, p: (b, 0))]
            + [flat] * 4
            + [dq] * 4
            + [flat] * 4
            + [
                pl.BlockSpec(packs.shape, lambda b, p: (0, 0, 0)),
                pl.BlockSpec((1, width), lambda b, p: (0, 0)),
                pl.BlockSpec(tiny.shape, lambda b, p: (0, 0)),
                anywhere(),
            ],
            out_specs=[
                pl.BlockSpec((rows, 768), lambda b, p: (own_block(b, p), 0)),
                pl.BlockSpec((rows, 768), lambda b, p: (other_block(b, p), 0)),
            ]
            + [pl.BlockSpec(slab, lambda b, p: (0, 0))] * 4,
            scratch_shapes=[pltpu.VMEM((width, 768), f32)],
        ),
        out_shape=[
            jax.ShapeDtypeStruct((n // 2, 768), bf),
            jax.ShapeDtypeStruct((n // 2, 768), bf),
        ]
        + [jax.ShapeDtypeStruct(slab, bf)] * 4,
        compiler_params=params(26),
        cost_estimate=cost(5),
    )(place, stay(normed), *kvs, *qs, keep_a, keep_b, got_a, got_b, stay(packs), gain, tiny, dep)


def tokens_kernel(place, mine, got, packs, x_ref, back_resid, gain, dep, out):
    core = place[0]
    back = nt(mine[...], packs[core]) + nt(got[...], packs[1 - core])
    x = x_ref[...].astype(f32)
    inverse = lax.rsqrt(jnp.mean(x * x, axis=1, keepdims=True) + EPSILON)
    k = back * gain[...]
    mean = jnp.mean(k * x, axis=1, keepdims=True)
    out[...] = (back_resid[...] + inverse * k - x * (inverse * inverse * inverse * mean)).astype(bf)


def tokens_back(place, mine, got, packs, x, back_resid, gain, dep):
    n, width = x.shape
    rows = n // 4
    wide = pl.BlockSpec((rows, 768), lambda b, p: (b, 0))
    block = pl.BlockSpec((rows, width), lambda b, p: (b, 0))
    return pl.pallas_call(
        tokens_kernel,
        grid_spec=pltpu.PrefetchScalarGridSpec(
            num_scalar_prefetch=1,
            grid=(4,),
            in_specs=[wide, wide, pl.BlockSpec(packs.shape, lambda b, p: (0, 0, 0)), block, block, pl.BlockSpec((1, width), lambda b, p: (0, 0)), anywhere()],
            out_specs=block,
        ),
        out_shape=jax.ShapeDtypeStruct((n, width), bf),
        compiler_params=params(20),
        cost_estimate=cost(4),
    )(place, mine, got, stay(packs), stay(x), stay(back_resid), gain, dep)


def unfold_kernel(place, *refs):
    out, rows_out = refs[-2:]
    core, line = place[0], place[3]
    lines, rows = refs[0].shape[1], refs[0].shape[2]
    block = pl.program_id(0)

    def put(source, c, fresh):
        for k in range(lines):
            at = pl.ds(pl.multiple_of((line ^ k) * rows, rows), rows)
            value = source[k]
            base = c * 256
            out[at, pl.ds(pl.multiple_of(base, 128), 256)] = value[:, 0:256].astype(f32)
            for pair in range(2):
                a = value[:, 256 + 256 * pair : 384 + 256 * pair]
                b = value[:, 384 + 256 * pair : 512 + 256 * pair]
                out[at, pl.ds(pl.multiple_of(512 + base + 128 * pair, 128), 128)] = left(a, b).astype(f32)
                out[at, pl.ds(pl.multiple_of(1024 + base + 128 * pair, 128), 128)] = right(a, b).astype(f32)
            small = value[:, 768:].astype(f32)
            small = small + pltpu.roll(small, 120, axis=1)
            rows_out[at, :] = small if fresh else rows_out[at, :] + small

    for i in range(4):

        @pl.when(block == i)
        def _():
            put(refs[0].at[i], core, True)
            put(refs[1].at[i], 1 - core, False)


def unfold(place, near, far, width):
    whole = pl.BlockSpec(near.shape, lambda i, p: (0, 0, 0, 0))

    def at(i, p):
        return ((2 * p[1] + p[2]) ^ ((i % 2) * 2 + i // 2), 0)

    return pl.pallas_call(
        unfold_kernel,
        grid_spec=pltpu.PrefetchScalarGridSpec(
            num_scalar_prefetch=1,
            grid=(4,),
            in_specs=[whole] * 2,
            out_specs=[pl.BlockSpec((width // 4, 3 * width), at), pl.BlockSpec((width // 4, 128), at)],
        ),
        out_shape=[kept_out((width, 3 * width), f32), jax.ShapeDtypeStruct((width, 128), f32)],
        compiler_params=params(16),
        cost_estimate=cost(3),
    )(place, near, far)


def body(
    layer_activations,
    sequence_extents,
    position_cluster_label,
    cluster_sharpness,
    heed_scale_factor,
    triple_entry_matrix,
    heed_exit_matrix,
    blend_scale_factor,
    router_matrix,
    specialist_entry_matrix,
    specialist_exit_matrix,
    upstream_derivative,
):
    seq_count, pos_count, width = layer_activations.shape
    tokens = seq_count * pos_count
    hidden = specialist_entry_matrix.shape[2]
    spot = lax.axis_index("seq")
    row = lax.axis_index("batch")
    core, chip, side, line = spot % 2, spot // 2, row % 2, row // 2
    lines = lax.axis_size("batch") // 2
    place = jnp.stack([core, chip, side, line, row * 4 + spot]).astype(jnp.int32)
    core_pairs, chip_pairs = [(0, 1), (1, 0), (2, 3), (3, 2)], [(0, 2), (1, 3), (2, 0), (3, 1)]
    up, down = chip_pairs[:2], chip_pairs[2:]

    x = layer_activations.reshape(tokens, width)
    x_other = lax.ppermute(x, "seq", core_pairs)
    packs, w_own, router, gains = pack(
        place, triple_entry_matrix, router_matrix, heed_scale_factor.reshape(1, width), blend_scale_factor.reshape(1, width)
    )
    gain_a, gain_m = gains[0], gains[1]
    normed, qkv, send_a, send_b = project(place, x, x_other, gain_a, w_own)
    got_a = lax.ppermute(send_a, "seq", chip_pairs)
    got_b = lax.ppermute(send_b, "seq", up)
    limit = (sequence_extents - chip * 2 * pos_count).astype(jnp.int32)
    p_na, o_na, st_na = near_forward(0, limit, qkv, qkv)
    p_a, o_a, st_a, q_a, kv_a = far_forward(0, place, qkv, got_a, got_a, o_na)
    got_oa = lax.ppermute(o_a, "seq", up)
    p_b, o_b, st_b, q_b, kv_b = far_forward(1, place, qkv, got_a, got_b, o_a)
    got_ob = lax.ppermute(o_b, "seq", up)
    p_nb, o_nb, st_nb = near_forward(1, limit, qkv, o_b)
    att_mine, att_send, log = join(place, o_na, o_nb, st_na, st_nb, o_a, o_b, got_oa, got_ob)
    att_got = lax.ppermute(att_send, "seq", core_pairs)

    block_out, fac, gout, tiny, back_resid, ba_own, ba_send = mixture(
        place,
        cluster_sharpness,
        x,
        att_mine,
        att_got,
        heed_exit_matrix,
        gain_m,
        router,
        position_cluster_label.reshape(1, tokens),
        upstream_derivative.reshape(tokens, width),
        specialist_entry_matrix,
        specialist_exit_matrix,
    )

    ba_got = lax.ppermute(ba_send, "seq", core_pairs)
    fac_got = swap(take(fac, 1 - core), 1)
    gout_got = swap(take(gout, 1 - core), 1)
    grads, inner, payload = ready(place, ba_own, ba_got, att_mine, att_send, log)
    got_grad = lax.ppermute(payload, "seq", down)
    pay = factors(place, fac, fac_got, gout, gout_got, payload)
    pays = [pay[0]] + [swap(pay[i], 2 * m[0] + 4 * m[1]) for i, m in list(enumerate(MOVES))[1:]]
    def near(h, dep):
        p, stat = ((p_na, st_na), (p_nb, st_nb))[h // 2]
        return near_backward(h, qkv, p, grads, stat, log, inner, dep)

    kv_0, dq_0 = near(0, (pay[0],))
    kv_1, dq_1 = near(1, (stay(dq_0),))
    stages = turns()
    kept, sent = slabs(place, dq_1, pays, width, hidden // 4, lines)
    send_fa, keep_fa = far_backward(0, place, q_a, kv_a, p_a, st_a, grads, log, inner, got_grad, kept)
    got_fa = lax.ppermute(send_fa, "seq", chip_pairs)
    for t, turn in enumerate(stages):
        got = swap_by_core(sent, turn)
        if t == len(stages) - 1:
            send_fb, keep_fb = far_backward(1, place, q_b, kv_b, p_b, st_b, grads, log, inner, got_grad, kept)
            got_fb = lax.ppermute(send_fb, "seq", chip_pairs)
            whole = fold(None, place, keep_fb, kept, got)[0]
        else:
            kept, sent = fold(stages[t + 1], place, keep_fa, kept, got)
    kv_2, dq_2 = near(2, (whole,))
    for turn in stages[:0:-1]:
        whole = pile(whole, swap_by_core(whole, turn), stay(dq_2))
    got = swap_by_core(whole, stages[0])
    kv_3, dq_3 = near(3, (whole, got_fa))
    whole = pile(whole, got, stay(dq_3), got_fb)
    got_first = swap_by_core(whole, PLANE[0])
    d_mine, d_send, *parts = collect(
        place, normed, (kv_0, kv_1, kv_2, kv_3), (dq_0, dq_1, dq_2, dq_3), keep_fa, keep_fb, got_fa, got_fb, packs, gain_a, tiny, whole
    )

    moves = [2 * m[0] + 4 * m[1] for m in MOVES]
    parts = parts[:1] + [swap(part, bits) for part, bits in list(zip(parts, moves))[1:]]
    d_got = lax.ppermute(d_send, "seq", core_pairs)
    parts = list(add(place, parts, lines))
    whole = pile(whole, got_first, parts[0])
    got_second = swap_by_core(whole, PLANE[1])
    far_first = swap(whole, 1)
    tokens_grad = tokens_back(place, d_mine, d_got, packs, x, back_resid, gain_a, whole)
    parts = parts[:1] + [swap(part, 8 * k) for k, part in list(enumerate(parts))[1:]]
    part = add(place, parts, 1, tokens_grad)[0]
    block = (2, lines) + whole.shape[1:]
    halves = spread_experts(0, place, whole.reshape(block), far_first.reshape(block), hidden, width, (), part)
    zs = stack([part] + [swap(part, 8 * k) for k in range(1, lines)], stay(halves[2]))
    pieces = [zs] + [swap(zs, bits) for bits in moves[1:]]
    got_second = gate(got_second, zs)
    far_second = swap(got_second, 1)
    grad_in, grad_down, grad_out = spread_experts(
        1, place, got_second.reshape(block), far_second.reshape(block), hidden, width, tuple(halves)
    )
    pieces = stack(pieces, stay(grad_out))
    grad_qkv, small = unfold(place, pieces, swap(pieces, 1), width)
    return (
        block_out.reshape(layer_activations.shape),
        tokens_grad.reshape(layer_activations.shape),
        small[:, 3],
        grad_qkv,
        grad_out.reshape(width, width),
        small[:, 2],
        small[:, 0:2],
        grad_in,
        grad_down,
    )


def solution(mesh):
    rows = P("batch", "seq", None)
    placed = (rows, P("batch"), P("batch", "seq")) + (P(),) * 8 + (rows,)
    return jax.shard_map(body, mesh=mesh, in_specs=placed, out_specs=(rows, rows) + (P(),) * 7, check_vma=False)
```

```python
import functools

import jax
import jax.numpy as jnp
from jax import lax
from jax.experimental import pallas as pl
from jax.experimental.pallas import tpu as pltpu
from jax.sharding import PartitionSpec as P

HEADS = 8
HEAD = 64
GROUP = 32
EPSILON = 1e-06
LOG2E = 1.4426950408889634
SC = 0.125 * LOG2E
MASKED = -1e30
BQ = 512
CH = 512
bf = jnp.bfloat16
f32 = jnp.float32
AXES = ("batch", "seq")
NT = (((1,), (1,)), ((), ()))
TN = (((0,), (0,)), ((), ()))


def nt(a, b):
    return lax.dot_general(a, b, NT, preferred_element_type=f32)


def tn(a, b):
    return lax.dot_general(a, b, TN, preferred_element_type=f32)


def nn(a, b):
    return jnp.dot(a, b, preferred_element_type=f32)


def rows_of(shape):
    return lax.broadcasted_iota(jnp.int32, shape, 0)


def lanes_of(shape):
    return lax.broadcasted_iota(jnp.int32, shape, 1)


def vmem():
    return pl.BlockSpec(memory_space=pltpu.VMEM)


def smem():
    return pl.BlockSpec(memory_space=pltpu.SMEM)


def params(mib=16):
    return pltpu.CompilerParams(vmem_limit_bytes=mib * 2**20)


def anywhere():
    return pl.BlockSpec(memory_space=pl.ANY)


def hbm():
    return pl.BlockSpec(memory_space=pltpu.HBM)


def cost(us):
    return pl.CostEstimate(flops=int(us * 1e8), bytes_accessed=2**10, transcendentals=0)


def stay(value):
    return pltpu.with_memory_space_constraint(value, pltpu.HBM)


def kept_out(shape, dtype):
    return pltpu.HBM(shape, dtype)


def shift_lanes(value):
    return pltpu.roll(value.astype(f32), 64, axis=1).astype(bf)


def left(first, second):
    return jnp.where(lanes_of(first.shape) < 64, first, shift_lanes(second))


def right(first, second):
    return jnp.where(lanes_of(first.shape) < 64, shift_lanes(first), second)


def pack_kernel(place, w, router, gain_a, gain_m, packs, w_own, router_rows, gains):
    core = place[0]
    both = router[...].astype(f32)
    rows = rows_of(router_rows.shape)
    router_rows[...] = jnp.where(rows == 0, both[0:1, :], jnp.where(rows == 1, both[1:2, :], 0.0)).astype(bf)
    gains[0] = gain_a[...].astype(f32)
    gains[1] = gain_m[...].astype(f32)
    for c in range(2):
        packs[c, :, 0:256] = w[:, 256 * c : 256 * c + 256]
        for h in range(4):
            at = 256 * c + 128 * (h // 2)
            k = w[:, 512 + at : 640 + at]
            v = w[:, 1024 + at : 1152 + at]
            packs[c, :, 256 + 128 * h : 384 + 128 * h] = left(k, v) if h % 2 == 0 else right(k, v)
    for h in range(4):
        q = packs[core, :, 128 * (h // 2) : 128 * (h // 2) + 128]
        q = q if h % 2 == 0 else shift_lanes(q)
        w_own[:, 256 * h : 256 * h + 128] = jnp.where(lanes_of(q.shape) < 64, q, jnp.zeros((), bf))
        w_own[:, 256 * h + 128 : 256 * h + 256] = packs[core, :, 256 + 128 * h : 384 + 128 * h]


def pack(place, w, router, gain_a, gain_m):
    width = w.shape[0]
    return pl.pallas_call(
        pack_kernel,
        in_specs=[smem()] + [vmem()] * 4,
        out_specs=[vmem()] * 4,
        out_shape=[
            kept_out((2, width, 768), bf),
            jax.ShapeDtypeStruct((width, 1024), bf),
            jax.ShapeDtypeStruct((16, width), bf),
            jax.ShapeDtypeStruct((2, 1, width), f32),
        ],
        compiler_params=params(16),
        cost_estimate=cost(3),
    )(place, w, router, gain_a, gain_m)


def project_kernel(place, x_own, x_other, gain, w_own, normed, qkv, send_a, send_b):
    core, chip = place[0], place[1]
    block = pl.program_id(0)

    def go(x_ref):
        x = x_ref[...].astype(f32)
        inverse = lax.rsqrt(jnp.mean(x * x, axis=1, keepdims=True) + EPSILON)
        low = (x * inverse * gain[...]).astype(bf)
        normed[...] = low
        out = nn(low, w_own[...]).astype(bf)
        qkv[...] = out
        send_b[...] = out[:, 384:512]

        @pl.when(chip == 0)
        def _():
            send_a[...] = out[:, 128:256]

        @pl.when(chip == 1)
        def _():
            send_a[...] = left(out[:, 512:640], out[:, 768:896])

    @pl.when(block // 2 == core)
    def _():
        go(x_own)

    @pl.when(block // 2 != core)
    def _():
        go(x_other)


def project(place, x_own, x_other, gain, w_own):
    rows, width = x_own.shape

    def own(b, p):
        return (jnp.where(b // 2 == p[0], b % 2, jnp.where(b // 2 > p[0], 1, 0)), 0)

    def other(b, p):
        return (jnp.where(b // 2 != p[0], b % 2, jnp.where(b // 2 > 1 - p[0], 1, 0)), 0)

    half = rows // 2
    return pl.pallas_call(
        project_kernel,
        grid_spec=pltpu.PrefetchScalarGridSpec(
            num_scalar_prefetch=1,
            grid=(4,),
            in_specs=[
                pl.BlockSpec((half, width), own),
                pl.BlockSpec((half, width), other),
                pl.BlockSpec((1, width), lambda b, p: (0, 0)),
                pl.BlockSpec((width, 1024), lambda b, p: (0, 0)),
            ],
            out_specs=[
                pl.BlockSpec((half, width), lambda b, p: (b, 0)),
                pl.BlockSpec((half, 1024), lambda b, p: (b, 0)),
                pl.BlockSpec((half, 128), lambda b, p: (b, 0)),
                pl.BlockSpec((half, 128), lambda b, p: (b, 0)),
            ],
        ),
        out_shape=[
            kept_out((2 * rows, width), bf),
            kept_out((2 * rows, 1024), bf),
            jax.ShapeDtypeStruct((2 * rows, 128), bf),
            jax.ShapeDtypeStruct((2 * rows, 128), bf),
        ],
        compiler_params=params(20),
        cost_estimate=cost(4),
    )(place, x_own, x_other, gain, w_own)


def scores(kv, q, s_ref, slot, kmax, q0, limit, causal):
    peak = None
    for k0 in range(0, kmax, CH):
        s = nt(kv[k0 : k0 + CH, :], q)
        if causal:
            if k0 >= 1024:
                s = jnp.where(rows_of(s.shape) + k0 < limit, s, MASKED)
            if k0 + CH > q0:
                s = jnp.where(rows_of(s.shape) + (k0 - q0) <= lanes_of(s.shape), s, MASKED)
        s_ref[slot, k0 : k0 + CH, :] = s
        m = jnp.max(s, axis=0, keepdims=True)
        peak = m if peak is None else jnp.maximum(peak, m)
    return peak


def weigh(vt, s_ref, slot, peak, kmax, put):
    scaled = peak * SC
    acc = None
    for k0 in range(0, kmax, CH):
        p = jnp.exp2(s_ref[slot, k0 : k0 + CH, :] * SC - scaled).astype(bf)
        put(k0 // CH, p)
        d = nn(vt[:, k0 : k0 + CH], p)
        acc = d if acc is None else acc + d
    total = acc[0:1, :]
    return acc[64:128, :] * (1.0 / total), scaled, total


def ones_and_values(kv):
    vt = kv.T
    return jnp.where(rows_of(vt.shape) < 64, jnp.ones((), bf), vt)


def near_forward_kernel(limit_ref, qkv, dep, p_ref, o_ref, st_ref, s_ref, vt_ref, buf, sems):
    limit = limit_ref[0]
    count = qkv.shape[0] // BQ
    tasks = [(h, i) for h in range(2) for i in range(count)]

    def start_scores(at):
        h, i = tasks[at]
        kv = qkv.at[:, 256 * h + 128 : 256 * h + 256]
        q = qkv[i * BQ : (i + 1) * BQ, 256 * h : 256 * h + 128]
        return scores(kv, q, s_ref, at % 2, (i + 1) * BQ, i * BQ, limit, True)

    copies = []
    peak = start_scores(0)
    for at, (h, i) in enumerate(tasks):
        if i == 0:
            vt_ref[h] = ones_and_values(qkv[:, 256 * h + 128 : 256 * h + 256])
        later = start_scores(at + 1) if at + 1 < len(tasks) else None
        base = i * (i + 1) // 2

        def put(k, p):
            buf[h, base + k] = p

        out, scaled, total = weigh(vt_ref.at[h], s_ref, at % 2, peak, (i + 1) * BQ, put)
        copies.append(pltpu.make_async_copy(buf.at[h, base : base + i + 1], p_ref.at[h, base : base + i + 1], sems.at[h, i]))
        copies[-1].start()
        o_ref[h, :, i * BQ : (i + 1) * BQ] = out.astype(bf)
        st_ref[h, 0:1, i * BQ : (i + 1) * BQ] = scaled
        st_ref[h, 1:2, i * BQ : (i + 1) * BQ] = total
        peak = later
    for copy in copies:
        copy.wait()


def near_forward(pair, limit, qkv, dep):
    n = qkv.shape[0]
    count = n // BQ
    shape = (2, count * (count + 1) // 2, CH, BQ)
    return pl.pallas_call(
        near_forward_kernel,
        grid=(1,),
        in_specs=[smem(), pl.BlockSpec((n, 512), lambda g: (0, pair)), anywhere()],
        out_specs=[
            anywhere(),
            pl.BlockSpec((2, 64, n), lambda g: (0, 0, 0)),
            pl.BlockSpec((2, 8, n), lambda g: (0, 0, 0)),
        ],
        out_shape=[
            kept_out(shape, bf),
            jax.ShapeDtypeStruct((2, 64, n), bf),
            jax.ShapeDtypeStruct((2, 8, n), f32),
        ],
        scratch_shapes=[
            pltpu.VMEM((2, n, BQ), f32),
            pltpu.VMEM((2, 128, n), bf),
            pltpu.VMEM(shape, bf),
            pltpu.SemaphoreType.DMA((2, count)),
        ],
        compiler_params=params(34),
        cost_estimate=cost(9),
    )(limit, stay(qkv) if pair == 0 else qkv, dep)


def three(value):
    high = value.astype(bf)
    rest = value - high.astype(f32)
    mid = rest.astype(bf)
    return high, mid, (rest - mid.astype(f32)).astype(bf)


def far_forward_kernel(j, place, q_own, q_got, kv_own, kv_got, dep, p_ref, o_ref, st_ref, q_ref, kv_ref, s_ref, vt_ref, buf, sems):
    n = q_own.shape[0]

    @pl.when(place[1] == 1)
    def _():
        q_ref[...] = q_own[...]
        kv_ref[...] = kv_got[...]

    @pl.when(place[1] == 0)
    def _():
        q = q_got[...] if j == 0 else shift_lanes(q_got[...])
        q_ref[...] = jnp.where(lanes_of(q.shape) < 64, q, jnp.zeros((), bf))
        kv_ref[...] = kv_own[...]

    vt_ref[...] = ones_and_values(kv_ref[...])
    count = n // BQ
    copies = []
    peak = scores(kv_ref, q_ref[0:BQ, :], s_ref, 0, n, 0, None, False)
    for i in range(count):
        later = None
        at = slice(i * BQ, (i + 1) * BQ)
        if i + 1 < count:
            later = scores(kv_ref, q_ref[(i + 1) * BQ : (i + 2) * BQ, :], s_ref, (i + 1) % 2, n, 0, None, False)

        def put(k, p):
            buf[i, k] = p

        out, scaled, total = weigh(vt_ref, s_ref, i % 2, peak, n, put)
        copies.append(pltpu.make_async_copy(buf.at[i], p_ref.at[i], sems.at[i]))
        copies[-1].start()
        o_ref[0:64, at] = out.astype(bf)
        high, mid, low = three(scaled + jnp.log(total) * LOG2E)
        tail = jnp.concatenate([high.astype(f32), mid.astype(f32), low.astype(f32), jnp.zeros((13, BQ), f32)], 0)
        o_ref[64:80, at] = tail.astype(bf)
        st_ref[0:1, at] = scaled
        peak = later
    for copy in copies:
        copy.wait()


def far_forward(j, place, qkv, q_got, kv_got, dep):
    n = qkv.shape[0]
    whole = pl.BlockSpec((n, 128), lambda h: (0, 0))
    shape = (n // BQ, n // CH, CH, BQ)
    return pl.pallas_call(
        lambda *refs: far_forward_kernel(j, *refs),
        grid=(1,),
        in_specs=[
            smem(),
            pl.BlockSpec((n, 128), lambda h: (0, 2 * j)),
            whole,
            pl.BlockSpec((n, 128), lambda h: (0, 2 * j + 5)),
            whole,
            anywhere(),
        ],
        out_specs=[
            anywhere(),
            pl.BlockSpec((80, n), lambda h: (0, 0)),
            pl.BlockSpec((8, n), lambda h: (0, 0)),
            whole,
            whole,
        ],
        out_shape=[
            kept_out(shape, bf),
            jax.ShapeDtypeStruct((80, n), bf),
            jax.ShapeDtypeStruct((8, n), f32),
            kept_out((n, 128), bf),
            kept_out((n, 128), bf),
        ],
        scratch_shapes=[
            pltpu.VMEM((2, n, BQ), f32),
            pltpu.VMEM((128, n), bf),
            pltpu.VMEM(shape, bf),
            pltpu.SemaphoreType.DMA((n // BQ,)),
        ],
        compiler_params=params(34),
        cost_estimate=cost(10),
    )(place, qkv, q_got, qkv, kv_got, dep)


def unsplit(ref, at):
    return ref[at : at + 1, :].astype(f32) + ref[at + 1 : at + 2, :].astype(f32) + ref[at + 2 : at + 3, :].astype(f32)


def join_kernel(place, near_a, near_b, stat_a, stat_b, far_a, far_b, got_a, got_b, mine, other, log_ref):
    core, chip = place[0], place[1]
    half = mine.shape[1]
    for h in range(4):
        far = (far_a, far_b, got_a, got_b)[h]
        near, stat = (near_a, near_b)[h // 2], (stat_a, stat_b)[h // 2]
        log_near = stat[h % 2, 0:1, :] + jnp.log(stat[h % 2, 1:2, :]) * LOG2E
        log_far = jnp.where(chip == 1, unsplit(far, 64), MASKED)
        top = jnp.maximum(log_near, log_far)
        e_near, e_far = jnp.exp2(log_near - top), jnp.exp2(log_far - top)
        both = e_near + e_far
        log_ref[h] = jnp.broadcast_to(top + jnp.log(both) * LOG2E, log_ref.shape[1:])
        far_out = jnp.where(chip == 1, far[0:64, :].astype(f32), 0.0)
        joined = ((near[h % 2].astype(f32) * e_near + far_out * e_far) * (1.0 / both)).astype(bf)
        at = slice(64 * h, 64 * h + 64)

        @pl.when(core == 0)
        def _():
            mine[at, :] = joined[:, :half]
            other[at, :] = joined[:, half:]

        @pl.when(core == 1)
        def _():
            mine[at, :] = joined[:, half:]
            other[at, :] = joined[:, :half]


def join(place, near_a, near_b, stat_a, stat_b, far_a, far_b, got_a, got_b):
    n = near_a.shape[2]
    return pl.pallas_call(
        join_kernel,
        in_specs=[smem()] + [vmem()] * 8,
        out_specs=[vmem()] * 3,
        out_shape=[
            jax.ShapeDtypeStruct((256, n // 2), bf),
            jax.ShapeDtypeStruct((256, n // 2), bf),
            jax.ShapeDtypeStruct((4, 8, n), f32),
        ],
        compiler_params=params(),
        cost_estimate=cost(2),
    )(place, near_a, near_b, stat_a, stat_b, far_a, far_b, got_a, got_b)


def mixture_kernel(
    place, sharp, x, att_own, att_got, wout, gain, router, labels, gy, w1_hbm, w2_hbm,
    block_out, fac, gout, tiny, back_resid, ba_own, ba_other, w1, w2, sems,
):
    core = place[0]
    copy1 = pltpu.make_async_copy(w1_hbm, w1, sems.at[0])
    copy2 = pltpu.make_async_copy(w2_hbm, w2, sems.at[1])
    copy1.start()
    copy2.start()
    own_rows = pl.ds(pl.multiple_of(core * 256, 256), 256)
    other_rows = pl.ds(pl.multiple_of(256 - core * 256, 256), 256)
    wo_own, wo_other = wout[own_rows, :], wout[other_rows, :]
    resid = x[...].astype(f32) + tn(att_own[...], wo_own) + tn(att_got[...], wo_other)
    inverse = lax.rsqrt(jnp.mean(resid * resid, axis=1, keepdims=True) + EPSILON)
    unit = resid * inverse
    mix = (unit * gain[...]).astype(bf)
    temper = 1.0 / sharp[0]
    logits = nt(router[...], mix) * temper
    tokens = mix.shape[0]
    groups = tokens // GROUP
    member = labels[...] == rows_of((groups, tokens))
    weights, mixing = [], []
    for e in range(2):
        row = logits[e : e + 1, :]
        peak = jnp.max(jnp.where(member, row, -jnp.inf), axis=1, keepdims=True)
        token_peak = jnp.sum(jnp.where(member, peak, 0.0), axis=0, keepdims=True)
        raised = jnp.exp(row - token_peak)
        total = jnp.sum(jnp.where(member, raised, 0.0), axis=1, keepdims=True)
        token_total = jnp.sum(jnp.where(member, total, 0.0), axis=0, keepdims=True)
        w = raised / token_total
        weights.append(w)
        mixing.append(jnp.where(member, w, 0.0))
    mixing = jnp.concatenate(mixing, 0).astype(bf)
    mixed = nn(mixing, mix).astype(bf)
    back_expert = nn(mixing, gy[...]).astype(bf)
    copy1.wait()
    copy2.wait()
    expert_out, back_mixed = [], []
    quarter = w1.shape[2] // 4
    width = mix.shape[1]
    for e in range(2):
        at = slice(groups * e, groups * (e + 1))
        inner = nn(mixed[at], w1[e])
        cdf = 0.5 * (1.0 + lax.erf(inner * 0.7071067811865476))
        active = (inner * cdf).astype(bf)
        slope = cdf + inner * (jnp.exp(-0.5 * inner * inner) * 0.3989422804014327)
        expert_out.append(nn(active, w2[e]))
        back_inner = (slope * nt(back_expert[at], w2[e])).astype(bf)
        back_mixed.append(nt(back_inner, w1[e]))
        fac[e, :, 0:width] = mixed[at]
        fac[e, :, width : 2 * width] = back_expert[at]
        for q in range(4):
            base = 2 * width + 2 * quarter * q
            fac[e, :, base : base + quarter] = back_inner[:, quarter * q : quarter * (q + 1)]
            fac[e, :, base + quarter : base + 2 * quarter] = active[:, quarter * q : quarter * (q + 1)]
    expert_out = jnp.concatenate(expert_out, 0).astype(bf)
    back_mixed = jnp.concatenate(back_mixed, 0).astype(bf)
    block_out[...] = (resid + tn(mixing, expert_out)).astype(bf)
    spread = nt(expert_out, gy[...]) + nt(back_mixed, mix)
    rows16 = rows_of((16, tokens))
    back_logits = jnp.zeros((16, tokens), f32)
    for e in range(2):
        back_weight = jnp.sum(jnp.where(member, spread[groups * e : groups * (e + 1)], 0.0), axis=0, keepdims=True)
        w = weights[e]
        inner = jnp.sum(jnp.where(member, w * back_weight, 0.0), axis=1, keepdims=True)
        token_inner = jnp.sum(jnp.where(member, inner, 0.0), axis=0, keepdims=True)
        back_logits = jnp.where(rows16 == e, w * (back_weight - token_inner) * temper, back_logits)
    back_logits = back_logits.astype(bf)
    ctrl = nn(back_logits, mix)
    back_mix = tn(mixing, back_mixed) + tn(back_logits, router[...])
    tiny[...] = jnp.zeros_like(tiny)
    tiny[0:2, :] = ctrl[0:2, :]
    tiny[2:3, :] = jnp.sum(back_mix * unit, axis=0, keepdims=True)
    n = back_mix * gain[...]
    mean = jnp.mean(n * resid, axis=1, keepdims=True)
    back = gy[...].astype(f32) + inverse * n - resid * (inverse * inverse * inverse * mean)
    back_resid[...] = back
    branch = back.astype(bf)
    gout[core] = nn(att_own[...], branch).astype(bf)
    gout[1 - core] = nn(att_got[...], branch).astype(bf)
    ba_own[...] = nt(wo_own, branch).astype(bf)
    ba_other[...] = nt(wo_other, branch).astype(bf)


def mixture(place, sharp, x, att_own, att_got, wout, gain, router, labels, gy, w1, w2):
    tokens, width = x.shape
    hidden = w1.shape[2]
    groups = tokens // GROUP
    return pl.pallas_call(
        mixture_kernel,
        in_specs=[smem(), smem()] + [vmem()] * 8 + [pl.BlockSpec(memory_space=pl.ANY)] * 2,
        out_specs=[vmem()] * 7,
        out_shape=[
            kept_out((tokens, width), bf),
            jax.ShapeDtypeStruct((2, groups, 2 * width + 2 * hidden), bf),
            jax.ShapeDtypeStruct((2, width // 2, width), bf),
            jax.ShapeDtypeStruct((8, width), f32),
            kept_out((tokens, width), f32),
            jax.ShapeDtypeStruct((width // 2, tokens), bf),
            jax.ShapeDtypeStruct((width // 2, tokens), bf),
        ],
        scratch_shapes=[pltpu.VMEM(w1.shape, bf), pltpu.VMEM(w2.shape, bf), pltpu.SemaphoreType.DMA((2,))],
        compiler_params=params(48),
        cost_estimate=cost(15),
    )(place, sharp, x, att_own, att_got, stay(wout), gain, router, labels, gy, stay(w1), stay(w2))


def ready_kernel(place, ba_own, ba_got, mine, other, log_ref, grads, inner, payload):
    core = place[0]
    half = mine.shape[1]
    for h in range(4):
        at = slice(64 * h, 64 * h + 64)
        g_own, g_got = ba_own[at, :], ba_got[at, :]
        d_own = jnp.sum(g_own.astype(f32) * mine[at, :].astype(f32), axis=0, keepdims=True)
        d_got = jnp.sum(g_got.astype(f32) * other[at, :].astype(f32), axis=0, keepdims=True)

        def put(g0, g1, d0, d1):
            grads[h, :, :half] = g0
            grads[h, :, half:] = g1
            inner[h, :, :half] = jnp.broadcast_to(d0, (8, half))
            inner[h, :, half:] = jnp.broadcast_to(d1, (8, half))
            if h >= 2:
                for g, d, s in ((g0, d0, slice(0, half)), (g1, d1, slice(half, 2 * half))):
                    payload[h - 2, 0:64, s] = g
                    parts = three(log_ref[h, 0:1, s]) + three(d)
                    tail = jnp.concatenate([part.astype(f32) for part in parts] + [jnp.zeros((10, half), f32)], 0)
                    payload[h - 2, 64:80, s] = tail.astype(bf)

        @pl.when(core == 0)
        def _():
            put(g_own, g_got, d_own, d_got)

        @pl.when(core == 1)
        def _():
            put(g_got, g_own, d_got, d_own)


def ready(place, ba_own, ba_got, mine, other, log):
    half = mine.shape[1]
    return pl.pallas_call(
        ready_kernel,
        in_specs=[smem()] + [vmem()] * 5,
        out_specs=[vmem()] * 3,
        out_shape=[
            jax.ShapeDtypeStruct((4, 64, 2 * half), bf),
            jax.ShapeDtypeStruct((4, 8, 2 * half), f32),
            jax.ShapeDtypeStruct((2, 80, 2 * half), bf),
        ],
        compiler_params=params(),
        cost_estimate=cost(2),
    )(place, ba_own, ba_got, mine, other, log)


def back_block(kv_ref, kt_ref, q, grad, ratio, inner, block, kmax, first, put_kv):
    low = (grad.astype(f32) * ratio).astype(bf)
    rhs = jnp.concatenate([jnp.zeros((64, BQ), bf), low], axis=0)
    shift = inner * ratio
    natural = rhs.T
    acc = None
    for k0 in range(0, kmax, CH):
        dp = nn(kv_ref[k0 : k0 + CH, :], rhs)
        p = block(k0 // CH)
        ds = (p.astype(f32) * (dp - shift)).astype(bf)
        d = nn(kt_ref[:, k0 : k0 + CH], ds)
        acc = d if acc is None else acc + d
        put_kv(k0, k0 >= first, nn(ds, q) + nn(p, natural))
    return (acc * 0.125).astype(bf)


def near_backward_kernel(head, q_ref, kv_ref, p_ref, grad_ref, stat, log_ref, inner_ref, *refs):
    dkv_ref, dq_ref, kt_ref, buf, sems = refs[-5:]
    count = q_ref.shape[0] // BQ
    copies = []
    for i in range(count):
        at = slice(i * (i + 1) // 2, (i + 1) * (i + 2) // 2)
        copies.append(pltpu.make_async_copy(p_ref.at[head, at], buf.at[at], sems.at[i]))
        copies[-1].start()
    kt_ref[...] = kv_ref[...].T[0:64, :]

    def put(k0, fresh, value):
        if fresh:
            dkv_ref[k0 : k0 + CH, :] = value
        else:
            dkv_ref[k0 : k0 + CH, :] += value

    for i in range(count):
        at = slice(i * BQ, (i + 1) * BQ)
        base = i * (i + 1) // 2
        copies[i].wait()
        ratio = jnp.exp2(stat[0, 0:1, at] - log_ref[0, 0:1, at])

        def block(k):
            return buf[base + k]

        dq_ref[:, at] = back_block(
            kv_ref, kt_ref, q_ref[at, :], grad_ref[0, :, at], ratio, inner_ref[0, 0:1, at], block, (i + 1) * BQ, i * BQ, put
        )


def near_backward(h, qkv, p, grads, stat, log, inner, deps):
    n = qkv.shape[0]
    row = pl.BlockSpec((1, 8, n), lambda g: (h, 0, 0))
    return pl.pallas_call(
        functools.partial(near_backward_kernel, h % 2),
        grid=(1,),
        in_specs=[
            pl.BlockSpec((n, 128), lambda g: (0, 2 * h)),
            pl.BlockSpec((n, 128), lambda g: (0, 2 * h + 1)),
            hbm(),
            pl.BlockSpec((1, 64, n), lambda g: (h, 0, 0)),
            pl.BlockSpec((1, 8, n), lambda g: (h % 2, 0, 0)),
            row,
            row,
        ]
        + [anywhere()] * len(deps),
        out_specs=[pl.BlockSpec((n, 128), lambda g: (0, 0)), pl.BlockSpec((64, n), lambda g: (0, 0))],
        out_shape=[kept_out((n, 128), f32), kept_out((64, n), bf)],
        scratch_shapes=[pltpu.VMEM((64, n), bf), pltpu.VMEM(p.shape[1:], bf), pltpu.SemaphoreType.DMA((n // BQ,))],
        compiler_params=params(24),
        cost_estimate=cost(7),
    )(qkv, qkv, stay(p), grads, stat, log, inner, *deps)


def far_backward_kernel(
    place, q_ref, kv_ref, p_ref, stat, grad_own, log_own, inner_own, got, dep, send_ref, keep_ref, kt_ref, sum_ref, dq_ref, buf, sems
):
    kt_ref[...] = kv_ref[...].T[0:64, :]
    upper = place[1] == 1
    n = q_ref.shape[0]
    copies = [pltpu.make_async_copy(p_ref.at[i], buf.at[i], sems.at[i]) for i in range(n // BQ)]
    for copy in copies:
        copy.start()

    def put(k0, fresh, value):
        if fresh:
            sum_ref[k0 : k0 + CH, :] = value
        else:
            sum_ref[k0 : k0 + CH, :] += value

    for i in range(n // BQ):
        at = slice(i * BQ, (i + 1) * BQ)
        got_log = got[0, 64:67, at].astype(f32)
        got_inner = got[0, 67:70, at].astype(f32)
        log = jnp.where(upper, log_own[0, 0:1, at], jnp.sum(got_log, axis=0, keepdims=True))
        inner = jnp.where(upper, inner_own[0, 0:1, at], jnp.sum(got_inner, axis=0, keepdims=True))
        grad = jnp.where(upper, grad_own[0, :, at], got[0, 0:64, at])
        ratio = jnp.exp2(stat[0:1, at] - log)
        copies[i].wait()

        def block(k):
            return buf[i, k]

        dq = back_block(kv_ref, kt_ref, q_ref[at, :], grad, ratio, inner, block, n, 0 if i == 0 else n, put)
        dq_ref[at, :] = jnp.concatenate([dq, jnp.zeros((64, BQ), bf)], 0).T

    @pl.when(upper)
    def _():
        send_ref[...] = sum_ref[...].astype(bf)
        keep_ref[...] = dq_ref[...]

    @pl.when(jnp.logical_not(upper))
    def _():
        send_ref[...] = dq_ref[...]
        keep_ref[...] = sum_ref[...].astype(bf)


def far_backward(j, place, q, kv, p, stat, grads, log, inner, got, dep):
    n = q.shape[0]
    row = pl.BlockSpec((1, 8, n), lambda h: (j, 0, 0))
    whole = pl.BlockSpec((n, 128), lambda h: (0, 0))
    return pl.pallas_call(
        far_backward_kernel,
        grid=(1,),
        in_specs=[
            smem(),
            whole,
            whole,
            hbm(),
            pl.BlockSpec((8, n), lambda h: (0, 0)),
            pl.BlockSpec((1, 64, n), lambda h: (j, 0, 0)),
            row,
            row,
            pl.BlockSpec((1, 80, n), lambda h: (j, 0, 0)),
            pl.BlockSpec(memory_space=pl.ANY),
        ],
        out_specs=[whole, whole],
        out_shape=[jax.ShapeDtypeStruct((n, 128), bf)] * 2,
        scratch_shapes=[
            pltpu.VMEM((64, n), bf),
            pltpu.VMEM((n, 128), f32),
            pltpu.VMEM((n, 128), bf),
            pltpu.VMEM(p.shape, bf),
            pltpu.SemaphoreType.DMA((n // BQ,)),
        ],
        compiler_params=params(30),
        cost_estimate=cost(13),
    )(place, q, kv, stay(p), stat, grads, log, inner, got, dep)


def swap(value, bits):
    count = lax.axis_size("batch") * lax.axis_size("seq")
    return lax.ppermute(value, AXES, [(i, i ^ bits) for i in range(count)])


def turns():
    bits = (lax.axis_size("batch") // 2).bit_length() - 1
    return [(3 + t, 2 + bits - t) for t in range(bits)]


PLANE = [(1, 2), (2, 1)]


def swap_by_core(value, turn):
    count = lax.axis_size("batch") * lax.axis_size("seq")
    return lax.ppermute(value, AXES, [(i, i ^ (1 << turn[i % 2])) for i in range(count)])


def bit_of(number, core, turn):
    return (number >> jnp.where(core == 0, turn[0], turn[1])) & 1


def take(value, index, axis=0):
    return lax.dynamic_index_in_dim(value, index, axis, keepdims=False)


MOVES = ((0, 0), (1, 0), (0, 1), (1, 1))


def factors_kernel(place, fac, got, gout, got_out, dep, *outs):
    core, chip, side = place[0], place[1], place[2]
    groups = got.shape[0]
    width = gout.shape[2]
    part = (got.shape[1] - 2 * width) // 4
    rows = gout.shape[1] // 4
    for (x, y), out in zip(MOVES, outs):
        index = 2 * (chip ^ x) + (side ^ y)
        lanes = pl.ds(pl.multiple_of(2 * width + index * part, 128), part)
        at = pl.ds(pl.multiple_of(index * rows, rows), rows)
        out[0:groups, 0 : 2 * width] = fac[core, :, 0 : 2 * width]
        out[groups:, 0 : 2 * width] = got[:, 0 : 2 * width]
        out[0:groups, 2 * width : 2 * width + part] = fac[core, :, lanes]
        out[groups:, 2 * width : 2 * width + part] = got[:, lanes]
        out[:, 2 * width + part :] = (gout[core, at, :].astype(f32) + got_out[at, :].astype(f32)).astype(bf)


def factors(place, fac, got, gout, got_out, dep):
    groups, per = got.shape
    width = gout.shape[2]
    shape = jax.ShapeDtypeStruct((2 * groups, 2 * width + (per - 2 * width) // 4 + width), bf)
    return pl.pallas_call(
        factors_kernel,
        in_specs=[smem()] + [vmem()] * 4 + [anywhere()],
        out_specs=[vmem()] * 4,
        out_shape=[shape] * 4,
        compiler_params=params(),
        cost_estimate=cost(2),
    )(place, fac, got, gout, got_out, dep)


def slab_kernel(turn, lines, place, dep, a, b, c, d, keep, send):
    core, line = place[0], place[3]
    width = keep.shape[2]
    quarter = (a.shape[1] - 3 * width) // 2

    def lanes(start, size):
        return jnp.concatenate([ref[:, start : start + size] for ref in (a, b, c, d)], 0)

    g_in = tn(lanes(0, width), lanes(2 * width, quarter)).astype(bf)
    g_down = tn(lanes(2 * width + quarter, quarter), lanes(width, width)).astype(bf)
    total = a[:, 2 * width + 2 * quarter :].astype(f32)
    for ref in (b, c, d):
        total = total + ref[:, 2 * width + 2 * quarter :].astype(f32)
    pieces = [total.astype(bf), g_in, g_down]
    bits = lines.bit_length() - 1
    for z in range(lines):
        flipped = sum(((z >> t) & 1) << (bits - 1 - t) for t in range(bits))
        spot = jnp.where(core == 0, flipped, z)
        chosen = bit_of(8 * z, core, turn) == bit_of(8 * line, core, turn)

        def put(ref):
            start = 0
            for piece in pieces[1:] + pieces[:1]:
                rows = piece.shape[0] // lines
                ref[spot % (lines // 2), start : start + rows, :] = piece[z * rows : (z + 1) * rows, :]
                start += rows

        @pl.when(chosen)
        def _():
            put(keep)

        @pl.when(jnp.logical_not(chosen))
        def _():
            put(send)


def slabs(place, dep, payloads, width, quarter, lines):
    rows = (width + quarter + payloads[0].shape[0]) // lines
    shape = jax.ShapeDtypeStruct((lines // 2, rows, width), bf)
    turn = turns()[0]
    return pl.pallas_call(
        lambda *refs: slab_kernel(turn, lines, *refs),
        in_specs=[smem(), anywhere()] + [vmem()] * 4,
        out_specs=[vmem()] * 2,
        out_shape=[shape] * 2,
        compiler_params=params(),
        cost_estimate=cost(2),
    )(place, stay(dep), *payloads)


def fold_kernel(turn, place, dep, kept, got, keep, *send):
    if turn is None:
        keep[...] = (kept[...].astype(f32) + got[...].astype(f32)).astype(bf)
        return
    half = keep.shape[0]
    mine = bit_of(place[4], place[0], turn)
    at = pl.ds(mine * half, half)
    keep[...] = (kept[at].astype(f32) + got[at].astype(f32)).astype(bf)
    at = pl.ds((1 - mine) * half, half)
    send[0][...] = (kept[at].astype(f32) + got[at].astype(f32)).astype(bf)


def fold(turn, place, dep, kept, got):
    count = kept.shape[0] if turn is None else kept.shape[0] // 2
    shape = jax.ShapeDtypeStruct((count,) + kept.shape[1:], bf)
    outs = 1 if turn is None else 2
    return pl.pallas_call(
        lambda *refs: fold_kernel(turn, *refs),
        in_specs=[smem(), anywhere(), vmem(), vmem()],
        out_specs=[vmem()] * outs,
        out_shape=[shape] * outs,
        compiler_params=params(),
        cost_estimate=cost(1),
    )(place, dep, kept, got)


def pile_kernel(a, b, *refs):
    out = refs[-1]
    half = out.shape[0] // 2
    out[:half] = a[...]
    out[half:] = b[...]


def pile(a, b, *deps):
    return pl.pallas_call(
        pile_kernel,
        in_specs=[vmem(), vmem()] + [anywhere()] * len(deps),
        out_specs=vmem(),
        out_shape=jax.ShapeDtypeStruct((2 * a.shape[0],) + a.shape[1:], bf),
        compiler_params=params(),
        cost_estimate=cost(1),
    )(a, b, *deps)


def add_kernel(values, pieces, place, *refs):
    total = refs[0][...].astype(f32)
    for ref in refs[1:values]:
        total = total + ref[...].astype(f32)
    outs = refs[len(refs) - pieces :]
    if pieces == 1:
        outs[0][...] = total.astype(bf)
        return
    total = total.astype(bf)
    rows = outs[0].shape[0]
    for z in range(pieces):
        for k in range(pieces):

            @pl.when((place[3] ^ k) == z)
            def _():
                outs[k][...] = total[z * rows : (z + 1) * rows]


def add(place, values, pieces, *deps):
    rows, lanes = values[0].shape
    return pl.pallas_call(
        functools.partial(add_kernel, len(values), pieces),
        in_specs=[smem()] + [vmem()] * len(values) + [anywhere()] * len(deps),
        out_specs=[vmem()] * pieces,
        out_shape=[jax.ShapeDtypeStruct((rows // pieces, lanes), bf)] * pieces,
        compiler_params=params(),
        cost_estimate=cost(1),
    )(place, *values, *deps)


def stack_kernel(count, *refs):
    for k in range(count):
        refs[-1][k] = refs[k][...]


def stack(values, *deps):
    return pl.pallas_call(
        functools.partial(stack_kernel, len(values)),
        in_specs=[vmem()] * len(values) + [anywhere()] * len(deps),
        out_specs=vmem(),
        out_shape=jax.ShapeDtypeStruct((len(values),) + values[0].shape, bf),
        compiler_params=params(),
        cost_estimate=cost(1),
    )(*values, *deps)


def gate_kernel(value, *refs):
    pass


def gate(value, *deps):
    return pl.pallas_call(
        gate_kernel,
        in_specs=[anywhere()] * (1 + len(deps)),
        out_specs=anywhere(),
        out_shape=jax.ShapeDtypeStruct(value.shape, value.dtype),
        input_output_aliases={0: 0},
        compiler_params=params(1),
        cost_estimate=cost(1),
    )(value, *deps)


def spread_kernel(place, near, far, *refs):
    in_ref, down_ref, out_ref = refs[-3:]
    expert = pl.program_id(0)
    line = place[3]
    lines = near.shape[1]
    width = in_ref.shape[1]
    cut_in = width // lines
    cut_down = down_ref.shape[1] // lines
    bits = lines.bit_length() - 1

    def put(ref):
        for k in range(lines):
            flipped = sum(((k >> t) & 1) << (bits - 1 - t) for t in range(bits))
            z = line ^ jnp.where(expert == 0, flipped, k)
            in_ref[0, pl.ds(pl.multiple_of(z * cut_in, cut_in), cut_in), :] = ref[0, k, :cut_in].astype(f32)
            down_ref[0, pl.ds(pl.multiple_of(z * cut_down, cut_down), cut_down), :] = ref[0, k, cut_in : cut_in + cut_down].astype(f32)
            out_ref[0, z] = ref[0, k, cut_in + cut_down :].astype(f32)

    @pl.when(expert == place[0])
    def _():
        put(near)

    @pl.when(expert != place[0])
    def _():
        put(far)


def spread_experts(outer, place, near, far, hidden, width, earlier, *deps):
    block = near.shape[1:]
    lines = block[0]

    def spec(is_near):
        def index(e, i, p):
            return (jnp.where((e == p[0]) == is_near, i, 0), 0, 0, 0)

        return pl.BlockSpec((1,) + block, index)

    def quarter(e, i, p):
        move_x, move_y = jnp.where(e == 0, i, outer), jnp.where(e == 0, outer, i)
        return 2 * (p[1] ^ move_x) + (p[2] ^ move_y)

    return pl.pallas_call(
        spread_kernel,
        grid_spec=pltpu.PrefetchScalarGridSpec(
            num_scalar_prefetch=1,
            grid=(2, 2),
            in_specs=[spec(True), spec(False)] + [anywhere()] * (len(earlier) + len(deps)),
            out_specs=[
                pl.BlockSpec((1, width, hidden // 4), lambda e, i, p: (e, 0, quarter(e, i, p))),
                pl.BlockSpec((1, hidden // 4, width), lambda e, i, p: (e, quarter(e, i, p), 0)),
                pl.BlockSpec((1, lines, width // 8 // lines, width), lambda e, i, p: (e * 4 + quarter(e, i, p), 0, 0, 0)),
            ],
        ),
        out_shape=[
            kept_out((2, width, hidden), f32),
            kept_out((2, hidden, width), f32),
            kept_out((8, lines, width // 8 // lines, width), f32),
        ],
        input_output_aliases={3: 0, 4: 1, 5: 2} if earlier else {},
        compiler_params=params(28),
        cost_estimate=cost(6),
    )(place, near, far, *earlier, *deps)


def own_block(b, p):
    return jnp.where(b // 2 == p[0], b % 2, jnp.where(b // 2 > p[0], 1, 0))


def other_block(b, p):
    return jnp.where(b // 2 != p[0], b % 2, jnp.where(b // 2 > 1 - p[0], 1, 0))


def collect_kernel(
    place, normed, kv_a, kv_b, kv_c, kv_d, q_a, q_b, q_c, q_d, keep_a, keep_b, got_a, got_b, packs, gain, tiny, dep,
    mine, other, slab_0, slab_1, slab_2, slab_3, sum_ref,
):
    block = pl.program_id(0)
    core, chip, side = place[0], place[1], place[2]
    upper = chip == 1
    dq = jnp.concatenate([q_a[...], q_b[...], q_c[...], q_d[...]], 0).T.astype(f32)
    far = jnp.concatenate([left(keep_a[...], keep_b[...]), left(got_a[...], got_b[...])], 1).astype(f32)
    pieces = [(dq + jnp.where(upper, far, 0.0)).astype(bf)]
    for near, extra in ((kv_a, got_a), (kv_b, got_b), (kv_c, keep_a), (kv_d, keep_b)):
        value = near[...] + jnp.where(upper, 0.0, extra[...].astype(f32))
        pieces.append(jnp.where(lanes_of(value.shape) < 64, value * 0.125, value).astype(bf))
    back = jnp.concatenate(pieces, 1)

    @pl.when(block // 2 == core)
    def _():
        mine[...] = back

    @pl.when(block // 2 != core)
    def _():
        other[...] = back

    part = tn(normed[...], back)

    @pl.when(block == 0)
    def _():
        sum_ref[...] = part

    @pl.when(block > 0)
    def _():
        sum_ref[...] += part

    @pl.when(block == 3)
    def _():
        total = sum_ref[...]
        width, wide = total.shape
        product = jnp.sum(total * packs[core].astype(f32), axis=1, keepdims=True)
        small = tiny[...].T
        small = jnp.concatenate([small, jnp.zeros((width, 120), f32)], 1)
        lanes = lanes_of(small.shape)
        small = jnp.where(lanes == 3, product / gain[...].T, small)
        high = small.astype(bf)
        low = (small - high.astype(f32)).astype(bf)
        small = jnp.where(lanes < 8, high.astype(f32), pltpu.roll(low.astype(f32), 8, axis=1)).astype(bf)
        low = total.astype(bf)
        rows = width // 4
        for (move_x, move_y), ref in zip(MOVES, (slab_0, slab_1, slab_2, slab_3)):
            for q in range(4):

                @pl.when(2 * (chip ^ move_x) + (side ^ move_y) == q)
                def _():
                    ref[:, :wide] = low[q * rows : (q + 1) * rows]
                    ref[:, wide:] = small[q * rows : (q + 1) * rows]


def collect(place, normed, kvs, qs, keep_a, keep_b, got_a, got_b, packs, gain, tiny, dep):
    n, width = normed.shape
    rows = n // 4
    dq = pl.BlockSpec((64, rows), lambda b, p: (0, b))
    flat = pl.BlockSpec((rows, 128), lambda b, p: (b, 0))
    slab = (width // 4, 896)
    return pl.pallas_call(
        collect_kernel,
        grid_spec=pltpu.PrefetchScalarGridSpec(
            num_scalar_prefetch=1,
            grid=(4,),
            in_specs=[pl.BlockSpec((rows, width), lambda b, p: (b, 0))]
            + [flat] * 4
            + [dq] * 4
            + [flat] * 4
            + [
                pl.BlockSpec(packs.shape, lambda b, p: (0, 0, 0)),
                pl.BlockSpec((1, width), lambda b, p: (0, 0)),
                pl.BlockSpec(tiny.shape, lambda b, p: (0, 0)),
                anywhere(),
            ],
            out_specs=[
                pl.BlockSpec((rows, 768), lambda b, p: (own_block(b, p), 0)),
                pl.BlockSpec((rows, 768), lambda b, p: (other_block(b, p), 0)),
            ]
            + [pl.BlockSpec(slab, lambda b, p: (0, 0))] * 4,
            scratch_shapes=[pltpu.VMEM((width, 768), f32)],
        ),
        out_shape=[
            jax.ShapeDtypeStruct((n // 2, 768), bf),
            jax.ShapeDtypeStruct((n // 2, 768), bf),
        ]
        + [jax.ShapeDtypeStruct(slab, bf)] * 4,
        compiler_params=params(26),
        cost_estimate=cost(5),
    )(place, stay(normed), *kvs[:3], stay(kvs[3]), *qs, keep_a, keep_b, got_a, got_b, stay(packs), gain, tiny, dep)


def tokens_kernel(place, mine, got, packs, x_ref, back_resid, gain, dep, out):
    core = place[0]
    back = nt(mine[...], packs[core]) + nt(got[...], packs[1 - core])
    x = x_ref[...].astype(f32)
    inverse = lax.rsqrt(jnp.mean(x * x, axis=1, keepdims=True) + EPSILON)
    k = back * gain[...]
    mean = jnp.mean(k * x, axis=1, keepdims=True)
    out[...] = (back_resid[...] + inverse * k - x * (inverse * inverse * inverse * mean)).astype(bf)


def tokens_back(place, mine, got, packs, x, back_resid, gain, dep):
    n, width = x.shape
    rows = n // 4
    wide = pl.BlockSpec((rows, 768), lambda b, p: (b, 0))
    block = pl.BlockSpec((rows, width), lambda b, p: (b, 0))
    return pl.pallas_call(
        tokens_kernel,
        grid_spec=pltpu.PrefetchScalarGridSpec(
            num_scalar_prefetch=1,
            grid=(4,),
            in_specs=[wide, wide, pl.BlockSpec(packs.shape, lambda b, p: (0, 0, 0)), block, block, pl.BlockSpec((1, width), lambda b, p: (0, 0)), anywhere()],
            out_specs=block,
        ),
        out_shape=kept_out((n, width), bf),
        compiler_params=params(20),
        cost_estimate=cost(4),
    )(place, mine, got, stay(packs), stay(x), stay(back_resid), gain, dep)


def unfold_kernel(place, *refs):
    out, rows_out, small_ref = refs[-3:]
    core, line = place[0], place[3]
    lines, rows = refs[0].shape[1], refs[0].shape[2]
    block = pl.program_id(0)

    def put(source, c, fresh):
        for k in range(lines):
            at = pl.ds(pl.multiple_of((line ^ k) * rows, rows), rows)
            value = source[k]
            base = c * 256
            out[at, pl.ds(pl.multiple_of(base, 128), 256)] = value[:, 0:256].astype(f32)
            for pair in range(2):
                a = value[:, 256 + 256 * pair : 384 + 256 * pair]
                b = value[:, 384 + 256 * pair : 512 + 256 * pair]
                out[at, pl.ds(pl.multiple_of(512 + base + 128 * pair, 128), 128)] = left(a, b).astype(f32)
                out[at, pl.ds(pl.multiple_of(1024 + base + 128 * pair, 128), 128)] = right(a, b).astype(f32)
            small = value[:, 768:].astype(f32)
            small = small + pltpu.roll(small, 120, axis=1)
            small_ref[at, :] = small if fresh else small_ref[at, :] + small

    for i in range(4):

        @pl.when(block == i)
        def _():
            put(refs[0].at[i], core, True)
            put(refs[1].at[i], 1 - core, False)
            rows_out[...] = small_ref[...].T[0:8, :]


def unfold(place, near, far, width):
    whole = pl.BlockSpec(near.shape, lambda i, p: (0, 0, 0, 0))

    def at(i, p):
        return ((2 * p[1] + p[2]) ^ ((i % 2) * 2 + i // 2), 0)

    def across(i, p):
        return at(i, p)[::-1]

    return pl.pallas_call(
        unfold_kernel,
        grid_spec=pltpu.PrefetchScalarGridSpec(
            num_scalar_prefetch=1,
            grid=(4,),
            in_specs=[whole] * 2,
            out_specs=[pl.BlockSpec((width // 4, 3 * width), at), pl.BlockSpec((8, width // 4), across)],
            scratch_shapes=[pltpu.VMEM((width // 4, 128), f32)],
        ),
        out_shape=[kept_out((width, 3 * width), f32), jax.ShapeDtypeStruct((8, width), f32)],
        compiler_params=params(16),
        cost_estimate=cost(3),
    )(place, near, far)


def body(
    layer_activations,
    sequence_extents,
    position_cluster_label,
    cluster_sharpness,
    heed_scale_factor,
    triple_entry_matrix,
    heed_exit_matrix,
    blend_scale_factor,
    router_matrix,
    specialist_entry_matrix,
    specialist_exit_matrix,
    upstream_derivative,
):
    seq_count, pos_count, width = layer_activations.shape
    tokens = seq_count * pos_count
    hidden = specialist_entry_matrix.shape[2]
    spot = lax.axis_index("seq")
    row = lax.axis_index("batch")
    core, chip, side, line = spot % 2, spot // 2, row % 2, row // 2
    lines = lax.axis_size("batch") // 2
    place = jnp.stack([core, chip, side, line, row * 4 + spot]).astype(jnp.int32)
    core_pairs, chip_pairs = [(0, 1), (1, 0), (2, 3), (3, 2)], [(0, 2), (1, 3), (2, 0), (3, 1)]
    up, down = chip_pairs[:2], chip_pairs[2:]

    x = layer_activations.reshape(tokens, width)
    x_other = lax.ppermute(x, "seq", core_pairs)
    packs, w_own, router, gains = pack(
        place, triple_entry_matrix, router_matrix.T, heed_scale_factor.reshape(1, width), blend_scale_factor.reshape(1, width)
    )
    gain_a, gain_m = gains[0], gains[1]
    normed, qkv, send_a, send_b = project(place, x, x_other, gain_a, w_own)
    got_a = lax.ppermute(send_a, "seq", chip_pairs)
    got_b = lax.ppermute(send_b, "seq", up)
    limit = (sequence_extents - chip * 2 * pos_count).astype(jnp.int32)
    p_na, o_na, st_na = near_forward(0, limit, qkv, qkv)
    p_a, o_a, st_a, q_a, kv_a = far_forward(0, place, qkv, got_a, got_a, o_na)
    got_oa = lax.ppermute(o_a, "seq", up)
    p_b, o_b, st_b, q_b, kv_b = far_forward(1, place, qkv, got_a, got_b, o_a)
    got_ob = lax.ppermute(o_b, "seq", up)
    p_nb, o_nb, st_nb = near_forward(1, limit, qkv, o_b)
    att_mine, att_send, log = join(place, o_na, o_nb, st_na, st_nb, o_a, o_b, got_oa, got_ob)
    att_got = lax.ppermute(att_send, "seq", core_pairs)

    block_out, fac, gout, tiny, back_resid, ba_own, ba_send = mixture(
        place,
        cluster_sharpness,
        x,
        att_mine,
        att_got,
        heed_exit_matrix,
        gain_m,
        router,
        position_cluster_label.reshape(1, tokens),
        upstream_derivative.reshape(tokens, width),
        specialist_entry_matrix,
        specialist_exit_matrix,
    )

    ba_got = lax.ppermute(ba_send, "seq", core_pairs)
    fac_got = swap(take(fac, 1 - core), 1)
    gout_got = swap(take(gout, 1 - core), 1)
    grads, inner, payload = ready(place, ba_own, ba_got, att_mine, att_send, log)
    got_grad = lax.ppermute(payload, "seq", down)
    pay = factors(place, fac, fac_got, gout, gout_got, payload)
    pays = [pay[0]] + [swap(pay[i], 2 * m[0] + 4 * m[1]) for i, m in list(enumerate(MOVES))[1:]]
    def near(h, dep):
        p, stat = ((p_na, st_na), (p_nb, st_nb))[h // 2]
        return near_backward(h, qkv, p, grads, stat, log, inner, dep)

    kv_0, dq_0 = near(0, (pay[0],))
    kv_1, dq_1 = near(1, (stay(dq_0),))
    stages = turns()
    kept, sent = slabs(place, dq_1, pays, width, hidden // 4, lines)
    send_fa, keep_fa = far_backward(0, place, q_a, kv_a, p_a, st_a, grads, log, inner, got_grad, kept)
    got_fa = lax.ppermute(send_fa, "seq", chip_pairs)
    for t, turn in enumerate(stages):
        got = swap_by_core(sent, turn)
        if t == len(stages) - 1:
            send_fb, keep_fb = far_backward(1, place, q_b, kv_b, p_b, st_b, grads, log, inner, got_grad, kept)
            got_fb = lax.ppermute(send_fb, "seq", chip_pairs)
            whole = fold(None, place, keep_fb, kept, got)[0]
        else:
            kept, sent = fold(stages[t + 1], place, keep_fa, kept, got)
    kv_2, dq_2 = near(2, (whole,))
    for turn in stages[:0:-1]:
        whole = pile(whole, swap_by_core(whole, turn), stay(dq_2))
    got = swap_by_core(whole, stages[0])
    kv_3, dq_3 = near(3, (whole, got_fa))
    whole = pile(whole, got, stay(dq_3), got_fb)
    got_first = swap_by_core(whole, PLANE[0])
    d_mine, d_send, *parts = collect(
        place, normed, (kv_0, kv_1, kv_2, kv_3), (dq_0, dq_1, dq_2, dq_3), keep_fa, keep_fb, got_fa, got_fb, packs, gain_a, tiny, whole
    )

    moves = [2 * m[0] + 4 * m[1] for m in MOVES]
    parts = parts[:1] + [swap(part, bits) for part, bits in list(zip(parts, moves))[1:]]
    d_got = lax.ppermute(d_send, "seq", core_pairs)
    parts = list(add(place, parts, lines))
    whole = pile(whole, got_first, parts[0])
    got_second = swap_by_core(whole, PLANE[1])
    far_first = swap(whole, 1)
    tokens_grad = tokens_back(place, d_mine, d_got, packs, x, back_resid, gain_a, whole)
    parts = parts[:1] + [swap(part, 8 * k) for k, part in list(enumerate(parts))[1:]]
    part = add(place, parts, 1, stay(tokens_grad))[0]
    block = (2, lines) + whole.shape[1:]
    halves = spread_experts(0, place, whole.reshape(block), far_first.reshape(block), hidden, width, (), part)
    zs = stack([part] + [swap(part, 8 * k) for k in range(1, lines)], stay(halves[2]))
    pieces = [zs] + [swap(zs, bits) for bits in moves[1:]]
    got_second = gate(got_second, zs)
    far_second = swap(got_second, 1)
    grad_in, grad_down, grad_out = spread_experts(
        1, place, got_second.reshape(block), far_second.reshape(block), hidden, width, tuple(halves)
    )
    pieces = stack(pieces, stay(grad_out))
    grad_qkv, small = unfold(place, pieces, swap(pieces, 1), width)
    return (
        block_out.reshape(layer_activations.shape),
        tokens_grad.reshape(layer_activations.shape),
        small[3],
        grad_qkv,
        grad_out.reshape(width, width),
        small[2],
        small[0:2].T,
        grad_in,
        grad_down,
    )


def solution(mesh):
    rows = P("batch", "seq", None)
    placed = (rows, P("batch"), P("batch", "seq")) + (P(),) * 8 + (rows,)
    return jax.shard_map(body, mesh=mesh, in_specs=placed, out_specs=(rows, rows) + (P(),) * 7, check_vma=False)
```

```python
import functools

import jax
import jax.numpy as jnp
from jax import lax
from jax.experimental import pallas as pl
from jax.experimental.pallas import tpu as pltpu
from jax.sharding import PartitionSpec as P

HEADS = 8
HEAD = 64
GROUP = 32
EPSILON = 1e-06
LOG2E = 1.4426950408889634
SC = 0.125 * LOG2E
MASKED = -1e30
BQ = 512
CH = 512
bf = jnp.bfloat16
f32 = jnp.float32
AXES = ("batch", "seq")
NT = (((1,), (1,)), ((), ()))
TN = (((0,), (0,)), ((), ()))


def nt(a, b):
    return lax.dot_general(a, b, NT, preferred_element_type=f32)


def tn(a, b):
    return lax.dot_general(a, b, TN, preferred_element_type=f32)


def nn(a, b):
    return jnp.dot(a, b, preferred_element_type=f32)


def rows_of(shape):
    return lax.broadcasted_iota(jnp.int32, shape, 0)


def lanes_of(shape):
    return lax.broadcasted_iota(jnp.int32, shape, 1)


def vmem():
    return pl.BlockSpec(memory_space=pltpu.VMEM)


def smem():
    return pl.BlockSpec(memory_space=pltpu.SMEM)


def params(mib=16):
    return pltpu.CompilerParams(vmem_limit_bytes=mib * 2**20)


def anywhere():
    return pl.BlockSpec(memory_space=pl.ANY)


def hbm():
    return pl.BlockSpec(memory_space=pltpu.HBM)


def cost(us):
    return pl.CostEstimate(flops=int(us * 1e8), bytes_accessed=2**10, transcendentals=0)


def stay(value):
    return pltpu.with_memory_space_constraint(value, pltpu.HBM)


def kept_out(shape, dtype):
    return pltpu.HBM(shape, dtype)


def shift_lanes(value):
    return pltpu.roll(value.astype(f32), 64, axis=1).astype(bf)


def left(first, second):
    return jnp.where(lanes_of(first.shape) < 64, first, shift_lanes(second))


def right(first, second):
    return jnp.where(lanes_of(first.shape) < 64, shift_lanes(first), second)


def pack_kernel(place, w, router, gain_a, gain_m, packs, w_own, router_rows, gains):
    core = place[0]
    both = router[...].astype(f32)
    rows = rows_of(router_rows.shape)
    router_rows[...] = jnp.where(rows == 0, both[0:1, :], jnp.where(rows == 1, both[1:2, :], 0.0)).astype(bf)
    gains[0] = gain_a[...].astype(f32).reshape(1, -1)
    gains[1] = gain_m[...].astype(f32).reshape(1, -1)
    for c in range(2):
        packs[c, :, 0:256] = w[:, 256 * c : 256 * c + 256]
        for h in range(4):
            at = 256 * c + 128 * (h // 2)
            k = w[:, 512 + at : 640 + at]
            v = w[:, 1024 + at : 1152 + at]
            packs[c, :, 256 + 128 * h : 384 + 128 * h] = left(k, v) if h % 2 == 0 else right(k, v)
    for h in range(4):
        q = packs[core, :, 128 * (h // 2) : 128 * (h // 2) + 128]
        q = q if h % 2 == 0 else shift_lanes(q)
        w_own[:, 256 * h : 256 * h + 128] = jnp.where(lanes_of(q.shape) < 64, q, jnp.zeros((), bf))
        w_own[:, 256 * h + 128 : 256 * h + 256] = packs[core, :, 256 + 128 * h : 384 + 128 * h]


def pack(place, w, router, gain_a, gain_m):
    width = w.shape[0]
    return pl.pallas_call(
        pack_kernel,
        in_specs=[smem()] + [vmem()] * 4,
        out_specs=[vmem()] * 4,
        out_shape=[
            kept_out((2, width, 768), bf),
            jax.ShapeDtypeStruct((width, 1024), bf),
            jax.ShapeDtypeStruct((16, width), bf),
            jax.ShapeDtypeStruct((2, 1, width), f32),
        ],
        compiler_params=params(16),
        cost_estimate=cost(3),
    )(place, stay(w), stay(router), stay(gain_a), stay(gain_m))


def project_kernel(place, x_own, x_other, gain, w_own, normed, qkv, send_a, send_b):
    core, chip = place[0], place[1]
    block = pl.program_id(0)

    def go(x_ref):
        x = x_ref[...].astype(f32)
        inverse = lax.rsqrt(jnp.mean(x * x, axis=1, keepdims=True) + EPSILON)
        low = (x * inverse * gain[...]).astype(bf)
        normed[...] = low
        out = nn(low, w_own[...]).astype(bf)
        qkv[...] = out
        send_b[...] = out[:, 384:512]

        @pl.when(chip == 0)
        def _():
            send_a[...] = out[:, 128:256]

        @pl.when(chip == 1)
        def _():
            send_a[...] = left(out[:, 512:640], out[:, 768:896])

    @pl.when(block // 2 == core)
    def _():
        go(x_own)

    @pl.when(block // 2 != core)
    def _():
        go(x_other)


def project(place, x_own, x_other, gain, w_own):
    rows, width = x_own.shape

    def own(b, p):
        return (jnp.where(b // 2 == p[0], b % 2, jnp.where(b // 2 > p[0], 1, 0)), 0)

    def other(b, p):
        return (jnp.where(b // 2 != p[0], b % 2, jnp.where(b // 2 > 1 - p[0], 1, 0)), 0)

    half = rows // 2
    return pl.pallas_call(
        project_kernel,
        grid_spec=pltpu.PrefetchScalarGridSpec(
            num_scalar_prefetch=1,
            grid=(4,),
            in_specs=[
                pl.BlockSpec((half, width), own),
                pl.BlockSpec((half, width), other),
                pl.BlockSpec((1, width), lambda b, p: (0, 0)),
                pl.BlockSpec((width, 1024), lambda b, p: (0, 0)),
            ],
            out_specs=[
                pl.BlockSpec((half, width), lambda b, p: (b, 0)),
                pl.BlockSpec((half, 1024), lambda b, p: (b, 0)),
                pl.BlockSpec((half, 128), lambda b, p: (b, 0)),
                pl.BlockSpec((half, 128), lambda b, p: (b, 0)),
            ],
        ),
        out_shape=[
            kept_out((2 * rows, width), bf),
            kept_out((2 * rows, 1024), bf),
            jax.ShapeDtypeStruct((2 * rows, 128), bf),
            jax.ShapeDtypeStruct((2 * rows, 128), bf),
        ],
        compiler_params=params(20),
        cost_estimate=cost(4),
    )(place, x_own, x_other, gain, w_own)


def scores(kv, q, s_ref, slot, kmax, q0, limit, causal):
    peak = None
    for k0 in range(0, kmax, CH):
        s = nt(kv[k0 : k0 + CH, :], q)
        if causal:
            if k0 >= 1024:
                s = jnp.where(rows_of(s.shape) + k0 < limit, s, MASKED)
            if k0 + CH > q0:
                s = jnp.where(rows_of(s.shape) + (k0 - q0) <= lanes_of(s.shape), s, MASKED)
        s_ref[slot, k0 : k0 + CH, :] = s
        m = jnp.max(s, axis=0, keepdims=True)
        peak = m if peak is None else jnp.maximum(peak, m)
    return peak


def weigh(vt, s_ref, slot, peak, kmax, put):
    scaled = peak * SC
    acc = None
    for k0 in range(0, kmax, CH):
        p = jnp.exp2(s_ref[slot, k0 : k0 + CH, :] * SC - scaled).astype(bf)
        put(k0 // CH, p)
        d = nn(vt[:, k0 : k0 + CH], p)
        acc = d if acc is None else acc + d
    total = acc[0:1, :]
    return acc[64:128, :] * (1.0 / total), scaled, total


def ones_and_values(kv):
    vt = kv.T
    return jnp.where(rows_of(vt.shape) < 64, jnp.ones((), bf), vt)


def near_forward_kernel(limit_ref, qkv, dep, p_ref, o_ref, st_ref, s_ref, vt_ref, buf, sems):
    limit = limit_ref[0]
    count = qkv.shape[0] // BQ
    tasks = [(h, i) for h in range(2) for i in range(count)]

    def start_scores(at):
        h, i = tasks[at]
        kv = qkv.at[:, 256 * h + 128 : 256 * h + 256]
        q = qkv[i * BQ : (i + 1) * BQ, 256 * h : 256 * h + 128]
        return scores(kv, q, s_ref, at % 2, (i + 1) * BQ, i * BQ, limit, True)

    copies = []
    peak = start_scores(0)
    for at, (h, i) in enumerate(tasks):
        if i == 0:
            vt_ref[h] = ones_and_values(qkv[:, 256 * h + 128 : 256 * h + 256])
        later = start_scores(at + 1) if at + 1 < len(tasks) else None
        base = i * (i + 1) // 2

        def put(k, p):
            buf[h, base + k] = p

        out, scaled, total = weigh(vt_ref.at[h], s_ref, at % 2, peak, (i + 1) * BQ, put)
        copies.append(pltpu.make_async_copy(buf.at[h, base : base + i + 1], p_ref.at[h, base : base + i + 1], sems.at[h, i]))
        copies[-1].start()
        o_ref[h, :, i * BQ : (i + 1) * BQ] = out.astype(bf)
        st_ref[h, 0:1, i * BQ : (i + 1) * BQ] = scaled
        st_ref[h, 1:2, i * BQ : (i + 1) * BQ] = total
        peak = later
    for copy in copies:
        copy.wait()


def near_forward(pair, limit, qkv, dep):
    n = qkv.shape[0]
    count = n // BQ
    shape = (2, count * (count + 1) // 2, CH, BQ)
    return pl.pallas_call(
        near_forward_kernel,
        grid=(1,),
        in_specs=[smem(), pl.BlockSpec((n, 512), lambda g: (0, pair)), anywhere()],
        out_specs=[
            anywhere(),
            pl.BlockSpec((2, 64, n), lambda g: (0, 0, 0)),
            pl.BlockSpec((2, 8, n), lambda g: (0, 0, 0)),
        ],
        out_shape=[
            kept_out(shape, bf),
            jax.ShapeDtypeStruct((2, 64, n), bf),
            jax.ShapeDtypeStruct((2, 8, n), f32),
        ],
        scratch_shapes=[
            pltpu.VMEM((2, n, BQ), f32),
            pltpu.VMEM((2, 128, n), bf),
            pltpu.VMEM(shape, bf),
            pltpu.SemaphoreType.DMA((2, count)),
        ],
        compiler_params=params(34),
        cost_estimate=cost(9),
    )(limit, stay(qkv) if pair == 0 else qkv, dep)


def three(value):
    high = value.astype(bf)
    rest = value - high.astype(f32)
    mid = rest.astype(bf)
    return high, mid, (rest - mid.astype(f32)).astype(bf)


def far_forward_kernel(j, place, q_own, q_got, kv_own, kv_got, dep, p_ref, o_ref, st_ref, q_ref, kv_ref, s_ref, vt_ref, buf, sems):
    n = q_own.shape[0]

    @pl.when(place[1] == 1)
    def _():
        q_ref[...] = q_own[...]
        kv_ref[...] = kv_got[...]

    @pl.when(place[1] == 0)
    def _():
        q = q_got[...] if j == 0 else shift_lanes(q_got[...])
        q_ref[...] = jnp.where(lanes_of(q.shape) < 64, q, jnp.zeros((), bf))
        kv_ref[...] = kv_own[...]

    vt_ref[...] = ones_and_values(kv_ref[...])
    count = n // BQ
    copies = []
    peak = scores(kv_ref, q_ref[0:BQ, :], s_ref, 0, n, 0, None, False)
    for i in range(count):
        later = None
        at = slice(i * BQ, (i + 1) * BQ)
        if i + 1 < count:
            later = scores(kv_ref, q_ref[(i + 1) * BQ : (i + 2) * BQ, :], s_ref, (i + 1) % 2, n, 0, None, False)

        def put(k, p):
            buf[i, k] = p

        out, scaled, total = weigh(vt_ref, s_ref, i % 2, peak, n, put)
        copies.append(pltpu.make_async_copy(buf.at[i], p_ref.at[i], sems.at[i]))
        copies[-1].start()
        o_ref[0:64, at] = out.astype(bf)
        high, mid, low = three(scaled + jnp.log(total) * LOG2E)
        tail = jnp.concatenate([high.astype(f32), mid.astype(f32), low.astype(f32), jnp.zeros((13, BQ), f32)], 0)
        o_ref[64:80, at] = tail.astype(bf)
        st_ref[0:1, at] = scaled
        peak = later
    for copy in copies:
        copy.wait()


def far_forward(j, place, qkv, q_got, kv_got, dep):
    n = qkv.shape[0]
    whole = pl.BlockSpec((n, 128), lambda h: (0, 0))
    shape = (n // BQ, n // CH, CH, BQ)
    return pl.pallas_call(
        lambda *refs: far_forward_kernel(j, *refs),
        grid=(1,),
        in_specs=[
            smem(),
            pl.BlockSpec((n, 128), lambda h: (0, 2 * j)),
            whole,
            pl.BlockSpec((n, 128), lambda h: (0, 2 * j + 5)),
            whole,
            anywhere(),
        ],
        out_specs=[
            anywhere(),
            pl.BlockSpec((80, n), lambda h: (0, 0)),
            pl.BlockSpec((8, n), lambda h: (0, 0)),
            whole,
            whole,
        ],
        out_shape=[
            kept_out(shape, bf),
            jax.ShapeDtypeStruct((80, n), bf),
            jax.ShapeDtypeStruct((8, n), f32),
            kept_out((n, 128), bf),
            kept_out((n, 128), bf),
        ],
        scratch_shapes=[
            pltpu.VMEM((2, n, BQ), f32),
            pltpu.VMEM((128, n), bf),
            pltpu.VMEM(shape, bf),
            pltpu.SemaphoreType.DMA((n // BQ,)),
        ],
        compiler_params=params(34),
        cost_estimate=cost(10),
    )(place, qkv, q_got, qkv, kv_got, dep)


def unsplit(ref, at):
    return ref[at : at + 1, :].astype(f32) + ref[at + 1 : at + 2, :].astype(f32) + ref[at + 2 : at + 3, :].astype(f32)


def join_kernel(place, near_a, near_b, stat_a, stat_b, far_a, far_b, got_a, got_b, mine, other, log_ref):
    core, chip = place[0], place[1]
    half = mine.shape[1]
    for h in range(4):
        far = (far_a, far_b, got_a, got_b)[h]
        near, stat = (near_a, near_b)[h // 2], (stat_a, stat_b)[h // 2]
        log_near = stat[h % 2, 0:1, :] + jnp.log(stat[h % 2, 1:2, :]) * LOG2E
        log_far = jnp.where(chip == 1, unsplit(far, 64), MASKED)
        top = jnp.maximum(log_near, log_far)
        e_near, e_far = jnp.exp2(log_near - top), jnp.exp2(log_far - top)
        both = e_near + e_far
        log_ref[h] = jnp.broadcast_to(top + jnp.log(both) * LOG2E, log_ref.shape[1:])
        far_out = jnp.where(chip == 1, far[0:64, :].astype(f32), 0.0)
        joined = ((near[h % 2].astype(f32) * e_near + far_out * e_far) * (1.0 / both)).astype(bf)
        at = slice(64 * h, 64 * h + 64)

        @pl.when(core == 0)
        def _():
            mine[at, :] = joined[:, :half]
            other[at, :] = joined[:, half:]

        @pl.when(core == 1)
        def _():
            mine[at, :] = joined[:, half:]
            other[at, :] = joined[:, :half]


def join(place, near_a, near_b, stat_a, stat_b, far_a, far_b, got_a, got_b):
    n = near_a.shape[2]
    return pl.pallas_call(
        join_kernel,
        in_specs=[smem()] + [vmem()] * 8,
        out_specs=[vmem()] * 3,
        out_shape=[
            jax.ShapeDtypeStruct((256, n // 2), bf),
            jax.ShapeDtypeStruct((256, n // 2), bf),
            jax.ShapeDtypeStruct((4, 8, n), f32),
        ],
        compiler_params=params(),
        cost_estimate=cost(2),
    )(place, near_a, near_b, stat_a, stat_b, far_a, far_b, got_a, got_b)


def mixture_kernel(
    place, sharp, x, att_own, att_got, wout, gain, router, labels, gy, w1_hbm, w2_hbm,
    block_out, fac, gout, tiny, back_resid, ba_own, ba_other, w1, w2, block_ref, back_ref, sems,
):
    core = place[0]
    copy1 = pltpu.make_async_copy(w1_hbm, w1, sems.at[0])
    copy2 = pltpu.make_async_copy(w2_hbm, w2, sems.at[1])
    copy1.start()
    copy2.start()
    copy3 = pltpu.make_async_copy(block_ref, block_out, sems.at[2])
    copy4 = pltpu.make_async_copy(back_ref, back_resid, sems.at[3])
    own_rows = pl.ds(pl.multiple_of(core * 256, 256), 256)
    other_rows = pl.ds(pl.multiple_of(256 - core * 256, 256), 256)
    wo_own, wo_other = wout[own_rows, :], wout[other_rows, :]
    resid = x[...].astype(f32) + tn(att_own[...], wo_own) + tn(att_got[...], wo_other)
    inverse = lax.rsqrt(jnp.mean(resid * resid, axis=1, keepdims=True) + EPSILON)
    unit = resid * inverse
    mix = (unit * gain[...]).astype(bf)
    temper = 1.0 / sharp[0]
    logits = nt(router[...], mix) * temper
    tokens = mix.shape[0]
    groups = tokens // GROUP
    member = labels[...] == rows_of((groups, tokens))
    weights, mixing = [], []
    for e in range(2):
        row = logits[e : e + 1, :]
        peak = jnp.max(jnp.where(member, row, -jnp.inf), axis=1, keepdims=True)
        token_peak = jnp.sum(jnp.where(member, peak, 0.0), axis=0, keepdims=True)
        raised = jnp.exp(row - token_peak)
        total = jnp.sum(jnp.where(member, raised, 0.0), axis=1, keepdims=True)
        token_total = jnp.sum(jnp.where(member, total, 0.0), axis=0, keepdims=True)
        w = raised / token_total
        weights.append(w)
        mixing.append(jnp.where(member, w, 0.0))
    mixing = jnp.concatenate(mixing, 0).astype(bf)
    mixed = nn(mixing, mix).astype(bf)
    back_expert = nn(mixing, gy[...]).astype(bf)
    copy1.wait()
    copy2.wait()
    expert_out, back_mixed = [], []
    quarter = w1.shape[2] // 4
    width = mix.shape[1]
    for e in range(2):
        at = slice(groups * e, groups * (e + 1))
        inner = nn(mixed[at], w1[e])
        cdf = 0.5 * (1.0 + lax.erf(inner * 0.7071067811865476))
        active = (inner * cdf).astype(bf)
        slope = cdf + inner * (jnp.exp(-0.5 * inner * inner) * 0.3989422804014327)
        expert_out.append(nn(active, w2[e]))
        back_inner = (slope * nt(back_expert[at], w2[e])).astype(bf)
        back_mixed.append(nt(back_inner, w1[e]))
        fac[e, :, 0:width] = mixed[at]
        fac[e, :, width : 2 * width] = back_expert[at]
        for q in range(4):
            base = 2 * width + 2 * quarter * q
            fac[e, :, base : base + quarter] = back_inner[:, quarter * q : quarter * (q + 1)]
            fac[e, :, base + quarter : base + 2 * quarter] = active[:, quarter * q : quarter * (q + 1)]
    expert_out = jnp.concatenate(expert_out, 0).astype(bf)
    back_mixed = jnp.concatenate(back_mixed, 0).astype(bf)
    block_ref[...] = (resid + tn(mixing, expert_out)).astype(bf)
    copy3.start()
    spread = nt(expert_out, gy[...]) + nt(back_mixed, mix)
    rows16 = rows_of((16, tokens))
    back_logits = jnp.zeros((16, tokens), f32)
    for e in range(2):
        back_weight = jnp.sum(jnp.where(member, spread[groups * e : groups * (e + 1)], 0.0), axis=0, keepdims=True)
        w = weights[e]
        inner = jnp.sum(jnp.where(member, w * back_weight, 0.0), axis=1, keepdims=True)
        token_inner = jnp.sum(jnp.where(member, inner, 0.0), axis=0, keepdims=True)
        back_logits = jnp.where(rows16 == e, w * (back_weight - token_inner) * temper, back_logits)
    back_logits = back_logits.astype(bf)
    ctrl = nn(back_logits, mix)
    back_mix = tn(mixing, back_mixed) + tn(back_logits, router[...])
    tiny[...] = jnp.zeros_like(tiny)
    tiny[0:2, :] = ctrl[0:2, :]
    tiny[2:3, :] = jnp.sum(back_mix * unit, axis=0, keepdims=True)
    n = back_mix * gain[...]
    mean = jnp.mean(n * resid, axis=1, keepdims=True)
    back = gy[...].astype(f32) + inverse * n - resid * (inverse * inverse * inverse * mean)
    back_ref[...] = back
    copy4.start()
    branch = back.astype(bf)
    gout[core] = nn(att_own[...], branch).astype(bf)
    gout[1 - core] = nn(att_got[...], branch).astype(bf)
    ba_own[...] = nt(wo_own, branch).astype(bf)
    ba_other[...] = nt(wo_other, branch).astype(bf)
    copy3.wait()
    copy4.wait()


def mixture(place, sharp, x, att_own, att_got, wout, gain, router, labels, gy, w1, w2):
    tokens, width = x.shape
    hidden = w1.shape[2]
    groups = tokens // GROUP
    return pl.pallas_call(
        mixture_kernel,
        in_specs=[smem(), smem()] + [vmem()] * 8 + [pl.BlockSpec(memory_space=pl.ANY)] * 2,
        out_specs=[anywhere()] + [vmem()] * 3 + [anywhere()] + [vmem()] * 2,
        out_shape=[
            kept_out((tokens, width), bf),
            jax.ShapeDtypeStruct((2, groups, 2 * width + 2 * hidden), bf),
            jax.ShapeDtypeStruct((2, width // 2, width), bf),
            jax.ShapeDtypeStruct((8, width), f32),
            kept_out((tokens, width), f32),
            jax.ShapeDtypeStruct((width // 2, tokens), bf),
            jax.ShapeDtypeStruct((width // 2, tokens), bf),
        ],
        scratch_shapes=[
            pltpu.VMEM(w1.shape, bf),
            pltpu.VMEM(w2.shape, bf),
            pltpu.VMEM((tokens, width), bf),
            pltpu.VMEM((tokens, width), f32),
            pltpu.SemaphoreType.DMA((4,)),
        ],
        compiler_params=params(48),
        cost_estimate=cost(15),
    )(place, sharp, x, att_own, att_got, stay(wout), gain, router, labels, gy, stay(w1), stay(w2))


def ready_kernel(place, ba_own, ba_got, mine, other, log_ref, grads, inner, payload, tails):
    core = place[0]
    half = mine.shape[1]
    tails[...] = jnp.zeros_like(tails)
    for h in range(4):
        at = slice(64 * h, 64 * h + 64)
        g_own, g_got = ba_own[at, :], ba_got[at, :]
        d_own = jnp.sum(g_own.astype(f32) * mine[at, :].astype(f32), axis=0, keepdims=True)
        d_got = jnp.sum(g_got.astype(f32) * other[at, :].astype(f32), axis=0, keepdims=True)

        def put(g0, g1, d0, d1):
            grads[h, :, :half] = g0
            grads[h, :, half:] = g1
            inner[h, :, :half] = jnp.broadcast_to(d0, (8, half))
            inner[h, :, half:] = jnp.broadcast_to(d1, (8, half))
            if h >= 2:
                for g, d, s in ((g0, d0, slice(0, half)), (g1, d1, slice(half, 2 * half))):
                    payload[64 * (h - 2) : 64 * (h - 1), s] = g
                    parts = three(log_ref[h, 0:1, s]) + three(d)
                    tails[8 * (h - 2) : 8 * (h - 2) + 6, s] = jnp.concatenate([part.astype(f32) for part in parts], 0)

        @pl.when(core == 0)
        def _():
            put(g_own, g_got, d_own, d_got)

        @pl.when(core == 1)
        def _():
            put(g_got, g_own, d_got, d_own)
    payload[128:144, :] = tails[...].astype(bf)


def ready(place, ba_own, ba_got, mine, other, log):
    half = mine.shape[1]
    return pl.pallas_call(
        ready_kernel,
        in_specs=[smem()] + [vmem()] * 5,
        out_specs=[vmem()] * 3,
        out_shape=[
            jax.ShapeDtypeStruct((4, 64, 2 * half), bf),
            jax.ShapeDtypeStruct((4, 8, 2 * half), f32),
            jax.ShapeDtypeStruct((144, 2 * half), bf),
        ],
        scratch_shapes=[pltpu.VMEM((16, 2 * half), f32)],
        compiler_params=params(),
        cost_estimate=cost(2),
    )(place, ba_own, ba_got, mine, other, log)


def back_block(kv_ref, kt_ref, q, grad, ratio, inner, block, kmax, first, put_kv):
    low = (grad.astype(f32) * ratio).astype(bf)
    rhs = jnp.concatenate([jnp.zeros((64, BQ), bf), low], axis=0)
    shift = inner * ratio
    natural = rhs.T
    acc = None
    for k0 in range(0, kmax, CH):
        dp = nn(kv_ref[k0 : k0 + CH, :], rhs)
        p = block(k0 // CH)
        ds = (p.astype(f32) * (dp - shift)).astype(bf)
        d = nn(kt_ref[:, k0 : k0 + CH], ds)
        acc = d if acc is None else acc + d
        put_kv(k0, k0 >= first, nn(ds, q) + nn(p, natural))
    return (acc * 0.125).astype(bf)


def near_backward_kernel(head, q_ref, kv_ref, p_ref, grad_ref, stat, log_ref, inner_ref, *refs):
    dkv_ref, dq_ref, kt_ref, buf, sems = refs[-5:]
    count = q_ref.shape[0] // BQ
    copies = []
    for i in range(count):
        at = slice(i * (i + 1) // 2, (i + 1) * (i + 2) // 2)
        copies.append(pltpu.make_async_copy(p_ref.at[head, at], buf.at[at], sems.at[i]))
        copies[-1].start()
    kt_ref[...] = kv_ref[...].T[0:64, :]

    def put(k0, fresh, value):
        if fresh:
            dkv_ref[k0 : k0 + CH, :] = value
        else:
            dkv_ref[k0 : k0 + CH, :] += value

    for i in range(count):
        at = slice(i * BQ, (i + 1) * BQ)
        base = i * (i + 1) // 2
        copies[i].wait()
        ratio = jnp.exp2(stat[0, 0:1, at] - log_ref[0, 0:1, at])

        def block(k):
            return buf[base + k]

        dq_ref[:, at] = back_block(
            kv_ref, kt_ref, q_ref[at, :], grad_ref[0, :, at], ratio, inner_ref[0, 0:1, at], block, (i + 1) * BQ, i * BQ, put
        )


def near_backward(h, qkv, p, grads, stat, log, inner, deps):
    n = qkv.shape[0]
    row = pl.BlockSpec((1, 8, n), lambda g: (h, 0, 0))
    return pl.pallas_call(
        functools.partial(near_backward_kernel, h % 2),
        grid=(1,),
        in_specs=[
            pl.BlockSpec((n, 128), lambda g: (0, 2 * h)),
            pl.BlockSpec((n, 128), lambda g: (0, 2 * h + 1)),
            hbm(),
            pl.BlockSpec((1, 64, n), lambda g: (h, 0, 0)),
            pl.BlockSpec((1, 8, n), lambda g: (h % 2, 0, 0)),
            row,
            row,
        ]
        + [anywhere()] * len(deps),
        out_specs=[pl.BlockSpec((n, 128), lambda g: (0, 0)), pl.BlockSpec((64, n), lambda g: (0, 0))],
        out_shape=[kept_out((n, 128), f32), kept_out((64, n), bf)],
        scratch_shapes=[pltpu.VMEM((64, n), bf), pltpu.VMEM(p.shape[1:], bf), pltpu.SemaphoreType.DMA((n // BQ,))],
        compiler_params=params(24),
        cost_estimate=cost(7),
    )(qkv, qkv, stay(p), grads, stat, log, inner, *deps)


def far_backward_kernel(
    j, place, q_ref, kv_ref, p_ref, stat, grad_own, log_own, inner_own, got, got_tail, dep, send_ref, keep_ref, kt_ref, sum_ref, dq_ref, buf, sems
):
    kt_ref[...] = kv_ref[...].T[0:64, :]
    upper = place[1] == 1
    n = q_ref.shape[0]
    copies = [pltpu.make_async_copy(p_ref.at[i], buf.at[i], sems.at[i]) for i in range(n // BQ)]
    for copy in copies:
        copy.start()

    def put(k0, fresh, value):
        if fresh:
            sum_ref[k0 : k0 + CH, :] = value
        else:
            sum_ref[k0 : k0 + CH, :] += value

    for i in range(n // BQ):
        at = slice(i * BQ, (i + 1) * BQ)
        got_log = got_tail[8 * j : 8 * j + 3, at].astype(f32)
        got_inner = got_tail[8 * j + 3 : 8 * j + 6, at].astype(f32)
        log = jnp.where(upper, log_own[0, 0:1, at], jnp.sum(got_log, axis=0, keepdims=True))
        inner = jnp.where(upper, inner_own[0, 0:1, at], jnp.sum(got_inner, axis=0, keepdims=True))
        grad = jnp.where(upper, grad_own[0, :, at], got[:, at])
        ratio = jnp.exp2(stat[0:1, at] - log)
        copies[i].wait()

        def block(k):
            return buf[i, k]

        dq = back_block(kv_ref, kt_ref, q_ref[at, :], grad, ratio, inner, block, n, 0 if i == 0 else n, put)
        dq_ref[at, :] = jnp.concatenate([dq, jnp.zeros((64, BQ), bf)], 0).T

    @pl.when(upper)
    def _():
        send_ref[...] = sum_ref[...].astype(bf)
        keep_ref[...] = dq_ref[...]

    @pl.when(jnp.logical_not(upper))
    def _():
        send_ref[...] = dq_ref[...]
        keep_ref[...] = sum_ref[...].astype(bf)


def far_backward(j, place, q, kv, p, stat, grads, log, inner, got, dep):
    n = q.shape[0]
    row = pl.BlockSpec((1, 8, n), lambda h: (j, 0, 0))
    whole = pl.BlockSpec((n, 128), lambda h: (0, 0))
    return pl.pallas_call(
        functools.partial(far_backward_kernel, j),
        grid=(1,),
        in_specs=[
            smem(),
            whole,
            whole,
            hbm(),
            pl.BlockSpec((8, n), lambda h: (0, 0)),
            pl.BlockSpec((1, 64, n), lambda h: (j, 0, 0)),
            row,
            row,
            pl.BlockSpec((64, n), lambda h: (j, 0)),
            pl.BlockSpec((16, n), lambda h: (8, 0)),
            pl.BlockSpec(memory_space=pl.ANY),
        ],
        out_specs=[whole, whole],
        out_shape=[jax.ShapeDtypeStruct((n, 128), bf)] * 2,
        scratch_shapes=[
            pltpu.VMEM((64, n), bf),
            pltpu.VMEM((n, 128), f32),
            pltpu.VMEM((n, 128), bf),
            pltpu.VMEM(p.shape, bf),
            pltpu.SemaphoreType.DMA((n // BQ,)),
        ],
        compiler_params=params(30),
        cost_estimate=cost(13),
    )(place, q, kv, stay(p), stat, grads, log, inner, got, got, dep)


def swap(value, bits):
    count = lax.axis_size("batch") * lax.axis_size("seq")
    return lax.ppermute(value, AXES, [(i, i ^ bits) for i in range(count)])


def turns():
    bits = (lax.axis_size("batch") // 2).bit_length() - 1
    return [(3 + t, 2 + bits - t) for t in range(bits)]


PLANE = [(1, 2), (2, 1)]


def swap_by_core(value, turn):
    count = lax.axis_size("batch") * lax.axis_size("seq")
    return lax.ppermute(value, AXES, [(i, i ^ (1 << turn[i % 2])) for i in range(count)])


def bit_of(number, core, turn):
    return (number >> jnp.where(core == 0, turn[0], turn[1])) & 1


def take(value, index, axis=0):
    return lax.dynamic_index_in_dim(value, index, axis, keepdims=False)


MOVES = ((0, 0), (1, 0), (0, 1), (1, 1))


def factors_kernel(place, fac, got, gout, got_out, dep, *outs):
    core, chip, side = place[0], place[1], place[2]
    groups = got.shape[0]
    width = gout.shape[2]
    part = (got.shape[1] - 2 * width) // 4
    rows = gout.shape[1] // 4
    for (x, y), out in zip(MOVES, outs):
        index = 2 * (chip ^ x) + (side ^ y)
        lanes = pl.ds(pl.multiple_of(2 * width + index * part, 128), part)
        at = pl.ds(pl.multiple_of(index * rows, rows), rows)
        out[0:groups, 0 : 2 * width] = fac[core, :, 0 : 2 * width]
        out[groups:, 0 : 2 * width] = got[:, 0 : 2 * width]
        out[0:groups, 2 * width : 2 * width + part] = fac[core, :, lanes]
        out[groups:, 2 * width : 2 * width + part] = got[:, lanes]
        out[:, 2 * width + part :] = (gout[core, at, :].astype(f32) + got_out[at, :].astype(f32)).astype(bf)


def factors(place, fac, got, gout, got_out, dep):
    groups, per = got.shape
    width = gout.shape[2]
    shape = jax.ShapeDtypeStruct((2 * groups, 2 * width + (per - 2 * width) // 4 + width), bf)
    return pl.pallas_call(
        factors_kernel,
        in_specs=[smem()] + [vmem()] * 4 + [anywhere()],
        out_specs=[vmem()] * 4,
        out_shape=[shape] * 4,
        compiler_params=params(),
        cost_estimate=cost(2),
    )(place, fac, got, gout, got_out, dep)


def slab_kernel(turn, lines, place, dep, a, b, c, d, keep, send):
    core, line = place[0], place[3]
    width = keep.shape[2]
    quarter = (a.shape[1] - 3 * width) // 2

    def lanes(start, size):
        return jnp.concatenate([ref[:, start : start + size] for ref in (a, b, c, d)], 0)

    g_in = tn(lanes(0, width), lanes(2 * width, quarter)).astype(bf)
    g_down = tn(lanes(2 * width + quarter, quarter), lanes(width, width)).astype(bf)
    total = a[:, 2 * width + 2 * quarter :].astype(f32)
    for ref in (b, c, d):
        total = total + ref[:, 2 * width + 2 * quarter :].astype(f32)
    pieces = [total.astype(bf), g_in, g_down]
    bits = lines.bit_length() - 1
    for z in range(lines):
        flipped = sum(((z >> t) & 1) << (bits - 1 - t) for t in range(bits))
        spot = jnp.where(core == 0, flipped, z)
        chosen = bit_of(8 * z, core, turn) == bit_of(8 * line, core, turn)

        def put(ref):
            start = 0
            for piece in pieces[1:] + pieces[:1]:
                rows = piece.shape[0] // lines
                ref[spot % (lines // 2), start : start + rows, :] = piece[z * rows : (z + 1) * rows, :]
                start += rows

        @pl.when(chosen)
        def _():
            put(keep)

        @pl.when(jnp.logical_not(chosen))
        def _():
            put(send)


def slabs(place, dep, payloads, width, quarter, lines):
    rows = (width + quarter + payloads[0].shape[0]) // lines
    shape = jax.ShapeDtypeStruct((lines // 2, rows, width), bf)
    turn = turns()[0]
    return pl.pallas_call(
        lambda *refs: slab_kernel(turn, lines, *refs),
        in_specs=[smem(), anywhere()] + [vmem()] * 4,
        out_specs=[vmem()] * 2,
        out_shape=[shape] * 2,
        compiler_params=params(),
        cost_estimate=cost(2),
    )(place, stay(dep), *payloads)


def fold_kernel(turn, place, dep, kept, got, keep, *send):
    if turn is None:
        keep[...] = (kept[...].astype(f32) + got[...].astype(f32)).astype(bf)
        return
    half = keep.shape[0]
    mine = bit_of(place[4], place[0], turn)
    at = pl.ds(mine * half, half)
    keep[...] = (kept[at].astype(f32) + got[at].astype(f32)).astype(bf)
    at = pl.ds((1 - mine) * half, half)
    send[0][...] = (kept[at].astype(f32) + got[at].astype(f32)).astype(bf)


def fold(turn, place, dep, kept, got):
    count = kept.shape[0] if turn is None else kept.shape[0] // 2
    shape = jax.ShapeDtypeStruct((count,) + kept.shape[1:], bf)
    outs = 1 if turn is None else 2
    return pl.pallas_call(
        lambda *refs: fold_kernel(turn, *refs),
        in_specs=[smem(), anywhere(), vmem(), vmem()],
        out_specs=[vmem()] * outs,
        out_shape=[shape] * outs,
        compiler_params=params(),
        cost_estimate=cost(1),
    )(place, dep, kept, got)


def pile_kernel(a, b, *refs):
    out = refs[-1]
    half = out.shape[0] // 2
    out[:half] = a[...]
    out[half:] = b[...]


def pile(a, b, *deps):
    return pl.pallas_call(
        pile_kernel,
        in_specs=[vmem(), vmem()] + [anywhere()] * len(deps),
        out_specs=vmem(),
        out_shape=jax.ShapeDtypeStruct((2 * a.shape[0],) + a.shape[1:], bf),
        compiler_params=params(),
        cost_estimate=cost(1),
    )(a, b, *deps)


def add_kernel(values, pieces, place, *refs):
    total = refs[0][...].astype(f32)
    for ref in refs[1:values]:
        total = total + ref[...].astype(f32)
    outs = refs[len(refs) - pieces :]
    if pieces == 1:
        outs[0][...] = total.astype(bf)
        return
    total = total.astype(bf)
    rows = outs[0].shape[0]
    for z in range(pieces):
        for k in range(pieces):

            @pl.when((place[3] ^ k) == z)
            def _():
                outs[k][...] = total[z * rows : (z + 1) * rows]


def add(place, values, pieces, *deps):
    rows, lanes = values[0].shape
    return pl.pallas_call(
        functools.partial(add_kernel, len(values), pieces),
        in_specs=[smem()] + [vmem()] * len(values) + [anywhere()] * len(deps),
        out_specs=[vmem()] * pieces,
        out_shape=[jax.ShapeDtypeStruct((rows // pieces, lanes), bf)] * pieces,
        compiler_params=params(),
        cost_estimate=cost(1),
    )(place, *values, *deps)


def stack_kernel(count, *refs):
    for k in range(count):
        refs[-1][k] = refs[k][...]


def stack(values, *deps):
    return pl.pallas_call(
        functools.partial(stack_kernel, len(values)),
        in_specs=[vmem()] * len(values) + [anywhere()] * len(deps),
        out_specs=vmem(),
        out_shape=jax.ShapeDtypeStruct((len(values),) + values[0].shape, bf),
        compiler_params=params(),
        cost_estimate=cost(1),
    )(*values, *deps)


def gate_kernel(value, *refs):
    pass


def gate(value, *deps):
    return pl.pallas_call(
        gate_kernel,
        in_specs=[anywhere()] * (1 + len(deps)),
        out_specs=anywhere(),
        out_shape=jax.ShapeDtypeStruct(value.shape, value.dtype),
        input_output_aliases={0: 0},
        compiler_params=params(1),
        cost_estimate=cost(1),
    )(value, *deps)


def spread_kernel(place, near, far, *refs):
    in_ref, down_ref, out_ref = refs[-3:]
    expert = pl.program_id(0)
    line = place[3]
    lines = near.shape[1]
    width = in_ref.shape[1]
    cut_in = width // lines
    cut_down = down_ref.shape[1] // lines
    bits = lines.bit_length() - 1

    def put(ref):
        for k in range(lines):
            flipped = sum(((k >> t) & 1) << (bits - 1 - t) for t in range(bits))
            z = line ^ jnp.where(expert == 0, flipped, k)
            in_ref[0, pl.ds(pl.multiple_of(z * cut_in, cut_in), cut_in), :] = ref[0, k, :cut_in].astype(f32)
            down_ref[0, pl.ds(pl.multiple_of(z * cut_down, cut_down), cut_down), :] = ref[0, k, cut_in : cut_in + cut_down].astype(f32)
            out_ref[0, z] = ref[0, k, cut_in + cut_down :].astype(f32)

    @pl.when(expert == place[0])
    def _():
        put(near)

    @pl.when(expert != place[0])
    def _():
        put(far)


def spread_experts(outer, place, near, far, hidden, width, earlier, *deps):
    block = near.shape[1:]
    lines = block[0]

    def spec(is_near):
        def index(e, i, p):
            return (jnp.where((e == p[0]) == is_near, i, 0), 0, 0, 0)

        return pl.BlockSpec((1,) + block, index)

    def quarter(e, i, p):
        move_x, move_y = jnp.where(e == 0, i, outer), jnp.where(e == 0, outer, i)
        return 2 * (p[1] ^ move_x) + (p[2] ^ move_y)

    return pl.pallas_call(
        spread_kernel,
        grid_spec=pltpu.PrefetchScalarGridSpec(
            num_scalar_prefetch=1,
            grid=(2, 2),
            in_specs=[spec(True), spec(False)] + [anywhere()] * (len(earlier) + len(deps)),
            out_specs=[
                pl.BlockSpec((1, width, hidden // 4), lambda e, i, p: (e, 0, quarter(e, i, p))),
                pl.BlockSpec((1, hidden // 4, width), lambda e, i, p: (e, quarter(e, i, p), 0)),
                pl.BlockSpec((1, lines, width // 8 // lines, width), lambda e, i, p: (e * 4 + quarter(e, i, p), 0, 0, 0)),
            ],
        ),
        out_shape=[
            kept_out((2, width, hidden), f32),
            kept_out((2, hidden, width), f32),
            kept_out((8, lines, width // 8 // lines, width), f32),
        ],
        input_output_aliases={3: 0, 4: 1, 5: 2} if earlier else {},
        compiler_params=params(28),
        cost_estimate=cost(6),
    )(place, near, far, *earlier, *deps)


def own_block(b, p):
    return jnp.where(b // 2 == p[0], b % 2, jnp.where(b // 2 > p[0], 1, 0))


def other_block(b, p):
    return jnp.where(b // 2 != p[0], b % 2, jnp.where(b // 2 > 1 - p[0], 1, 0))


def collect_kernel(
    place, normed, kv_a, kv_b, kv_c, kv_d, q_a, q_b, q_c, q_d, keep_a, keep_b, got_a, got_b, packs, gain, tiny, dep,
    mine, other, slab_0, slab_1, slab_2, slab_3, sum_ref,
):
    block = pl.program_id(0)
    core, chip, side = place[0], place[1], place[2]
    upper = chip == 1
    dq = jnp.concatenate([q_a[...], q_b[...], q_c[...], q_d[...]], 0).T.astype(f32)
    far = jnp.concatenate([left(keep_a[...], keep_b[...]), left(got_a[...], got_b[...])], 1).astype(f32)
    pieces = [(dq + jnp.where(upper, far, 0.0)).astype(bf)]
    for near, extra in ((kv_a, got_a), (kv_b, got_b), (kv_c, keep_a), (kv_d, keep_b)):
        value = near[...] + jnp.where(upper, 0.0, extra[...].astype(f32))
        pieces.append(jnp.where(lanes_of(value.shape) < 64, value * 0.125, value).astype(bf))
    back = jnp.concatenate(pieces, 1)

    @pl.when(block // 2 == core)
    def _():
        mine[...] = back

    @pl.when(block // 2 != core)
    def _():
        other[...] = back

    part = tn(normed[...], back)

    @pl.when(block == 0)
    def _():
        sum_ref[...] = part

    @pl.when(block > 0)
    def _():
        sum_ref[...] += part

    @pl.when(block == 3)
    def _():
        total = sum_ref[...]
        width, wide = total.shape
        product = jnp.sum(total * packs[core].astype(f32), axis=1, keepdims=True)
        small = tiny[...].T
        small = jnp.concatenate([small, jnp.zeros((width, 120), f32)], 1)
        lanes = lanes_of(small.shape)
        small = jnp.where(lanes == 3, product / gain[...].T, small)
        high = small.astype(bf)
        low = (small - high.astype(f32)).astype(bf)
        small = jnp.where(lanes < 8, high.astype(f32), pltpu.roll(low.astype(f32), 8, axis=1)).astype(bf)
        low = total.astype(bf)
        rows = width // 4
        for (move_x, move_y), ref in zip(MOVES, (slab_0, slab_1, slab_2, slab_3)):
            for q in range(4):

                @pl.when(2 * (chip ^ move_x) + (side ^ move_y) == q)
                def _():
                    ref[:, :wide] = low[q * rows : (q + 1) * rows]
                    ref[:, wide:] = small[q * rows : (q + 1) * rows]


def collect(place, normed, kvs, qs, keep_a, keep_b, got_a, got_b, packs, gain, tiny, dep):
    n, width = normed.shape
    rows = n // 4
    dq = pl.BlockSpec((64, rows), lambda b, p: (0, b))
    flat = pl.BlockSpec((rows, 128), lambda b, p: (b, 0))
    slab = (width // 4, 896)
    return pl.pallas_call(
        collect_kernel,
        grid_spec=pltpu.PrefetchScalarGridSpec(
            num_scalar_prefetch=1,
            grid=(4,),
            in_specs=[pl.BlockSpec((rows, width), lambda b, p: (b, 0))]
            + [flat] * 4
            + [dq] * 4
            + [flat] * 4
            + [
                pl.BlockSpec(packs.shape, lambda b, p: (0, 0, 0)),
                pl.BlockSpec((1, width), lambda b, p: (0, 0)),
                pl.BlockSpec(tiny.shape, lambda b, p: (0, 0)),
                anywhere(),
            ],
            out_specs=[
                pl.BlockSpec((rows, 768), lambda b, p: (own_block(b, p), 0)),
                pl.BlockSpec((rows, 768), lambda b, p: (other_block(b, p), 0)),
            ]
            + [pl.BlockSpec(slab, lambda b, p: (0, 0))] * 4,
            scratch_shapes=[pltpu.VMEM((width, 768), f32)],
        ),
        out_shape=[
            jax.ShapeDtypeStruct((n // 2, 768), bf),
            jax.ShapeDtypeStruct((n // 2, 768), bf),
        ]
        + [jax.ShapeDtypeStruct(slab, bf)] * 4,
        compiler_params=params(26),
        cost_estimate=cost(5),
    )(place, stay(normed), *kvs[:3], stay(kvs[3]), *qs, keep_a, keep_b, got_a, got_b, stay(packs), gain, tiny, dep)


def tokens_kernel(place, mine, got, packs, x_ref, back_resid, gain, dep, out):
    core = place[0]
    back = nt(mine[...], packs[core]) + nt(got[...], packs[1 - core])
    x = x_ref[...].astype(f32)
    inverse = lax.rsqrt(jnp.mean(x * x, axis=1, keepdims=True) + EPSILON)
    k = back * gain[...]
    mean = jnp.mean(k * x, axis=1, keepdims=True)
    out[...] = (back_resid[...] + inverse * k - x * (inverse * inverse * inverse * mean)).astype(bf)


def tokens_back(place, mine, got, packs, x, back_resid, gain, dep):
    n, width = x.shape
    rows = n // 4
    wide = pl.BlockSpec((rows, 768), lambda b, p: (b, 0))
    block = pl.BlockSpec((rows, width), lambda b, p: (b, 0))
    return pl.pallas_call(
        tokens_kernel,
        grid_spec=pltpu.PrefetchScalarGridSpec(
            num_scalar_prefetch=1,
            grid=(4,),
            in_specs=[wide, wide, pl.BlockSpec(packs.shape, lambda b, p: (0, 0, 0)), block, block, pl.BlockSpec((1, width), lambda b, p: (0, 0)), anywhere()],
            out_specs=block,
        ),
        out_shape=kept_out((n, width), bf),
        compiler_params=params(20),
        cost_estimate=cost(4),
    )(place, mine, got, stay(packs), stay(x), stay(back_resid), gain, dep)


def unfold_kernel(place, *refs):
    out, rows_out, small_ref = refs[-3:]
    core, line = place[0], place[3]
    lines, rows = refs[0].shape[1], refs[0].shape[2]
    block = pl.program_id(0)

    def put(source, c, fresh):
        for k in range(lines):
            at = pl.ds(pl.multiple_of((line ^ k) * rows, rows), rows)
            value = source[k]
            base = c * 256
            out[at, pl.ds(pl.multiple_of(base, 128), 256)] = value[:, 0:256].astype(f32)
            for pair in range(2):
                a = value[:, 256 + 256 * pair : 384 + 256 * pair]
                b = value[:, 384 + 256 * pair : 512 + 256 * pair]
                out[at, pl.ds(pl.multiple_of(512 + base + 128 * pair, 128), 128)] = left(a, b).astype(f32)
                out[at, pl.ds(pl.multiple_of(1024 + base + 128 * pair, 128), 128)] = right(a, b).astype(f32)
            small = value[:, 768:].astype(f32)
            small = small + pltpu.roll(small, 120, axis=1)
            small_ref[at, :] = small if fresh else small_ref[at, :] + small

    for i in range(4):

        @pl.when(block == i)
        def _():
            put(refs[0].at[i], core, True)
            put(refs[1].at[i], 1 - core, False)
            rows_out[...] = small_ref[...].T[0:8, :]


def unfold(place, near, far, width):
    whole = pl.BlockSpec(near.shape, lambda i, p: (0, 0, 0, 0))

    def at(i, p):
        return ((2 * p[1] + p[2]) ^ ((i % 2) * 2 + i // 2), 0)

    def across(i, p):
        return at(i, p)[::-1]

    return pl.pallas_call(
        unfold_kernel,
        grid_spec=pltpu.PrefetchScalarGridSpec(
            num_scalar_prefetch=1,
            grid=(4,),
            in_specs=[whole] * 2,
            out_specs=[pl.BlockSpec((width // 4, 3 * width), at), pl.BlockSpec((8, width // 4), across)],
            scratch_shapes=[pltpu.VMEM((width // 4, 128), f32)],
        ),
        out_shape=[kept_out((width, 3 * width), f32), jax.ShapeDtypeStruct((8, width), f32)],
        compiler_params=params(16),
        cost_estimate=cost(3),
    )(place, near, far)


def body(
    layer_activations,
    sequence_extents,
    position_cluster_label,
    cluster_sharpness,
    heed_scale_factor,
    triple_entry_matrix,
    heed_exit_matrix,
    blend_scale_factor,
    router_matrix,
    specialist_entry_matrix,
    specialist_exit_matrix,
    upstream_derivative,
):
    seq_count, pos_count, width = layer_activations.shape
    tokens = seq_count * pos_count
    hidden = specialist_entry_matrix.shape[2]
    spot = lax.axis_index("seq")
    row = lax.axis_index("batch")
    core, chip, side, line = spot % 2, spot // 2, row % 2, row // 2
    lines = lax.axis_size("batch") // 2
    place = jnp.stack([core, chip, side, line, row * 4 + spot]).astype(jnp.int32)
    core_pairs, chip_pairs = [(0, 1), (1, 0), (2, 3), (3, 2)], [(0, 2), (1, 3), (2, 0), (3, 1)]
    up, down = chip_pairs[:2], chip_pairs[2:]

    x = layer_activations.reshape(tokens, width)
    x_other = lax.ppermute(x, "seq", core_pairs)
    packs, w_own, router, gains = pack(
        place, triple_entry_matrix, router_matrix.T, heed_scale_factor, blend_scale_factor
    )
    gain_a, gain_m = gains[0], gains[1]
    normed, qkv, send_a, send_b = project(place, x, x_other, gain_a, w_own)
    got_a = lax.ppermute(send_a, "seq", chip_pairs)
    got_b = lax.ppermute(send_b, "seq", up)
    limit = (sequence_extents - chip * 2 * pos_count).astype(jnp.int32)
    p_na, o_na, st_na = near_forward(0, limit, qkv, qkv)
    p_a, o_a, st_a, q_a, kv_a = far_forward(0, place, qkv, got_a, got_a, o_na)
    got_oa = lax.ppermute(o_a, "seq", up)
    p_b, o_b, st_b, q_b, kv_b = far_forward(1, place, qkv, got_a, got_b, o_a)
    got_ob = lax.ppermute(o_b, "seq", up)
    p_nb, o_nb, st_nb = near_forward(1, limit, qkv, o_b)
    att_mine, att_send, log = join(place, o_na, o_nb, st_na, st_nb, o_a, o_b, got_oa, got_ob)
    att_got = lax.ppermute(att_send, "seq", core_pairs)

    block_out, fac, gout, tiny, back_resid, ba_own, ba_send = mixture(
        place,
        cluster_sharpness,
        x,
        att_mine,
        att_got,
        heed_exit_matrix,
        gain_m,
        router,
        position_cluster_label.reshape(1, tokens),
        upstream_derivative.reshape(tokens, width),
        specialist_entry_matrix,
        specialist_exit_matrix,
    )

    ba_got = lax.ppermute(ba_send, "seq", core_pairs)
    fac_got = swap(take(fac, 1 - core), 1)
    gout_got = swap(take(gout, 1 - core), 1)
    grads, inner, payload = ready(place, ba_own, ba_got, att_mine, att_send, log)
    got_grad = lax.ppermute(payload, "seq", down)
    pay = factors(place, fac, fac_got, gout, gout_got, payload)
    pays = [pay[0]] + [swap(pay[i], 2 * m[0] + 4 * m[1]) for i, m in list(enumerate(MOVES))[1:]]
    def near(h, dep):
        p, stat = ((p_na, st_na), (p_nb, st_nb))[h // 2]
        return near_backward(h, qkv, p, grads, stat, log, inner, dep)

    kv_0, dq_0 = near(0, (pay[0],))
    kv_1, dq_1 = near(1, (stay(dq_0),))
    stages = turns()
    kept, sent = slabs(place, dq_1, pays, width, hidden // 4, lines)
    send_fa, keep_fa = far_backward(0, place, q_a, kv_a, p_a, st_a, grads, log, inner, got_grad, kept)
    got_fa = lax.ppermute(send_fa, "seq", chip_pairs)
    for t, turn in enumerate(stages):
        got = swap_by_core(sent, turn)
        if t == len(stages) - 1:
            send_fb, keep_fb = far_backward(1, place, q_b, kv_b, p_b, st_b, grads, log, inner, got_grad, kept)
            got_fb = lax.ppermute(send_fb, "seq", chip_pairs)
            whole = fold(None, place, keep_fb, kept, got)[0]
        else:
            kept, sent = fold(stages[t + 1], place, keep_fa, kept, got)
    kv_2, dq_2 = near(2, (whole,))
    for turn in stages[:0:-1]:
        whole = pile(whole, swap_by_core(whole, turn), stay(dq_2))
    got = swap_by_core(whole, stages[0])
    kv_3, dq_3 = near(3, (whole, got_fa))
    whole = pile(whole, got, stay(dq_3), got_fb)
    got_first = swap_by_core(whole, PLANE[0])
    d_mine, d_send, *parts = collect(
        place, normed, (kv_0, kv_1, kv_2, kv_3), (dq_0, dq_1, dq_2, dq_3), keep_fa, keep_fb, got_fa, got_fb, packs, gain_a, tiny, whole
    )

    moves = [2 * m[0] + 4 * m[1] for m in MOVES]
    parts = parts[:1] + [swap(part, bits) for part, bits in list(zip(parts, moves))[1:]]
    d_got = lax.ppermute(d_send, "seq", core_pairs)
    parts = list(add(place, parts, lines))
    whole = pile(whole, got_first, parts[0])
    got_second = swap_by_core(whole, PLANE[1])
    far_first = swap(whole, 1)
    tokens_grad = tokens_back(place, d_mine, d_got, packs, x, back_resid, gain_a, whole)
    parts = parts[:1] + [swap(part, 8 * k) for k, part in list(enumerate(parts))[1:]]
    part = add(place, parts, 1, stay(tokens_grad))[0]
    block = (2, lines) + whole.shape[1:]
    halves = spread_experts(0, place, whole.reshape(block), far_first.reshape(block), hidden, width, (), part)
    zs = stack([part] + [swap(part, 8 * k) for k in range(1, lines)], stay(halves[2]))
    pieces = [zs] + [swap(zs, bits) for bits in moves[1:]]
    got_second = gate(got_second, zs)
    far_second = swap(got_second, 1)
    grad_in, grad_down, grad_out = spread_experts(
        1, place, got_second.reshape(block), far_second.reshape(block), hidden, width, tuple(halves)
    )
    pieces = stack(pieces, stay(grad_out))
    grad_qkv, small = unfold(place, pieces, swap(pieces, 1), width)
    return (
        block_out.reshape(layer_activations.shape),
        tokens_grad.reshape(layer_activations.shape),
        small[3],
        grad_qkv,
        grad_out.reshape(width, width),
        small[2],
        small[0:2].T,
        grad_in,
        grad_down,
    )


def solution(mesh):
    rows = P("batch", "seq", None)
    placed = (rows, P("batch"), P("batch", "seq")) + (P(),) * 8 + (rows,)
    return jax.shard_map(body, mesh=mesh, in_specs=placed, out_specs=(rows, rows) + (P(),) * 7, check_vma=False)
```

```python
import functools

import jax
import jax.numpy as jnp
from jax import lax
from jax.experimental import pallas as pl
from jax.experimental.pallas import tpu as pltpu
from jax.sharding import PartitionSpec as P

HEADS = 8
HEAD = 64
GROUP = 32
EPSILON = 1e-06
LOG2E = 1.4426950408889634
SC = 0.125 * LOG2E
MASKED = -1e30
BQ = 512
CH = 512
bf = jnp.bfloat16
f32 = jnp.float32
AXES = ("batch", "seq")
NT = (((1,), (1,)), ((), ()))
TN = (((0,), (0,)), ((), ()))


def nt(a, b):
    return lax.dot_general(a, b, NT, preferred_element_type=f32)


def tn(a, b):
    return lax.dot_general(a, b, TN, preferred_element_type=f32)


def nn(a, b):
    return jnp.dot(a, b, preferred_element_type=f32)


def rows_of(shape):
    return lax.broadcasted_iota(jnp.int32, shape, 0)


def lanes_of(shape):
    return lax.broadcasted_iota(jnp.int32, shape, 1)


def vmem():
    return pl.BlockSpec(memory_space=pltpu.VMEM)


def smem():
    return pl.BlockSpec(memory_space=pltpu.SMEM)


def params(mib=16):
    return pltpu.CompilerParams(vmem_limit_bytes=mib * 2**20)


def anywhere():
    return pl.BlockSpec(memory_space=pl.ANY)


def hbm():
    return pl.BlockSpec(memory_space=pltpu.HBM)


def cost(us):
    return pl.CostEstimate(flops=int(us * 1e8), bytes_accessed=2**10, transcendentals=0)


def stay(value):
    return pltpu.with_memory_space_constraint(value, pltpu.HBM)


def kept_out(shape, dtype):
    return pltpu.HBM(shape, dtype)


def shift_lanes(value):
    return pltpu.roll(value.astype(f32), 64, axis=1).astype(bf)


def left(first, second):
    return jnp.where(lanes_of(first.shape) < 64, first, shift_lanes(second))


def right(first, second):
    return jnp.where(lanes_of(first.shape) < 64, shift_lanes(first), second)


def pack_kernel(place, w, router, gain_a, gain_m, packs, w_own, router_rows, gains):
    core = place[0]
    both = router[...].astype(f32)
    rows = rows_of(router_rows.shape)
    router_rows[...] = jnp.where(rows == 0, both[0:1, :], jnp.where(rows == 1, both[1:2, :], 0.0)).astype(bf)
    gains[0] = gain_a[...].astype(f32).reshape(1, -1)
    gains[1] = gain_m[...].astype(f32).reshape(1, -1)
    for c in range(2):
        packs[c, :, 0:256] = w[:, 256 * c : 256 * c + 256]
        for h in range(4):
            at = 256 * c + 128 * (h // 2)
            k = w[:, 512 + at : 640 + at]
            v = w[:, 1024 + at : 1152 + at]
            packs[c, :, 256 + 128 * h : 384 + 128 * h] = left(k, v) if h % 2 == 0 else right(k, v)
    for h in range(4):
        q = packs[core, :, 128 * (h // 2) : 128 * (h // 2) + 128]
        q = q if h % 2 == 0 else shift_lanes(q)
        w_own[:, 256 * h : 256 * h + 128] = jnp.where(lanes_of(q.shape) < 64, q, jnp.zeros((), bf))
        w_own[:, 256 * h + 128 : 256 * h + 256] = packs[core, :, 256 + 128 * h : 384 + 128 * h]


def pack(place, w, router, gain_a, gain_m):
    width = w.shape[0]
    return pl.pallas_call(
        pack_kernel,
        in_specs=[smem()] + [vmem()] * 4,
        out_specs=[vmem()] * 4,
        out_shape=[
            kept_out((2, width, 768), bf),
            jax.ShapeDtypeStruct((width, 1024), bf),
            jax.ShapeDtypeStruct((16, width), bf),
            jax.ShapeDtypeStruct((2, 1, width), f32),
        ],
        compiler_params=params(16),
        cost_estimate=cost(3),
    )(place, stay(w), stay(router), stay(gain_a), stay(gain_m))


def project_kernel(place, x_own, x_other, gain, w_own, normed, qkv, send_a, send_b):
    core, chip = place[0], place[1]
    block = pl.program_id(0)

    def go(x_ref):
        x = x_ref[...].astype(f32)
        inverse = lax.rsqrt(jnp.mean(x * x, axis=1, keepdims=True) + EPSILON)
        low = (x * inverse * gain[...]).astype(bf)
        normed[...] = low
        out = nn(low, w_own[...]).astype(bf)
        qkv[...] = out
        send_b[...] = out[:, 384:512]

        @pl.when(chip == 0)
        def _():
            send_a[...] = out[:, 128:256]

        @pl.when(chip == 1)
        def _():
            send_a[...] = left(out[:, 512:640], out[:, 768:896])

    @pl.when(block // 2 == core)
    def _():
        go(x_own)

    @pl.when(block // 2 != core)
    def _():
        go(x_other)


def project(place, x_own, x_other, gain, w_own):
    rows, width = x_own.shape

    def own(b, p):
        return (jnp.where(b // 2 == p[0], b % 2, jnp.where(b // 2 > p[0], 1, 0)), 0)

    def other(b, p):
        return (jnp.where(b // 2 != p[0], b % 2, jnp.where(b // 2 > 1 - p[0], 1, 0)), 0)

    half = rows // 2
    return pl.pallas_call(
        project_kernel,
        grid_spec=pltpu.PrefetchScalarGridSpec(
            num_scalar_prefetch=1,
            grid=(4,),
            in_specs=[
                pl.BlockSpec((half, width), own),
                pl.BlockSpec((half, width), other),
                pl.BlockSpec((1, width), lambda b, p: (0, 0)),
                pl.BlockSpec((width, 1024), lambda b, p: (0, 0)),
            ],
            out_specs=[
                pl.BlockSpec((half, width), lambda b, p: (b, 0)),
                pl.BlockSpec((half, 1024), lambda b, p: (b, 0)),
                pl.BlockSpec((half, 128), lambda b, p: (b, 0)),
                pl.BlockSpec((half, 128), lambda b, p: (b, 0)),
            ],
        ),
        out_shape=[
            kept_out((2 * rows, width), bf),
            kept_out((2 * rows, 1024), bf),
            jax.ShapeDtypeStruct((2 * rows, 128), bf),
            jax.ShapeDtypeStruct((2 * rows, 128), bf),
        ],
        compiler_params=params(20),
        cost_estimate=cost(4),
    )(place, x_own, x_other, gain, w_own)


def scores(kv, q, s_ref, slot, kmax, q0, limit, causal):
    peak = None
    for k0 in range(0, kmax, CH):
        s = nt(kv[k0 : k0 + CH, :], q)
        if causal:
            if k0 >= 1024:
                s = jnp.where(rows_of(s.shape) + k0 < limit, s, MASKED)
            if k0 + CH > q0:
                s = jnp.where(rows_of(s.shape) + (k0 - q0) <= lanes_of(s.shape), s, MASKED)
        s_ref[slot, k0 : k0 + CH, :] = s
        m = jnp.max(s, axis=0, keepdims=True)
        peak = m if peak is None else jnp.maximum(peak, m)
    return peak


def weigh(vt, s_ref, slot, peak, kmax, put):
    scaled = peak * SC
    acc = None
    for k0 in range(0, kmax, CH):
        p = jnp.exp2(s_ref[slot, k0 : k0 + CH, :] * SC - scaled).astype(bf)
        put(k0 // CH, p)
        d = nn(vt[:, k0 : k0 + CH], p)
        acc = d if acc is None else acc + d
    total = acc[0:1, :]
    return acc[64:128, :] * (1.0 / total), scaled, total


def ones_and_values(kv):
    vt = kv.T
    return jnp.where(rows_of(vt.shape) < 64, jnp.ones((), bf), vt)


def near_forward_kernel(limit_ref, qkv, dep, p_ref, o_ref, st_ref, s_ref, vt_ref, buf, sems):
    limit = limit_ref[0]
    count = qkv.shape[0] // BQ
    tasks = [(h, i) for h in range(2) for i in range(count)]

    def start_scores(at):
        h, i = tasks[at]
        kv = qkv.at[:, 256 * h + 128 : 256 * h + 256]
        q = qkv[i * BQ : (i + 1) * BQ, 256 * h : 256 * h + 128]
        return scores(kv, q, s_ref, at % 2, (i + 1) * BQ, i * BQ, limit, True)

    copies = []
    peak = start_scores(0)
    for at, (h, i) in enumerate(tasks):
        if i == 0:
            vt_ref[h] = ones_and_values(qkv[:, 256 * h + 128 : 256 * h + 256])
        later = start_scores(at + 1) if at + 1 < len(tasks) else None
        base = i * (i + 1) // 2

        def put(k, p):
            buf[h, base + k] = p

        out, scaled, total = weigh(vt_ref.at[h], s_ref, at % 2, peak, (i + 1) * BQ, put)
        copies.append(pltpu.make_async_copy(buf.at[h, base : base + i + 1], p_ref.at[h, base : base + i + 1], sems.at[h, i]))
        copies[-1].start()
        o_ref[h, :, i * BQ : (i + 1) * BQ] = out.astype(bf)
        st_ref[h, 0:1, i * BQ : (i + 1) * BQ] = scaled
        st_ref[h, 1:2, i * BQ : (i + 1) * BQ] = total
        peak = later
    for copy in copies:
        copy.wait()


def near_forward(pair, limit, qkv, dep):
    n = qkv.shape[0]
    count = n // BQ
    shape = (2, count * (count + 1) // 2, CH, BQ)
    return pl.pallas_call(
        near_forward_kernel,
        grid=(1,),
        in_specs=[smem(), pl.BlockSpec((n, 512), lambda g: (0, pair)), anywhere()],
        out_specs=[
            anywhere(),
            pl.BlockSpec((2, 64, n), lambda g: (0, 0, 0)),
            pl.BlockSpec((2, 8, n), lambda g: (0, 0, 0)),
        ],
        out_shape=[
            kept_out(shape, bf),
            jax.ShapeDtypeStruct((2, 64, n), bf),
            jax.ShapeDtypeStruct((2, 8, n), f32),
        ],
        scratch_shapes=[
            pltpu.VMEM((2, n, BQ), f32),
            pltpu.VMEM((2, 128, n), bf),
            pltpu.VMEM(shape, bf),
            pltpu.SemaphoreType.DMA((2, count)),
        ],
        compiler_params=params(34),
        cost_estimate=cost(9),
    )(limit, stay(qkv) if pair == 0 else qkv, dep)


def three(value):
    high = value.astype(bf)
    rest = value - high.astype(f32)
    mid = rest.astype(bf)
    return high, mid, (rest - mid.astype(f32)).astype(bf)


def far_forward_kernel(j, place, q_own, q_got, kv_own, kv_got, dep, p_ref, o_ref, st_ref, q_ref, kv_ref, s_ref, vt_ref, buf, sems):
    n = q_own.shape[0]

    @pl.when(place[1] == 1)
    def _():
        q_ref[...] = q_own[...]
        kv_ref[...] = kv_got[...]

    @pl.when(place[1] == 0)
    def _():
        q = q_got[...] if j == 0 else shift_lanes(q_got[...])
        q_ref[...] = jnp.where(lanes_of(q.shape) < 64, q, jnp.zeros((), bf))
        kv_ref[...] = kv_own[...]

    vt_ref[...] = ones_and_values(kv_ref[...])
    count = n // BQ
    copies = []
    peak = scores(kv_ref, q_ref[0:BQ, :], s_ref, 0, n, 0, None, False)
    for i in range(count):
        later = None
        at = slice(i * BQ, (i + 1) * BQ)
        if i + 1 < count:
            later = scores(kv_ref, q_ref[(i + 1) * BQ : (i + 2) * BQ, :], s_ref, (i + 1) % 2, n, 0, None, False)

        def put(k, p):
            buf[i, k] = p

        out, scaled, total = weigh(vt_ref, s_ref, i % 2, peak, n, put)
        copies.append(pltpu.make_async_copy(buf.at[i], p_ref.at[i], sems.at[i]))
        copies[-1].start()
        o_ref[0:64, at] = out.astype(bf)
        high, mid, low = three(scaled + jnp.log(total) * LOG2E)
        tail = jnp.concatenate([high.astype(f32), mid.astype(f32), low.astype(f32), jnp.zeros((13, BQ), f32)], 0)
        o_ref[64:80, at] = tail.astype(bf)
        st_ref[0:1, at] = scaled
        peak = later
    for copy in copies:
        copy.wait()


def far_forward(j, place, qkv, q_got, kv_got, dep):
    n = qkv.shape[0]
    whole = pl.BlockSpec((n, 128), lambda h: (0, 0))
    shape = (n // BQ, n // CH, CH, BQ)
    return pl.pallas_call(
        lambda *refs: far_forward_kernel(j, *refs),
        grid=(1,),
        in_specs=[
            smem(),
            pl.BlockSpec((n, 128), lambda h: (0, 2 * j)),
            whole,
            pl.BlockSpec((n, 128), lambda h: (0, 2 * j + 5)),
            whole,
            anywhere(),
        ],
        out_specs=[
            anywhere(),
            pl.BlockSpec((80, n), lambda h: (0, 0)),
            pl.BlockSpec((8, n), lambda h: (0, 0)),
            whole,
            whole,
        ],
        out_shape=[
            kept_out(shape, bf),
            jax.ShapeDtypeStruct((80, n), bf),
            jax.ShapeDtypeStruct((8, n), f32),
            kept_out((n, 128), bf),
            kept_out((n, 128), bf),
        ],
        scratch_shapes=[
            pltpu.VMEM((2, n, BQ), f32),
            pltpu.VMEM((128, n), bf),
            pltpu.VMEM(shape, bf),
            pltpu.SemaphoreType.DMA((n // BQ,)),
        ],
        compiler_params=params(34),
        cost_estimate=cost(10),
    )(place, qkv, q_got, qkv, kv_got, dep)


def unsplit(ref, at):
    return ref[at : at + 1, :].astype(f32) + ref[at + 1 : at + 2, :].astype(f32) + ref[at + 2 : at + 3, :].astype(f32)


def join_kernel(place, near_a, near_b, stat_a, stat_b, far_a, far_b, got_a, got_b, mine, other, log_ref):
    core, chip = place[0], place[1]
    half = mine.shape[1]
    for h in range(4):
        far = (far_a, far_b, got_a, got_b)[h]
        near, stat = (near_a, near_b)[h // 2], (stat_a, stat_b)[h // 2]
        log_near = stat[h % 2, 0:1, :] + jnp.log(stat[h % 2, 1:2, :]) * LOG2E
        log_far = jnp.where(chip == 1, unsplit(far, 64), MASKED)
        top = jnp.maximum(log_near, log_far)
        e_near, e_far = jnp.exp2(log_near - top), jnp.exp2(log_far - top)
        both = e_near + e_far
        log_ref[h] = jnp.broadcast_to(top + jnp.log(both) * LOG2E, log_ref.shape[1:])
        far_out = jnp.where(chip == 1, far[0:64, :].astype(f32), 0.0)
        joined = ((near[h % 2].astype(f32) * e_near + far_out * e_far) * (1.0 / both)).astype(bf)
        at = slice(64 * h, 64 * h + 64)

        @pl.when(core == 0)
        def _():
            mine[at, :] = joined[:, :half]
            other[at, :] = joined[:, half:]

        @pl.when(core == 1)
        def _():
            mine[at, :] = joined[:, half:]
            other[at, :] = joined[:, :half]


def join(place, near_a, near_b, stat_a, stat_b, far_a, far_b, got_a, got_b):
    n = near_a.shape[2]
    return pl.pallas_call(
        join_kernel,
        in_specs=[smem()] + [vmem()] * 8,
        out_specs=[vmem()] * 3,
        out_shape=[
            jax.ShapeDtypeStruct((256, n // 2), bf),
            jax.ShapeDtypeStruct((256, n // 2), bf),
            jax.ShapeDtypeStruct((4, 8, n), f32),
        ],
        compiler_params=params(),
        cost_estimate=cost(2),
    )(place, near_a, near_b, stat_a, stat_b, far_a, far_b, got_a, got_b)


def mixture_kernel(
    place, sharp, x, att_own, att_got, wout, gain, router, labels, gy, w1_hbm, w2_hbm,
    block_out, fac, gout, tiny, back_resid, ba_own, ba_other, w1, w2, block_ref, back_ref, sems,
):
    core = place[0]
    copy1 = pltpu.make_async_copy(w1_hbm, w1, sems.at[0])
    copy2 = pltpu.make_async_copy(w2_hbm, w2, sems.at[1])
    copy1.start()
    copy2.start()
    copy3 = pltpu.make_async_copy(block_ref, block_out, sems.at[2])
    copy4 = pltpu.make_async_copy(back_ref, back_resid, sems.at[3])
    own_rows = pl.ds(pl.multiple_of(core * 256, 256), 256)
    other_rows = pl.ds(pl.multiple_of(256 - core * 256, 256), 256)
    wo_own, wo_other = wout[own_rows, :], wout[other_rows, :]
    resid = x[...].astype(f32) + tn(att_own[...], wo_own) + tn(att_got[...], wo_other)
    inverse = lax.rsqrt(jnp.mean(resid * resid, axis=1, keepdims=True) + EPSILON)
    unit = resid * inverse
    mix = (unit * gain[...]).astype(bf)
    temper = 1.0 / sharp[0]
    logits = nt(router[...], mix) * temper
    tokens = mix.shape[0]
    groups = tokens // GROUP
    member = labels[...] == rows_of((groups, tokens))
    weights, mixing = [], []
    for e in range(2):
        row = logits[e : e + 1, :]
        peak = jnp.max(jnp.where(member, row, -jnp.inf), axis=1, keepdims=True)
        token_peak = jnp.sum(jnp.where(member, peak, 0.0), axis=0, keepdims=True)
        raised = jnp.exp(row - token_peak)
        total = jnp.sum(jnp.where(member, raised, 0.0), axis=1, keepdims=True)
        token_total = jnp.sum(jnp.where(member, total, 0.0), axis=0, keepdims=True)
        w = raised / token_total
        weights.append(w)
        mixing.append(jnp.where(member, w, 0.0))
    mixing = jnp.concatenate(mixing, 0).astype(bf)
    mixed = nn(mixing, mix).astype(bf)
    back_expert = nn(mixing, gy[...]).astype(bf)
    copy1.wait()
    copy2.wait()
    expert_out, back_mixed = [], []
    quarter = w1.shape[2] // 4
    width = mix.shape[1]
    for e in range(2):
        at = slice(groups * e, groups * (e + 1))
        inner = nn(mixed[at], w1[e])
        cdf = 0.5 * (1.0 + lax.erf(inner * 0.7071067811865476))
        active = (inner * cdf).astype(bf)
        slope = cdf + inner * (jnp.exp(-0.5 * inner * inner) * 0.3989422804014327)
        expert_out.append(nn(active, w2[e]))
        back_inner = (slope * nt(back_expert[at], w2[e])).astype(bf)
        back_mixed.append(nt(back_inner, w1[e]))
        fac[e, :, 0:width] = mixed[at]
        fac[e, :, width : 2 * width] = back_expert[at]
        for q in range(4):
            base = 2 * width + 2 * quarter * q
            fac[e, :, base : base + quarter] = back_inner[:, quarter * q : quarter * (q + 1)]
            fac[e, :, base + quarter : base + 2 * quarter] = active[:, quarter * q : quarter * (q + 1)]
    expert_out = jnp.concatenate(expert_out, 0).astype(bf)
    back_mixed = jnp.concatenate(back_mixed, 0).astype(bf)
    block_ref[...] = (resid + tn(mixing, expert_out)).astype(bf)
    copy3.start()
    spread = nt(expert_out, gy[...]) + nt(back_mixed, mix)
    rows16 = rows_of((16, tokens))
    back_logits = jnp.zeros((16, tokens), f32)
    for e in range(2):
        back_weight = jnp.sum(jnp.where(member, spread[groups * e : groups * (e + 1)], 0.0), axis=0, keepdims=True)
        w = weights[e]
        inner = jnp.sum(jnp.where(member, w * back_weight, 0.0), axis=1, keepdims=True)
        token_inner = jnp.sum(jnp.where(member, inner, 0.0), axis=0, keepdims=True)
        back_logits = jnp.where(rows16 == e, w * (back_weight - token_inner) * temper, back_logits)
    back_logits = back_logits.astype(bf)
    ctrl = nn(back_logits, mix)
    back_mix = tn(mixing, back_mixed) + tn(back_logits, router[...])
    tiny[...] = jnp.zeros_like(tiny)
    tiny[0:2, :] = ctrl[0:2, :]
    tiny[2:3, :] = jnp.sum(back_mix * unit, axis=0, keepdims=True)
    n = back_mix * gain[...]
    mean = jnp.mean(n * resid, axis=1, keepdims=True)
    back = gy[...].astype(f32) + inverse * n - resid * (inverse * inverse * inverse * mean)
    back_ref[...] = back
    copy4.start()
    branch = back.astype(bf)
    gout[core] = nn(att_own[...], branch).astype(bf)
    gout[1 - core] = nn(att_got[...], branch).astype(bf)
    ba_own[...] = nt(wo_own, branch).astype(bf)
    ba_other[...] = nt(wo_other, branch).astype(bf)
    copy3.wait()
    copy4.wait()


def mixture(place, sharp, x, att_own, att_got, wout, gain, router, labels, gy, w1, w2):
    tokens, width = x.shape
    hidden = w1.shape[2]
    groups = tokens // GROUP
    return pl.pallas_call(
        mixture_kernel,
        in_specs=[smem(), smem()] + [vmem()] * 8 + [pl.BlockSpec(memory_space=pl.ANY)] * 2,
        out_specs=[anywhere()] + [vmem()] * 3 + [anywhere()] + [vmem()] * 2,
        out_shape=[
            kept_out((tokens, width), bf),
            jax.ShapeDtypeStruct((2, groups, 2 * width + 2 * hidden), bf),
            jax.ShapeDtypeStruct((2, width // 2, width), bf),
            jax.ShapeDtypeStruct((8, width), f32),
            kept_out((tokens, width), f32),
            jax.ShapeDtypeStruct((width // 2, tokens), bf),
            jax.ShapeDtypeStruct((width // 2, tokens), bf),
        ],
        scratch_shapes=[
            pltpu.VMEM(w1.shape, bf),
            pltpu.VMEM(w2.shape, bf),
            pltpu.VMEM((tokens, width), bf),
            pltpu.VMEM((tokens, width), f32),
            pltpu.SemaphoreType.DMA((4,)),
        ],
        compiler_params=params(48),
        cost_estimate=cost(15),
    )(place, sharp, x, att_own, att_got, stay(wout), gain, router, labels, gy, stay(w1), stay(w2))


def ready_kernel(place, ba_own, ba_got, mine, other, log_ref, grads, inner, payload, tails):
    core = place[0]
    half = mine.shape[1]
    tails[...] = jnp.zeros_like(tails)
    for h in range(4):
        at = slice(64 * h, 64 * h + 64)
        g_own, g_got = ba_own[at, :], ba_got[at, :]
        d_own = jnp.sum(g_own.astype(f32) * mine[at, :].astype(f32), axis=0, keepdims=True)
        d_got = jnp.sum(g_got.astype(f32) * other[at, :].astype(f32), axis=0, keepdims=True)

        def put(g0, g1, d0, d1):
            grads[h, :, :half] = g0
            grads[h, :, half:] = g1
            inner[h, :, :half] = jnp.broadcast_to(d0, (8, half))
            inner[h, :, half:] = jnp.broadcast_to(d1, (8, half))
            if h >= 2:
                for g, d, s in ((g0, d0, slice(0, half)), (g1, d1, slice(half, 2 * half))):
                    payload[64 * (h - 2) : 64 * (h - 1), s] = g
                    parts = three(log_ref[h, 0:1, s]) + three(d)
                    tails[8 * (h - 2) : 8 * (h - 2) + 6, s] = jnp.concatenate([part.astype(f32) for part in parts], 0)

        @pl.when(core == 0)
        def _():
            put(g_own, g_got, d_own, d_got)

        @pl.when(core == 1)
        def _():
            put(g_got, g_own, d_got, d_own)
    payload[128:144, :] = tails[...].astype(bf)


def ready(place, ba_own, ba_got, mine, other, log):
    half = mine.shape[1]
    return pl.pallas_call(
        ready_kernel,
        in_specs=[smem()] + [vmem()] * 5,
        out_specs=[vmem()] * 3,
        out_shape=[
            jax.ShapeDtypeStruct((4, 64, 2 * half), bf),
            jax.ShapeDtypeStruct((4, 8, 2 * half), f32),
            jax.ShapeDtypeStruct((144, 2 * half), bf),
        ],
        scratch_shapes=[pltpu.VMEM((16, 2 * half), f32)],
        compiler_params=params(),
        cost_estimate=cost(2),
    )(place, ba_own, ba_got, mine, other, log)


def back_block(kv_ref, kt_ref, q, grad, ratio, inner, block, kmax, first, put_kv):
    low = (grad.astype(f32) * ratio).astype(bf)
    rhs = jnp.concatenate([jnp.zeros((64, BQ), bf), low], axis=0)
    shift = inner * ratio
    natural = rhs.T
    acc = None
    for k0 in range(0, kmax, CH):
        dp = nn(kv_ref[k0 : k0 + CH, :], rhs)
        p = block(k0 // CH)
        ds = (p.astype(f32) * (dp - shift)).astype(bf)
        d = nn(kt_ref[:, k0 : k0 + CH], ds)
        acc = d if acc is None else acc + d
        put_kv(k0, k0 >= first, nn(ds, q) + nn(p, natural))
    return (acc * 0.125).astype(bf)


def near_backward_kernel(head, q_ref, kv_ref, p_ref, grad_ref, stat, log_ref, inner_ref, *refs):
    dkv_ref, dq_ref, kt_ref, buf, sems = refs[-5:]
    count = q_ref.shape[0] // BQ
    copies = []
    for i in range(count):
        at = slice(i * (i + 1) // 2, (i + 1) * (i + 2) // 2)
        copies.append(pltpu.make_async_copy(p_ref.at[head, at], buf.at[at], sems.at[i]))
        copies[-1].start()
    kt_ref[...] = kv_ref[...].T[0:64, :]

    def put(k0, fresh, value):
        if fresh:
            dkv_ref[k0 : k0 + CH, :] = value
        else:
            dkv_ref[k0 : k0 + CH, :] += value

    for i in range(count):
        at = slice(i * BQ, (i + 1) * BQ)
        base = i * (i + 1) // 2
        copies[i].wait()
        ratio = jnp.exp2(stat[0, 0:1, at] - log_ref[0, 0:1, at])

        def block(k):
            return buf[base + k]

        dq_ref[:, at] = back_block(
            kv_ref, kt_ref, q_ref[at, :], grad_ref[0, :, at], ratio, inner_ref[0, 0:1, at], block, (i + 1) * BQ, i * BQ, put
        )


def near_backward(h, qkv, p, grads, stat, log, inner, deps):
    n = qkv.shape[0]
    row = pl.BlockSpec((1, 8, n), lambda g: (h, 0, 0))
    return pl.pallas_call(
        functools.partial(near_backward_kernel, h % 2),
        grid=(1,),
        in_specs=[
            pl.BlockSpec((n, 128), lambda g: (0, 2 * h)),
            pl.BlockSpec((n, 128), lambda g: (0, 2 * h + 1)),
            hbm(),
            pl.BlockSpec((1, 64, n), lambda g: (h, 0, 0)),
            pl.BlockSpec((1, 8, n), lambda g: (h % 2, 0, 0)),
            row,
            row,
        ]
        + [anywhere()] * len(deps),
        out_specs=[pl.BlockSpec((n, 128), lambda g: (0, 0)), pl.BlockSpec((64, n), lambda g: (0, 0))],
        out_shape=[kept_out((n, 128), f32), kept_out((64, n), bf)],
        scratch_shapes=[pltpu.VMEM((64, n), bf), pltpu.VMEM(p.shape[1:], bf), pltpu.SemaphoreType.DMA((n // BQ,))],
        compiler_params=params(24),
        cost_estimate=cost(7),
    )(qkv, qkv, stay(p), grads, stat, log, inner, *deps)


def far_backward_kernel(
    j, place, q_ref, kv_ref, p_ref, stat, grad_own, log_own, inner_own, got, got_tail, dep, send_ref, keep_ref, kt_ref, sum_ref, dq_ref, buf, sems
):
    kt_ref[...] = kv_ref[...].T[0:64, :]
    upper = place[1] == 1
    n = q_ref.shape[0]
    copies = [pltpu.make_async_copy(p_ref.at[i], buf.at[i], sems.at[i]) for i in range(n // BQ)]
    for copy in copies:
        copy.start()

    def put(k0, fresh, value):
        if fresh:
            sum_ref[k0 : k0 + CH, :] = value
        else:
            sum_ref[k0 : k0 + CH, :] += value

    for i in range(n // BQ):
        at = slice(i * BQ, (i + 1) * BQ)
        got_log = got_tail[8 * j : 8 * j + 3, at].astype(f32)
        got_inner = got_tail[8 * j + 3 : 8 * j + 6, at].astype(f32)
        log = jnp.where(upper, log_own[0, 0:1, at], jnp.sum(got_log, axis=0, keepdims=True))
        inner = jnp.where(upper, inner_own[0, 0:1, at], jnp.sum(got_inner, axis=0, keepdims=True))
        grad = jnp.where(upper, grad_own[0, :, at], got[:, at])
        ratio = jnp.exp2(stat[0:1, at] - log)
        copies[i].wait()

        def block(k):
            return buf[i, k]

        dq = back_block(kv_ref, kt_ref, q_ref[at, :], grad, ratio, inner, block, n, 0 if i == 0 else n, put)
        dq_ref[at, :] = jnp.concatenate([dq, jnp.zeros((64, BQ), bf)], 0).T

    @pl.when(upper)
    def _():
        send_ref[...] = sum_ref[...].astype(bf)
        keep_ref[...] = dq_ref[...]

    @pl.when(jnp.logical_not(upper))
    def _():
        send_ref[...] = dq_ref[...]
        keep_ref[...] = sum_ref[...].astype(bf)


def far_backward(j, place, q, kv, p, stat, grads, log, inner, got, dep):
    n = q.shape[0]
    row = pl.BlockSpec((1, 8, n), lambda h: (j, 0, 0))
    whole = pl.BlockSpec((n, 128), lambda h: (0, 0))
    return pl.pallas_call(
        functools.partial(far_backward_kernel, j),
        grid=(1,),
        in_specs=[
            smem(),
            whole,
            whole,
            hbm(),
            pl.BlockSpec((8, n), lambda h: (0, 0)),
            pl.BlockSpec((1, 64, n), lambda h: (j, 0, 0)),
            row,
            row,
            pl.BlockSpec((64, n), lambda h: (j, 0)),
            pl.BlockSpec((16, n), lambda h: (8, 0)),
            pl.BlockSpec(memory_space=pl.ANY),
        ],
        out_specs=[whole, whole],
        out_shape=[jax.ShapeDtypeStruct((n, 128), bf)] * 2,
        scratch_shapes=[
            pltpu.VMEM((64, n), bf),
            pltpu.VMEM((n, 128), f32),
            pltpu.VMEM((n, 128), bf),
            pltpu.VMEM(p.shape, bf),
            pltpu.SemaphoreType.DMA((n // BQ,)),
        ],
        compiler_params=params(30),
        cost_estimate=cost(13),
    )(place, q, kv, stay(p), stat, grads, log, inner, got, got, dep)


def swap(value, bits):
    count = lax.axis_size("batch") * lax.axis_size("seq")
    return lax.ppermute(value, AXES, [(i, i ^ bits) for i in range(count)])


def turns():
    bits = (lax.axis_size("batch") // 2).bit_length() - 1
    return [(3 + t, 2 + bits - t) for t in range(bits)]


PLANE = [(1, 2), (2, 1)]


def swap_by_core(value, turn):
    count = lax.axis_size("batch") * lax.axis_size("seq")
    return lax.ppermute(value, AXES, [(i, i ^ (1 << turn[i % 2])) for i in range(count)])


def bit_of(number, core, turn):
    return (number >> jnp.where(core == 0, turn[0], turn[1])) & 1


def take(value, index, axis=0):
    return lax.dynamic_index_in_dim(value, index, axis, keepdims=False)


MOVES = ((0, 0), (1, 0), (0, 1), (1, 1))


def factors_kernel(place, fac, got, gout, got_out, dep, *outs):
    core, chip, side = place[0], place[1], place[2]
    groups = got.shape[0]
    width = gout.shape[2]
    part = (got.shape[1] - 2 * width) // 4
    rows = gout.shape[1] // 4
    for (x, y), out in zip(MOVES, outs):
        index = 2 * (chip ^ x) + (side ^ y)
        lanes = pl.ds(pl.multiple_of(2 * width + index * part, 128), part)
        at = pl.ds(pl.multiple_of(index * rows, rows), rows)
        out[0:groups, 0 : 2 * width] = fac[core, :, 0 : 2 * width]
        out[groups:, 0 : 2 * width] = got[:, 0 : 2 * width]
        out[0:groups, 2 * width : 2 * width + part] = fac[core, :, lanes]
        out[groups:, 2 * width : 2 * width + part] = got[:, lanes]
        out[:, 2 * width + part :] = (gout[core, at, :].astype(f32) + got_out[at, :].astype(f32)).astype(bf)


def factors(place, fac, got, gout, got_out, dep):
    groups, per = got.shape
    width = gout.shape[2]
    shape = jax.ShapeDtypeStruct((2 * groups, 2 * width + (per - 2 * width) // 4 + width), bf)
    return pl.pallas_call(
        factors_kernel,
        in_specs=[smem()] + [vmem()] * 4 + [anywhere()],
        out_specs=[vmem()] * 4,
        out_shape=[shape] * 4,
        compiler_params=params(),
        cost_estimate=cost(2),
    )(place, fac, got, gout, got_out, dep)


def slab_kernel(turn, lines, place, dep, a, b, c, d, keep, send):
    core, line = place[0], place[3]
    width = keep.shape[2]
    quarter = (a.shape[1] - 3 * width) // 2

    def lanes(start, size):
        return jnp.concatenate([ref[:, start : start + size] for ref in (a, b, c, d)], 0)

    g_in = tn(lanes(0, width), lanes(2 * width, quarter)).astype(bf)
    g_down = tn(lanes(2 * width + quarter, quarter), lanes(width, width)).astype(bf)
    total = a[:, 2 * width + 2 * quarter :].astype(f32)
    for ref in (b, c, d):
        total = total + ref[:, 2 * width + 2 * quarter :].astype(f32)
    pieces = [total.astype(bf), g_in, g_down]
    bits = lines.bit_length() - 1
    for z in range(lines):
        flipped = sum(((z >> t) & 1) << (bits - 1 - t) for t in range(bits))
        spot = jnp.where(core == 0, flipped, z)
        chosen = bit_of(8 * z, core, turn) == bit_of(8 * line, core, turn)

        def put(ref):
            start = 0
            for piece in pieces[1:] + pieces[:1]:
                rows = piece.shape[0] // lines
                ref[spot % (lines // 2), start : start + rows, :] = piece[z * rows : (z + 1) * rows, :]
                start += rows

        @pl.when(chosen)
        def _():
            put(keep)

        @pl.when(jnp.logical_not(chosen))
        def _():
            put(send)


def slabs(place, dep, payloads, width, quarter, lines):
    rows = (width + quarter + payloads[0].shape[0]) // lines
    shape = jax.ShapeDtypeStruct((lines // 2, rows, width), bf)
    turn = turns()[0]
    return pl.pallas_call(
        lambda *refs: slab_kernel(turn, lines, *refs),
        in_specs=[smem(), anywhere()] + [vmem()] * 4,
        out_specs=[vmem()] * 2,
        out_shape=[shape] * 2,
        compiler_params=params(),
        cost_estimate=cost(2),
    )(place, stay(dep), *payloads)


def fold_kernel(turn, place, dep, kept, got, keep, *send):
    if turn is None:
        keep[...] = (kept[...].astype(f32) + got[...].astype(f32)).astype(bf)
        return
    half = keep.shape[0]
    mine = bit_of(place[4], place[0], turn)
    at = pl.ds(mine * half, half)
    keep[...] = (kept[at].astype(f32) + got[at].astype(f32)).astype(bf)
    at = pl.ds((1 - mine) * half, half)
    send[0][...] = (kept[at].astype(f32) + got[at].astype(f32)).astype(bf)


def fold(turn, place, dep, kept, got):
    count = kept.shape[0] if turn is None else kept.shape[0] // 2
    shape = jax.ShapeDtypeStruct((count,) + kept.shape[1:], bf)
    outs = 1 if turn is None else 2
    return pl.pallas_call(
        lambda *refs: fold_kernel(turn, *refs),
        in_specs=[smem(), anywhere(), vmem(), vmem()],
        out_specs=[vmem()] * outs,
        out_shape=[shape] * outs,
        compiler_params=params(),
        cost_estimate=cost(1),
    )(place, dep, kept, got)


def pile_kernel(a, b, *refs):
    out = refs[-1]
    half = out.shape[0] // 2
    out[:half] = a[...]
    out[half:] = b[...]


def pile(a, b, *deps):
    return pl.pallas_call(
        pile_kernel,
        in_specs=[vmem(), vmem()] + [anywhere()] * len(deps),
        out_specs=vmem(),
        out_shape=jax.ShapeDtypeStruct((2 * a.shape[0],) + a.shape[1:], bf),
        compiler_params=params(),
        cost_estimate=cost(1),
    )(a, b, *deps)


def add_kernel(values, pieces, place, *refs):
    total = refs[0][...].astype(f32)
    for ref in refs[1:values]:
        total = total + ref[...].astype(f32)
    outs = refs[len(refs) - pieces :]
    if pieces == 1:
        outs[0][...] = total.astype(bf)
        return
    total = total.astype(bf)
    rows = outs[0].shape[0]
    for z in range(pieces):
        for k in range(pieces):

            @pl.when((place[3] ^ k) == z)
            def _():
                outs[k][...] = total[z * rows : (z + 1) * rows]


def add(place, values, pieces, *deps):
    rows, lanes = values[0].shape
    return pl.pallas_call(
        functools.partial(add_kernel, len(values), pieces),
        in_specs=[smem()] + [vmem()] * len(values) + [anywhere()] * len(deps),
        out_specs=[vmem()] * pieces,
        out_shape=[jax.ShapeDtypeStruct((rows // pieces, lanes), bf)] * pieces,
        compiler_params=params(),
        cost_estimate=cost(1),
    )(place, *values, *deps)


def stack_kernel(count, *refs):
    for k in range(count):
        refs[-1][k] = refs[k][...]


def stack(values, *deps):
    return pl.pallas_call(
        functools.partial(stack_kernel, len(values)),
        in_specs=[vmem()] * len(values) + [anywhere()] * len(deps),
        out_specs=vmem(),
        out_shape=jax.ShapeDtypeStruct((len(values),) + values[0].shape, bf),
        compiler_params=params(),
        cost_estimate=cost(1),
    )(*values, *deps)


def gate_kernel(value, *refs):
    pass


def gate(value, *deps):
    return pl.pallas_call(
        gate_kernel,
        in_specs=[anywhere()] * (1 + len(deps)),
        out_specs=anywhere(),
        out_shape=jax.ShapeDtypeStruct(value.shape, value.dtype),
        input_output_aliases={0: 0},
        compiler_params=params(1),
        cost_estimate=cost(1),
    )(value, *deps)


def spread_kernel(place, near, far, *refs):
    in_ref, down_ref, out_ref = refs[-3:]
    expert = pl.program_id(0)
    line = place[3]
    lines = near.shape[1]
    width = in_ref.shape[1]
    cut_in = width // lines
    cut_down = down_ref.shape[1] // lines
    bits = lines.bit_length() - 1

    def put(ref):
        for k in range(lines):
            flipped = sum(((k >> t) & 1) << (bits - 1 - t) for t in range(bits))
            z = line ^ jnp.where(expert == 0, flipped, k)
            in_ref[0, pl.ds(pl.multiple_of(z * cut_in, cut_in), cut_in), :] = ref[0, k, :cut_in].astype(f32)
            down_ref[0, pl.ds(pl.multiple_of(z * cut_down, cut_down), cut_down), :] = ref[0, k, cut_in : cut_in + cut_down].astype(f32)
            out_ref[0, z] = ref[0, k, cut_in + cut_down :].astype(f32)

    @pl.when(expert == place[0])
    def _():
        put(near)

    @pl.when(expert != place[0])
    def _():
        put(far)


def spread_experts(outer, place, near, far, hidden, width, earlier, *deps):
    block = near.shape[1:]
    lines = block[0]

    def spec(is_near):
        def index(e, i, p):
            return (jnp.where((e == p[0]) == is_near, i, 0), 0, 0, 0)

        return pl.BlockSpec((1,) + block, index)

    def quarter(e, i, p):
        move_x, move_y = jnp.where(e == 0, i, outer), jnp.where(e == 0, outer, i)
        return 2 * (p[1] ^ move_x) + (p[2] ^ move_y)

    return pl.pallas_call(
        spread_kernel,
        grid_spec=pltpu.PrefetchScalarGridSpec(
            num_scalar_prefetch=1,
            grid=(2, 2),
            in_specs=[spec(True), spec(False)] + [anywhere()] * (len(earlier) + len(deps)),
            out_specs=[
                pl.BlockSpec((1, width, hidden // 4), lambda e, i, p: (e, 0, quarter(e, i, p))),
                pl.BlockSpec((1, hidden // 4, width), lambda e, i, p: (e, quarter(e, i, p), 0)),
                pl.BlockSpec((1, lines, width // 8 // lines, width), lambda e, i, p: (e * 4 + quarter(e, i, p), 0, 0, 0)),
            ],
        ),
        out_shape=[
            kept_out((2, width, hidden), f32),
            kept_out((2, hidden, width), f32),
            kept_out((8, lines, width // 8 // lines, width), f32),
        ],
        input_output_aliases={3: 0, 4: 1, 5: 2} if earlier else {},
        compiler_params=params(28),
        cost_estimate=cost(6),
    )(place, near, far, *earlier, *deps)


def own_block(b, p):
    return jnp.where(b // 2 == p[0], b % 2, jnp.where(b // 2 > p[0], 1, 0))


def other_block(b, p):
    return jnp.where(b // 2 != p[0], b % 2, jnp.where(b // 2 > 1 - p[0], 1, 0))


def collect_kernel(
    place, normed, kv_a, kv_b, kv_c, kv_d, q_a, q_b, q_c, q_d, keep_a, keep_b, got_a, got_b, packs, gain, tiny, dep,
    mine, other, slab_0, slab_1, slab_2, slab_3, sum_ref,
):
    block = pl.program_id(0)
    core, chip, side = place[0], place[1], place[2]
    upper = chip == 1
    dq = jnp.concatenate([q_a[...], q_b[...], q_c[...], q_d[...]], 0).T.astype(f32)
    far = jnp.concatenate([left(keep_a[...], keep_b[...]), left(got_a[...], got_b[...])], 1).astype(f32)
    pieces = [(dq + jnp.where(upper, far, 0.0)).astype(bf)]
    for near, extra in ((kv_a, got_a), (kv_b, got_b), (kv_c, keep_a), (kv_d, keep_b)):
        value = near[...] + jnp.where(upper, 0.0, extra[...].astype(f32))
        pieces.append(jnp.where(lanes_of(value.shape) < 64, value * 0.125, value).astype(bf))
    back = jnp.concatenate(pieces, 1)

    @pl.when(block // 2 == core)
    def _():
        mine[...] = back

    @pl.when(block // 2 != core)
    def _():
        other[...] = back

    part = tn(normed[...], back)

    @pl.when(block == 0)
    def _():
        sum_ref[...] = part

    @pl.when(block > 0)
    def _():
        sum_ref[...] += part

    @pl.when(block == 3)
    def _():
        total = sum_ref[...]
        width, wide = total.shape
        product = jnp.sum(total * packs[core].astype(f32), axis=1, keepdims=True)
        small = tiny[...].T
        small = jnp.concatenate([small, jnp.zeros((width, 120), f32)], 1)
        lanes = lanes_of(small.shape)
        small = jnp.where(lanes == 3, product / gain[...].T, small)
        high = small.astype(bf)
        low = (small - high.astype(f32)).astype(bf)
        small = jnp.where(lanes < 8, high.astype(f32), pltpu.roll(low.astype(f32), 8, axis=1)).astype(bf)
        low = total.astype(bf)
        rows = width // 4
        for (move_x, move_y), ref in zip(MOVES, (slab_0, slab_1, slab_2, slab_3)):
            for q in range(4):

                @pl.when(2 * (chip ^ move_x) + (side ^ move_y) == q)
                def _():
                    ref[:, :wide] = low[q * rows : (q + 1) * rows]
                    ref[:, wide:] = small[q * rows : (q + 1) * rows]


def collect(place, normed, kvs, qs, keep_a, keep_b, got_a, got_b, packs, gain, tiny, dep):
    n, width = normed.shape
    rows = n // 4
    dq = pl.BlockSpec((64, rows), lambda b, p: (0, b))
    flat = pl.BlockSpec((rows, 128), lambda b, p: (b, 0))
    slab = (width // 4, 896)
    return pl.pallas_call(
        collect_kernel,
        grid_spec=pltpu.PrefetchScalarGridSpec(
            num_scalar_prefetch=1,
            grid=(4,),
            in_specs=[pl.BlockSpec((rows, width), lambda b, p: (b, 0))]
            + [flat] * 4
            + [dq] * 4
            + [flat] * 4
            + [
                pl.BlockSpec(packs.shape, lambda b, p: (0, 0, 0)),
                pl.BlockSpec((1, width), lambda b, p: (0, 0)),
                pl.BlockSpec(tiny.shape, lambda b, p: (0, 0)),
                anywhere(),
            ],
            out_specs=[
                pl.BlockSpec((rows, 768), lambda b, p: (own_block(b, p), 0)),
                pl.BlockSpec((rows, 768), lambda b, p: (other_block(b, p), 0)),
            ]
            + [pl.BlockSpec(slab, lambda b, p: (0, 0))] * 4,
            scratch_shapes=[pltpu.VMEM((width, 768), f32)],
        ),
        out_shape=[
            jax.ShapeDtypeStruct((n // 2, 768), bf),
            jax.ShapeDtypeStruct((n // 2, 768), bf),
        ]
        + [jax.ShapeDtypeStruct(slab, bf)] * 4,
        compiler_params=params(26),
        cost_estimate=cost(5),
    )(place, stay(normed), *kvs[:3], stay(kvs[3]), *qs, keep_a, keep_b, got_a, got_b, stay(packs), gain, tiny, dep)


def tokens_kernel(place, mine, got, packs, x_ref, back_resid, gain, dep, out):
    core = place[0]
    back = nt(mine[...], packs[core]) + nt(got[...], packs[1 - core])
    x = x_ref[...].astype(f32)
    inverse = lax.rsqrt(jnp.mean(x * x, axis=1, keepdims=True) + EPSILON)
    k = back * gain[...]
    mean = jnp.mean(k * x, axis=1, keepdims=True)
    out[...] = (back_resid[...] + inverse * k - x * (inverse * inverse * inverse * mean)).astype(bf)


def tokens_back(place, mine, got, packs, x, back_resid, gain, dep):
    n, width = x.shape
    rows = n // 4
    wide = pl.BlockSpec((rows, 768), lambda b, p: (b, 0))
    block = pl.BlockSpec((rows, width), lambda b, p: (b, 0))
    return pl.pallas_call(
        tokens_kernel,
        grid_spec=pltpu.PrefetchScalarGridSpec(
            num_scalar_prefetch=1,
            grid=(4,),
            in_specs=[wide, wide, pl.BlockSpec(packs.shape, lambda b, p: (0, 0, 0)), block, block, pl.BlockSpec((1, width), lambda b, p: (0, 0)), anywhere()],
            out_specs=block,
        ),
        out_shape=kept_out((n, width), bf),
        compiler_params=params(20),
        cost_estimate=cost(4),
    )(place, mine, got, stay(packs), stay(x), stay(back_resid), gain, dep)


def unfold_kernel(place, *refs):
    out, attn_out, mix_out, ctrl_out, small_ref = refs[-5:]
    core, line = place[0], place[3]
    lines, rows = refs[0].shape[1], refs[0].shape[2]
    block = pl.program_id(0)

    def put(source, c, fresh):
        for k in range(lines):
            at = pl.ds(pl.multiple_of((line ^ k) * rows, rows), rows)
            value = source[k]
            base = c * 256
            out[at, pl.ds(pl.multiple_of(base, 128), 256)] = value[:, 0:256].astype(f32)
            for pair in range(2):
                a = value[:, 256 + 256 * pair : 384 + 256 * pair]
                b = value[:, 384 + 256 * pair : 512 + 256 * pair]
                out[at, pl.ds(pl.multiple_of(512 + base + 128 * pair, 128), 128)] = left(a, b).astype(f32)
                out[at, pl.ds(pl.multiple_of(1024 + base + 128 * pair, 128), 128)] = right(a, b).astype(f32)
            small = value[:, 768:].astype(f32)
            small = small + pltpu.roll(small, 120, axis=1)
            small_ref[at, :] = small if fresh else small_ref[at, :] + small

    for i in range(4):

        @pl.when(block == i)
        def _():
            put(refs[0].at[i], core, True)
            put(refs[1].at[i], 1 - core, False)
            rows_out = small_ref[...].T
            attn_out[...] = rows_out[3:4, :]
            mix_out[...] = rows_out[2:3, :]
            ctrl_out[...] = rows_out[0:2, :]


def unfold(place, near, far, width):
    whole = pl.BlockSpec(near.shape, lambda i, p: (0, 0, 0, 0))

    def at(i, p):
        return ((2 * p[1] + p[2]) ^ ((i % 2) * 2 + i // 2), 0)

    def across(i, p):
        return at(i, p)[::-1]

    return pl.pallas_call(
        unfold_kernel,
        grid_spec=pltpu.PrefetchScalarGridSpec(
            num_scalar_prefetch=1,
            grid=(4,),
            in_specs=[whole] * 2,
            out_specs=[pl.BlockSpec((width // 4, 3 * width), at)] + [pl.BlockSpec((n, width // 4), across) for n in (1, 1, 2)],
            scratch_shapes=[pltpu.VMEM((width // 4, 128), f32)],
        ),
        out_shape=[kept_out((width, 3 * width), f32)] + [kept_out((n, width), f32) for n in (1, 1, 2)],
        compiler_params=params(16),
        cost_estimate=cost(3),
    )(place, near, far)


def body(
    layer_activations,
    sequence_extents,
    position_cluster_label,
    cluster_sharpness,
    heed_scale_factor,
    triple_entry_matrix,
    heed_exit_matrix,
    blend_scale_factor,
    router_matrix,
    specialist_entry_matrix,
    specialist_exit_matrix,
    upstream_derivative,
):
    seq_count, pos_count, width = layer_activations.shape
    tokens = seq_count * pos_count
    hidden = specialist_entry_matrix.shape[2]
    spot = lax.axis_index("seq")
    row = lax.axis_index("batch")
    core, chip, side, line = spot % 2, spot // 2, row % 2, row // 2
    lines = lax.axis_size("batch") // 2
    place = jnp.stack([core, chip, side, line, row * 4 + spot]).astype(jnp.int32)
    core_pairs, chip_pairs = [(0, 1), (1, 0), (2, 3), (3, 2)], [(0, 2), (1, 3), (2, 0), (3, 1)]
    up, down = chip_pairs[:2], chip_pairs[2:]

    x = layer_activations.reshape(tokens, width)
    x_other = lax.ppermute(x, "seq", core_pairs)
    packs, w_own, router, gains = pack(
        place, triple_entry_matrix, router_matrix.T, heed_scale_factor, blend_scale_factor
    )
    gain_a, gain_m = gains[0], gains[1]
    normed, qkv, send_a, send_b = project(place, x, x_other, gain_a, w_own)
    got_a = lax.ppermute(send_a, "seq", chip_pairs)
    got_b = lax.ppermute(send_b, "seq", up)
    limit = (sequence_extents - chip * 2 * pos_count).astype(jnp.int32)
    p_na, o_na, st_na = near_forward(0, limit, qkv, qkv)
    p_a, o_a, st_a, q_a, kv_a = far_forward(0, place, qkv, got_a, got_a, o_na)
    got_oa = lax.ppermute(o_a, "seq", up)
    p_b, o_b, st_b, q_b, kv_b = far_forward(1, place, qkv, got_a, got_b, o_a)
    got_ob = lax.ppermute(o_b, "seq", up)
    p_nb, o_nb, st_nb = near_forward(1, limit, qkv, o_b)
    att_mine, att_send, log = join(place, o_na, o_nb, st_na, st_nb, o_a, o_b, got_oa, got_ob)
    att_got = lax.ppermute(att_send, "seq", core_pairs)

    block_out, fac, gout, tiny, back_resid, ba_own, ba_send = mixture(
        place,
        cluster_sharpness,
        x,
        att_mine,
        att_got,
        heed_exit_matrix,
        gain_m,
        router,
        position_cluster_label.reshape(1, tokens),
        upstream_derivative.reshape(tokens, width),
        specialist_entry_matrix,
        specialist_exit_matrix,
    )

    ba_got = lax.ppermute(ba_send, "seq", core_pairs)
    fac_got = swap(take(fac, 1 - core), 1)
    gout_got = swap(take(gout, 1 - core), 1)
    grads, inner, payload = ready(place, ba_own, ba_got, att_mine, att_send, log)
    got_grad = lax.ppermute(payload, "seq", down)
    pay = factors(place, fac, fac_got, gout, gout_got, payload)
    pays = [pay[0]] + [swap(pay[i], 2 * m[0] + 4 * m[1]) for i, m in list(enumerate(MOVES))[1:]]
    def near(h, dep):
        p, stat = ((p_na, st_na), (p_nb, st_nb))[h // 2]
        return near_backward(h, qkv, p, grads, stat, log, inner, dep)

    kv_0, dq_0 = near(0, (pay[0],))
    kv_1, dq_1 = near(1, (stay(dq_0),))
    stages = turns()
    kept, sent = slabs(place, dq_1, pays, width, hidden // 4, lines)
    send_fa, keep_fa = far_backward(0, place, q_a, kv_a, p_a, st_a, grads, log, inner, got_grad, kept)
    got_fa = lax.ppermute(send_fa, "seq", chip_pairs)
    for t, turn in enumerate(stages):
        got = swap_by_core(sent, turn)
        if t == len(stages) - 1:
            send_fb, keep_fb = far_backward(1, place, q_b, kv_b, p_b, st_b, grads, log, inner, got_grad, kept)
            got_fb = lax.ppermute(send_fb, "seq", chip_pairs)
            whole = fold(None, place, keep_fb, kept, got)[0]
        else:
            kept, sent = fold(stages[t + 1], place, keep_fa, kept, got)
    kv_2, dq_2 = near(2, (whole,))
    for turn in stages[:0:-1]:
        whole = pile(whole, swap_by_core(whole, turn), stay(dq_2))
    got = swap_by_core(whole, stages[0])
    kv_3, dq_3 = near(3, (whole, got_fa))
    whole = pile(whole, got, stay(dq_3), got_fb)
    got_first = swap_by_core(whole, PLANE[0])
    d_mine, d_send, *parts = collect(
        place, normed, (kv_0, kv_1, kv_2, kv_3), (dq_0, dq_1, dq_2, dq_3), keep_fa, keep_fb, got_fa, got_fb, packs, gain_a, tiny, whole
    )

    moves = [2 * m[0] + 4 * m[1] for m in MOVES]
    parts = parts[:1] + [swap(part, bits) for part, bits in list(zip(parts, moves))[1:]]
    d_got = lax.ppermute(d_send, "seq", core_pairs)
    parts = list(add(place, parts, lines))
    whole = pile(whole, got_first, parts[0])
    got_second = swap_by_core(whole, PLANE[1])
    far_first = swap(whole, 1)
    tokens_grad = tokens_back(place, d_mine, d_got, packs, x, back_resid, gain_a, whole)
    parts = parts[:1] + [swap(part, 8 * k) for k, part in list(enumerate(parts))[1:]]
    part = add(place, parts, 1, stay(tokens_grad))[0]
    block = (2, lines) + whole.shape[1:]
    halves = spread_experts(0, place, whole.reshape(block), far_first.reshape(block), hidden, width, (), part)
    zs = stack([part] + [swap(part, 8 * k) for k in range(1, lines)], stay(halves[2]))
    pieces = [zs] + [swap(zs, bits) for bits in moves[1:]]
    got_second = gate(got_second, zs)
    far_second = swap(got_second, 1)
    grad_in, grad_down, grad_out = spread_experts(
        1, place, got_second.reshape(block), far_second.reshape(block), hidden, width, tuple(halves)
    )
    pieces = stack(pieces, stay(grad_out))
    grad_qkv, grad_attn, grad_mix, grad_ctrl = unfold(place, pieces, swap(pieces, 1), width)
    return (
        block_out.reshape(layer_activations.shape),
        tokens_grad.reshape(layer_activations.shape),
        grad_attn.reshape(width),
        grad_qkv,
        grad_out.reshape(width, width),
        grad_mix.reshape(width),
        grad_ctrl.T,
        grad_in,
        grad_down,
    )


def solution(mesh):
    rows = P("batch", "seq", None)
    placed = (rows, P("batch"), P("batch", "seq")) + (P(),) * 8 + (rows,)
    return jax.shard_map(body, mesh=mesh, in_specs=placed, out_specs=(rows, rows) + (P(),) * 7, check_vma=False)
```
